32 devices in a mesh: wide: 8 (over z, y), narrow: 4 (over x, core).
Axes of the slice: x: 2, y: 2, z: 4, core: 2. Of those that a mesh axis runs over, the one named last changes fastest.
Arguments:
- units: bfloat16 [16384, 1024], P('wide'), may hold values from -6 to 6
- text: bfloat16 [4096, 1024], P('wide'), may hold values from -6 to 6
- out_grad: bfloat16 [16384, 1024], P('wide'), may hold values from -6 to 6
- unit_lengths: int32 [16], P('wide'), may hold values from 512 to 1024, as said below
- text_lengths: int32 [16], P('wide'), may hold values from 128 to 256
- bucket_counts: int32 [8], P('wide'), may hold values from 1 to 2
- norm_gain: float32 [3, 1024], replicated, may hold values from 0.25 to 1.75
- norm_shift: float32 [3, 1024], replicated, may hold values from -2 to 2
- self_qkv: bfloat16 [1024, 3, 1024], P(None, None, 'narrow'), may hold values from -0.1875 to 0.1875
- self_bias: float32 [2, 1024], P(None, 'narrow'), may hold values from -3 to 3
- self_out: bfloat16 [1024, 1024], P('narrow'), may hold values from -0.75 to 0.75
- cross_q: bfloat16 [1024, 1024], P(None, 'narrow'), may hold values from -0.1875 to 0.1875
- cross_kv: bfloat16 [1024, 2, 1024], P(None, None, 'narrow'), may hold values from -0.1875 to 0.1875
- cross_bias: float32 [2, 1024], P(None, 'narrow'), may hold values from -3 to 3
- cross_out: bfloat16 [1024, 1024], P('narrow'), may hold values from -0.75 to 0.75
- ffn_in: bfloat16 [1024, 8192], P(None, 'narrow'), may hold values from -0.1875 to 0.1875
- ffn_in_bias: float32 [8192], P('narrow'), may hold values from -3 to 3
- ffn_out: bfloat16 [8192, 1024], P('narrow'), may hold values from -0.0625 to 0.0625
- out_bias: float32 [3, 1024], replicated, may hold values from -3 to 3
Outputs:
- output: bfloat16 [16384, 1024], P(('wide', 'narrow'))
- units_grad: float32 [16384, 1024], P(('wide', 'narrow'))
- text_grad: float32 [4096, 1024], P(('wide', 'narrow'))
- norm_gain_grad: float32 [3, 1024], replicated
- norm_shift_grad: float32 [3, 1024], replicated
- self_qkv_grad: float32 [1024, 3, 1024], P(None, None, 'narrow')
- self_bias_grad: float32 [2, 1024], P(None, 'narrow')
- self_out_grad: float32 [1024, 1024], P('narrow')
- cross_q_grad: float32 [1024, 1024], P(None, 'narrow')
- cross_kv_grad: float32 [1024, 2, 1024], P(None, None, 'narrow')
- cross_bias_grad: float32 [2, 1024], P(None, 'narrow')
- cross_out_grad: float32 [1024, 1024], P('narrow')
- ffn_in_grad: float32 [1024, 8192], P(None, 'narrow')
- ffn_in_bias_grad: float32 [8192], P('narrow')
- ffn_out_grad: float32 [8192, 1024], P('narrow')
- out_bias_grad: float32 [3, 1024], replicated
The draws below stay inside these ranges and needn't reach their ends.
Inputs may be any that keep to these rules, and one draw needn't show every extreme that they name: `unit_lengths`: A multiple of 256; slots at or past their bucket's count hold no sequence.
All inputs are finite; a program needn't handle non-finite values.
Results may differ from the reference program's by a relative error of at most 0.03.
Values may be sent and summed in bfloat16 or wider, within the bound.
A program may use at most 192 MiB of HBM per device.

```python
import jax
import jax.numpy as jnp
from jax import lax

D = 1024
HEADS = 16
HEAD_DIM = 64
FF = 8192
SLOTS = 2
UNITS = 1024
TEXT = 256
ROWS = 16384
TEXT_ROWS = 4096
N_WIDE = 8
N_NARROW = 4


def force_two(values, key, high_value, low_value):
    shuffled = jax.random.permutation(key, values.shape[0])
    values = values.at[shuffled[0]].set(high_value)
    return values.at[shuffled[1]].set(low_value)


def draw_unit_lengths(key, part):
    count_all = N_WIDE * SLOTS
    quarters = jax.random.randint(jax.random.fold_in(key, 11), (count_all,), 2, 5)
    values = (quarters * (UNITS // 4)).astype(jnp.int32)
    return force_two(values, jax.random.fold_in(key, 12), UNITS, UNITS // 2)


def draw_text_lengths(key, part):
    count_all = N_WIDE * SLOTS
    values = jax.random.randint(jax.random.fold_in(key, 21), (count_all,), TEXT // 2, TEXT + 1).astype(jnp.int32)
    return force_two(values, jax.random.fold_in(key, 22), TEXT, TEXT // 2)


def draw_bucket_counts(key, part):
    values = jax.random.randint(jax.random.fold_in(key, 31), (N_WIDE,), 1, SLOTS + 1).astype(jnp.int32)
    return force_two(values, jax.random.fold_in(key, 32), SLOTS, 1)


def block_levels(key, shape, pieces, smallest, largest):
    level = 1.0
    for dim, parts in pieces:
        steps = jax.random.uniform(jax.random.fold_in(jax.random.fold_in(key, 6), dim), (parts,), jnp.float32, smallest / len(pieces), largest / len(pieces))
        level = level * jnp.repeat(jnp.exp(steps), shape[dim] // parts).reshape((-1,) + (1,) * (len(shape) - 1 - dim))
    return level


def normal_values(own_key, extent, scale, limit, pieces=(), kind=jnp.bfloat16):
    level = block_levels(own_key, extent, pieces, -0.22, 0.18) if pieces else 1.0
    drawn = jax.random.normal(own_key, extent, jnp.float32) * scale * level
    return jnp.minimum(jnp.maximum(drawn, -limit), limit).astype(kind)


def setup_inputs(seed: int = 0) -> dict:
    streams_of = jax.random.split(jax.random.key(seed), 20)
    units = normal_values(streams_of[0], (ROWS, D), 1.0, 6.0, ((0, 8),))
    text = normal_values(streams_of[1], (TEXT_ROWS, D), 1.0, 6.0, ((0, 8),))
    out_grad = normal_values(streams_of[2], (ROWS, D), 1.0, 6.0, ((0, 8),))
    unit_lengths = draw_unit_lengths(jax.random.fold_in(streams_of[19], 71), 0)
    text_lengths = draw_text_lengths(jax.random.fold_in(streams_of[19], 71), 0)
    bucket_counts = draw_bucket_counts(jax.random.fold_in(streams_of[19], 71), 0)
    norm_gain = jnp.clip(1.0 + 0.15 * jax.random.normal(streams_of[6], (3, D), jnp.float32), 0.25, 1.75)
    norm_shift = normal_values(streams_of[7], (3, D), 0.3, 2.0, (), jnp.float32)
    self_qkv = normal_values(streams_of[8], (D, 3, D), D ** -0.5, 0.1875, ((2, 4),))
    self_bias = normal_values(streams_of[9], (2, D), 0.5, 3.0, ((1, 4),), jnp.float32)
    self_out = normal_values(streams_of[10], (D, D), (D // 16) ** -0.5, 0.75, ((0, 4),))
    cross_q = normal_values(streams_of[11], (D, D), D ** -0.5, 0.1875, ((1, 4),))
    cross_kv = normal_values(streams_of[12], (D, 2, D), D ** -0.5, 0.1875, ((2, 4),))
    cross_bias = normal_values(streams_of[13], (2, D), 0.5, 3.0, ((1, 4),), jnp.float32)
    cross_out = normal_values(streams_of[14], (D, D), (D // 16) ** -0.5, 0.75, ((0, 4),))
    ffn_in = normal_values(streams_of[15], (D, FF), D ** -0.5, 0.1875, ((1, 4),))
    ffn_in_bias = normal_values(streams_of[16], (FF,), 0.5, 3.0, ((0, 4),), jnp.float32)
    ffn_out = normal_values(streams_of[17], (FF, D), FF ** -0.5, 0.0625, ((0, 4),))
    out_bias = normal_values(streams_of[18], (3, D), 0.5, 3.0, (), jnp.float32)
    return dict(units=units, text=text, out_grad=out_grad, unit_lengths=unit_lengths, text_lengths=text_lengths, bucket_counts=bucket_counts, norm_gain=norm_gain, norm_shift=norm_shift, self_qkv=self_qkv, self_bias=self_bias, self_out=self_out, cross_q=cross_q, cross_kv=cross_kv, cross_bias=cross_bias, cross_out=cross_out, ffn_in=ffn_in, ffn_in_bias=ffn_in_bias, ffn_out=ffn_out, out_bias=out_bias)


NORM_EPSILON = 1e-05
MASKED_SCORE = -1000000000.0
EXACT = lax.Precision.HIGHEST

@jax.custom_vjp
def low(v):
    return lax.optimization_barrier(v.astype(jnp.bfloat16)).astype(jnp.float32)

@jax.custom_vjp
def low_back(v):
    return v

def low_keep(v):
    return (low(v), None)

def low_pass(kept, grad):
    return (grad,)

def back_keep(v):
    return (v, None)

def back_low(kept, grad):
    return (low(grad),)
low.defvjp(low_keep, low_pass)
low_back.defvjp(back_keep, back_low)

def both_ways(values):
    return low(low_back(values))

def smooth_gate(values):
    return jax.nn.gelu(values, approximate=False)

def layer_norm(values, gain_vec, shift_vec):
    row_mean = lax.optimization_barrier(jnp.mean(values, axis=-1, keepdims=True))
    centered = values - row_mean
    variance = lax.optimization_barrier(jnp.mean(centered * centered, axis=-1, keepdims=True))
    return centered * lax.rsqrt(variance + NORM_EPSILON) * gain_vec + shift_vec

def attend(queries, key_rows, value_rows, allowed):
    scores = jnp.einsum('qhd,khd->hqk', queries, key_rows, precision=EXACT) * HEAD_DIM ** (-0.5)
    scores = jnp.where(allowed[None], scores, MASKED_SCORE)
    weights = low(jax.nn.softmax(scores, axis=-1))
    return jnp.einsum('hqk,khd->qhd', weights, value_rows, precision=EXACT)

def slot_attention(queries, key_rows, value_rows, lengths, key_count, causal):
    query_block = min(512, UNITS)
    key_pos = jnp.arange(key_count, dtype=jnp.int32)

    def one_slot(packed):
        slot_queries, slot_keys, slot_values, length = packed

        def one_block(first_row):
            rows_here = first_row + jnp.arange(query_block, dtype=jnp.int32)
            block_queries = lax.dynamic_slice_in_dim(slot_queries, first_row, query_block, 0)
            if causal:
                before = key_pos[None, :] <= rows_here[:, None]
                allowed = before & ((key_pos[None, :] < length) | (key_pos[None, :] == rows_here[:, None]))
            else:
                allowed = jnp.broadcast_to(key_pos[None, :] < length, (query_block, key_count))
            return attend(block_queries, slot_keys, slot_values, allowed)
        firsts = jnp.arange(UNITS // query_block, dtype=jnp.int32) * query_block
        return lax.map(jax.checkpoint(one_block), firsts).reshape(UNITS, HEADS, HEAD_DIM)
    packed_all = (queries.reshape(SLOTS, UNITS, HEADS, HEAD_DIM), key_rows.reshape(SLOTS, key_count, HEADS, HEAD_DIM), value_rows.reshape(SLOTS, key_count, HEADS, HEAD_DIM), lengths)
    return lax.map(one_slot, packed_all).reshape(SLOTS * UNITS, D)

def split_heads(values):
    return values.reshape(values.shape[0], HEADS, HEAD_DIM)

def group_forward(params, units, text, lengths, text_len, row_valid):
    row_count = units.shape[0]
    text_count = text.shape[0]
    column_count = D // N_NARROW
    hidden_count = FF // N_NARROW
    norm_gains = params['norm_gain']
    shifts = params['norm_shift']
    biases = params['out_bias']
    first_in = low(layer_norm(units, norm_gains[0], shifts[0]))
    first_copies = low_back(jnp.broadcast_to(first_in, (N_NARROW, row_count, D)))
    projected = jnp.einsum('grd,dcgn->rcgn', first_copies, params['self_qkv'].reshape(D, 3, N_NARROW, column_count), precision=EXACT).reshape(row_count, 3, D)
    queries = both_ways(projected[:, 0] + params['self_bias'][0])
    key_rows = both_ways(projected[:, 1])
    value_rows = both_ways(projected[:, 2] + params['self_bias'][1])
    context = both_ways(slot_attention(split_heads(queries), split_heads(key_rows), split_heads(value_rows), lengths, UNITS, True))
    self_parts = low(jnp.einsum('rgn,gnd->grd', context.reshape(row_count, N_NARROW, column_count), params['self_out'].reshape(N_NARROW, column_count, D), precision=EXACT))
    resid_one = units + low_back(lax.optimization_barrier(jnp.sum(self_parts, axis=0))) + biases[0]
    second_in = low(layer_norm(resid_one, norm_gains[1], shifts[1]))
    second_copies = low_back(jnp.broadcast_to(second_in, (N_NARROW, row_count, D)))
    cross_queries = jnp.einsum('grd,dgn->rgn', second_copies, params['cross_q'].reshape(D, N_NARROW, column_count), precision=EXACT).reshape(row_count, D)
    cross_queries = both_ways(cross_queries + params['cross_bias'][0])
    text_copies = low_back(jnp.broadcast_to(text, (N_NARROW, text_count, D)))
    text_proj = jnp.einsum('gtd,dcgn->tcgn', text_copies, params['cross_kv'].reshape(D, 2, N_NARROW, column_count), precision=EXACT).reshape(text_count, 2, D)
    text_keys = both_ways(text_proj[:, 0])
    text_values = both_ways(text_proj[:, 1] + params['cross_bias'][1])
    cross_context = both_ways(slot_attention(split_heads(cross_queries), split_heads(text_keys), split_heads(text_values), text_len, TEXT, False))
    cross_parts = low(jnp.einsum('rgn,gnd->grd', cross_context.reshape(row_count, N_NARROW, column_count), params['cross_out'].reshape(N_NARROW, column_count, D), precision=EXACT))
    resid_two = resid_one + low_back(lax.optimization_barrier(jnp.sum(cross_parts, axis=0))) + biases[1]
    third_in = low(layer_norm(resid_two, norm_gains[2], shifts[2]))
    third_copies = low_back(jnp.broadcast_to(third_in, (N_NARROW, row_count, D)))
    hidden_pre = jnp.einsum('grd,dgn->rgn', third_copies, params['ffn_in'].reshape(D, N_NARROW, hidden_count), precision=EXACT).reshape(row_count, FF) + params['ffn_in_bias']
    hidden = low(smooth_gate(low_back(hidden_pre)))
    ffn_parts = low(jnp.einsum('rgn,gnd->grd', hidden.reshape(row_count, N_NARROW, hidden_count), params['ffn_out'].reshape(N_NARROW, hidden_count, D), precision=EXACT))
    return (resid_two + low_back(lax.optimization_barrier(jnp.sum(ffn_parts, axis=0))) + biases[2]) * row_valid

def reference(units, text, out_grad, unit_lengths, text_lengths, bucket_counts, norm_gain, norm_shift, self_qkv, self_bias, self_out, cross_q, cross_kv, cross_bias, cross_out, ffn_in, ffn_in_bias, ffn_out, out_bias):
    params = {'norm_gain': norm_gain.astype(jnp.float32), 'norm_shift': norm_shift.astype(jnp.float32), 'self_qkv': self_qkv.astype(jnp.float32), 'self_bias': self_bias.astype(jnp.float32), 'self_out': self_out.astype(jnp.float32), 'cross_q': cross_q.astype(jnp.float32), 'cross_kv': cross_kv.astype(jnp.float32), 'cross_bias': cross_bias.astype(jnp.float32), 'cross_out': cross_out.astype(jnp.float32), 'ffn_in': ffn_in.astype(jnp.float32), 'ffn_in_bias': ffn_in_bias.astype(jnp.float32), 'ffn_out': ffn_out.astype(jnp.float32), 'out_bias': out_bias.astype(jnp.float32)}
    group_rows = SLOTS * UNITS
    unit_groups = units.astype(jnp.float32).reshape(N_WIDE, group_rows, D)
    text_groups = text.astype(jnp.float32).reshape(N_WIDE, SLOTS * TEXT, D)
    grad_groups = out_grad.astype(jnp.float32).reshape(N_WIDE, group_rows, D)
    slot_live = jnp.arange(SLOTS, dtype=jnp.int32)[None, :] < bucket_counts[:, None]
    length_groups = jnp.where(slot_live, unit_lengths.reshape(N_WIDE, SLOTS), 0).astype(jnp.int32)
    text_len_groups = text_lengths.reshape(N_WIDE, SLOTS)
    positions = jnp.arange(group_rows, dtype=jnp.int32)

    def one_group(totals, packed):
        unit_rows, text_rows, grad_rows, lengths, text_len = packed
        row_limit = lengths[positions // UNITS]
        row_valid = (positions % UNITS < row_limit).astype(jnp.float32)[:, None]

        def forward(weights, unit_in, text_in):
            return group_forward(weights, unit_in, text_in, lengths, text_len, row_valid)
        result, pullback = jax.vjp(forward, params, unit_rows, text_rows)
        param_grads, unit_grad, text_grad = pullback(grad_rows)
        totals = jax.tree.map(jnp.add, totals, param_grads)
        return (totals, (result, unit_grad, text_grad))
    zero_grads = jax.tree.map(jnp.zeros_like, params)
    totals, stacked = lax.scan(one_group, zero_grads, (unit_groups, text_groups, grad_groups, length_groups, text_len_groups))
    results, unit_grads, text_grads = stacked
    return (results.reshape(N_WIDE * group_rows, D).astype(jnp.bfloat16), unit_grads.reshape(N_WIDE * group_rows, D), text_grads.reshape(N_WIDE * SLOTS * TEXT, D), totals['norm_gain'], totals['norm_shift'], totals['self_qkv'], totals['self_bias'], totals['self_out'], totals['cross_q'], totals['cross_kv'], totals['cross_bias'], totals['cross_out'], totals['ffn_in'], totals['ffn_in_bias'], totals['ffn_out'], totals['out_bias'])
```

```python
import jax
import jax.numpy as jnp
from jax import lax
from jax.experimental import pallas as pl
from jax.experimental.pallas import tpu as pltpu
from jax.sharding import PartitionSpec as P

HEAD_DIM = 64
UNITS = 1024
TEXT = 256


NORM_EPSILON = 1e-05
MASKED_SCORE = -1000000000.0
EXACT = lax.Precision.HIGHEST


def smooth_gate(values):
    return jax.nn.gelu(values, approximate=False)


def norm_forward(values, gain_vec, shift_vec):
    row_mean = jnp.mean(values, axis=-1, keepdims=True)
    centered = values - row_mean
    inv_std = lax.rsqrt(jnp.mean(centered * centered, axis=-1, keepdims=True) + NORM_EPSILON)
    normed = centered * inv_std
    return (normed * gain_vec + shift_vec, normed, inv_std)


def norm_backward(grad_in, normed, inv_std, gain_vec):
    scaled = grad_in * gain_vec
    inner_term = scaled - jnp.mean(scaled, axis=-1, keepdims=True)
    inner_term = inner_term - normed * jnp.mean(scaled * normed, axis=-1, keepdims=True)
    return inner_term * inv_std


def split_heads(values):
    return values.reshape(values.shape[0], -1, HEAD_DIM)


def block_slices(block_index, queries, key_rows, value_rows, key_count, query_block):
    per_slot = UNITS // query_block
    slot_id = block_index // per_slot
    first_row = block_index * query_block
    block_queries = lax.dynamic_slice_in_dim(queries, first_row, query_block, 0)
    block_keys = lax.dynamic_slice_in_dim(key_rows, slot_id * key_count, key_count, 0)
    block_values = lax.dynamic_slice_in_dim(value_rows, slot_id * key_count, key_count, 0)
    return (slot_id, first_row - slot_id * UNITS, block_queries, block_keys, block_values)


def masked_scores(block_queries, block_keys, allowed, score_scale):
    scores = (
        jnp.einsum("qhd,khd->hqk", block_queries, block_keys, preferred_element_type=jnp.float32)
        * score_scale
    )
    return jnp.where(allowed[None], scores, MASKED_SCORE)


def attention_forward(
    queries, key_rows, value_rows, key_count, query_block, score_scale, allowed_fn
):

    def one_block(block_index):
        slot_id, offset, block_queries, block_keys, block_values = block_slices(
            block_index, queries, key_rows, value_rows, key_count, query_block
        )
        scores = masked_scores(block_queries, block_keys, allowed_fn(slot_id, offset), score_scale)
        row_max = jnp.max(scores, axis=-1, keepdims=True)
        exp_scores = jnp.exp(scores - row_max)
        row_total = jnp.sum(exp_scores, axis=-1, keepdims=True)
        weights = (exp_scores / row_total).astype(jnp.bfloat16)
        context = jnp.einsum(
            "hqk,khd->qhd", weights, block_values, preferred_element_type=jnp.float32
        )
        return (context, (row_max + jnp.log(row_total))[:, :, 0])

    block_total = queries.shape[0] // query_block
    context, log_total = lax.map(one_block, jnp.arange(block_total, dtype=jnp.int32))
    return (context.reshape(queries.shape[0], -1), log_total)


def attention_backward(
    queries,
    key_rows,
    value_rows,
    context_grad,
    log_total,
    key_count,
    query_block,
    score_scale,
    allowed_fn,
):

    def one_block(packed):
        block_index, block_log = packed
        slot_id, offset, block_queries, block_keys, block_values = block_slices(
            block_index, queries, key_rows, value_rows, key_count, query_block
        )
        block_grad = lax.dynamic_slice_in_dim(
            context_grad, block_index * query_block, query_block, 0
        )
        scores = masked_scores(block_queries, block_keys, allowed_fn(slot_id, offset), score_scale)
        weights = jnp.exp(scores - block_log[:, :, None])
        value_grad = jnp.einsum(
            "hqk,qhd->khd",
            weights.astype(jnp.bfloat16),
            block_grad,
            preferred_element_type=jnp.float32,
        )
        weight_grad = jnp.einsum(
            "qhd,khd->hqk", block_grad, block_values, preferred_element_type=jnp.float32
        )
        score_grad = weights * (
            weight_grad - jnp.sum(weights * weight_grad, axis=-1, keepdims=True)
        )
        query_grad = (
            jnp.einsum("hqk,khd->qhd", score_grad, block_keys.astype(jnp.float32), precision=EXACT)
            * score_scale
        )
        key_grad = (
            jnp.einsum(
                "hqk,qhd->khd", score_grad, block_queries.astype(jnp.float32), precision=EXACT
            )
            * score_scale
        )
        return (query_grad, key_grad, value_grad)

    row_count = queries.shape[0]
    block_total = row_count // query_block
    per_slot = UNITS // query_block
    slot_count = row_count // UNITS
    query_grad, key_grad, value_grad = lax.map(
        one_block, (jnp.arange(block_total, dtype=jnp.int32), log_total)
    )
    query_grad = query_grad.reshape(row_count, -1)
    key_grad = jnp.sum(key_grad.reshape(slot_count, per_slot, key_count, -1), axis=1).reshape(
        slot_count * key_count, -1
    )
    value_grad = jnp.sum(value_grad.reshape(slot_count, per_slot, key_count, -1), axis=1).reshape(
        slot_count * key_count, -1
    )
    return (query_grad, key_grad, value_grad)


BLOCK = 256
MIB = 1 << 20


def head_mask(shape, head):
    lane = lax.broadcasted_iota(jnp.int32, shape, len(shape) - 1)
    return (lane >= head * HEAD_DIM) & (lane < (head + 1) * HEAD_DIM)


def pick_head(values, head):
    return jnp.where(head_mask(values.shape, head), values, jnp.zeros_like(values))


def dot_nt(a, b):
    return lax.dot_general(a, b, (((1,), (1,)), ((), ())), preferred_element_type=jnp.float32)


def dot_nn(a, b):
    return jnp.dot(a, b, preferred_element_type=jnp.float32)


def dot_tn(a, b):
    return lax.dot_general(a, b, (((0,), (0,)), ((), ())), preferred_element_type=jnp.float32)


def front_kernel(lens, x_ref, g_ref, s_ref, w_ref, qb_ref, vb_ref, h_ref, q_ref, k_ref, v_ref, c_ref):
    length = lens[pl.program_id(0)]
    width = q_ref.shape[1]
    for i in range(x_ref.shape[0] // BLOCK):
        rows = pl.ds(i * BLOCK, BLOCK)

        @pl.when(i * BLOCK < length)
        def _():
            normed, _, _ = norm_forward(x_ref[rows, :].astype(jnp.float32), g_ref[...], s_ref[...])
            h1 = normed.astype(jnp.bfloat16)
            h_ref[rows, :] = h1
            qkv = dot_nn(h1, w_ref[...])
            queries = (qkv[:, :width] + qb_ref[...]).astype(jnp.bfloat16)
            q_ref[rows, :] = queries
            k_ref[rows, :] = qkv[:, width : 2 * width].astype(jnp.bfloat16)
            v_ref[rows, :] = (qkv[:, 2 * width :] + vb_ref[...]).astype(jnp.bfloat16)
            count = (i + 1) * BLOCK
            keys, values = k_ref[:count, :], v_ref[:count, :]
            scaled = queries * jnp.bfloat16(HEAD_DIM**-0.5)
            row = lax.broadcasted_iota(jnp.int32, (BLOCK, count), 0) + i * BLOCK
            allowed = lax.broadcasted_iota(jnp.int32, (BLOCK, count), 1) <= row
            total = jnp.zeros((BLOCK, width), jnp.float32)
            for head in range(width // HEAD_DIM):
                scores = jnp.where(allowed, dot_nt(pick_head(scaled, head), keys), MASKED_SCORE)
                weights = jnp.exp(scores - jnp.max(scores, axis=1, keepdims=True))
                weights = weights * (1.0 / jnp.sum(weights, axis=1, keepdims=True))
                total += dot_nn(weights.astype(jnp.bfloat16), pick_head(values, head))
            c_ref[rows, :] = total.astype(jnp.bfloat16)

        @pl.when(i * BLOCK >= length)
        def _():
            for ref in (h_ref, q_ref, k_ref, v_ref, c_ref):
                ref[rows, :] = jnp.zeros((BLOCK, ref.shape[1]), ref.dtype)


def front(lengths, units, gain_vec, shift_vec, weights, q_bias, v_bias):
    rows, width = units.shape
    slots = lengths.shape[0]
    slot_rows = rows // slots
    cols = weights.shape[1] // 3
    whole = lambda a: pl.BlockSpec(a.shape, lambda s, *_: (0,) * a.ndim)
    slot = lambda w: pl.BlockSpec((slot_rows, w), lambda s, *_: (s, 0))
    small = [a.reshape(1, -1) for a in (gain_vec, shift_vec, q_bias, v_bias)]
    shape = lambda w: jax.ShapeDtypeStruct((rows, w), jnp.bfloat16)
    return pl.pallas_call(
        front_kernel,
        grid_spec=pltpu.PrefetchScalarGridSpec(
            num_scalar_prefetch=1,
            grid=(slots,),
            in_specs=[slot(width), whole(small[0]), whole(small[1]), whole(weights), whole(small[2]), whole(small[3])],
            out_specs=[slot(width), slot(cols), slot(cols), slot(cols), slot(cols)],
        ),
        out_shape=[shape(width), shape(cols), shape(cols), shape(cols), shape(cols)],
        compiler_params=pltpu.CompilerParams(vmem_limit_bytes=48 * MIB),
        cost_estimate=pl.CostEstimate(flops=20 * 10**9, bytes_accessed=16 * MIB, transcendentals=8 * MIB),
        name="front",
    )(lengths, units, small[0], small[1], weights, small[2], small[3])


def back_kernel(lens, q_ref, k_ref, v_ref, dc_ref, o_ref, dk_acc, dv_acc):
    length = lens[pl.program_id(0)]
    slot_rows, width = q_ref.shape
    dk_acc[...] = jnp.zeros_like(dk_acc)
    dv_acc[...] = jnp.zeros_like(dv_acc)
    for i in range(slot_rows // BLOCK):
        rows = pl.ds(i * BLOCK, BLOCK)

        @pl.when(i * BLOCK < length)
        def _():
            count = (i + 1) * BLOCK
            keys, values = k_ref[:count, :], v_ref[:count, :]
            scaled = q_ref[rows, :] * jnp.bfloat16(HEAD_DIM**-0.5)
            grads = dc_ref[rows, :]
            col = lax.broadcasted_iota(jnp.int32, (count, BLOCK), 1) + i * BLOCK
            allowed = lax.broadcasted_iota(jnp.int32, (count, BLOCK), 0) <= col
            total = jnp.zeros((BLOCK, width), jnp.float32)
            for head in range(width // HEAD_DIM):
                q_head, g_head = pick_head(scaled, head), pick_head(grads, head)
                scores = jnp.where(allowed, dot_nt(keys, q_head), MASKED_SCORE)
                weights = jnp.exp(scores - jnp.max(scores, axis=0, keepdims=True))
                weights = weights * (1.0 / jnp.sum(weights, axis=0, keepdims=True))
                dv_acc[:count, :] += dot_nn(weights.astype(jnp.bfloat16), g_head)
                weight_grad = dot_nt(values, g_head)
                inner = jnp.sum(weights * weight_grad, axis=0, keepdims=True)
                score_grad = (weights * (weight_grad - inner)).astype(jnp.bfloat16)
                dk_acc[:count, :] += dot_nn(score_grad, q_head)
                total += dot_tn(score_grad, pick_head(keys, head))
            o_ref[rows, :width] = (total * HEAD_DIM**-0.5).astype(jnp.bfloat16)

        @pl.when(i * BLOCK >= length)
        def _():
            o_ref[rows, :width] = jnp.zeros((BLOCK, width), jnp.bfloat16)

    o_ref[:, width : 2 * width] = dk_acc[...].astype(jnp.bfloat16)
    o_ref[:, 2 * width :] = dv_acc[...].astype(jnp.bfloat16)


def back(lengths, queries, keys, values, grads):
    rows, width = queries.shape
    slots = lengths.shape[0]
    slot_rows = rows // slots
    slot = lambda w: pl.BlockSpec((slot_rows, w), lambda s, *_: (s, 0))
    return pl.pallas_call(
        back_kernel,
        grid_spec=pltpu.PrefetchScalarGridSpec(
            num_scalar_prefetch=1,
            grid=(slots,),
            in_specs=[slot(width)] * 4,
            out_specs=slot(3 * width),
            scratch_shapes=[pltpu.VMEM((slot_rows, width), jnp.float32)] * 2,
        ),
        out_shape=jax.ShapeDtypeStruct((rows, 3 * width), jnp.bfloat16),
        compiler_params=pltpu.CompilerParams(vmem_limit_bytes=48 * MIB),
        cost_estimate=pl.CostEstimate(flops=30 * 10**9, bytes_accessed=8 * MIB, transcendentals=8 * MIB),
        name="back",
    )(lengths, queries, keys, values, grads)


def wide_sum(arrays, after=None):
    parts = tuple(a.astype(jnp.bfloat16) for a in arrays)
    if after is not None:
        parts, after = lax.optimization_barrier((parts, after))
    return lax.psum(parts, "wide"), after


def local(
    units,
    text,
    out_grad,
    unit_lengths,
    text_lengths,
    bucket_counts,
    norm_gain,
    norm_shift,
    self_qkv,
    self_bias,
    self_out,
    cross_q,
    cross_kv,
    cross_bias,
    cross_out,
    ffn_in,
    ffn_in_bias,
    ffn_out,
    out_bias,
):
    narrow_size = lax.axis_size("narrow")
    narrow_index = lax.axis_index("narrow")
    group_rows = units.shape[0]
    own_rows = group_rows // narrow_size
    first_own = narrow_index * own_rows
    slot_count = unit_lengths.shape[0]
    score_scale = HEAD_DIM ** (-0.5)
    query_block = min(512, UNITS)
    slot_live = jnp.arange(slot_count, dtype=jnp.int32) < bucket_counts[0]
    lengths = jnp.where(slot_live, unit_lengths, 0)
    positions = jnp.arange(group_rows, dtype=jnp.int32)
    slot_match = (positions // UNITS)[:, None] == jnp.arange(slot_count, dtype=jnp.int32)[None, :]
    row_limit = jnp.sum(jnp.where(slot_match, lengths[None, :], 0), axis=1)
    row_valid = positions % UNITS < row_limit
    valid_own = lax.dynamic_slice_in_dim(row_valid, first_own, own_rows, 0)
    unit_pos = jnp.arange(UNITS, dtype=jnp.int32)
    text_pos = jnp.arange(TEXT, dtype=jnp.int32)

    def self_allowed(slot_id, offset):
        rows_here = offset + jnp.arange(query_block, dtype=jnp.int32)
        length = lax.dynamic_index_in_dim(lengths, slot_id, keepdims=False)
        before = unit_pos[None, :] <= rows_here[:, None]
        return before & ((unit_pos[None, :] < length) | (unit_pos[None, :] == rows_here[:, None]))

    def cross_allowed(slot_id, offset):
        length = lax.dynamic_index_in_dim(text_lengths, slot_id, keepdims=False)
        return jnp.broadcast_to(text_pos[None, :] < length, (query_block, TEXT))

    qkv_weights = self_qkv.reshape(self_qkv.shape[0], -1)
    first_in, queries, key_rows, value_rows, self_context = front(
        lengths, units, norm_gain[0], norm_shift[0], qkv_weights, self_bias[0], self_bias[1]
    )
    own_units = lax.dynamic_slice_in_dim(units, first_own, own_rows, 0).astype(jnp.float32)
    _, normed_one, inv_one = norm_forward(own_units, norm_gain[0], norm_shift[0])
    self_sum = lax.psum_scatter(
        jnp.dot(self_context, self_out, preferred_element_type=jnp.float32).astype(jnp.bfloat16),
        "narrow",
        scatter_dimension=0,
        tiled=True,
    ).astype(jnp.float32)
    resid_one = own_units + self_sum + out_bias[0]
    norm_two, normed_two, inv_two = norm_forward(resid_one, norm_gain[1], norm_shift[1])
    second_all = lax.all_gather(norm_two.astype(jnp.bfloat16), "narrow", axis=0, tiled=True)
    cross_queries = (
        jnp.dot(second_all, cross_q, preferred_element_type=jnp.float32) + cross_bias[0]
    ).astype(jnp.bfloat16)
    text_proj = jnp.einsum("td,dcn->tcn", text, cross_kv, preferred_element_type=jnp.float32)
    text_keys = text_proj[:, 0].astype(jnp.bfloat16)
    text_values = (text_proj[:, 1] + cross_bias[1]).astype(jnp.bfloat16)
    cross_context, cross_log = attention_forward(
        split_heads(cross_queries),
        split_heads(text_keys),
        split_heads(text_values),
        TEXT,
        query_block,
        score_scale,
        cross_allowed,
    )
    cross_context = cross_context.astype(jnp.bfloat16)
    cross_sum = lax.psum_scatter(
        jnp.dot(cross_context, cross_out, preferred_element_type=jnp.float32).astype(jnp.bfloat16),
        "narrow",
        scatter_dimension=0,
        tiled=True,
    ).astype(jnp.float32)
    resid_two = resid_one + cross_sum + out_bias[1]
    norm_three, normed_three, inv_three = norm_forward(resid_two, norm_gain[2], norm_shift[2])
    third_all = lax.all_gather(norm_three.astype(jnp.bfloat16), "narrow", axis=0, tiled=True)
    hidden_pre = jnp.dot(third_all, ffn_in, preferred_element_type=jnp.float32) + ffn_in_bias
    hidden_full, gate_pullback = jax.vjp(smooth_gate, hidden_pre)
    hidden = hidden_full.astype(jnp.bfloat16)
    ffn_sum = lax.psum_scatter(
        jnp.dot(hidden, ffn_out, preferred_element_type=jnp.float32).astype(jnp.bfloat16),
        "narrow",
        scatter_dimension=0,
        tiled=True,
    ).astype(jnp.float32)
    output = jnp.where(valid_own[:, None], resid_two + ffn_sum + out_bias[2], 0.0).astype(
        jnp.bfloat16
    )
    grad_all = jnp.where(row_valid[:, None], out_grad, jnp.zeros_like(out_grad))
    grad_two = lax.dynamic_slice_in_dim(grad_all, first_own, own_rows, 0).astype(jnp.float32)
    ffn_out_grad = jnp.einsum("rf,rd->fd", hidden, grad_all, preferred_element_type=jnp.float32)
    hidden_grad = jnp.einsum("rd,fd->rf", grad_all, ffn_out, preferred_element_type=jnp.float32)
    pre_grad = gate_pullback(hidden_grad)[0].astype(jnp.bfloat16)
    ffn_in_bias_grad = jnp.sum(pre_grad, axis=0, dtype=jnp.float32)
    ffn_in_grad = jnp.einsum("rd,rf->df", third_all, pre_grad, preferred_element_type=jnp.float32)
    third_part = jnp.einsum("rf,df->rd", pre_grad, ffn_in, preferred_element_type=jnp.float32)
    third_grad = lax.psum_scatter(
        third_part.astype(jnp.bfloat16), "narrow", scatter_dimension=0, tiled=True
    ).astype(jnp.float32)
    gain_three = jnp.sum(third_grad * normed_three, axis=0)
    shift_three = jnp.sum(third_grad, axis=0)
    resid_two_grad = grad_two + norm_backward(third_grad, normed_three, inv_three, norm_gain[2])
    bias_two_grad = jnp.sum(grad_two, axis=0)
    cross_out_all = lax.all_gather(
        resid_two_grad.astype(jnp.bfloat16), "narrow", axis=0, tiled=True
    )
    cross_out_grad = jnp.einsum(
        "rn,rd->nd", cross_context, cross_out_all, preferred_element_type=jnp.float32
    )
    cross_context_grad = jnp.einsum(
        "rd,nd->rn", cross_out_all, cross_out, preferred_element_type=jnp.float32
    ).astype(jnp.bfloat16)
    cross_query_grad, text_key_grad, text_value_grad = attention_backward(
        split_heads(cross_queries),
        split_heads(text_keys),
        split_heads(text_values),
        split_heads(cross_context_grad),
        cross_log,
        TEXT,
        query_block,
        score_scale,
        cross_allowed,
    )
    cross_query_grad = cross_query_grad.astype(jnp.bfloat16)
    text_kv_grad = jnp.stack([text_key_grad, text_value_grad], axis=1).astype(jnp.bfloat16)
    cross_q_grad = jnp.einsum(
        "rd,rn->dn", second_all, cross_query_grad, preferred_element_type=jnp.float32
    )
    cross_kv_grad = jnp.einsum(
        "td,tcn->dcn", text, text_kv_grad, preferred_element_type=jnp.float32
    )
    cross_bias_grad = jnp.stack(
        [
            jnp.sum(cross_query_grad, axis=0, dtype=jnp.float32),
            jnp.sum(text_kv_grad[:, 1], axis=0, dtype=jnp.float32),
        ]
    )
    second_part = jnp.einsum(
        "rn,dn->rd", cross_query_grad, cross_q, preferred_element_type=jnp.float32
    )
    text_part = jnp.einsum(
        "tcn,dcn->td", text_kv_grad, cross_kv, preferred_element_type=jnp.float32
    )
    second_grad, text_grad = (
        lax.psum_scatter(
            second_part.astype(jnp.bfloat16), "narrow", scatter_dimension=0, tiled=True
        ).astype(jnp.float32),
        lax.psum_scatter(
            text_part.astype(jnp.bfloat16), "narrow", scatter_dimension=0, tiled=True
        ).astype(jnp.float32),
    )
    gain_two = jnp.sum(second_grad * normed_two, axis=0)
    shift_two = jnp.sum(second_grad, axis=0)
    resid_one_grad = resid_two_grad + norm_backward(second_grad, normed_two, inv_two, norm_gain[1])
    bias_one_grad = jnp.sum(resid_two_grad, axis=0)
    self_out_all = lax.all_gather(resid_one_grad.astype(jnp.bfloat16), "narrow", axis=0, tiled=True)
    self_out_grad = jnp.einsum(
        "rn,rd->nd", self_context, self_out_all, preferred_element_type=jnp.float32
    )
    self_context_grad = jnp.einsum(
        "rd,nd->rn", self_out_all, self_out, preferred_element_type=jnp.float32
    ).astype(jnp.bfloat16)
    qkv_grad = back(lengths, queries, key_rows, value_rows, self_context_grad)
    self_qkv_grad = dot_tn(first_in, qkv_grad).reshape(self_qkv.shape)
    cols = queries.shape[1]
    self_bias_grad = jnp.stack(
        [
            jnp.sum(qkv_grad[:, :cols], axis=0, dtype=jnp.float32),
            jnp.sum(qkv_grad[:, 2 * cols :], axis=0, dtype=jnp.float32),
        ]
    )
    first_part = dot_nt(qkv_grad, qkv_weights)
    first_grad = lax.psum_scatter(
        first_part.astype(jnp.bfloat16), "narrow", scatter_dimension=0, tiled=True
    ).astype(jnp.float32)
    gain_one = jnp.sum(first_grad * normed_one, axis=0)
    shift_one = jnp.sum(first_grad, axis=0)
    units_grad = resid_one_grad + norm_backward(first_grad, normed_one, inv_one, norm_gain[0])
    bias_zero_grad = jnp.sum(resid_one_grad, axis=0)
    small_sums = lax.psum(
        jnp.stack(
            [
                gain_one,
                gain_two,
                gain_three,
                shift_one,
                shift_two,
                shift_three,
                bias_zero_grad,
                bias_one_grad,
                bias_two_grad,
            ]
        ),
        ("wide", "narrow"),
    )
    (ffn_in_grad, ffn_out_grad), _ = wide_sum((ffn_in_grad, ffn_out_grad))
    (cross_q_grad, cross_kv_grad, cross_out_grad), ffn_in_grad = wide_sum(
        (cross_q_grad, cross_kv_grad, cross_out_grad), ffn_in_grad
    )
    (self_qkv_grad, self_out_grad), cross_q_grad = wide_sum((self_qkv_grad, self_out_grad), cross_q_grad)
    self_bias_grad, cross_bias_grad, ffn_in_bias_grad = lax.psum(
        (self_bias_grad, cross_bias_grad, ffn_in_bias_grad), "wide"
    )
    (
        self_qkv_grad,
        self_out_grad,
        cross_q_grad,
        cross_kv_grad,
        cross_out_grad,
        ffn_in_grad,
        ffn_out_grad,
    ) = (
        a.astype(jnp.float32)
        for a in (
            self_qkv_grad,
            self_out_grad,
            cross_q_grad,
            cross_kv_grad,
            cross_out_grad,
            ffn_in_grad,
            ffn_out_grad,
        )
    )
    return (
        output,
        units_grad,
        text_grad,
        small_sums[0:3],
        small_sums[3:6],
        self_qkv_grad,
        self_bias_grad,
        self_out_grad,
        cross_q_grad,
        cross_kv_grad,
        cross_bias_grad,
        cross_out_grad,
        ffn_in_grad,
        ffn_in_bias_grad,
        ffn_out_grad,
        small_sums[6:9],
    )


def solution(mesh):
    placed = (
        P("wide", None),
        P("wide", None),
        P("wide", None),
        P("wide"),
        P("wide"),
        P("wide"),
        P(),
        P(),
        P(None, None, "narrow"),
        P(None, "narrow"),
        P("narrow", None),
        P(None, "narrow"),
        P(None, None, "narrow"),
        P(None, "narrow"),
        P("narrow", None),
        P(None, "narrow"),
        P("narrow"),
        P("narrow", None),
        P(),
    )
    return jax.shard_map(
        local,
        mesh=mesh,
        in_specs=placed,
        out_specs=(
            P(("wide", "narrow"), None),
            P(("wide", "narrow"), None),
            P(("wide", "narrow"), None),
            P(),
            P(),
            P(None, None, "narrow"),
            P(None, "narrow"),
            P("narrow", None),
            P(None, "narrow"),
            P(None, None, "narrow"),
            P(None, "narrow"),
            P("narrow", None),
            P(None, "narrow"),
            P("narrow"),
            P("narrow", None),
            P(),
        ),
        check_vma=False,
    )
```

```python
import jax
import jax.numpy as jnp
from jax import lax
from jax.experimental import pallas as pl
from jax.experimental.pallas import tpu as pltpu
from jax.sharding import PartitionSpec as P

HEAD_DIM = 64
UNITS = 1024
TEXT = 256


NORM_EPSILON = 1e-05
MASKED_SCORE = -1000000000.0
EXACT = lax.Precision.HIGHEST


def smooth_gate(values):
    return jax.nn.gelu(values, approximate=False)


def norm_forward(values, gain_vec, shift_vec):
    row_mean = jnp.mean(values, axis=-1, keepdims=True)
    centered = values - row_mean
    inv_std = lax.rsqrt(jnp.mean(centered * centered, axis=-1, keepdims=True) + NORM_EPSILON)
    normed = centered * inv_std
    return (normed * gain_vec + shift_vec, normed, inv_std)


def norm_backward(grad_in, normed, inv_std, gain_vec):
    scaled = grad_in * gain_vec
    inner_term = scaled - jnp.mean(scaled, axis=-1, keepdims=True)
    inner_term = inner_term - normed * jnp.mean(scaled * normed, axis=-1, keepdims=True)
    return inner_term * inv_std


def split_heads(values):
    return values.reshape(values.shape[0], -1, HEAD_DIM)


def block_slices(block_index, queries, key_rows, value_rows, key_count, query_block):
    per_slot = UNITS // query_block
    slot_id = block_index // per_slot
    first_row = block_index * query_block
    block_queries = lax.dynamic_slice_in_dim(queries, first_row, query_block, 0)
    block_keys = lax.dynamic_slice_in_dim(key_rows, slot_id * key_count, key_count, 0)
    block_values = lax.dynamic_slice_in_dim(value_rows, slot_id * key_count, key_count, 0)
    return (slot_id, first_row - slot_id * UNITS, block_queries, block_keys, block_values)


def masked_scores(block_queries, block_keys, allowed, score_scale):
    scores = (
        jnp.einsum("qhd,khd->hqk", block_queries, block_keys, preferred_element_type=jnp.float32)
        * score_scale
    )
    return jnp.where(allowed[None], scores, MASKED_SCORE)


def attention_forward(
    queries, key_rows, value_rows, key_count, query_block, score_scale, allowed_fn
):

    def one_block(block_index):
        slot_id, offset, block_queries, block_keys, block_values = block_slices(
            block_index, queries, key_rows, value_rows, key_count, query_block
        )
        scores = masked_scores(block_queries, block_keys, allowed_fn(slot_id, offset), score_scale)
        row_max = jnp.max(scores, axis=-1, keepdims=True)
        exp_scores = jnp.exp(scores - row_max)
        row_total = jnp.sum(exp_scores, axis=-1, keepdims=True)
        weights = (exp_scores / row_total).astype(jnp.bfloat16)
        context = jnp.einsum(
            "hqk,khd->qhd", weights, block_values, preferred_element_type=jnp.float32
        )
        return (context, (row_max + jnp.log(row_total))[:, :, 0])

    block_total = queries.shape[0] // query_block
    context, log_total = lax.map(one_block, jnp.arange(block_total, dtype=jnp.int32))
    return (context.reshape(queries.shape[0], -1), log_total)


def attention_backward(
    queries,
    key_rows,
    value_rows,
    context_grad,
    log_total,
    key_count,
    query_block,
    score_scale,
    allowed_fn,
):

    def one_block(packed):
        block_index, block_log = packed
        slot_id, offset, block_queries, block_keys, block_values = block_slices(
            block_index, queries, key_rows, value_rows, key_count, query_block
        )
        block_grad = lax.dynamic_slice_in_dim(
            context_grad, block_index * query_block, query_block, 0
        )
        scores = masked_scores(block_queries, block_keys, allowed_fn(slot_id, offset), score_scale)
        weights = jnp.exp(scores - block_log[:, :, None])
        value_grad = jnp.einsum(
            "hqk,qhd->khd",
            weights.astype(jnp.bfloat16),
            block_grad,
            preferred_element_type=jnp.float32,
        )
        weight_grad = jnp.einsum(
            "qhd,khd->hqk", block_grad, block_values, preferred_element_type=jnp.float32
        )
        score_grad = weights * (
            weight_grad - jnp.sum(weights * weight_grad, axis=-1, keepdims=True)
        )
        query_grad = (
            jnp.einsum("hqk,khd->qhd", score_grad, block_keys.astype(jnp.float32), precision=EXACT)
            * score_scale
        )
        key_grad = (
            jnp.einsum(
                "hqk,qhd->khd", score_grad, block_queries.astype(jnp.float32), precision=EXACT
            )
            * score_scale
        )
        return (query_grad, key_grad, value_grad)

    row_count = queries.shape[0]
    block_total = row_count // query_block
    per_slot = UNITS // query_block
    slot_count = row_count // UNITS
    query_grad, key_grad, value_grad = lax.map(
        one_block, (jnp.arange(block_total, dtype=jnp.int32), log_total)
    )
    query_grad = query_grad.reshape(row_count, -1)
    key_grad = jnp.sum(key_grad.reshape(slot_count, per_slot, key_count, -1), axis=1).reshape(
        slot_count * key_count, -1
    )
    value_grad = jnp.sum(value_grad.reshape(slot_count, per_slot, key_count, -1), axis=1).reshape(
        slot_count * key_count, -1
    )
    return (query_grad, key_grad, value_grad)


BLOCK = 256
MIB = 1 << 20
NARROW = 4
STEPS = 8
MESH = pl.DeviceIdType.MESH


def head_mask(shape, head):
    lane = lax.broadcasted_iota(jnp.int32, shape, len(shape) - 1)
    return (lane >= head * HEAD_DIM) & (lane < (head + 1) * HEAD_DIM)


def pick_head(values, head):
    return jnp.where(head_mask(values.shape, head), values, jnp.zeros_like(values))


def dot_nt(a, b):
    return lax.dot_general(a, b, (((1,), (1,)), ((), ())), preferred_element_type=jnp.float32)


def dot_nn(a, b):
    return jnp.dot(a, b, preferred_element_type=jnp.float32)


def dot_tn(a, b):
    return lax.dot_general(a, b, (((0,), (0,)), ((), ())), preferred_element_type=jnp.float32)


def front_kernel(lens, x_ref, g_ref, s_ref, w_ref, qb_ref, vb_ref, h_ref, q_ref, k_ref, v_ref, c_ref):
    length = lens[pl.program_id(0)]
    width = q_ref.shape[1]
    for i in range(x_ref.shape[0] // BLOCK):
        rows = pl.ds(i * BLOCK, BLOCK)

        @pl.when(i * BLOCK < length)
        def _():
            normed, _, _ = norm_forward(x_ref[rows, :].astype(jnp.float32), g_ref[...], s_ref[...])
            h1 = normed.astype(jnp.bfloat16)
            h_ref[rows, :] = h1
            qkv = dot_nn(h1, w_ref[...])
            queries = (qkv[:, :width] + qb_ref[...]).astype(jnp.bfloat16)
            q_ref[rows, :] = queries
            k_ref[rows, :] = qkv[:, width : 2 * width].astype(jnp.bfloat16)
            v_ref[rows, :] = (qkv[:, 2 * width :] + vb_ref[...]).astype(jnp.bfloat16)
            count = (i + 1) * BLOCK
            keys, values = k_ref[:count, :], v_ref[:count, :]
            scaled = queries * jnp.bfloat16(HEAD_DIM**-0.5)
            row = lax.broadcasted_iota(jnp.int32, (BLOCK, count), 0) + i * BLOCK
            allowed = lax.broadcasted_iota(jnp.int32, (BLOCK, count), 1) <= row
            total = jnp.zeros((BLOCK, width), jnp.float32)
            for head in range(width // HEAD_DIM):
                scores = jnp.where(allowed, dot_nt(pick_head(scaled, head), keys), MASKED_SCORE)
                weights = jnp.exp(scores - jnp.max(scores, axis=1, keepdims=True))
                weights = weights * (1.0 / jnp.sum(weights, axis=1, keepdims=True))
                total += dot_nn(weights.astype(jnp.bfloat16), pick_head(values, head))
            c_ref[rows, :] = total.astype(jnp.bfloat16)

        @pl.when(i * BLOCK >= length)
        def _():
            for ref in (h_ref, q_ref, k_ref, v_ref, c_ref):
                ref[rows, :] = jnp.zeros((BLOCK, ref.shape[1]), ref.dtype)


def front(lengths, units, gain_vec, shift_vec, weights, q_bias, v_bias):
    rows, width = units.shape
    slots = lengths.shape[0]
    slot_rows = rows // slots
    cols = weights.shape[1] // 3
    whole = lambda a: pl.BlockSpec(a.shape, lambda s, *_: (0,) * a.ndim)
    slot = lambda w: pl.BlockSpec((slot_rows, w), lambda s, *_: (s, 0))
    small = [a.reshape(1, -1) for a in (gain_vec, shift_vec, q_bias, v_bias)]
    shape = lambda w: jax.ShapeDtypeStruct((rows, w), jnp.bfloat16)
    return pl.pallas_call(
        front_kernel,
        grid_spec=pltpu.PrefetchScalarGridSpec(
            num_scalar_prefetch=1,
            grid=(slots,),
            in_specs=[slot(width), whole(small[0]), whole(small[1]), whole(weights), whole(small[2]), whole(small[3])],
            out_specs=[slot(width), slot(cols), slot(cols), slot(cols), slot(cols)],
        ),
        out_shape=[shape(width), shape(cols), shape(cols), shape(cols), shape(cols)],
        compiler_params=pltpu.CompilerParams(vmem_limit_bytes=48 * MIB),
        cost_estimate=pl.CostEstimate(flops=20 * 10**9, bytes_accessed=16 * MIB, transcendentals=8 * MIB),
        name="front",
    )(lengths, units, small[0], small[1], weights, small[2], small[3])


def back_kernel(lens, q_ref, k_ref, v_ref, dc_ref, o_ref, dk_acc, dv_acc):
    length = lens[pl.program_id(0)]
    slot_rows, width = q_ref.shape
    dk_acc[...] = jnp.zeros_like(dk_acc)
    dv_acc[...] = jnp.zeros_like(dv_acc)
    for i in range(slot_rows // BLOCK):
        rows = pl.ds(i * BLOCK, BLOCK)

        @pl.when(i * BLOCK < length)
        def _():
            count = (i + 1) * BLOCK
            keys, values = k_ref[:count, :], v_ref[:count, :]
            scaled = q_ref[rows, :] * jnp.bfloat16(HEAD_DIM**-0.5)
            grads = dc_ref[rows, :]
            col = lax.broadcasted_iota(jnp.int32, (count, BLOCK), 1) + i * BLOCK
            allowed = lax.broadcasted_iota(jnp.int32, (count, BLOCK), 0) <= col
            total = jnp.zeros((BLOCK, width), jnp.float32)
            for head in range(width // HEAD_DIM):
                q_head, g_head = pick_head(scaled, head), pick_head(grads, head)
                scores = jnp.where(allowed, dot_nt(keys, q_head), MASKED_SCORE)
                weights = jnp.exp(scores - jnp.max(scores, axis=0, keepdims=True))
                weights = weights * (1.0 / jnp.sum(weights, axis=0, keepdims=True))
                dv_acc[:count, :] += dot_nn(weights.astype(jnp.bfloat16), g_head)
                weight_grad = dot_nt(values, g_head)
                inner = jnp.sum(weights * weight_grad, axis=0, keepdims=True)
                score_grad = (weights * (weight_grad - inner)).astype(jnp.bfloat16)
                dk_acc[:count, :] += dot_nn(score_grad, q_head)
                total += dot_tn(score_grad, pick_head(keys, head))
            o_ref[rows, :width] = (total * HEAD_DIM**-0.5).astype(jnp.bfloat16)

        @pl.when(i * BLOCK >= length)
        def _():
            o_ref[rows, :width] = jnp.zeros((BLOCK, width), jnp.bfloat16)

    o_ref[:, width : 2 * width] = dk_acc[...].astype(jnp.bfloat16)
    o_ref[:, 2 * width :] = dv_acc[...].astype(jnp.bfloat16)


def back(lengths, queries, keys, values, grads):
    rows, width = queries.shape
    slots = lengths.shape[0]
    slot_rows = rows // slots
    slot = lambda w: pl.BlockSpec((slot_rows, w), lambda s, *_: (s, 0))
    return pl.pallas_call(
        back_kernel,
        grid_spec=pltpu.PrefetchScalarGridSpec(
            num_scalar_prefetch=1,
            grid=(slots,),
            in_specs=[slot(width)] * 4,
            out_specs=slot(3 * width),
            scratch_shapes=[pltpu.VMEM((slot_rows, width), jnp.float32)] * 2,
        ),
        out_shape=jax.ShapeDtypeStruct((rows, 3 * width), jnp.bfloat16),
        compiler_params=pltpu.CompilerParams(vmem_limit_bytes=48 * MIB),
        cost_estimate=pl.CostEstimate(flops=30 * 10**9, bytes_accessed=8 * MIB, transcendentals=8 * MIB),
        name="back",
    )(lengths, queries, keys, values, grads)


def place():
    index = lax.axis_index("narrow")
    core = index + 1 - 2 * (index % 2)
    return index, core, (index + 2) % NARROW, (core + 2) % NARROW


def greet():
    _, core, cross, _ = place()
    barrier = pltpu.get_barrier_semaphore()
    for peer in (core, cross):
        pl.semaphore_signal(barrier, inc=1, device_id={"narrow": peer}, device_id_type=MESH)
    pl.semaphore_wait(barrier, 2)


def remote(source, target, sems, kind, step, peer):
    return pltpu.make_async_remote_copy(
        src_ref=source,
        dst_ref=target,
        send_sem=sems.at[0, kind, step],
        recv_sem=sems.at[1, kind, step],
        device_id={"narrow": peer},
        device_id_type=MESH,
    )


class Hop:
    KINDS = 6

    def __init__(self, part, from_core, to_cross, from_cross, full, sems, chunk):
        self.part, self.from_core, self.to_cross, self.from_cross = part, from_core, to_cross, from_cross
        self.full, self.sems, self.chunk = full, sems, chunk
        self.own = part.shape[0] // NARROW
        self.index, self.core, self.cross, self.diagonal = place()

    def rows(self, owner, step):
        return pl.ds(pl.multiple_of(owner * self.own + step * self.chunk, self.chunk), self.chunk)

    def own_rows(self, step):
        return pl.ds(pl.multiple_of(step * self.chunk, self.chunk), self.chunk)

    def core_copies(self, step):
        return [
            remote(self.part.at[self.rows(owner, step)], self.from_core.at[step, slot], self.sems, slot, step, self.core)
            for slot, owner in enumerate((self.core, self.diagonal))
        ]

    def cross_copy(self, step):
        return remote(self.to_cross.at[step], self.from_cross.at[step], self.sems, 2, step, self.cross)

    def gather_copy(self, step, kind):
        owner = self.cross if kind == 5 else self.index
        rows = self.full.at[self.rows(owner, step)]
        return remote(rows, rows, self.sems, kind, step, self.cross if kind == 3 else self.core)

    def send_core(self, step):
        for copy in self.core_copies(step):
            copy.start()

    def send_cross(self, step):
        for copy in self.core_copies(step):
            copy.wait_recv()
        total = self.part[self.rows(self.cross, step), :].astype(jnp.float32)
        total += self.from_core[step, 1].astype(jnp.float32)
        self.to_cross[step] = total.astype(jnp.bfloat16)
        self.cross_copy(step).start()

    def result(self, step):
        total = self.part[self.rows(self.index, step), :].astype(jnp.float32)
        total += self.from_core[step, 0].astype(jnp.float32)
        self.cross_copy(step).wait_recv()
        return total + self.from_cross[step].astype(jnp.float32)

    def send_gather(self, step, values):
        self.full[self.rows(self.index, step), :] = values
        self.gather_copy(step, 3).start()
        self.gather_copy(step, 4).start()

    def forward(self, step):
        self.gather_copy(step, 3).wait_recv()
        self.gather_copy(step, 5).start()

    def gathered(self, step):
        self.gather_copy(step, 4).wait_recv()
        self.gather_copy(step, 5).wait_recv()

    def finish(self, step, gather=True):
        for copy in self.core_copies(step):
            copy.wait_send()
        self.cross_copy(step).wait_send()
        if gather:
            for kind in (3, 4, 5):
                self.gather_copy(step, kind).wait_send()

    def take(self, ref, step):
        return jnp.concatenate([ref[self.rows(owner, step), :] for owner in range(NARROW)], axis=0)

    def put(self, ref, step, values):
        for owner in range(NARROW):
            ref[self.rows(owner, step), :] = values[owner * self.chunk : (owner + 1) * self.chunk]


def hop_scratch(own, chunk, width):
    steps = own // chunk
    return [
        pltpu.VMEM((steps, 2, chunk, width), jnp.bfloat16),
        pltpu.VMEM((steps, chunk, width), jnp.bfloat16),
        pltpu.VMEM((steps, chunk, width), jnp.bfloat16),
        pltpu.SemaphoreType.DMA((2, Hop.KINDS, steps)),
    ]


def stages(steps, work):
    def body(tick, carry):
        for delay, stage in enumerate(work):
            step = tick - delay

            @pl.when((step >= 0) & (step < steps))
            def _():
                stage(step)

        return carry

    lax.fori_loop(0, steps + len(work) - 1, body, 0)


def middle_kernel(
    c1, units, text, vec, bias, keep, so_w, cq_w, kv_w, co_w,
    h2, h3, q2, c2, kv2, x1, x2,
    part1, part2, core1, tox1, fromx1, sem1, core2, tox2, fromx2, sem2,
):
    steps, chunk, width = tox1.shape
    cols = q2.shape[1]
    slots = keep.shape[0]
    texts = text.shape[0] // slots
    greet()
    one = Hop(part1, core1, tox1, fromx1, h2, sem1, chunk)
    two = Hop(part2, core2, tox2, fromx2, h3, sem2, chunk)
    scale = jnp.bfloat16(HEAD_DIM**-0.5)

    def project(step):
        one.put(part1, step, dot_nn(one.take(c1, step), so_w[...]).astype(jnp.bfloat16))
        one.send_core(step)

        @pl.when(step == 1)
        def _():
            both = dot_nn(text[...], kv_w[...])
            kv2[:, :cols] = both[:, :cols].astype(jnp.bfloat16)
            kv2[:, cols:] = (both[:, cols:] + bias[1:2, :]).astype(jnp.bfloat16)

    def norm_one(step):
        rows = one.own_rows(step)
        resid = units[rows, :].astype(jnp.float32) + one.result(step) + vec[2:3, :]
        x1[rows, :] = resid
        one.send_gather(step, norm_forward(resid, vec[0:1, :], vec[1:2, :])[0].astype(jnp.bfloat16))

    def cross(step):
        one.gathered(step)
        queries = (dot_nn(one.take(h2, step), cq_w[...]) + bias[0:1, :]).astype(jnp.bfloat16)
        one.put(q2, step, queries)
        scaled = queries * scale
        count = queries.shape[0] // slots
        context = []
        for slot in range(slots):
            mine = scaled[slot * count : (slot + 1) * count]
            keys = kv2[slot * texts : (slot + 1) * texts, :cols]
            values = kv2[slot * texts : (slot + 1) * texts, cols:]
            total = jnp.zeros((count, cols), jnp.float32)
            for head in range(cols // HEAD_DIM):
                scores = dot_nt(pick_head(mine, head), keys)
                scores = jnp.where(keep[slot : slot + 1, :] > 0.5, scores, MASKED_SCORE)
                weights = jnp.exp(scores - jnp.max(scores, axis=1, keepdims=True))
                weights = weights * (1.0 / jnp.sum(weights, axis=1, keepdims=True))
                total += dot_nn(weights.astype(jnp.bfloat16), pick_head(values, head))
            context.append(total.astype(jnp.bfloat16))
        context = jnp.concatenate(context, axis=0)
        one.put(c2, step, context)
        two.put(part2, step, dot_nn(context, co_w[...]).astype(jnp.bfloat16))
        two.send_core(step)

    def norm_two(step):
        rows = one.own_rows(step)
        resid = x1[rows, :] + two.result(step) + vec[5:6, :]
        x2[rows, :] = resid
        two.send_gather(step, norm_forward(resid, vec[3:4, :], vec[4:5, :])[0].astype(jnp.bfloat16))

    stages(
        steps,
        [
            project, one.send_cross, norm_one, one.forward, cross,
            two.send_cross, norm_two, two.forward, two.gathered,
        ],
    )

    def finish(step, carry):
        one.finish(step)
        two.finish(step)
        return carry

    lax.fori_loop(0, steps, finish, 0)


def middle(c1, units_own, text, vec, bias, keep, so_w, cq_w, kv_w, co_w):
    rows, cols = c1.shape
    own, width = units_own.shape
    chunk = own // STEPS
    bf, f32 = jnp.bfloat16, jnp.float32
    shape = jax.ShapeDtypeStruct
    vmem = pl.BlockSpec(memory_space=pltpu.VMEM)
    hop = hop_scratch(own, chunk, width)
    return pl.pallas_call(
        middle_kernel,
        in_specs=[vmem] * 10,
        out_specs=[vmem] * 7,
        out_shape=[
            shape((rows, width), bf),
            shape((rows, width), bf),
            shape((rows, cols), bf),
            shape((rows, cols), bf),
            shape((text.shape[0], 2 * cols), bf),
            shape((own, width), f32),
            shape((own, width), f32),
        ],
        scratch_shapes=[pltpu.VMEM((rows, width), bf)] * 2 + hop + hop,
        compiler_params=pltpu.CompilerParams(collective_id=0, has_side_effects=True, vmem_limit_bytes=58 * MIB),
        cost_estimate=pl.CostEstimate(flops=100 * 10**9, bytes_accessed=24 * MIB, transcendentals=4 * MIB),
        name="middle",
    )(c1, units_own, text, vec, bias, keep, so_w, cq_w, kv_w, co_w)


def wide_sum(arrays, after=None):
    parts = tuple(a.astype(jnp.bfloat16) for a in arrays)
    if after is not None:
        parts, after = lax.optimization_barrier((parts, after))
    return lax.psum(parts, "wide"), after


def local(
    units,
    text,
    out_grad,
    unit_lengths,
    text_lengths,
    bucket_counts,
    norm_gain,
    norm_shift,
    self_qkv,
    self_bias,
    self_out,
    cross_q,
    cross_kv,
    cross_bias,
    cross_out,
    ffn_in,
    ffn_in_bias,
    ffn_out,
    out_bias,
):
    narrow_size = lax.axis_size("narrow")
    narrow_index = lax.axis_index("narrow")
    group_rows = units.shape[0]
    own_rows = group_rows // narrow_size
    first_own = narrow_index * own_rows
    slot_count = unit_lengths.shape[0]
    score_scale = HEAD_DIM ** (-0.5)
    query_block = min(512, UNITS)
    slot_live = jnp.arange(slot_count, dtype=jnp.int32) < bucket_counts[0]
    lengths = jnp.where(slot_live, unit_lengths, 0)
    positions = jnp.arange(group_rows, dtype=jnp.int32)
    slot_match = (positions // UNITS)[:, None] == jnp.arange(slot_count, dtype=jnp.int32)[None, :]
    row_limit = jnp.sum(jnp.where(slot_match, lengths[None, :], 0), axis=1)
    row_valid = positions % UNITS < row_limit
    valid_own = lax.dynamic_slice_in_dim(row_valid, first_own, own_rows, 0)
    unit_pos = jnp.arange(UNITS, dtype=jnp.int32)
    text_pos = jnp.arange(TEXT, dtype=jnp.int32)

    def self_allowed(slot_id, offset):
        rows_here = offset + jnp.arange(query_block, dtype=jnp.int32)
        length = lax.dynamic_index_in_dim(lengths, slot_id, keepdims=False)
        before = unit_pos[None, :] <= rows_here[:, None]
        return before & ((unit_pos[None, :] < length) | (unit_pos[None, :] == rows_here[:, None]))

    def cross_allowed(slot_id, offset):
        length = lax.dynamic_index_in_dim(text_lengths, slot_id, keepdims=False)
        return jnp.broadcast_to(text_pos[None, :] < length, (query_block, TEXT))

    qkv_weights = self_qkv.reshape(self_qkv.shape[0], -1)
    first_in, queries, key_rows, value_rows, self_context = front(
        lengths, units, norm_gain[0], norm_shift[0], qkv_weights, self_bias[0], self_bias[1]
    )
    own_units = lax.dynamic_slice_in_dim(units, first_own, own_rows, 0).astype(jnp.float32)
    _, normed_one, inv_one = norm_forward(own_units, norm_gain[0], norm_shift[0])
    vec = jnp.stack(
        [norm_gain[1], norm_shift[1], out_bias[0], norm_gain[2], norm_shift[2], out_bias[1], out_bias[2], out_bias[2]]
    )
    keep = (text_pos[None, :] < text_lengths[:, None]).astype(jnp.float32)
    second_all, third_all, cross_queries, cross_context, text_kv, resid_one, resid_two = middle(
        self_context,
        lax.dynamic_slice_in_dim(units, first_own, own_rows, 0),
        text,
        vec,
        cross_bias,
        keep,
        self_out,
        cross_q,
        cross_kv.reshape(cross_kv.shape[0], -1),
        cross_out,
    )
    text_keys, text_values = jnp.split(text_kv, 2, axis=1)
    _, normed_two, inv_two = norm_forward(resid_one, norm_gain[1], norm_shift[1])
    _, normed_three, inv_three = norm_forward(resid_two, norm_gain[2], norm_shift[2])
    hidden_pre = jnp.dot(third_all, ffn_in, preferred_element_type=jnp.float32) + ffn_in_bias
    hidden_full, gate_pullback = jax.vjp(smooth_gate, hidden_pre)
    hidden = hidden_full.astype(jnp.bfloat16)
    ffn_sum = lax.psum_scatter(
        jnp.dot(hidden, ffn_out, preferred_element_type=jnp.float32).astype(jnp.bfloat16),
        "narrow",
        scatter_dimension=0,
        tiled=True,
    ).astype(jnp.float32)
    output = jnp.where(valid_own[:, None], resid_two + ffn_sum + out_bias[2], 0.0).astype(
        jnp.bfloat16
    )
    grad_all = jnp.where(row_valid[:, None], out_grad, jnp.zeros_like(out_grad))
    grad_two = lax.dynamic_slice_in_dim(grad_all, first_own, own_rows, 0).astype(jnp.float32)
    ffn_out_grad = jnp.einsum("rf,rd->fd", hidden, grad_all, preferred_element_type=jnp.float32)
    hidden_grad = jnp.einsum("rd,fd->rf", grad_all, ffn_out, preferred_element_type=jnp.float32)
    pre_grad = gate_pullback(hidden_grad)[0].astype(jnp.bfloat16)
    ffn_in_bias_grad = jnp.sum(pre_grad, axis=0, dtype=jnp.float32)
    ffn_in_grad = jnp.einsum("rd,rf->df", third_all, pre_grad, preferred_element_type=jnp.float32)
    third_part = jnp.einsum("rf,df->rd", pre_grad, ffn_in, preferred_element_type=jnp.float32)
    third_grad = lax.psum_scatter(
        third_part.astype(jnp.bfloat16), "narrow", scatter_dimension=0, tiled=True
    ).astype(jnp.float32)
    gain_three = jnp.sum(third_grad * normed_three, axis=0)
    shift_three = jnp.sum(third_grad, axis=0)
    resid_two_grad = grad_two + norm_backward(third_grad, normed_three, inv_three, norm_gain[2])
    bias_two_grad = jnp.sum(grad_two, axis=0)
    cross_out_all = lax.all_gather(
        resid_two_grad.astype(jnp.bfloat16), "narrow", axis=0, tiled=True
    )
    cross_out_grad = jnp.einsum(
        "rn,rd->nd", cross_context, cross_out_all, preferred_element_type=jnp.float32
    )
    cross_context_grad = jnp.einsum(
        "rd,nd->rn", cross_out_all, cross_out, preferred_element_type=jnp.float32
    ).astype(jnp.bfloat16)
    _, cross_log = attention_forward(
        split_heads(cross_queries),
        split_heads(text_keys),
        split_heads(text_values),
        TEXT,
        query_block,
        score_scale,
        cross_allowed,
    )
    cross_query_grad, text_key_grad, text_value_grad = attention_backward(
        split_heads(cross_queries),
        split_heads(text_keys),
        split_heads(text_values),
        split_heads(cross_context_grad),
        cross_log,
        TEXT,
        query_block,
        score_scale,
        cross_allowed,
    )
    cross_query_grad = cross_query_grad.astype(jnp.bfloat16)
    text_kv_grad = jnp.stack([text_key_grad, text_value_grad], axis=1).astype(jnp.bfloat16)
    cross_q_grad = jnp.einsum(
        "rd,rn->dn", second_all, cross_query_grad, preferred_element_type=jnp.float32
    )
    cross_kv_grad = jnp.einsum(
        "td,tcn->dcn", text, text_kv_grad, preferred_element_type=jnp.float32
    )
    cross_bias_grad = jnp.stack(
        [
            jnp.sum(cross_query_grad, axis=0, dtype=jnp.float32),
            jnp.sum(text_kv_grad[:, 1], axis=0, dtype=jnp.float32),
        ]
    )
    second_part = jnp.einsum(
        "rn,dn->rd", cross_query_grad, cross_q, preferred_element_type=jnp.float32
    )
    text_part = jnp.einsum(
        "tcn,dcn->td", text_kv_grad, cross_kv, preferred_element_type=jnp.float32
    )
    second_grad, text_grad = (
        lax.psum_scatter(
            second_part.astype(jnp.bfloat16), "narrow", scatter_dimension=0, tiled=True
        ).astype(jnp.float32),
        lax.psum_scatter(
            text_part.astype(jnp.bfloat16), "narrow", scatter_dimension=0, tiled=True
        ).astype(jnp.float32),
    )
    gain_two = jnp.sum(second_grad * normed_two, axis=0)
    shift_two = jnp.sum(second_grad, axis=0)
    resid_one_grad = resid_two_grad + norm_backward(second_grad, normed_two, inv_two, norm_gain[1])
    bias_one_grad = jnp.sum(resid_two_grad, axis=0)
    self_out_all = lax.all_gather(resid_one_grad.astype(jnp.bfloat16), "narrow", axis=0, tiled=True)
    self_out_grad = jnp.einsum(
        "rn,rd->nd", self_context, self_out_all, preferred_element_type=jnp.float32
    )
    self_context_grad = jnp.einsum(
        "rd,nd->rn", self_out_all, self_out, preferred_element_type=jnp.float32
    ).astype(jnp.bfloat16)
    qkv_grad = back(lengths, queries, key_rows, value_rows, self_context_grad)
    self_qkv_grad = dot_tn(first_in, qkv_grad).reshape(self_qkv.shape)
    cols = queries.shape[1]
    self_bias_grad = jnp.stack(
        [
            jnp.sum(qkv_grad[:, :cols], axis=0, dtype=jnp.float32),
            jnp.sum(qkv_grad[:, 2 * cols :], axis=0, dtype=jnp.float32),
        ]
    )
    first_part = dot_nt(qkv_grad, qkv_weights)
    first_grad = lax.psum_scatter(
        first_part.astype(jnp.bfloat16), "narrow", scatter_dimension=0, tiled=True
    ).astype(jnp.float32)
    gain_one = jnp.sum(first_grad * normed_one, axis=0)
    shift_one = jnp.sum(first_grad, axis=0)
    units_grad = resid_one_grad + norm_backward(first_grad, normed_one, inv_one, norm_gain[0])
    bias_zero_grad = jnp.sum(resid_one_grad, axis=0)
    small_sums = lax.psum(
        jnp.stack(
            [
                gain_one,
                gain_two,
                gain_three,
                shift_one,
                shift_two,
                shift_three,
                bias_zero_grad,
                bias_one_grad,
                bias_two_grad,
            ]
        ),
        ("wide", "narrow"),
    )
    (ffn_in_grad, ffn_out_grad), _ = wide_sum((ffn_in_grad, ffn_out_grad))
    (cross_q_grad, cross_kv_grad, cross_out_grad), ffn_in_grad = wide_sum(
        (cross_q_grad, cross_kv_grad, cross_out_grad), ffn_in_grad
    )
    (self_qkv_grad, self_out_grad), cross_q_grad = wide_sum((self_qkv_grad, self_out_grad), cross_q_grad)
    self_bias_grad, cross_bias_grad, ffn_in_bias_grad = lax.psum(
        (self_bias_grad, cross_bias_grad, ffn_in_bias_grad), "wide"
    )
    (
        self_qkv_grad,
        self_out_grad,
        cross_q_grad,
        cross_kv_grad,
        cross_out_grad,
        ffn_in_grad,
        ffn_out_grad,
    ) = (
        a.astype(jnp.float32)
        for a in (
            self_qkv_grad,
            self_out_grad,
            cross_q_grad,
            cross_kv_grad,
            cross_out_grad,
            ffn_in_grad,
            ffn_out_grad,
        )
    )
    return (
        output,
        units_grad,
        text_grad,
        small_sums[0:3],
        small_sums[3:6],
        self_qkv_grad,
        self_bias_grad,
        self_out_grad,
        cross_q_grad,
        cross_kv_grad,
        cross_bias_grad,
        cross_out_grad,
        ffn_in_grad,
        ffn_in_bias_grad,
        ffn_out_grad,
        small_sums[6:9],
    )


def solution(mesh):
    placed = (
        P("wide", None),
        P("wide", None),
        P("wide", None),
        P("wide"),
        P("wide"),
        P("wide"),
        P(),
        P(),
        P(None, None, "narrow"),
        P(None, "narrow"),
        P("narrow", None),
        P(None, "narrow"),
        P(None, None, "narrow"),
        P(None, "narrow"),
        P("narrow", None),
        P(None, "narrow"),
        P("narrow"),
        P("narrow", None),
        P(),
    )
    return jax.shard_map(
        local,
        mesh=mesh,
        in_specs=placed,
        out_specs=(
            P(("wide", "narrow"), None),
            P(("wide", "narrow"), None),
            P(("wide", "narrow"), None),
            P(),
            P(),
            P(None, None, "narrow"),
            P(None, "narrow"),
            P("narrow", None),
            P(None, "narrow"),
            P(None, None, "narrow"),
            P(None, "narrow"),
            P("narrow", None),
            P(None, "narrow"),
            P("narrow"),
            P("narrow", None),
            P(),
        ),
        check_vma=False,
    )
```

```python
import jax
import jax.numpy as jnp
from jax import lax
from jax.experimental import pallas as pl
from jax.experimental.pallas import tpu as pltpu
from jax.sharding import PartitionSpec as P

HEAD_DIM = 64
UNITS = 1024
TEXT = 256


NORM_EPSILON = 1e-05
MASKED_SCORE = -1000000000.0
EXACT = lax.Precision.HIGHEST


def norm_forward(values, gain_vec, shift_vec):
    row_mean = jnp.mean(values, axis=-1, keepdims=True)
    centered = values - row_mean
    inv_std = lax.rsqrt(jnp.mean(centered * centered, axis=-1, keepdims=True) + NORM_EPSILON)
    normed = centered * inv_std
    return (normed * gain_vec + shift_vec, normed, inv_std)


def norm_backward(grad_in, normed, inv_std, gain_vec):
    scaled = grad_in * gain_vec
    inner_term = scaled - jnp.mean(scaled, axis=-1, keepdims=True)
    inner_term = inner_term - normed * jnp.mean(scaled * normed, axis=-1, keepdims=True)
    return inner_term * inv_std


BLOCK = 256
MIB = 1 << 20
NARROW = 4
STEPS = 8
HIDDEN = 512
MESH = pl.DeviceIdType.MESH


def head_mask(shape, head):
    lane = lax.broadcasted_iota(jnp.int32, shape, len(shape) - 1)
    return (lane >= head * HEAD_DIM) & (lane < (head + 1) * HEAD_DIM)


def pick_head(values, head):
    return jnp.where(head_mask(values.shape, head), values, jnp.zeros_like(values))


def dot_nt(a, b):
    return lax.dot_general(a, b, (((1,), (1,)), ((), ())), preferred_element_type=jnp.float32)


def dot_nn(a, b):
    return jnp.dot(a, b, preferred_element_type=jnp.float32)


def dot_tn(a, b):
    return lax.dot_general(a, b, (((0,), (0,)), ((), ())), preferred_element_type=jnp.float32)


def front_kernel(lens, x_ref, g_ref, s_ref, w_ref, qb_ref, vb_ref, h_ref, q_ref, k_ref, v_ref, c_ref):
    length = lens[pl.program_id(0)]
    width = q_ref.shape[1]
    for i in range(x_ref.shape[0] // BLOCK):
        rows = pl.ds(i * BLOCK, BLOCK)

        @pl.when(i * BLOCK < length)
        def _():
            normed, _, _ = norm_forward(x_ref[rows, :].astype(jnp.float32), g_ref[...], s_ref[...])
            h1 = normed.astype(jnp.bfloat16)
            h_ref[rows, :] = h1
            qkv = dot_nn(h1, w_ref[...])
            queries = (qkv[:, :width] + qb_ref[...]).astype(jnp.bfloat16)
            q_ref[rows, :] = queries
            k_ref[rows, :] = qkv[:, width : 2 * width].astype(jnp.bfloat16)
            v_ref[rows, :] = (qkv[:, 2 * width :] + vb_ref[...]).astype(jnp.bfloat16)
            count = (i + 1) * BLOCK
            keys, values = k_ref[:count, :], v_ref[:count, :]
            scaled = queries * jnp.bfloat16(HEAD_DIM**-0.5)
            row = lax.broadcasted_iota(jnp.int32, (BLOCK, count), 0) + i * BLOCK
            allowed = lax.broadcasted_iota(jnp.int32, (BLOCK, count), 1) <= row
            total = jnp.zeros((BLOCK, width), jnp.float32)
            for head in range(width // HEAD_DIM):
                scores = jnp.where(allowed, dot_nt(pick_head(scaled, head), keys), MASKED_SCORE)
                weights = jnp.exp(scores - jnp.max(scores, axis=1, keepdims=True))
                weights = weights * (1.0 / jnp.sum(weights, axis=1, keepdims=True))
                total += dot_nn(weights.astype(jnp.bfloat16), pick_head(values, head))
            c_ref[rows, :] = total.astype(jnp.bfloat16)

        @pl.when(i * BLOCK >= length)
        def _():
            for ref in (h_ref, q_ref, k_ref, v_ref, c_ref):
                ref[rows, :] = jnp.zeros((BLOCK, ref.shape[1]), ref.dtype)


def front(lengths, units, gain_vec, shift_vec, weights, q_bias, v_bias):
    rows, width = units.shape
    slots = lengths.shape[0]
    slot_rows = rows // slots
    cols = weights.shape[1] // 3
    whole = lambda a: pl.BlockSpec(a.shape, lambda s, *_: (0,) * a.ndim)
    slot = lambda w: pl.BlockSpec((slot_rows, w), lambda s, *_: (s, 0))
    small = [a.reshape(1, -1) for a in (gain_vec, shift_vec, q_bias, v_bias)]
    shape = lambda w: jax.ShapeDtypeStruct((rows, w), jnp.bfloat16)
    return pl.pallas_call(
        front_kernel,
        grid_spec=pltpu.PrefetchScalarGridSpec(
            num_scalar_prefetch=1,
            grid=(slots,),
            in_specs=[slot(width), whole(small[0]), whole(small[1]), whole(weights), whole(small[2]), whole(small[3])],
            out_specs=[slot(width), slot(cols), slot(cols), slot(cols), slot(cols)],
        ),
        out_shape=[shape(width), shape(cols), shape(cols), shape(cols), shape(cols)],
        compiler_params=pltpu.CompilerParams(vmem_limit_bytes=48 * MIB),
        cost_estimate=pl.CostEstimate(flops=20 * 10**9, bytes_accessed=16 * MIB, transcendentals=8 * MIB),
        name="front",
    )(lengths, units, small[0], small[1], weights, small[2], small[3])


def back_kernel(lens, q_ref, k_ref, v_ref, dc_ref, o_ref, dk_acc, dv_acc):
    length = lens[pl.program_id(0)]
    slot_rows, width = q_ref.shape
    dk_acc[...] = jnp.zeros_like(dk_acc)
    dv_acc[...] = jnp.zeros_like(dv_acc)
    for i in range(slot_rows // BLOCK):
        rows = pl.ds(i * BLOCK, BLOCK)

        @pl.when(i * BLOCK < length)
        def _():
            count = (i + 1) * BLOCK
            keys, values = k_ref[:count, :], v_ref[:count, :]
            scaled = q_ref[rows, :] * jnp.bfloat16(HEAD_DIM**-0.5)
            grads = dc_ref[rows, :]
            col = lax.broadcasted_iota(jnp.int32, (count, BLOCK), 1) + i * BLOCK
            allowed = lax.broadcasted_iota(jnp.int32, (count, BLOCK), 0) <= col
            total = jnp.zeros((BLOCK, width), jnp.float32)
            for head in range(width // HEAD_DIM):
                q_head, g_head = pick_head(scaled, head), pick_head(grads, head)
                scores = jnp.where(allowed, dot_nt(keys, q_head), MASKED_SCORE)
                weights = jnp.exp(scores - jnp.max(scores, axis=0, keepdims=True))
                weights = weights * (1.0 / jnp.sum(weights, axis=0, keepdims=True))
                dv_acc[:count, :] += dot_nn(weights.astype(jnp.bfloat16), g_head)
                weight_grad = dot_nt(values, g_head)
                inner = jnp.sum(weights * weight_grad, axis=0, keepdims=True)
                score_grad = (weights * (weight_grad - inner)).astype(jnp.bfloat16)
                dk_acc[:count, :] += dot_nn(score_grad, q_head)
                total += dot_tn(score_grad, pick_head(keys, head))
            o_ref[rows, :width] = (total * HEAD_DIM**-0.5).astype(jnp.bfloat16)

        @pl.when(i * BLOCK >= length)
        def _():
            o_ref[rows, :width] = jnp.zeros((BLOCK, width), jnp.bfloat16)

    o_ref[:, width : 2 * width] = dk_acc[...].astype(jnp.bfloat16)
    o_ref[:, 2 * width :] = dv_acc[...].astype(jnp.bfloat16)


def back(lengths, queries, keys, values, grads):
    rows, width = queries.shape
    slots = lengths.shape[0]
    slot_rows = rows // slots
    slot = lambda w: pl.BlockSpec((slot_rows, w), lambda s, *_: (s, 0))
    return pl.pallas_call(
        back_kernel,
        grid_spec=pltpu.PrefetchScalarGridSpec(
            num_scalar_prefetch=1,
            grid=(slots,),
            in_specs=[slot(width)] * 4,
            out_specs=slot(3 * width),
            scratch_shapes=[pltpu.VMEM((slot_rows, width), jnp.float32)] * 2,
        ),
        out_shape=jax.ShapeDtypeStruct((rows, 3 * width), jnp.bfloat16),
        compiler_params=pltpu.CompilerParams(vmem_limit_bytes=48 * MIB),
        cost_estimate=pl.CostEstimate(flops=30 * 10**9, bytes_accessed=8 * MIB, transcendentals=8 * MIB),
        name="back",
    )(lengths, queries, keys, values, grads)


def place():
    index = lax.axis_index("narrow")
    core = index + 1 - 2 * (index % 2)
    return index, core, (index + 2) % NARROW, (core + 2) % NARROW


def greet():
    _, core, cross, _ = place()
    barrier = pltpu.get_barrier_semaphore()
    for peer in (core, cross):
        pl.semaphore_signal(barrier, inc=1, device_id={"narrow": peer}, device_id_type=MESH)
    pl.semaphore_wait(barrier, 2)


def remote(source, target, sems, kind, step, peer):
    return pltpu.make_async_remote_copy(
        src_ref=source,
        dst_ref=target,
        send_sem=sems.at[0, kind, step],
        recv_sem=sems.at[1, kind, step],
        device_id={"narrow": peer},
        device_id_type=MESH,
    )


class Hop:
    KINDS = 6

    def __init__(self, part, from_core, to_cross, from_cross, full, sems, chunk):
        self.part, self.from_core, self.to_cross, self.from_cross = part, from_core, to_cross, from_cross
        self.full, self.sems, self.chunk = full, sems, chunk
        self.own = part.shape[0] // NARROW
        self.index, self.core, self.cross, self.diagonal = place()

    def rows(self, owner, step):
        return pl.ds(pl.multiple_of(owner * self.own + step * self.chunk, self.chunk), self.chunk)

    def own_rows(self, step):
        return pl.ds(pl.multiple_of(step * self.chunk, self.chunk), self.chunk)

    def core_copies(self, step):
        return [
            remote(self.part.at[self.rows(owner, step)], self.from_core.at[step, slot], self.sems, slot, step, self.core)
            for slot, owner in enumerate((self.core, self.diagonal))
        ]

    def cross_copy(self, step):
        return remote(self.to_cross.at[step], self.from_cross.at[step], self.sems, 2, step, self.cross)

    def gather_copy(self, step, kind):
        owner = self.cross if kind == 5 else self.index
        rows = self.full.at[self.rows(owner, step)]
        return remote(rows, rows, self.sems, kind, step, self.cross if kind == 3 else self.core)

    def send_core(self, step):
        for copy in self.core_copies(step):
            copy.start()

    def send_cross(self, step):
        for copy in self.core_copies(step):
            copy.wait_recv()
        total = self.part[self.rows(self.cross, step), :].astype(jnp.float32)
        total += self.from_core[step, 1].astype(jnp.float32)
        self.to_cross[step] = total.astype(jnp.bfloat16)
        self.cross_copy(step).start()

    def result(self, step):
        total = self.part[self.rows(self.index, step), :].astype(jnp.float32)
        total += self.from_core[step, 0].astype(jnp.float32)
        self.cross_copy(step).wait_recv()
        return total + self.from_cross[step].astype(jnp.float32)

    def send_gather(self, step, values):
        self.full[self.rows(self.index, step), :] = values
        self.gather_copy(step, 3).start()
        self.gather_copy(step, 4).start()

    def forward(self, step):
        self.gather_copy(step, 3).wait_recv()
        self.gather_copy(step, 5).start()

    def gathered(self, step):
        self.gather_copy(step, 4).wait_recv()
        self.gather_copy(step, 5).wait_recv()

    def finish(self, step, gather=True):
        for copy in self.core_copies(step):
            copy.wait_send()
        self.cross_copy(step).wait_send()
        if gather:
            for kind in (3, 4, 5):
                self.gather_copy(step, kind).wait_send()

    def take(self, ref, step):
        return jnp.concatenate([ref[self.rows(owner, step), :] for owner in range(NARROW)], axis=0)

    def put(self, ref, step, values):
        for owner in range(NARROW):
            ref[self.rows(owner, step), :] = values[owner * self.chunk : (owner + 1) * self.chunk]


def hop_scratch(own, chunk, width):
    steps = own // chunk
    return [
        pltpu.VMEM((steps, 2, chunk, width), jnp.bfloat16),
        pltpu.VMEM((steps, chunk, width), jnp.bfloat16),
        pltpu.VMEM((steps, chunk, width), jnp.bfloat16),
        pltpu.SemaphoreType.DMA((2, Hop.KINDS, steps)),
    ]


def stages(steps, work):
    def body(tick, carry):
        for delay, stage in enumerate(work):
            step = tick - delay

            @pl.when((step >= 0) & (step < steps))
            def _():
                stage(step)

        return carry

    lax.fori_loop(0, steps + len(work) - 1, body, 0)


def middle_kernel(
    c1, units, text, vec, bias, keep, so_w, cq_w, kv_w, co_w,
    h2, h3, q2, c2, kv2, x1, x2,
    part1, part2, core1, tox1, fromx1, sem1, core2, tox2, fromx2, sem2,
):
    steps, chunk, width = tox1.shape
    cols = q2.shape[1]
    slots = keep.shape[0]
    texts = text.shape[0] // slots
    greet()
    one = Hop(part1, core1, tox1, fromx1, h2, sem1, chunk)
    two = Hop(part2, core2, tox2, fromx2, h3, sem2, chunk)
    scale = jnp.bfloat16(HEAD_DIM**-0.5)

    def project(step):
        one.put(part1, step, dot_nn(one.take(c1, step), so_w[...]).astype(jnp.bfloat16))
        one.send_core(step)

        @pl.when(step == 1)
        def _():
            both = dot_nn(text[...], kv_w[...])
            kv2[:, :cols] = both[:, :cols].astype(jnp.bfloat16)
            kv2[:, cols:] = (both[:, cols:] + bias[1:2, :]).astype(jnp.bfloat16)

    def norm_one(step):
        rows = one.own_rows(step)
        resid = units[rows, :].astype(jnp.float32) + one.result(step) + vec[2:3, :]
        x1[rows, :] = resid
        one.send_gather(step, norm_forward(resid, vec[0:1, :], vec[1:2, :])[0].astype(jnp.bfloat16))

    def cross(step):
        one.gathered(step)
        queries = (dot_nn(one.take(h2, step), cq_w[...]) + bias[0:1, :]).astype(jnp.bfloat16)
        one.put(q2, step, queries)
        scaled = queries * scale
        count = queries.shape[0] // slots
        context = []
        for slot in range(slots):
            mine = scaled[slot * count : (slot + 1) * count]
            keys = kv2[slot * texts : (slot + 1) * texts, :cols]
            values = kv2[slot * texts : (slot + 1) * texts, cols:]
            total = jnp.zeros((count, cols), jnp.float32)
            for head in range(cols // HEAD_DIM):
                scores = dot_nt(pick_head(mine, head), keys)
                scores = jnp.where(keep[slot : slot + 1, :] > 0.5, scores, MASKED_SCORE)
                weights = jnp.exp(scores - jnp.max(scores, axis=1, keepdims=True))
                weights = weights * (1.0 / jnp.sum(weights, axis=1, keepdims=True))
                total += dot_nn(weights.astype(jnp.bfloat16), pick_head(values, head))
            context.append(total.astype(jnp.bfloat16))
        context = jnp.concatenate(context, axis=0)
        one.put(c2, step, context)
        two.put(part2, step, dot_nn(context, co_w[...]).astype(jnp.bfloat16))
        two.send_core(step)

    def norm_two(step):
        rows = one.own_rows(step)
        resid = x1[rows, :] + two.result(step) + vec[5:6, :]
        x2[rows, :] = resid
        two.send_gather(step, norm_forward(resid, vec[3:4, :], vec[4:5, :])[0].astype(jnp.bfloat16))

    stages(
        steps,
        [
            project, one.send_cross, norm_one, one.forward, cross,
            two.send_cross, norm_two, two.forward, two.gathered,
        ],
    )

    def finish(step, carry):
        one.finish(step)
        two.finish(step)
        return carry

    lax.fori_loop(0, steps, finish, 0)


def middle(c1, units_own, text, vec, bias, keep, so_w, cq_w, kv_w, co_w):
    rows, cols = c1.shape
    own, width = units_own.shape
    chunk = own // STEPS
    bf, f32 = jnp.bfloat16, jnp.float32
    shape = jax.ShapeDtypeStruct
    vmem = pl.BlockSpec(memory_space=pltpu.VMEM)
    hop = hop_scratch(own, chunk, width)
    return pl.pallas_call(
        middle_kernel,
        in_specs=[vmem] * 10,
        out_specs=[vmem] * 7,
        out_shape=[
            shape((rows, width), bf),
            shape((rows, width), bf),
            shape((rows, cols), bf),
            shape((rows, cols), bf),
            shape((text.shape[0], 2 * cols), bf),
            shape((own, width), f32),
            shape((own, width), f32),
        ],
        scratch_shapes=[pltpu.VMEM((rows, width), bf)] * 2 + hop + hop,
        compiler_params=pltpu.CompilerParams(collective_id=0, has_side_effects=True, vmem_limit_bytes=58 * MIB),
        cost_estimate=pl.CostEstimate(flops=100 * 10**9, bytes_accessed=24 * MIB, transcendentals=4 * MIB),
        name="middle",
    )(c1, units_own, text, vec, bias, keep, so_w, cq_w, kv_w, co_w)


def ffn_kernel(lens, h_ref, e_ref, wi_ref, b_ref, wo_ref, a_ref, d_ref, gi_ref, go_ref, gb_ref, gi_acc, go_acc):
    block = pl.program_id(0)
    per_slot = pl.num_programs(0) // lens.shape[0]
    length = lens[block // per_slot]

    @pl.when(block == 0)
    def _():
        gi_acc[...] = jnp.zeros_like(gi_acc)
        go_acc[...] = jnp.zeros_like(go_acc)
        gb_ref[...] = jnp.zeros_like(gb_ref)

    live = (block % per_slot) * BLOCK < length

    @pl.when(live)
    def _():
        rows, grads = h_ref[...], e_ref[...]
        out = jnp.zeros(a_ref.shape, jnp.float32)
        back_out = jnp.zeros(d_ref.shape, jnp.float32)
        hidden_count = wo_ref.shape[0]
        for first in range(0, hidden_count, HIDDEN):
            part = slice(first, first + HIDDEN)
            pre = dot_nn(rows, wi_ref[:, part]) + b_ref[:, part]
            cdf = 0.5 + 0.5 * lax.erf(pre * (0.5**0.5))
            pdf = jnp.exp(-0.5 * pre * pre) * 0.3989422804014327
            hidden = (pre * cdf).astype(jnp.bfloat16)
            slope = cdf + pre * pdf
            pre_grad = slope * dot_nt(grads, wo_ref[part, :])
            pre_low = pre_grad.astype(jnp.bfloat16)
            gb_ref[:, part] += jnp.sum(pre_low.astype(jnp.float32), axis=0, keepdims=True)
            out += dot_nn(hidden, wo_ref[part, :])
            back_out += dot_nt(pre_low, wi_ref[:, part])
            go_acc[part, :] += dot_tn(hidden, grads)
            gi_acc[:, part] += dot_tn(rows, pre_low)
        a_ref[...] = out.astype(jnp.bfloat16)
        d_ref[...] = back_out.astype(jnp.bfloat16)

    @pl.when(jnp.logical_not(live))
    def _():
        a_ref[...] = jnp.zeros_like(a_ref)
        d_ref[...] = jnp.zeros_like(d_ref)

    @pl.when(block == pl.num_programs(0) - 1)
    def _():
        gi_ref[...] = gi_acc[...].astype(jnp.bfloat16)
        go_ref[...] = go_acc[...].astype(jnp.bfloat16)


def ffn(lengths, rows_in, grads, w_in, b_in, w_out):
    rows, width = rows_in.shape
    count = w_out.shape[0]
    bf, f32 = jnp.bfloat16, jnp.float32
    shape = jax.ShapeDtypeStruct
    block = pl.BlockSpec((BLOCK, width), lambda i, *_: (i, 0))
    whole = lambda a, b: pl.BlockSpec((a, b), lambda i, *_: (0, 0), pipeline_mode=pl.Buffered(1))
    return pl.pallas_call(
        ffn_kernel,
        grid_spec=pltpu.PrefetchScalarGridSpec(
            num_scalar_prefetch=1,
            grid=(rows // BLOCK,),
            in_specs=[block, block, whole(width, count), whole(1, count), whole(count, width)],
            out_specs=[block, block, whole(width, count), whole(count, width), whole(1, count)],
            scratch_shapes=[pltpu.VMEM((width, count), f32), pltpu.VMEM((count, width), f32)],
        ),
        out_shape=[
            shape((rows, width), bf),
            shape((rows, width), bf),
            shape((width, count), bf),
            shape((count, width), bf),
            shape((1, count), f32),
        ],
        compiler_params=pltpu.CompilerParams(vmem_limit_bytes=58 * MIB),
        cost_estimate=pl.CostEstimate(flops=60 * 10**9, bytes_accessed=32 * MIB, transcendentals=8 * MIB),
        name="ffn",
    )(lengths, rows_in, grads, w_in, b_in.reshape(1, -1), w_out)


class FarHop(Hop):
    def fetch(self, mine, theirs, sems):
        self.mine, self.theirs = mine, theirs
        rows = lambda owner: pl.ds(pl.multiple_of(owner * self.own, self.own), self.own)
        self.fetches = [
            pltpu.make_async_copy(self.part.at[rows(owner)], ref, sems.at[slot])
            for slot, (owner, ref) in enumerate(((self.index, mine), (self.cross, theirs)))
        ]
        for copy in self.fetches:
            copy.start()

    def fetched(self):
        for copy in self.fetches:
            copy.wait()

    def cross_copy(self, step):
        return remote(
            self.theirs.at[self.own_rows(step)], self.from_cross.at[step], self.sems, 2, step, self.cross
        )

    def send_cross(self, step):
        for copy in self.core_copies(step):
            copy.wait_recv()
        total = self.theirs[self.own_rows(step), :].astype(jnp.float32)
        total += self.from_core[step, 1].astype(jnp.float32)
        self.theirs[self.own_rows(step), :] = total.astype(jnp.bfloat16)
        self.cross_copy(step).start()

    def result(self, step):
        total = self.mine[self.own_rows(step), :].astype(jnp.float32)
        total += self.from_core[step, 0].astype(jnp.float32)
        self.cross_copy(step).wait_recv()
        return total + self.from_cross[step].astype(jnp.float32)


def column_sum(values):
    return jnp.sum(values, axis=0, keepdims=True)


def turn_kernel(
    third, ffn_part, x1, x2, e_own, valid, h2, q2, c2, kv2, c1, keep, vec, co_w, cq_w, so_w,
    y, dx1, dc1, dkv, co_g, cq_g, so_g, bias_g, stats,
    mine3, theirs3, core3, fromx3, sem3, mine4, theirs4, core4, fromx4, sem4,
    part5, core5, tox5, fromx5, sem5, full3, full5, dx2, co_acc, cq_acc, so_acc, dkv_acc, fetch_sem,
):
    steps, chunk, width = tox5.shape
    cols = q2.shape[1]
    slots = bias_g.shape[0]
    texts = kv2.shape[0] // slots
    greet()
    three = FarHop(third, core3, None, fromx3, full3, sem3, chunk)
    four = FarHop(ffn_part, core4, None, fromx4, None, sem4, chunk)
    five = Hop(part5, core5, tox5, fromx5, full5, sem5, chunk)
    three.fetch(mine3, theirs3, fetch_sem.at[0])
    four.fetch(mine4, theirs4, fetch_sem.at[1])

    def start(step, carry):
        three.send_core(step)
        return carry

    lax.fori_loop(0, steps, start, 0)
    for ref in (co_acc, cq_acc, so_acc, dkv_acc, bias_g, stats):
        ref[...] = jnp.zeros_like(ref)
    three.fetched()
    four.fetched()
    scale = jnp.bfloat16(HEAD_DIM**-0.5)

    def norm_three(step):
        rows = three.own_rows(step)
        grad_in = three.result(step)
        _, normed, inv_std = norm_forward(x2[rows, :], vec[0:1, :], vec[0:1, :])
        stats[0:1, :] += column_sum(grad_in * normed)
        stats[1:2, :] += column_sum(grad_in)
        above = e_own[rows, :].astype(jnp.float32)
        total = above + norm_backward(grad_in, normed, inv_std, vec[0:1, :])
        stats[2:3, :] += column_sum(above)
        stats[3:4, :] += column_sum(total)
        dx2[rows, :] = total
        three.send_gather(step, total.astype(jnp.bfloat16))
        four.send_core(step)

    def cross(step):
        three.gathered(step)
        grads = three.take(full3, step)
        co_acc[...] += dot_tn(three.take(c2, step), grads)
        context = dot_nt(grads, co_w[...]).astype(jnp.bfloat16)
        queries = three.take(q2, step) * scale
        count = queries.shape[0] // slots
        q_grad = []
        for slot in range(slots):
            rows = slice(slot * count, (slot + 1) * count)
            texts_here = slice(slot * texts, (slot + 1) * texts)
            keys, values = kv2[texts_here, :cols], kv2[texts_here, cols:]
            total = jnp.zeros((count, cols), jnp.float32)
            for head in range(cols // HEAD_DIM):
                q_head, g_head = pick_head(queries[rows], head), pick_head(context[rows], head)
                scores = jnp.where(keep[texts_here, :] > 0.5, dot_nt(keys, q_head), MASKED_SCORE)
                weights = jnp.exp(scores - jnp.max(scores, axis=0, keepdims=True))
                weights = weights * (1.0 / jnp.sum(weights, axis=0, keepdims=True))
                dkv_acc[texts_here, cols:] += dot_nn(weights.astype(jnp.bfloat16), g_head)
                weight_grad = dot_nt(values, g_head)
                inner = jnp.sum(weights * weight_grad, axis=0, keepdims=True)
                score_grad = (weights * (weight_grad - inner)).astype(jnp.bfloat16)
                dkv_acc[texts_here, :cols] += dot_nn(score_grad, q_head)
                total += dot_tn(score_grad, pick_head(keys, head))
            q_grad.append((total * HEAD_DIM**-0.5).astype(jnp.bfloat16))
        q_grad = jnp.concatenate(q_grad, axis=0)
        five.put(part5, step, dot_nt(q_grad, cq_w[...]).astype(jnp.bfloat16))
        five.send_core(step)
        bias_g[0:1, :] += column_sum(q_grad.astype(jnp.float32))
        cq_acc[...] += dot_tn(five.take(h2, step), q_grad)

    def norm_two(step):
        rows = five.own_rows(step)
        grad_in = five.result(step)
        _, normed, inv_std = norm_forward(x1[rows, :], vec[1:2, :], vec[1:2, :])
        stats[4:5, :] += column_sum(grad_in * normed)
        stats[5:6, :] += column_sum(grad_in)
        total = dx2[rows, :] + norm_backward(grad_in, normed, inv_std, vec[1:2, :])
        stats[6:7, :] += column_sum(total)
        dx1[rows, :] = total
        five.send_gather(step, total.astype(jnp.bfloat16))

    def last(step):
        five.gathered(step)
        grads = five.take(full5, step)
        dc1_rows = dot_nt(grads, so_w[...]).astype(jnp.bfloat16)
        five.put(dc1, step, dc1_rows)
        so_acc[...] += dot_tn(five.take(c1, step), grads)

    def output(step):
        rows = four.own_rows(step)
        total = x2[rows, :] + four.result(step) + vec[2:3, :]
        y[rows, :] = jnp.where(valid[rows, :1] > 0.5, total, 0.0).astype(jnp.bfloat16)

    stages(
        steps,
        [
            three.send_cross, norm_three, three.forward, cross,
            five.send_cross, norm_two, five.forward, last,
            four.send_cross, output,
        ],
    )
    dkv[...] = dkv_acc[...].astype(jnp.bfloat16)
    bias_g[1:2, :] = column_sum(dkv[:, cols:].astype(jnp.float32))
    co_g[...] = co_acc[...].astype(jnp.bfloat16)
    cq_g[...] = cq_acc[...].astype(jnp.bfloat16)
    so_g[...] = so_acc[...].astype(jnp.bfloat16)

    def finish(step, carry):
        three.finish(step)
        four.finish(step, False)
        five.finish(step)
        return carry

    lax.fori_loop(0, steps, finish, 0)


def turn(third, ffn_part, x1, x2, e_own, valid, h2, q2, c2, kv2, c1, keep, vec, co_w, cq_w, so_w):
    rows, cols = c1.shape
    own, width = x1.shape
    chunk = own // STEPS
    bf, f32 = jnp.bfloat16, jnp.float32
    shape = jax.ShapeDtypeStruct
    vmem = pl.BlockSpec(memory_space=pltpu.VMEM)
    hbm = pl.BlockSpec(memory_space=pl.ANY)
    hop = hop_scratch(own, chunk, width)
    far = [pltpu.VMEM((own, width), bf)] * 2 + [hop[0], hop[2], hop[3]]
    return pl.pallas_call(
        turn_kernel,
        in_specs=[hbm, hbm] + [vmem] * 14,
        out_specs=[vmem] * 9,
        out_shape=[
            shape((own, width), bf),
            shape((own, width), f32),
            shape((rows, cols), bf),
            shape(kv2.shape, bf),
            shape((cols, width), bf),
            shape((width, cols), bf),
            shape((cols, width), bf),
            shape((2, cols), f32),
            shape((8, width), f32),
        ],
        scratch_shapes=far
        + far
        + [pltpu.VMEM((rows, width), bf)]
        + hop
        + [pltpu.VMEM((rows, width), bf)] * 2
        + [
            pltpu.VMEM((own, width), f32),
            pltpu.VMEM((cols, width), f32),
            pltpu.VMEM((width, cols), f32),
            pltpu.VMEM((cols, width), f32),
            pltpu.VMEM(kv2.shape, f32),
            pltpu.SemaphoreType.DMA((2, 2)),
        ],
        compiler_params=pltpu.CompilerParams(collective_id=1, has_side_effects=True, vmem_limit_bytes=60 * MIB),
        cost_estimate=pl.CostEstimate(flops=100 * 10**9, bytes_accessed=24 * MIB, transcendentals=4 * MIB),
        name="turn",
    )(third, ffn_part, x1, x2, e_own, valid, h2, q2, c2, kv2, c1, keep, vec, co_w, cq_w, so_w)


def last_kernel(
    dqkv, dkv, units, dx1, gain, qkv_w, kv_w, units_g, text_g, stats,
    part6, core6, tox6, fromx6, sem6, part7, core7, tox7, fromx7, sem7,
):
    steps, chunk, _ = tox6.shape
    text_steps = tox7.shape[0]
    greet()
    six = Hop(part6, core6, tox6, fromx6, None, sem6, chunk)
    seven = Hop(part7, core7, tox7, fromx7, None, sem7, chunk)
    stats[...] = jnp.zeros_like(stats)

    def project(step):
        six.put(part6, step, dot_nt(six.take(dqkv, step), qkv_w[...]).astype(jnp.bfloat16))
        six.send_core(step)

    def norm_one(step):
        rows = six.own_rows(step)
        grad_in = six.result(step)
        _, normed, inv_std = norm_forward(units[rows, :].astype(jnp.float32), gain[...], gain[...])
        stats[0:1, :] += column_sum(grad_in * normed)
        stats[1:2, :] += column_sum(grad_in)
        units_g[rows, :] = dx1[rows, :] + norm_backward(grad_in, normed, inv_std, gain[...])

    def text_only(work):
        def stage(step):
            @pl.when(step < text_steps)
            def _():
                work(step)

        return stage

    def text_project(step):
        seven.put(part7, step, dot_nt(seven.take(dkv, step), kv_w[...]).astype(jnp.bfloat16))
        seven.send_core(step)

    def text_result(step):
        text_g[seven.own_rows(step), :] = seven.result(step)

    stages(
        steps,
        [project, six.send_cross, norm_one, text_only(text_project), text_only(seven.send_cross), text_only(text_result)],
    )

    def finish(step, carry):
        six.finish(step, False)
        text_only(lambda s: seven.finish(s, False))(step)
        return carry

    lax.fori_loop(0, steps, finish, 0)


def last(dqkv, dkv, units_own, dx1, gain_vec, qkv_w, kv_w):
    rows = dqkv.shape[0]
    own, width = units_own.shape
    chunk = own // STEPS
    text_own = dkv.shape[0] // NARROW
    bf, f32 = jnp.bfloat16, jnp.float32
    shape = jax.ShapeDtypeStruct
    vmem = pl.BlockSpec(memory_space=pltpu.VMEM)
    return pl.pallas_call(
        last_kernel,
        in_specs=[vmem] * 7,
        out_specs=[vmem] * 3,
        out_shape=[shape((own, width), f32), shape((text_own, width), f32), shape((8, width), f32)],
        scratch_shapes=[pltpu.VMEM((rows, width), bf)]
        + hop_scratch(own, chunk, width)
        + [pltpu.VMEM((dkv.shape[0], width), bf)]
        + hop_scratch(text_own, chunk, width),
        compiler_params=pltpu.CompilerParams(collective_id=2, has_side_effects=True, vmem_limit_bytes=58 * MIB),
        cost_estimate=pl.CostEstimate(flops=30 * 10**9, bytes_accessed=16 * MIB, transcendentals=0),
        name="last",
    )(dqkv, dkv, units_own, dx1, gain_vec.reshape(1, -1), qkv_w, kv_w)


def wide_sum(arrays, after=None):
    parts = tuple(a.astype(jnp.bfloat16) for a in arrays)
    if after is not None:
        parts, after = lax.optimization_barrier((parts, after))
    return lax.psum(parts, "wide"), after


def local(
    units,
    text,
    out_grad,
    unit_lengths,
    text_lengths,
    bucket_counts,
    norm_gain,
    norm_shift,
    self_qkv,
    self_bias,
    self_out,
    cross_q,
    cross_kv,
    cross_bias,
    cross_out,
    ffn_in,
    ffn_in_bias,
    ffn_out,
    out_bias,
):
    own_rows = units.shape[0] // NARROW
    first_own = lax.axis_index("narrow") * own_rows
    slot_count = unit_lengths.shape[0]
    slot_live = jnp.arange(slot_count, dtype=jnp.int32) < bucket_counts[0]
    lengths = jnp.where(slot_live, unit_lengths, 0)
    positions = first_own + jnp.arange(own_rows, dtype=jnp.int32)
    slot_match = (positions // UNITS)[:, None] == jnp.arange(slot_count, dtype=jnp.int32)[None, :]
    row_limit = jnp.sum(jnp.where(slot_match, lengths[None, :], 0), axis=1)
    valid_own = positions % UNITS < row_limit
    text_pos = jnp.arange(TEXT, dtype=jnp.int32)
    keep = (text_pos[None, :] < text_lengths[:, None]).astype(jnp.float32)

    def own(rows):
        return lax.dynamic_slice_in_dim(rows, first_own, own_rows, 0)

    qkv_weights = self_qkv.reshape(self_qkv.shape[0], -1)
    kv_weights = cross_kv.reshape(cross_kv.shape[0], -1)
    own_units = own(units)
    first_in, queries, key_rows, value_rows, self_context = front(
        lengths, units, norm_gain[0], norm_shift[0], qkv_weights, self_bias[0], self_bias[1]
    )
    last_bias = jnp.zeros((3,) + out_bias.shape[1:], jnp.float32)
    second_all, third_all, cross_queries, cross_context, text_kv, resid_one, resid_two = middle(
        self_context,
        own_units,
        text,
        jnp.concatenate([norm_gain[1:2], norm_shift[1:2], out_bias[0:1], norm_gain[2:3], norm_shift[2:3], out_bias[1:2], last_bias[:2]]),
        cross_bias,
        keep,
        self_out,
        cross_q,
        kv_weights,
        cross_out,
    )
    ffn_part, third_part, ffn_in_grad, ffn_out_grad, ffn_in_bias_grad = ffn(
        lengths, third_all, out_grad, ffn_in, ffn_in_bias, ffn_out
    )
    grad_own = jnp.where(valid_own[:, None], own(out_grad), jnp.zeros((), out_grad.dtype))
    spread = own_rows // STEPS * NARROW // slot_count
    output, resid_one_grad, self_context_grad, text_kv_grad, cross_out_grad, cross_q_grad, self_out_grad, cross_bias_grad, stats = turn(
        third_part,
        ffn_part,
        resid_one,
        resid_two,
        grad_own,
        jnp.broadcast_to(valid_own[:, None].astype(jnp.float32), (own_rows, 128)),
        second_all,
        cross_queries,
        cross_context,
        text_kv,
        self_context,
        jnp.broadcast_to(keep.reshape(-1, 1), (keep.size, spread)),
        jnp.concatenate([norm_gain[2:3], norm_gain[1:2], out_bias[2:3]]),
        cross_out,
        cross_q,
        self_out,
    )
    qkv_grad = back(lengths, queries, key_rows, value_rows, self_context_grad)
    cols = queries.shape[1]
    self_bias_grad = jnp.stack(
        [
            jnp.sum(qkv_grad[:, :cols], axis=0, dtype=jnp.float32),
            jnp.sum(qkv_grad[:, 2 * cols :], axis=0, dtype=jnp.float32),
        ]
    )
    self_qkv_grad = dot_tn(first_in, qkv_grad).astype(jnp.bfloat16).reshape(self_qkv.shape)
    cross_kv_grad = dot_tn(text, text_kv_grad).astype(jnp.bfloat16).reshape(cross_kv.shape)
    units_grad, text_grad, last_stats = last(
        qkv_grad, text_kv_grad, own_units, resid_one_grad, norm_gain[0], qkv_weights, kv_weights
    )
    ffn_in_bias_grad = ffn_in_bias_grad.reshape(ffn_in_bias.shape)
    small_sums = lax.psum(
        jnp.stack(
            [
                last_stats[0],
                stats[4],
                stats[0],
                last_stats[1],
                stats[5],
                stats[1],
                stats[6],
                stats[3],
                stats[2],
            ]
        ),
        ("wide", "narrow"),
    )
    (ffn_in_grad, ffn_out_grad), _ = wide_sum((ffn_in_grad, ffn_out_grad))
    (cross_q_grad, cross_kv_grad, cross_out_grad), ffn_in_grad = wide_sum(
        (cross_q_grad, cross_kv_grad, cross_out_grad), ffn_in_grad
    )
    (self_qkv_grad, self_out_grad), cross_q_grad = wide_sum((self_qkv_grad, self_out_grad), cross_q_grad)
    self_bias_grad, cross_bias_grad, ffn_in_bias_grad = lax.psum(
        (self_bias_grad, cross_bias_grad, ffn_in_bias_grad), "wide"
    )
    (
        self_qkv_grad,
        self_out_grad,
        cross_q_grad,
        cross_kv_grad,
        cross_out_grad,
        ffn_in_grad,
        ffn_out_grad,
    ) = (
        a.astype(jnp.float32)
        for a in (
            self_qkv_grad,
            self_out_grad,
            cross_q_grad,
            cross_kv_grad,
            cross_out_grad,
            ffn_in_grad,
            ffn_out_grad,
        )
    )
    return (
        output,
        units_grad,
        text_grad,
        small_sums[0:3],
        small_sums[3:6],
        self_qkv_grad,
        self_bias_grad,
        self_out_grad,
        cross_q_grad,
        cross_kv_grad,
        cross_bias_grad,
        cross_out_grad,
        ffn_in_grad,
        ffn_in_bias_grad,
        ffn_out_grad,
        small_sums[6:9],
    )


def solution(mesh):
    placed = (
        P("wide", None),
        P("wide", None),
        P("wide", None),
        P("wide"),
        P("wide"),
        P("wide"),
        P(),
        P(),
        P(None, None, "narrow"),
        P(None, "narrow"),
        P("narrow", None),
        P(None, "narrow"),
        P(None, None, "narrow"),
        P(None, "narrow"),
        P("narrow", None),
        P(None, "narrow"),
        P("narrow"),
        P("narrow", None),
        P(),
    )
    return jax.shard_map(
        local,
        mesh=mesh,
        in_specs=placed,
        out_specs=(
            P(("wide", "narrow"), None),
            P(("wide", "narrow"), None),
            P(("wide", "narrow"), None),
            P(),
            P(),
            P(None, None, "narrow"),
            P(None, "narrow"),
            P("narrow", None),
            P(None, "narrow"),
            P(None, None, "narrow"),
            P(None, "narrow"),
            P("narrow", None),
            P(None, "narrow"),
            P("narrow"),
            P("narrow", None),
            P(),
        ),
        check_vma=False,
    )
```

```python
import functools

import jax
import jax.numpy as jnp
from jax import lax
from jax.experimental import pallas as pl
from jax.experimental.pallas import tpu as pltpu
from jax.sharding import PartitionSpec as P

HEAD_DIM = 64
UNITS = 1024
TEXT = 256


NORM_EPSILON = 1e-05
MASKED_SCORE = -1000000000.0
EXACT = lax.Precision.HIGHEST


def norm_forward(values, gain_vec, shift_vec):
    row_mean = jnp.mean(values, axis=-1, keepdims=True)
    centered = values - row_mean
    inv_std = lax.rsqrt(jnp.mean(centered * centered, axis=-1, keepdims=True) + NORM_EPSILON)
    normed = centered * inv_std
    return (normed * gain_vec + shift_vec, normed, inv_std)


def norm_backward(grad_in, normed, inv_std, gain_vec):
    scaled = grad_in * gain_vec
    inner_term = scaled - jnp.mean(scaled, axis=-1, keepdims=True)
    inner_term = inner_term - normed * jnp.mean(scaled * normed, axis=-1, keepdims=True)
    return inner_term * inv_std


BLOCK = 256
MIB = 1 << 20
NARROW = 4
STEPS = 8
HIDDEN = 512
MESH = pl.DeviceIdType.MESH


def head_mask(shape, head):
    lane = lax.broadcasted_iota(jnp.int32, shape, len(shape) - 1)
    return (lane >= head * HEAD_DIM) & (lane < (head + 1) * HEAD_DIM)


def pick_head(values, head):
    return jnp.where(head_mask(values.shape, head), values, jnp.zeros_like(values))


def dot_nt(a, b):
    return lax.dot_general(a, b, (((1,), (1,)), ((), ())), preferred_element_type=jnp.float32)


def dot_nn(a, b):
    return jnp.dot(a, b, preferred_element_type=jnp.float32)


def dot_tn(a, b):
    return lax.dot_general(a, b, (((0,), (0,)), ((), ())), preferred_element_type=jnp.float32)


def front_kernel(lens, x_ref, g_ref, s_ref, w_ref, qb_ref, vb_ref, h_ref, q_ref, k_ref, v_ref, c_ref):
    length = lens[pl.program_id(0)]
    width = q_ref.shape[1]
    for i in range(x_ref.shape[0] // BLOCK):
        rows = pl.ds(i * BLOCK, BLOCK)

        @pl.when(i * BLOCK < length)
        def _():
            normed, _, _ = norm_forward(x_ref[rows, :].astype(jnp.float32), g_ref[...], s_ref[...])
            h1 = normed.astype(jnp.bfloat16)
            h_ref[rows, :] = h1
            qkv = dot_nn(h1, w_ref[...])
            queries = (qkv[:, :width] + qb_ref[...]).astype(jnp.bfloat16)
            q_ref[rows, :] = queries
            k_ref[rows, :] = qkv[:, width : 2 * width].astype(jnp.bfloat16)
            v_ref[rows, :] = (qkv[:, 2 * width :] + vb_ref[...]).astype(jnp.bfloat16)
            count = (i + 1) * BLOCK
            keys, values = k_ref[:count, :], v_ref[:count, :]
            scaled = queries * jnp.bfloat16(HEAD_DIM**-0.5)
            row = lax.broadcasted_iota(jnp.int32, (BLOCK, count), 0) + i * BLOCK
            allowed = lax.broadcasted_iota(jnp.int32, (BLOCK, count), 1) <= row
            total = jnp.zeros((BLOCK, width), jnp.float32)
            for head in range(width // HEAD_DIM):
                scores = jnp.where(allowed, dot_nt(pick_head(scaled, head), keys), MASKED_SCORE)
                weights = jnp.exp(scores - jnp.max(scores, axis=1, keepdims=True))
                weights = weights * (1.0 / jnp.sum(weights, axis=1, keepdims=True))
                total += dot_nn(weights.astype(jnp.bfloat16), pick_head(values, head))
            c_ref[rows, :] = total.astype(jnp.bfloat16)

        @pl.when(i * BLOCK >= length)
        def _():
            for ref in (h_ref, q_ref, k_ref, v_ref, c_ref):
                ref[rows, :] = jnp.zeros((BLOCK, ref.shape[1]), ref.dtype)


def front(lengths, units, gain_vec, shift_vec, weights, q_bias, v_bias):
    rows, width = units.shape
    slots = lengths.shape[0]
    slot_rows = rows // slots
    cols = weights.shape[1] // 3
    whole = lambda a: pl.BlockSpec(a.shape, lambda s, *_: (0,) * a.ndim)
    slot = lambda w: pl.BlockSpec((slot_rows, w), lambda s, *_: (s, 0))
    small = [a.reshape(1, -1) for a in (gain_vec, shift_vec, q_bias, v_bias)]
    shape = lambda w: jax.ShapeDtypeStruct((rows, w), jnp.bfloat16)
    return pl.pallas_call(
        front_kernel,
        grid_spec=pltpu.PrefetchScalarGridSpec(
            num_scalar_prefetch=1,
            grid=(slots,),
            in_specs=[slot(width), whole(small[0]), whole(small[1]), whole(weights), whole(small[2]), whole(small[3])],
            out_specs=[slot(width), slot(cols), slot(cols), slot(cols), slot(cols)],
        ),
        out_shape=[shape(width), shape(cols), shape(cols), shape(cols), shape(cols)],
        compiler_params=pltpu.CompilerParams(vmem_limit_bytes=48 * MIB),
        cost_estimate=pl.CostEstimate(flops=20 * 10**9, bytes_accessed=16 * MIB, transcendentals=8 * MIB),
        name="front",
    )(lengths, units, small[0], small[1], weights, small[2], small[3])


def back_kernel(lens, q_ref, k_ref, v_ref, dc_ref, o_ref, dk_acc, dv_acc):
    length = lens[pl.program_id(0)]
    slot_rows, width = q_ref.shape
    dk_acc[...] = jnp.zeros_like(dk_acc)
    dv_acc[...] = jnp.zeros_like(dv_acc)
    for i in range(slot_rows // BLOCK):
        rows = pl.ds(i * BLOCK, BLOCK)

        @pl.when(i * BLOCK < length)
        def _():
            count = (i + 1) * BLOCK
            keys, values = k_ref[:count, :], v_ref[:count, :]
            scaled = q_ref[rows, :] * jnp.bfloat16(HEAD_DIM**-0.5)
            grads = dc_ref[rows, :]
            col = lax.broadcasted_iota(jnp.int32, (count, BLOCK), 1) + i * BLOCK
            allowed = lax.broadcasted_iota(jnp.int32, (count, BLOCK), 0) <= col
            total = jnp.zeros((BLOCK, width), jnp.float32)
            for head in range(width // HEAD_DIM):
                q_head, g_head = pick_head(scaled, head), pick_head(grads, head)
                scores = jnp.where(allowed, dot_nt(keys, q_head), MASKED_SCORE)
                weights = jnp.exp(scores - jnp.max(scores, axis=0, keepdims=True))
                weights = weights * (1.0 / jnp.sum(weights, axis=0, keepdims=True))
                dv_acc[:count, :] += dot_nn(weights.astype(jnp.bfloat16), g_head)
                weight_grad = dot_nt(values, g_head)
                inner = jnp.sum(weights * weight_grad, axis=0, keepdims=True)
                score_grad = (weights * (weight_grad - inner)).astype(jnp.bfloat16)
                dk_acc[:count, :] += dot_nn(score_grad, q_head)
                total += dot_tn(score_grad, pick_head(keys, head))
            o_ref[rows, :width] = (total * HEAD_DIM**-0.5).astype(jnp.bfloat16)

        @pl.when(i * BLOCK >= length)
        def _():
            o_ref[rows, :width] = jnp.zeros((BLOCK, width), jnp.bfloat16)

    o_ref[:, width : 2 * width] = dk_acc[...].astype(jnp.bfloat16)
    o_ref[:, 2 * width :] = dv_acc[...].astype(jnp.bfloat16)


def back(lengths, queries, keys, values, grads):
    rows, width = queries.shape
    slots = lengths.shape[0]
    slot_rows = rows // slots
    slot = lambda w: pl.BlockSpec((slot_rows, w), lambda s, *_: (s, 0))
    return pl.pallas_call(
        back_kernel,
        grid_spec=pltpu.PrefetchScalarGridSpec(
            num_scalar_prefetch=1,
            grid=(slots,),
            in_specs=[slot(width)] * 4,
            out_specs=slot(3 * width),
            scratch_shapes=[pltpu.VMEM((slot_rows, width), jnp.float32)] * 2,
        ),
        out_shape=jax.ShapeDtypeStruct((rows, 3 * width), jnp.bfloat16),
        compiler_params=pltpu.CompilerParams(vmem_limit_bytes=48 * MIB),
        cost_estimate=pl.CostEstimate(flops=30 * 10**9, bytes_accessed=8 * MIB, transcendentals=8 * MIB),
        name="back",
    )(lengths, queries, keys, values, grads)


def place():
    index = lax.axis_index("narrow")
    core = index + 1 - 2 * (index % 2)
    return index, core, (index + 2) % NARROW, (core + 2) % NARROW


def greet(*wide_peers):
    _, core, cross, _ = place()
    barrier = pltpu.get_barrier_semaphore()
    for peer in (core, cross):
        pl.semaphore_signal(barrier, inc=1, device_id={"narrow": peer}, device_id_type=MESH)
    for peer in wide_peers:
        pl.semaphore_signal(barrier, inc=1, device_id={"wide": peer}, device_id_type=MESH)
    pl.semaphore_wait(barrier, 2 + len(wide_peers))


def remote(source, target, sems, kind, step, peer, axis="narrow"):
    return pltpu.make_async_remote_copy(
        src_ref=source,
        dst_ref=target,
        send_sem=sems.at[0, kind, step],
        recv_sem=sems.at[1, kind, step],
        device_id={axis: peer},
        device_id_type=MESH,
    )


def ring_place(count):
    wide = lax.axis_index("wide")
    odd, half = wide % 2, wide // 2
    spot = odd * (half + 1) + (1 - odd) * ((count - half) % count)

    def at(where):
        high = ((where + count - 1) % count) // (count // 2)
        return (1 - high) * (2 * where - 1) + high * ((2 * (count - where)) % (2 * count))

    return spot, at((spot + 1) % count), at((spot + count - 1) % count)


class Ring:
    UNITS = 4

    def __init__(self, count, sources, outs, view, arrived, held, sems, fetch_sems, keep_sems):
        self.count, self.sources, self.outs, self.view = count, sources, outs, view
        self.arrived, self.held, self.sems = arrived, held, sems
        self.fetch_sems, self.keep_sems = fetch_sems, keep_sems
        spot, following, previous = ring_place(count)
        self.spots = (spot, (count - spot) % count)
        self.peers = (following, previous)

    def block(self, refs, unit, back_by):
        shard = (self.spots[unit // 2] + 2 * self.count - back_by) % self.count
        return self.view(refs[unit // 2], unit // 2, unit % 2, shard)

    def send(self, source, target, kind, unit, step):
        return remote(source, target, self.sems, kind * self.UNITS + unit, step, self.peers[unit // 2], "wide")

    def sum_copy(self, unit, step, first=False):
        source = self.block(self.sources, unit, 0) if first else self.arrived.at[unit, jnp.maximum(step - 1, 0)]
        return self.send(source, self.arrived.at[unit, step], 0, unit, step)

    def fetch(self, unit, step):
        slot = step % 2
        return pltpu.make_async_copy(
            self.block(self.sources, unit, step + 1), self.held.at[unit, slot], self.fetch_sems.at[unit, slot]
        )

    def keep(self, unit):
        return pltpu.make_async_copy(
            self.arrived.at[unit, self.count - 2], self.block(self.outs, unit, self.count - 1), self.keep_sems.at[unit]
        )

    def spread_copy(self, unit, step, first=False):
        target = self.block(self.outs, unit, self.count - 1 + step)
        source = self.arrived.at[unit, self.count - 2] if first else target
        return self.send(source, target, 1, unit, step)

    def start(self):
        for unit in range(self.UNITS):
            self.sum_copy(unit, 0, True).start()
            self.fetch(unit, 0).start()
            self.fetch(unit, 1).start()

    def serve(self, turn, unit):
        last = self.count - 2

        @pl.when(turn <= last)
        def _():
            self.sum_copy(unit, turn).wait_recv()
            self.fetch(unit, turn).wait()
            total = self.held[unit, turn % 2].astype(jnp.float32) + self.arrived[unit, turn].astype(jnp.float32)
            self.arrived[unit, turn] = total.astype(jnp.bfloat16)

            @pl.when(turn < last)
            def _():
                self.sum_copy(unit, turn + 1).start()

            @pl.when(turn < last - 1)
            def _():
                self.fetch(unit, turn + 2).start()

            @pl.when(turn == last)
            def _():
                self.spread_copy(unit, 0, True).start()
                self.keep(unit).start()

        @pl.when((turn > last) & (turn <= 2 * last + 1))
        def _():
            step = turn - last - 1
            self.spread_copy(unit, step).wait_recv()

            @pl.when(step < last)
            def _():
                self.spread_copy(unit, step + 1).start()

    def finish(self):
        for unit in range(self.UNITS):
            self.keep(unit).wait()

        def body(step, carry):
            for unit in range(self.UNITS):
                self.sum_copy(unit, step).wait_send()
                self.spread_copy(unit, step).wait_send()
            return carry

        lax.fori_loop(0, self.count - 1, body, 0)


def ring_scratch(count, block):
    return [
        pltpu.VMEM((Ring.UNITS, count - 1) + block, jnp.bfloat16),
        pltpu.VMEM((Ring.UNITS, 2) + block, jnp.bfloat16),
        pltpu.SemaphoreType.DMA((2, 2 * Ring.UNITS, count - 1)),
        pltpu.SemaphoreType.DMA((Ring.UNITS, 2)),
        pltpu.SemaphoreType.DMA((Ring.UNITS,)),
    ]


class Hop:
    KINDS = 6

    def __init__(self, part, from_core, to_cross, from_cross, full, sems, chunk):
        self.part, self.from_core, self.to_cross, self.from_cross = part, from_core, to_cross, from_cross
        self.full, self.sems, self.chunk = full, sems, chunk
        self.own = part.shape[0] // NARROW
        self.index, self.core, self.cross, self.diagonal = place()

    def rows(self, owner, step):
        return pl.ds(pl.multiple_of(owner * self.own + step * self.chunk, self.chunk), self.chunk)

    def own_rows(self, step):
        return pl.ds(pl.multiple_of(step * self.chunk, self.chunk), self.chunk)

    def core_copies(self, step):
        return [
            remote(self.part.at[self.rows(owner, step)], self.from_core.at[step, slot], self.sems, slot, step, self.core)
            for slot, owner in enumerate((self.core, self.diagonal))
        ]

    def cross_copy(self, step):
        return remote(self.to_cross.at[step], self.from_cross.at[step], self.sems, 2, step, self.cross)

    def gather_copy(self, step, kind):
        owner = self.cross if kind == 5 else self.index
        rows = self.full.at[self.rows(owner, step)]
        return remote(rows, rows, self.sems, kind, step, self.cross if kind == 3 else self.core)

    def send_core(self, step):
        for copy in self.core_copies(step):
            copy.start()

    def send_cross(self, step):
        for copy in self.core_copies(step):
            copy.wait_recv()
        total = self.part[self.rows(self.cross, step), :].astype(jnp.float32)
        total += self.from_core[step, 1].astype(jnp.float32)
        self.to_cross[step] = total.astype(jnp.bfloat16)
        self.cross_copy(step).start()

    def result(self, step):
        total = self.part[self.rows(self.index, step), :].astype(jnp.float32)
        total += self.from_core[step, 0].astype(jnp.float32)
        self.cross_copy(step).wait_recv()
        return total + self.from_cross[step].astype(jnp.float32)

    def send_gather(self, step, values):
        self.full[self.rows(self.index, step), :] = values
        self.gather_copy(step, 3).start()
        self.gather_copy(step, 4).start()

    def forward(self, step):
        self.gather_copy(step, 3).wait_recv()
        self.gather_copy(step, 5).start()

    def gathered(self, step):
        self.gather_copy(step, 4).wait_recv()
        self.gather_copy(step, 5).wait_recv()

    def finish(self, step, gather=True):
        for copy in self.core_copies(step):
            copy.wait_send()
        self.cross_copy(step).wait_send()
        if gather:
            for kind in (3, 4, 5):
                self.gather_copy(step, kind).wait_send()

    def take(self, ref, step):
        return jnp.concatenate([ref[self.rows(owner, step), :] for owner in range(NARROW)], axis=0)

    def put(self, ref, step, values):
        for owner in range(NARROW):
            ref[self.rows(owner, step), :] = values[owner * self.chunk : (owner + 1) * self.chunk]


def hop_scratch(own, chunk, width):
    steps = own // chunk
    return [
        pltpu.VMEM((steps, 2, chunk, width), jnp.bfloat16),
        pltpu.VMEM((steps, chunk, width), jnp.bfloat16),
        pltpu.VMEM((steps, chunk, width), jnp.bfloat16),
        pltpu.SemaphoreType.DMA((2, Hop.KINDS, steps)),
    ]


def stages(steps, work, ring=None, extra=None, ticks=0):
    ticks = max(ticks, steps + len(work) - 1)
    per_tick = 0 if ring is None else -(-2 * (ring.count - 1) // ticks)

    def body(tick, carry):
        for delay, stage in enumerate(work):
            step = tick - delay

            @pl.when((step >= 0) & (step < steps))
            def _():
                stage(step)

            unit = (delay + 1) * Ring.UNITS // len(work) - 1
            if per_tick and unit != delay * Ring.UNITS // len(work) - 1:
                if per_tick == 1:
                    ring.serve(tick, unit)
                else:
                    lax.fori_loop(0, per_tick, lambda i, c: (ring.serve(tick * per_tick + i, unit), c)[1], 0)
        if extra is not None:
            extra(tick)
        return carry

    lax.fori_loop(0, ticks, body, 0)


def middle_kernel(
    c1, units, text, vec, bias, keep, so_w, cq_w, kv_w, co_w,
    h2, h3, q2, c2, kv2, x1, x2,
    part1, part2, core1, tox1, fromx1, sem1, core2, tox2, fromx2, sem2,
):
    steps, chunk, width = tox1.shape
    cols = q2.shape[1]
    slots = keep.shape[0]
    texts = text.shape[0] // slots
    greet()
    one = Hop(part1, core1, tox1, fromx1, h2, sem1, chunk)
    two = Hop(part2, core2, tox2, fromx2, h3, sem2, chunk)
    scale = jnp.bfloat16(HEAD_DIM**-0.5)

    def project(step):
        one.put(part1, step, dot_nn(one.take(c1, step), so_w[...]).astype(jnp.bfloat16))
        one.send_core(step)

        @pl.when(step == 1)
        def _():
            both = dot_nn(text[...], kv_w[...])
            kv2[:, :cols] = both[:, :cols].astype(jnp.bfloat16)
            kv2[:, cols:] = (both[:, cols:] + bias[1:2, :]).astype(jnp.bfloat16)

    def norm_one(step):
        rows = one.own_rows(step)
        resid = units[rows, :].astype(jnp.float32) + one.result(step) + vec[2:3, :]
        x1[rows, :] = resid
        one.send_gather(step, norm_forward(resid, vec[0:1, :], vec[1:2, :])[0].astype(jnp.bfloat16))

    def cross(step):
        one.gathered(step)
        queries = (dot_nn(one.take(h2, step), cq_w[...]) + bias[0:1, :]).astype(jnp.bfloat16)
        one.put(q2, step, queries)
        scaled = queries * scale
        count = queries.shape[0] // slots
        context = []
        for slot in range(slots):
            mine = scaled[slot * count : (slot + 1) * count]
            keys = kv2[slot * texts : (slot + 1) * texts, :cols]
            values = kv2[slot * texts : (slot + 1) * texts, cols:]
            total = jnp.zeros((count, cols), jnp.float32)
            for head in range(cols // HEAD_DIM):
                scores = dot_nt(pick_head(mine, head), keys)
                scores = jnp.where(keep[slot : slot + 1, :] > 0.5, scores, MASKED_SCORE)
                weights = jnp.exp(scores - jnp.max(scores, axis=1, keepdims=True))
                weights = weights * (1.0 / jnp.sum(weights, axis=1, keepdims=True))
                total += dot_nn(weights.astype(jnp.bfloat16), pick_head(values, head))
            context.append(total.astype(jnp.bfloat16))
        context = jnp.concatenate(context, axis=0)
        one.put(c2, step, context)
        two.put(part2, step, dot_nn(context, co_w[...]).astype(jnp.bfloat16))
        two.send_core(step)

    def norm_two(step):
        rows = one.own_rows(step)
        resid = x1[rows, :] + two.result(step) + vec[5:6, :]
        x2[rows, :] = resid
        two.send_gather(step, norm_forward(resid, vec[3:4, :], vec[4:5, :])[0].astype(jnp.bfloat16))

    stages(
        steps,
        [
            project, one.send_cross, norm_one, one.forward, cross,
            two.send_cross, norm_two, two.forward, two.gathered,
        ],
    )

    def finish(step, carry):
        one.finish(step)
        two.finish(step)
        return carry

    lax.fori_loop(0, steps, finish, 0)


def middle(c1, units_own, text, vec, bias, keep, so_w, cq_w, kv_w, co_w):
    rows, cols = c1.shape
    own, width = units_own.shape
    chunk = own // STEPS
    bf, f32 = jnp.bfloat16, jnp.float32
    shape = jax.ShapeDtypeStruct
    vmem = pl.BlockSpec(memory_space=pltpu.VMEM)
    hop = hop_scratch(own, chunk, width)
    return pl.pallas_call(
        middle_kernel,
        in_specs=[vmem] * 10,
        out_specs=[vmem] * 7,
        out_shape=[
            shape((rows, width), bf),
            shape((rows, width), bf),
            shape((rows, cols), bf),
            shape((rows, cols), bf),
            shape((text.shape[0], 2 * cols), bf),
            shape((own, width), f32),
            shape((own, width), f32),
        ],
        scratch_shapes=[pltpu.VMEM((rows, width), bf)] * 2 + hop + hop,
        compiler_params=pltpu.CompilerParams(collective_id=0, has_side_effects=True, vmem_limit_bytes=58 * MIB),
        cost_estimate=pl.CostEstimate(flops=100 * 10**9, bytes_accessed=24 * MIB, transcendentals=4 * MIB),
        name="middle",
    )(c1, units_own, text, vec, bias, keep, so_w, cq_w, kv_w, co_w)


def ffn_kernel(lens, h_ref, e_ref, wi_ref, b_ref, wo_ref, a_ref, d_ref, gi_ref, go_ref, gb_ref, gi_acc, go_acc):
    block = pl.program_id(0)
    per_slot = pl.num_programs(0) // lens.shape[0]
    length = lens[block // per_slot]

    @pl.when(block == 0)
    def _():
        gi_acc[...] = jnp.zeros_like(gi_acc)
        go_acc[...] = jnp.zeros_like(go_acc)
        gb_ref[...] = jnp.zeros_like(gb_ref)

    live = (block % per_slot) * BLOCK < length

    @pl.when(live)
    def _():
        rows, grads = h_ref[...], e_ref[...]
        out = jnp.zeros(a_ref.shape, jnp.float32)
        back_out = jnp.zeros(d_ref.shape, jnp.float32)
        hidden_count = wo_ref.shape[0]
        for first in range(0, hidden_count, HIDDEN):
            part = slice(first, first + HIDDEN)
            pre = dot_nn(rows, wi_ref[:, part]) + b_ref[:, part]
            cdf = 0.5 + 0.5 * lax.erf(pre * (0.5**0.5))
            pdf = jnp.exp(-0.5 * pre * pre) * 0.3989422804014327
            hidden = (pre * cdf).astype(jnp.bfloat16)
            slope = cdf + pre * pdf
            pre_grad = slope * dot_nt(grads, wo_ref[part, :])
            pre_low = pre_grad.astype(jnp.bfloat16)
            gb_ref[:, part] += jnp.sum(pre_low.astype(jnp.float32), axis=0, keepdims=True)
            out += dot_nn(hidden, wo_ref[part, :])
            back_out += dot_nt(pre_low, wi_ref[:, part])
            go_acc[part, :] += dot_tn(hidden, grads)
            gi_acc[:, part] += dot_tn(rows, pre_low)
        a_ref[...] = out.astype(jnp.bfloat16)
        d_ref[...] = back_out.astype(jnp.bfloat16)

    @pl.when(jnp.logical_not(live))
    def _():
        a_ref[...] = jnp.zeros_like(a_ref)
        d_ref[...] = jnp.zeros_like(d_ref)

    @pl.when(block == pl.num_programs(0) - 1)
    def _():
        gi_ref[...] = gi_acc[...].astype(jnp.bfloat16)
        go_ref[...] = go_acc[...].astype(jnp.bfloat16)


def ffn(lengths, rows_in, grads, w_in, b_in, w_out):
    rows, width = rows_in.shape
    count = w_out.shape[0]
    bf, f32 = jnp.bfloat16, jnp.float32
    shape = jax.ShapeDtypeStruct
    block = pl.BlockSpec((BLOCK, width), lambda i, *_: (i, 0))
    whole = lambda a, b: pl.BlockSpec((a, b), lambda i, *_: (0, 0), pipeline_mode=pl.Buffered(1))
    return pl.pallas_call(
        ffn_kernel,
        grid_spec=pltpu.PrefetchScalarGridSpec(
            num_scalar_prefetch=1,
            grid=(rows // BLOCK,),
            in_specs=[block, block, whole(width, count), whole(1, count), whole(count, width)],
            out_specs=[block, block, whole(width, count), whole(count, width), whole(1, count)],
            scratch_shapes=[pltpu.VMEM((width, count), f32), pltpu.VMEM((count, width), f32)],
        ),
        out_shape=[
            shape((rows, width), bf),
            shape((rows, width), bf),
            shape((width, count), bf),
            shape((count, width), bf),
            shape((1, count), f32),
        ],
        compiler_params=pltpu.CompilerParams(vmem_limit_bytes=58 * MIB),
        cost_estimate=pl.CostEstimate(flops=60 * 10**9, bytes_accessed=32 * MIB, transcendentals=8 * MIB),
        name="ffn",
    )(lengths, rows_in, grads, w_in, b_in.reshape(1, -1), w_out)


class FarHop(Hop):
    def fetch(self, mine, theirs, sems):
        self.mine, self.theirs = mine, theirs
        rows = lambda owner: pl.ds(pl.multiple_of(owner * self.own, self.own), self.own)
        self.fetches = [
            pltpu.make_async_copy(self.part.at[rows(owner)], ref, sems.at[slot])
            for slot, (owner, ref) in enumerate(((self.index, mine), (self.cross, theirs)))
        ]
        for copy in self.fetches:
            copy.start()

    def fetched(self):
        for copy in self.fetches:
            copy.wait()

    def cross_copy(self, step):
        return remote(
            self.theirs.at[self.own_rows(step)], self.from_cross.at[step], self.sems, 2, step, self.cross
        )

    def send_cross(self, step):
        for copy in self.core_copies(step):
            copy.wait_recv()
        total = self.theirs[self.own_rows(step), :].astype(jnp.float32)
        total += self.from_core[step, 1].astype(jnp.float32)
        self.theirs[self.own_rows(step), :] = total.astype(jnp.bfloat16)
        self.cross_copy(step).start()

    def result(self, step):
        total = self.mine[self.own_rows(step), :].astype(jnp.float32)
        total += self.from_core[step, 0].astype(jnp.float32)
        self.cross_copy(step).wait_recv()
        return total + self.from_cross[step].astype(jnp.float32)


def column_sum(values):
    return jnp.sum(values, axis=0, keepdims=True)


def turn_kernel(
    third, in_g, out_g, x1, x2, e_own, h2, q2, c2, kv2, c1, keep, vec, co_w, cq_w, so_w,
    in_sum, out_sum, dx1, dc1, dkv, co_g, cq_g, so_g, bias_g, stats,
    mine3, theirs3, core3, fromx3, sem3,
    part5, core5, tox5, fromx5, sem5, full3, full5, dx2, co_acc, cq_acc, so_acc, dkv_acc, fetch_sem,
    *ring_refs, count,
):
    steps, chunk, width = tox5.shape
    cols = q2.shape[1]
    slots = bias_g.shape[0]
    texts = kv2.shape[0] // slots

    def ring_view(ref, way, half, shard):
        high = width // count
        if way == 0:
            return ref.at[pl.ds(pl.multiple_of(shard * high, high), high), pl.ds(half * width, width)]
        return ref.at[pl.ds(pl.multiple_of(shard * 2 * high + half * high, high), high), :]

    ring = Ring(count, (in_g, out_g), (in_sum, out_sum), ring_view, *ring_refs)
    greet(*ring.peers)
    ring.start()
    three = FarHop(third, core3, None, fromx3, full3, sem3, chunk)
    five = Hop(part5, core5, tox5, fromx5, full5, sem5, chunk)
    three.fetch(mine3, theirs3, fetch_sem)

    def start(step, carry):
        three.send_core(step)
        return carry

    lax.fori_loop(0, steps, start, 0)
    for ref in (co_acc, cq_acc, so_acc, dkv_acc, bias_g, stats):
        ref[...] = jnp.zeros_like(ref)
    three.fetched()
    scale = jnp.bfloat16(HEAD_DIM**-0.5)

    def norm_three(step):
        rows = three.own_rows(step)
        grad_in = three.result(step)
        _, normed, inv_std = norm_forward(x2[rows, :], vec[0:1, :], vec[0:1, :])
        stats[0:1, :] += column_sum(grad_in * normed)
        stats[1:2, :] += column_sum(grad_in)
        above = e_own[rows, :].astype(jnp.float32)
        total = above + norm_backward(grad_in, normed, inv_std, vec[0:1, :])
        stats[2:3, :] += column_sum(above)
        stats[3:4, :] += column_sum(total)
        dx2[rows, :] = total
        three.send_gather(step, total.astype(jnp.bfloat16))

    def cross(step):
        three.gathered(step)
        grads = three.take(full3, step)
        co_acc[...] += dot_tn(three.take(c2, step), grads)
        context = dot_nt(grads, co_w[...]).astype(jnp.bfloat16)
        queries = three.take(q2, step) * scale
        count = queries.shape[0] // slots
        q_grad = []
        for slot in range(slots):
            rows = slice(slot * count, (slot + 1) * count)
            texts_here = slice(slot * texts, (slot + 1) * texts)
            keys, values = kv2[texts_here, :cols], kv2[texts_here, cols:]
            total = jnp.zeros((count, cols), jnp.float32)
            for head in range(cols // HEAD_DIM):
                q_head, g_head = pick_head(queries[rows], head), pick_head(context[rows], head)
                scores = jnp.where(keep[texts_here, :] > 0.5, dot_nt(keys, q_head), MASKED_SCORE)
                weights = jnp.exp(scores - jnp.max(scores, axis=0, keepdims=True))
                weights = weights * (1.0 / jnp.sum(weights, axis=0, keepdims=True))
                dkv_acc[texts_here, cols:] += dot_nn(weights.astype(jnp.bfloat16), g_head)
                weight_grad = dot_nt(values, g_head)
                inner = jnp.sum(weights * weight_grad, axis=0, keepdims=True)
                score_grad = (weights * (weight_grad - inner)).astype(jnp.bfloat16)
                dkv_acc[texts_here, :cols] += dot_nn(score_grad, q_head)
                total += dot_tn(score_grad, pick_head(keys, head))
            q_grad.append((total * HEAD_DIM**-0.5).astype(jnp.bfloat16))
        q_grad = jnp.concatenate(q_grad, axis=0)
        five.put(part5, step, dot_nt(q_grad, cq_w[...]).astype(jnp.bfloat16))
        five.send_core(step)
        bias_g[0:1, :] += column_sum(q_grad.astype(jnp.float32))
        cq_acc[...] += dot_tn(five.take(h2, step), q_grad)

    def norm_two(step):
        rows = five.own_rows(step)
        grad_in = five.result(step)
        _, normed, inv_std = norm_forward(x1[rows, :], vec[1:2, :], vec[1:2, :])
        stats[4:5, :] += column_sum(grad_in * normed)
        stats[5:6, :] += column_sum(grad_in)
        total = dx2[rows, :] + norm_backward(grad_in, normed, inv_std, vec[1:2, :])
        stats[6:7, :] += column_sum(total)
        dx1[rows, :] = total
        five.send_gather(step, total.astype(jnp.bfloat16))

    def last(step):
        five.gathered(step)
        grads = five.take(full5, step)
        dc1_rows = dot_nt(grads, so_w[...]).astype(jnp.bfloat16)
        five.put(dc1, step, dc1_rows)
        so_acc[...] += dot_tn(five.take(c1, step), grads)

    stages(
        steps,
        [
            three.send_cross, norm_three, three.forward, cross,
            five.send_cross, norm_two, five.forward, last,
        ],
        ring,
    )
    dkv[...] = dkv_acc[...].astype(jnp.bfloat16)
    bias_g[1:2, :] = column_sum(dkv[:, cols:].astype(jnp.float32))
    co_g[...] = co_acc[...].astype(jnp.bfloat16)
    cq_g[...] = cq_acc[...].astype(jnp.bfloat16)
    so_g[...] = so_acc[...].astype(jnp.bfloat16)

    def finish(step, carry):
        three.finish(step)
        five.finish(step)
        return carry

    lax.fori_loop(0, steps, finish, 0)
    ring.finish()


def turn(count, third, in_g, out_g, x1, x2, e_own, h2, q2, c2, kv2, c1, keep, vec, co_w, cq_w, so_w):
    rows, cols = c1.shape
    own, width = x1.shape
    chunk = own // STEPS
    bf, f32 = jnp.bfloat16, jnp.float32
    shape = jax.ShapeDtypeStruct
    vmem = pl.BlockSpec(memory_space=pltpu.VMEM)
    hbm = pl.BlockSpec(memory_space=pl.ANY)
    hop = hop_scratch(own, chunk, width)
    far = [pltpu.VMEM((own, width), bf)] * 2 + [hop[0], hop[2], hop[3]]
    return pl.pallas_call(
        functools.partial(turn_kernel, count=count),
        in_specs=[hbm] * 3 + [vmem] * 13,
        out_specs=[hbm] * 2 + [vmem] * 8,
        out_shape=[
            shape(in_g.shape, bf),
            shape(out_g.shape, bf),
            shape((own, width), f32),
            shape((rows, cols), bf),
            shape(kv2.shape, bf),
            shape((cols, width), bf),
            shape((width, cols), bf),
            shape((cols, width), bf),
            shape((2, cols), f32),
            shape((8, width), f32),
        ],
        scratch_shapes=far
        + [pltpu.VMEM((rows, width), bf)]
        + hop
        + [pltpu.VMEM((rows, width), bf)] * 2
        + [
            pltpu.VMEM((own, width), f32),
            pltpu.VMEM((cols, width), f32),
            pltpu.VMEM((width, cols), f32),
            pltpu.VMEM((cols, width), f32),
            pltpu.VMEM(kv2.shape, f32),
            pltpu.SemaphoreType.DMA((2,)),
        ]
        + ring_scratch(count, (width // count, width)),
        compiler_params=pltpu.CompilerParams(collective_id=1, has_side_effects=True, vmem_limit_bytes=60 * MIB),
        cost_estimate=pl.CostEstimate(flops=100 * 10**9, bytes_accessed=24 * MIB, transcendentals=4 * MIB),
        name="turn",
    )(third, in_g, out_g, x1, x2, e_own, h2, q2, c2, kv2, c1, keep, vec, co_w, cq_w, so_w)


SMALL = 16
NORM_ROWS = 9


class Small:
    def __init__(self, count, block, near, far, sems):
        self.count, self.mine, self.near, self.far, self.sems = count, block, near, far, sems
        self.index, self.core, self.cross, _ = place()
        self.spot, self.following, _ = ring_place(count)

    def near_copy(self, kind):
        owner = self.cross if kind == 2 else self.index
        return remote(self.near.at[owner], self.near.at[owner], self.sems, 0, kind, (self.cross, self.core, self.core)[kind])

    def far_copy(self, step):
        block = self.far.at[(self.spot + self.count - step) % self.count]
        return remote(block, block, self.sems, 1, step, self.following, "wide")

    def begin(self):
        self.near[self.index] = self.mine[...]
        self.near_copy(0).start()
        self.near_copy(1).start()

    def forward(self):
        self.near_copy(0).wait_recv()
        self.near_copy(2).start()

    def launch(self):
        self.near_copy(1).wait_recv()
        self.near_copy(2).wait_recv()
        both = self.near[0]
        for owner in range(1, NARROW):
            both += self.near[owner]
        row = lax.broadcasted_iota(jnp.int32, both.shape, 0)
        self.far[self.spot] = jnp.where(row < SMALL - NORM_ROWS, self.mine[...], both)
        self.far_copy(0).start()

    def rotate(self, step):
        self.far_copy(step).wait_recv()

        @pl.when(step < self.count - 2)
        def _():
            self.far_copy(step + 1).start()

    def finish(self, out):
        for kind in range(3):
            self.near_copy(kind).wait_send()

        def body(step, carry):
            self.far_copy(step).wait_send()
            return carry

        lax.fori_loop(0, self.count - 1, body, 0)
        out[...] = jnp.zeros_like(out)

        def add(spot, carry):
            out[...] += self.far[spot]
            return carry

        lax.fori_loop(0, self.count, add, 0)


def last_kernel(
    ffn_part, g0, g1, dqkv, dkv, units, dx1, x2, valid, before, stats, vec, qkv_w, kv_w,
    sum0, sum1, y, units_g, text_g, small_sum,
    mine4, theirs4, core4, fromx4, sem4,
    part6, core6, tox6, fromx6, sem6, part7, core7, tox7, fromx7, sem7,
    fetch_sem, block, near, far, small_sem, *ring_refs, count,
):
    steps, chunk, width = tox6.shape
    text_steps = tox7.shape[0]

    def ring_view(ref, way, half, shard):
        high = width // count
        return ref.at[pl.ds(pl.multiple_of(shard * high, high), high), pl.ds(half * (width // 2), width // 2)]

    ring = Ring(count, (g0, g1), (sum0, sum1), ring_view, *ring_refs)
    small = Small(count, block, near, far, small_sem)
    greet(*ring.peers)
    ring.start()
    four = FarHop(ffn_part, core4, None, fromx4, None, sem4, chunk)
    six = Hop(part6, core6, tox6, fromx6, None, sem6, chunk)
    seven = Hop(part7, core7, tox7, fromx7, None, sem7, chunk)
    four.fetch(mine4, theirs4, fetch_sem)
    four.fetched()
    block[: SMALL - NORM_ROWS, :] = before[...]
    block[SMALL - NORM_ROWS :, :] = jnp.concatenate([stats[:7, :], jnp.zeros((2, width), jnp.float32)])
    gain = vec[0:1, :]

    def project(step):
        six.put(part6, step, dot_nt(six.take(dqkv, step), qkv_w[...]).astype(jnp.bfloat16))
        six.send_core(step)
        four.send_core(step)

    def norm_one(step):
        rows = six.own_rows(step)
        grad_in = six.result(step)
        _, normed, inv_std = norm_forward(units[rows, :].astype(jnp.float32), gain, gain)
        block[SMALL - 2 : SMALL - 1, :] += column_sum(grad_in * normed)
        block[SMALL - 1 : SMALL, :] += column_sum(grad_in)
        units_g[rows, :] = dx1[rows, :] + norm_backward(grad_in, normed, inv_std, gain)

    def text_only(work):
        def stage(step):
            @pl.when(step < text_steps)
            def _():
                work(step)

        return stage

    def text_project(step):
        seven.put(part7, step, dot_nt(seven.take(dkv, step), kv_w[...]).astype(jnp.bfloat16))
        seven.send_core(step)

    def text_result(step):
        text_g[seven.own_rows(step), :] = seven.result(step)

    def output(step):
        rows = four.own_rows(step)
        total = x2[rows, :] + four.result(step) + vec[1:2, :]
        y[rows, :] = jnp.where(valid[rows, :1] > 0.5, total, 0.0).astype(jnp.bfloat16)

    ready = steps + 2

    def extra(tick):
        for when, work in enumerate((small.begin, small.forward, small.launch)):
            pl.when(tick == ready + when)(work)
        step = tick - ready - 3

        @pl.when((step >= 0) & (step < count - 1))
        def _():
            small.rotate(step)

    stages(
        steps,
        [
            project, six.send_cross, norm_one, four.send_cross, output,
            text_only(text_project), text_only(seven.send_cross), text_only(text_result),
        ],
        ring,
        extra,
        ready + 3 + count - 1,
    )

    def finish(step, carry):
        four.finish(step, False)
        six.finish(step, False)
        text_only(lambda s: seven.finish(s, False))(step)
        return carry

    lax.fori_loop(0, steps, finish, 0)
    ring.finish()
    small.finish(small_sum)


def last(count, ffn_part, g0, g1, dqkv, dkv, units_own, dx1, x2, valid, before, stats, vec, qkv_w, kv_w):
    rows = dqkv.shape[0]
    own, width = units_own.shape
    chunk = own // STEPS
    text_own = dkv.shape[0] // NARROW
    bf, f32 = jnp.bfloat16, jnp.float32
    shape = jax.ShapeDtypeStruct
    vmem = pl.BlockSpec(memory_space=pltpu.VMEM)
    hbm = pl.BlockSpec(memory_space=pl.ANY)
    hop = hop_scratch(own, chunk, width)
    far = [pltpu.VMEM((own, width), bf)] * 2 + [hop[0], hop[2], hop[3]]
    return pl.pallas_call(
        functools.partial(last_kernel, count=count),
        in_specs=[hbm] * 3 + [vmem] * 11,
        out_specs=[hbm] * 2 + [vmem] * 4,
        out_shape=[
            shape(g0.shape, bf),
            shape(g1.shape, bf),
            shape((own, width), bf),
            shape((own, width), f32),
            shape((text_own, width), f32),
            shape((SMALL, width), f32),
        ],
        scratch_shapes=far
        + [pltpu.VMEM((rows, width), bf)]
        + hop
        + [pltpu.VMEM((dkv.shape[0], width), bf)]
        + hop_scratch(text_own, chunk, width)
        + [
            pltpu.SemaphoreType.DMA((2,)),
            pltpu.VMEM((SMALL, width), f32),
            pltpu.VMEM((NARROW, SMALL, width), f32),
            pltpu.VMEM((count, SMALL, width), f32),
            pltpu.SemaphoreType.DMA((2, 2, max(count - 1, 3))),
        ]
        + ring_scratch(count, (width // count, width // 2)),
        compiler_params=pltpu.CompilerParams(collective_id=2, has_side_effects=True, vmem_limit_bytes=58 * MIB),
        cost_estimate=pl.CostEstimate(flops=30 * 10**9, bytes_accessed=16 * MIB, transcendentals=0),
        name="last",
    )(ffn_part, g0, g1, dqkv, dkv, units_own, dx1, x2, valid, before, stats, vec, qkv_w, kv_w)


def local(
    units,
    text,
    out_grad,
    unit_lengths,
    text_lengths,
    bucket_counts,
    norm_gain,
    norm_shift,
    self_qkv,
    self_bias,
    self_out,
    cross_q,
    cross_kv,
    cross_bias,
    cross_out,
    ffn_in,
    ffn_in_bias,
    ffn_out,
    out_bias,
):
    own_rows = units.shape[0] // NARROW
    first_own = lax.axis_index("narrow") * own_rows
    slot_count = unit_lengths.shape[0]
    slot_live = jnp.arange(slot_count, dtype=jnp.int32) < bucket_counts[0]
    lengths = jnp.where(slot_live, unit_lengths, 0)
    positions = first_own + jnp.arange(own_rows, dtype=jnp.int32)
    slot_match = (positions // UNITS)[:, None] == jnp.arange(slot_count, dtype=jnp.int32)[None, :]
    row_limit = jnp.sum(jnp.where(slot_match, lengths[None, :], 0), axis=1)
    valid_own = positions % UNITS < row_limit
    text_pos = jnp.arange(TEXT, dtype=jnp.int32)
    keep = (text_pos[None, :] < text_lengths[:, None]).astype(jnp.float32)

    def own(rows):
        return lax.dynamic_slice_in_dim(rows, first_own, own_rows, 0)

    qkv_weights = self_qkv.reshape(self_qkv.shape[0], -1)
    kv_weights = cross_kv.reshape(cross_kv.shape[0], -1)
    own_units = own(units)
    first_in, queries, key_rows, value_rows, self_context = front(
        lengths, units, norm_gain[0], norm_shift[0], qkv_weights, self_bias[0], self_bias[1]
    )
    last_bias = jnp.zeros((3,) + out_bias.shape[1:], jnp.float32)
    second_all, third_all, cross_queries, cross_context, text_kv, resid_one, resid_two = middle(
        self_context,
        own_units,
        text,
        jnp.concatenate([norm_gain[1:2], norm_shift[1:2], out_bias[0:1], norm_gain[2:3], norm_shift[2:3], out_bias[1:2], last_bias[:2]]),
        cross_bias,
        keep,
        self_out,
        cross_q,
        kv_weights,
        cross_out,
    )
    ffn_part, third_part, ffn_in_grad, ffn_out_grad, ffn_in_bias_grad = ffn(
        lengths, third_all, out_grad, ffn_in, ffn_in_bias, ffn_out
    )
    grad_own = jnp.where(valid_own[:, None], own(out_grad), jnp.zeros((), out_grad.dtype))
    spread = own_rows // STEPS * NARROW // slot_count
    count = lax.axis_size("wide")
    ffn_in_grad, ffn_out_grad, resid_one_grad, self_context_grad, text_kv_grad, cross_out_grad, cross_q_grad, self_out_grad, cross_bias_grad, stats = turn(
        count,
        third_part,
        ffn_in_grad,
        ffn_out_grad,
        resid_one,
        resid_two,
        grad_own,
        second_all,
        cross_queries,
        cross_context,
        text_kv,
        self_context,
        jnp.broadcast_to(keep.reshape(-1, 1), (keep.size, spread)),
        jnp.concatenate([norm_gain[2:3], norm_gain[1:2]]),
        cross_out,
        cross_q,
        self_out,
    )
    qkv_grad = back(lengths, queries, key_rows, value_rows, self_context_grad)
    cols = queries.shape[1]
    self_qkv_grad = dot_tn(first_in, qkv_grad).astype(jnp.bfloat16)
    cross_kv_grad = dot_tn(text, text_kv_grad).astype(jnp.bfloat16)
    half = cross_kv_grad.shape[0] // 2
    width = units.shape[1]
    before = jnp.concatenate(
        [
            jnp.sum(qkv_grad[:, :cols], axis=0, dtype=jnp.float32),
            jnp.sum(qkv_grad[:, 2 * cols :], axis=0, dtype=jnp.float32),
            cross_bias_grad.reshape(-1),
            ffn_in_bias_grad.reshape(-1),
        ]
    ).reshape(-1, width)
    small_rows = SMALL // 2
    summed_one, summed_two, output, units_grad, text_grad, small = last(
        count,
        ffn_part,
        jnp.concatenate([self_qkv_grad, cross_q_grad], axis=1),
        jnp.concatenate(
            [cross_out_grad, self_out_grad, jnp.concatenate([cross_kv_grad[:half], cross_kv_grad[half:]], axis=1)]
        ),
        qkv_grad,
        text_kv_grad,
        own_units,
        resid_one_grad,
        resid_two,
        jnp.broadcast_to(valid_own[:, None].astype(jnp.float32), (own_rows, 128)),
        jnp.concatenate([before, jnp.zeros((SMALL - NORM_ROWS - before.shape[0], width), jnp.float32)]),
        stats,
        jnp.concatenate([norm_gain[0:1], out_bias[2:3]]),
        qkv_weights,
        kv_weights,
    )
    summed_one, summed_two = summed_one.astype(jnp.float32), summed_two.astype(jnp.float32)
    self_qkv_grad = summed_one[:, : 3 * cols].reshape(self_qkv.shape)
    cross_q_grad = summed_one[:, 3 * cols :]
    cross_out_grad, self_out_grad = summed_two[:cols], summed_two[cols : 2 * cols]
    cross_kv_grad = jnp.concatenate(
        [summed_two[2 * cols :, : 2 * cols], summed_two[2 * cols :, 2 * cols :]]
    ).reshape(cross_kv.shape)
    ffn_in_grad, ffn_out_grad = ffn_in_grad.astype(jnp.float32), ffn_out_grad.astype(jnp.float32)
    biases = small[: before.shape[0]].reshape(-1)
    self_bias_grad = biases[: 2 * cols].reshape(2, cols)
    cross_bias_grad = biases[2 * cols : 4 * cols].reshape(2, cols)
    ffn_in_bias_grad = biases[4 * cols :]
    norms = small[SMALL - NORM_ROWS :]
    gain_grad = jnp.stack([norms[7], norms[4], norms[0]])
    shift_grad = jnp.stack([norms[8], norms[5], norms[1]])
    bias_grad = jnp.stack([norms[6], norms[3], norms[2]])
    return (
        output,
        units_grad,
        text_grad,
        gain_grad,
        shift_grad,
        self_qkv_grad,
        self_bias_grad,
        self_out_grad,
        cross_q_grad,
        cross_kv_grad,
        cross_bias_grad,
        cross_out_grad,
        ffn_in_grad,
        ffn_in_bias_grad,
        ffn_out_grad,
        bias_grad,
    )


def solution(mesh):
    placed = (
        P("wide", None),
        P("wide", None),
        P("wide", None),
        P("wide"),
        P("wide"),
        P("wide"),
        P(),
        P(),
        P(None, None, "narrow"),
        P(None, "narrow"),
        P("narrow", None),
        P(None, "narrow"),
        P(None, None, "narrow"),
        P(None, "narrow"),
        P("narrow", None),
        P(None, "narrow"),
        P("narrow"),
        P("narrow", None),
        P(),
    )
    return jax.shard_map(
        local,
        mesh=mesh,
        in_specs=placed,
        out_specs=(
            P(("wide", "narrow"), None),
            P(("wide", "narrow"), None),
            P(("wide", "narrow"), None),
            P(),
            P(),
            P(None, None, "narrow"),
            P(None, "narrow"),
            P("narrow", None),
            P(None, "narrow"),
            P(None, None, "narrow"),
            P(None, "narrow"),
            P("narrow", None),
            P(None, "narrow"),
            P("narrow"),
            P("narrow", None),
            P(),
        ),
        check_vma=False,
    )
```

```python
import functools

import jax
import jax.numpy as jnp
from jax import lax
from jax.experimental import pallas as pl
from jax.experimental.pallas import tpu as pltpu
from jax.sharding import PartitionSpec as P

HEAD_DIM = 64


NORM_EPSILON = 1e-05
MASKED_SCORE = -1000000000.0
EXACT = lax.Precision.HIGHEST


def norm_forward(values, gain_vec, shift_vec):
    row_mean = jnp.mean(values, axis=-1, keepdims=True)
    centered = values - row_mean
    inv_std = lax.rsqrt(jnp.mean(centered * centered, axis=-1, keepdims=True) + NORM_EPSILON)
    normed = centered * inv_std
    return (normed * gain_vec + shift_vec, normed, inv_std)


def norm_backward(grad_in, normed, inv_std, gain_vec):
    scaled = grad_in * gain_vec
    inner_term = scaled - jnp.mean(scaled, axis=-1, keepdims=True)
    inner_term = inner_term - normed * jnp.mean(scaled * normed, axis=-1, keepdims=True)
    return inner_term * inv_std


BLOCK = 256
MIB = 1 << 20
NARROW = 4
STEPS = 8
HIDDEN = 512
MESH = pl.DeviceIdType.MESH


def head_mask(shape, head):
    lane = lax.broadcasted_iota(jnp.int32, shape, len(shape) - 1)
    return (lane >= head * HEAD_DIM) & (lane < (head + 1) * HEAD_DIM)


def pick_head(values, head):
    return jnp.where(head_mask(values.shape, head), values, jnp.zeros_like(values))


def dot_nt(a, b):
    return lax.dot_general(a, b, (((1,), (1,)), ((), ())), preferred_element_type=jnp.float32)


def dot_nn(a, b):
    return jnp.dot(a, b, preferred_element_type=jnp.float32)


def dot_tn(a, b):
    return lax.dot_general(a, b, (((0,), (0,)), ((), ())), preferred_element_type=jnp.float32)


def column_sum(values):
    return jnp.sum(values, axis=0, keepdims=True)


def front_kernel(lens, x_ref, g_ref, s_ref, w_ref, b_ref, h_ref, q_ref, k_ref, v_ref, c_ref):
    length = lens[pl.program_id(0)]
    width = q_ref.shape[1]
    for i in range(x_ref.shape[0] // BLOCK):
        rows = pl.ds(i * BLOCK, BLOCK)

        @pl.when(i * BLOCK < length)
        def _():
            normed, _, _ = norm_forward(x_ref[rows, :].astype(jnp.float32), g_ref[0:1, :], s_ref[0:1, :])
            h1 = normed.astype(jnp.bfloat16)
            h_ref[rows, :] = h1
            queries = (dot_nn(h1, w_ref[0]) + b_ref[0:1, :]).astype(jnp.bfloat16)
            q_ref[rows, :] = queries
            k_ref[rows, :] = dot_nn(h1, w_ref[1]).astype(jnp.bfloat16)
            v_ref[rows, :] = (dot_nn(h1, w_ref[2]) + b_ref[1:2, :]).astype(jnp.bfloat16)
            count = (i + 1) * BLOCK
            keys, values = k_ref[:count, :], v_ref[:count, :]
            scaled = queries * jnp.bfloat16(HEAD_DIM**-0.5)
            row = lax.broadcasted_iota(jnp.int32, (BLOCK, count), 0) + i * BLOCK
            allowed = lax.broadcasted_iota(jnp.int32, (BLOCK, count), 1) <= row
            total = jnp.zeros((BLOCK, width), jnp.float32)
            for head in range(width // HEAD_DIM):
                scores = jnp.where(allowed, dot_nt(pick_head(scaled, head), keys), MASKED_SCORE)
                weights = jnp.exp(scores - jnp.max(scores, axis=1, keepdims=True))
                weights = weights * (1.0 / jnp.sum(weights, axis=1, keepdims=True))
                total += dot_nn(weights.astype(jnp.bfloat16), pick_head(values, head))
            c_ref[rows, :] = total.astype(jnp.bfloat16)

        @pl.when(i * BLOCK >= length)
        def _():
            for ref in (h_ref, q_ref, k_ref, v_ref, c_ref):
                ref[rows, :] = jnp.zeros((BLOCK, ref.shape[1]), ref.dtype)


def front(lengths, units, gains, shifts, weights, bias):
    rows, width = units.shape
    slots = lengths.shape[0]
    slot_rows = rows // slots
    cols = weights.shape[2]
    whole = lambda a: pl.BlockSpec(a.shape, lambda s, *_: (0,) * a.ndim)
    slot = lambda w: pl.BlockSpec((slot_rows, w), lambda s, *_: (s, 0))
    shape = lambda w: jax.ShapeDtypeStruct((rows, w), jnp.bfloat16)
    far = lambda w: pltpu.HBM((rows, w), jnp.bfloat16)
    return pl.pallas_call(
        front_kernel,
        grid_spec=pltpu.PrefetchScalarGridSpec(
            num_scalar_prefetch=1,
            grid=(slots,),
            in_specs=[slot(width)] + [whole(a) for a in (gains, shifts, weights, bias)],
            out_specs=[slot(width), slot(cols), slot(cols), slot(cols), slot(cols)],
        ),
        out_shape=[far(width), far(cols), far(cols), far(cols), shape(cols)],
        compiler_params=pltpu.CompilerParams(vmem_limit_bytes=48 * MIB),
        cost_estimate=pl.CostEstimate(flops=20 * 10**9, bytes_accessed=16 * MIB, transcendentals=8 * MIB),
        name="front",
    )(lengths, units, gains, shifts, weights, bias)


def back_kernel(
    lens, q_ref, k_ref, v_ref, dc_ref, h_ref, text_ref, dkv_ref, in_ref, out_ref, _g0, _g1,
    o_ref, g0_ref, g1_ref, b_ref, in_f32, out_f32, dk_acc, dv_acc, w_acc,
):
    in_f32[...] = in_ref[...].astype(jnp.float32)
    out_f32[...] = out_ref[...].astype(jnp.float32)

    @pl.when(pl.program_id(0) == 0)
    def _():
        w_acc[...] = jnp.zeros_like(w_acc)
        b_ref[...] = jnp.zeros_like(b_ref)
        kv_grad = dot_tn(text_ref[...], dkv_ref[...]).astype(jnp.bfloat16)
        half, both = g1_ref.shape[0], dkv_ref.shape[1]
        g1_ref[:, :both] = kv_grad[:half]
        g1_ref[:, both:] = kv_grad[half:]

    length = lens[pl.program_id(0)]
    slot_rows, width = q_ref.shape
    dk_acc[...] = jnp.zeros_like(dk_acc)
    dv_acc[...] = jnp.zeros_like(dv_acc)
    for i in range(slot_rows // BLOCK):
        rows = pl.ds(i * BLOCK, BLOCK)

        @pl.when(i * BLOCK < length)
        def _():
            count = (i + 1) * BLOCK
            keys, values = k_ref[:count, :], v_ref[:count, :]
            scaled = q_ref[rows, :] * jnp.bfloat16(HEAD_DIM**-0.5)
            grads = dc_ref[rows, :]
            col = lax.broadcasted_iota(jnp.int32, (count, BLOCK), 1) + i * BLOCK
            allowed = lax.broadcasted_iota(jnp.int32, (count, BLOCK), 0) <= col
            total = jnp.zeros((BLOCK, width), jnp.float32)
            for head in range(width // HEAD_DIM):
                q_head, g_head = pick_head(scaled, head), pick_head(grads, head)
                scores = jnp.where(allowed, dot_nt(keys, q_head), MASKED_SCORE)
                weights = jnp.exp(scores - jnp.max(scores, axis=0, keepdims=True))
                weights = weights * (1.0 / jnp.sum(weights, axis=0, keepdims=True))
                dv_acc[:count, :] += dot_nn(weights.astype(jnp.bfloat16), g_head)
                weight_grad = dot_nt(values, g_head)
                inner = jnp.sum(weights * weight_grad, axis=0, keepdims=True)
                score_grad = (weights * (weight_grad - inner)).astype(jnp.bfloat16)
                dk_acc[:count, :] += dot_nn(score_grad, q_head)
                total += dot_tn(score_grad, pick_head(keys, head))
            o_ref[rows, :width] = (total * HEAD_DIM**-0.5).astype(jnp.bfloat16)

        @pl.when(i * BLOCK >= length)
        def _():
            o_ref[rows, :width] = jnp.zeros((BLOCK, width), jnp.bfloat16)

    o_ref[:, width : 2 * width] = dk_acc[...].astype(jnp.bfloat16)
    o_ref[:, 2 * width :] = dv_acc[...].astype(jnp.bfloat16)
    for i in range(slot_rows // BLOCK):
        rows = pl.ds(i * BLOCK, BLOCK)

        @pl.when(i * BLOCK < length)
        def _():
            grads = o_ref[rows, :]
            w_acc[...] += dot_tn(h_ref[rows, :], grads)
            sums = column_sum(grads.astype(jnp.float32))
            b_ref[0:1, :] += sums[:, :width]
            b_ref[1:2, :] += sums[:, 2 * width :]

    @pl.when(pl.program_id(0) == pl.num_programs(0) - 1)
    def _():
        g0_ref[...] = w_acc[...].astype(jnp.bfloat16)


def back(lengths, queries, keys, values, grads, rows_in, text, dkv, in_sum, out_sum, g0, g1):
    rows, cols = queries.shape
    width = rows_in.shape[1]
    slots = lengths.shape[0]
    bf, f32 = jnp.bfloat16, jnp.float32
    shape = jax.ShapeDtypeStruct
    slot = lambda a: pl.BlockSpec((a.shape[0] // slots, a.shape[1]), lambda s, *_: (s, 0))
    whole = lambda a: pl.BlockSpec(a.shape, lambda s, *_: (0, 0))
    hbm = pl.BlockSpec(memory_space=pl.ANY)
    half = text.shape[1] // 2
    return pl.pallas_call(
        back_kernel,
        grid_spec=pltpu.PrefetchScalarGridSpec(
            num_scalar_prefetch=1,
            grid=(slots,),
            in_specs=[slot(queries)] * 4
            + [slot(rows_in), whole(text), whole(dkv), slot(in_sum), slot(out_sum), hbm, hbm],
            out_specs=[
                pl.BlockSpec((rows // slots, 3 * cols), lambda s, *_: (s, 0)),
                pl.BlockSpec((width, 3 * cols), lambda s, *_: (0, 0)),
                pl.BlockSpec((half, width), lambda s, *_: (1, 0)),
                pl.BlockSpec((2, cols), lambda s, *_: (0, 0)),
                slot(in_sum),
                slot(out_sum),
            ],
            scratch_shapes=[pltpu.VMEM((rows // slots, cols), f32)] * 2 + [pltpu.VMEM((width, 3 * cols), f32)],
        ),
        out_shape=[
            shape((rows, 3 * cols), bf),
            pltpu.HBM(g0.shape, bf),
            pltpu.HBM(g1.shape, bf),
            shape((2, cols), f32),
            shape(in_sum.shape, f32),
            shape(out_sum.shape, f32),
        ],
        input_output_aliases={10: 1, 11: 2},
        compiler_params=pltpu.CompilerParams(vmem_limit_bytes=60 * MIB),
        cost_estimate=pl.CostEstimate(flops=30 * 10**9, bytes_accessed=40 * MIB, transcendentals=8 * MIB),
        name="back",
    )(lengths, queries, keys, values, grads, rows_in, text, dkv, in_sum, out_sum, g0, g1)


def place():
    index = lax.axis_index("narrow")
    core = index + 1 - 2 * (index % 2)
    return index, core, (index + 2) % NARROW, (core + 2) % NARROW


def greet(*wide_peers):
    _, core, cross, _ = place()
    barrier = pltpu.get_barrier_semaphore()
    for peer in (core, cross):
        pl.semaphore_signal(barrier, inc=1, device_id={"narrow": peer}, device_id_type=MESH)
    for peer in wide_peers:
        pl.semaphore_signal(barrier, inc=1, device_id={"wide": peer}, device_id_type=MESH)
    pl.semaphore_wait(barrier, 2 + len(wide_peers))


def remote(source, target, sems, kind, step, peer, axis="narrow"):
    return pltpu.make_async_remote_copy(
        src_ref=source,
        dst_ref=target,
        send_sem=sems.at[0, kind, step],
        recv_sem=sems.at[1, kind, step],
        device_id={axis: peer},
        device_id_type=MESH,
    )


def ring_place(count):
    wide = lax.axis_index("wide")
    odd, half = wide % 2, wide // 2
    spot = odd * (half + 1) + (1 - odd) * ((count - half) % count)

    def at(where):
        high = ((where + count - 1) % count) // (count // 2)
        return (1 - high) * (2 * where - 1) + high * ((2 * (count - where)) % (2 * count))

    return spot, at((spot + 1) % count), at((spot + count - 1) % count)


class Ring:
    UNITS = 4

    def __init__(self, count, sources, outs, view, arrived, held, sems, fetch_sems, keep_sems):
        self.count, self.sources, self.outs, self.view = count, sources, outs, view
        self.arrived, self.held, self.sems = arrived, held, sems
        self.fetch_sems, self.keep_sems = fetch_sems, keep_sems
        spot, following, previous = ring_place(count)
        self.spots = (spot, (count - spot) % count)
        self.peers = (following, previous)

    def block(self, refs, unit, back_by):
        shard = (self.spots[unit // 2] + 2 * self.count - back_by) % self.count
        return self.view(refs[unit // 2], unit // 2, unit % 2, shard)

    def send(self, source, target, kind, unit, step):
        return remote(source, target, self.sems, kind * self.UNITS + unit, step, self.peers[unit // 2], "wide")

    def sum_copy(self, unit, step, first=False):
        source = self.block(self.sources, unit, 0) if first else self.arrived.at[unit, jnp.maximum(step - 1, 0)]
        return self.send(source, self.arrived.at[unit, step], 0, unit, step)

    def fetch(self, unit, step):
        slot = step % 2
        return pltpu.make_async_copy(
            self.block(self.sources, unit, step + 1), self.held.at[unit, slot], self.fetch_sems.at[unit, slot]
        )

    def keep(self, unit):
        return pltpu.make_async_copy(
            self.arrived.at[unit, self.count - 2], self.block(self.outs, unit, self.count - 1), self.keep_sems.at[unit]
        )

    def spread_copy(self, unit, step, first=False):
        target = self.block(self.outs, unit, self.count - 1 + step)
        source = self.arrived.at[unit, self.count - 2] if first else target
        return self.send(source, target, 1, unit, step)

    def start(self):
        for unit in range(self.UNITS):
            self.sum_copy(unit, 0, True).start()
            self.fetch(unit, 0).start()
            self.fetch(unit, 1).start()

    def serve(self, turn, unit):
        last = self.count - 2

        @pl.when(turn <= last)
        def _():
            self.sum_copy(unit, turn).wait_recv()
            self.fetch(unit, turn).wait()
            total = self.held[unit, turn % 2].astype(jnp.float32) + self.arrived[unit, turn].astype(jnp.float32)
            self.arrived[unit, turn] = total.astype(jnp.bfloat16)

            @pl.when(turn < last)
            def _():
                self.sum_copy(unit, turn + 1).start()

            @pl.when(turn < last - 1)
            def _():
                self.fetch(unit, turn + 2).start()

            @pl.when(turn == last)
            def _():
                self.spread_copy(unit, 0, True).start()
                self.keep(unit).start()

        @pl.when((turn > last) & (turn <= 2 * last + 1))
        def _():
            step = turn - last - 1
            self.spread_copy(unit, step).wait_recv()

            @pl.when(step < last)
            def _():
                self.spread_copy(unit, step + 1).start()

    def finish(self):
        for unit in range(self.UNITS):
            self.keep(unit).wait()

        def body(step, carry):
            for unit in range(self.UNITS):
                self.sum_copy(unit, step).wait_send()
                self.spread_copy(unit, step).wait_send()
            return carry

        lax.fori_loop(0, self.count - 1, body, 0)


def ring_scratch(count, block):
    return [
        pltpu.VMEM((Ring.UNITS, count - 1) + block, jnp.bfloat16),
        pltpu.VMEM((Ring.UNITS, 2) + block, jnp.bfloat16),
        pltpu.SemaphoreType.DMA((2, 2 * Ring.UNITS, count - 1)),
        pltpu.SemaphoreType.DMA((Ring.UNITS, 2)),
        pltpu.SemaphoreType.DMA((Ring.UNITS,)),
    ]


def own_copy(whole, own, sem):
    size = own.shape[0]
    first = pl.multiple_of(lax.axis_index("narrow") * size, size)
    return pltpu.make_async_copy(whole.at[pl.ds(first, size), :], own, sem)


class Hop:
    KINDS = 6

    def __init__(self, part, from_core, to_cross, from_cross, full, sems, chunk):
        self.part, self.from_core, self.to_cross, self.from_cross = part, from_core, to_cross, from_cross
        self.full, self.sems, self.chunk = full, sems, chunk
        self.own = part.shape[0] // NARROW
        self.index, self.core, self.cross, self.diagonal = place()

    def rows(self, owner, step):
        return pl.ds(pl.multiple_of(owner * self.own + step * self.chunk, self.chunk), self.chunk)

    def own_rows(self, step):
        return pl.ds(pl.multiple_of(step * self.chunk, self.chunk), self.chunk)

    def core_copies(self, step):
        return [
            remote(self.part.at[self.rows(owner, step)], self.from_core.at[step, slot], self.sems, slot, step, self.core)
            for slot, owner in enumerate((self.core, self.diagonal))
        ]

    def cross_copy(self, step):
        return remote(self.to_cross.at[step], self.from_cross.at[step], self.sems, 2, step, self.cross)

    def gather_copy(self, step, kind):
        owner = self.cross if kind == 5 else self.index
        rows = self.full.at[self.rows(owner, step)]
        return remote(rows, rows, self.sems, kind, step, self.cross if kind == 3 else self.core)

    def send_core(self, step):
        for copy in self.core_copies(step):
            copy.start()

    def send_cross(self, step):
        for copy in self.core_copies(step):
            copy.wait_recv()
        total = self.part[self.rows(self.cross, step), :].astype(jnp.float32)
        total += self.from_core[step, 1].astype(jnp.float32)
        self.to_cross[step] = total.astype(jnp.bfloat16)
        self.cross_copy(step).start()

    def result(self, step):
        total = self.part[self.rows(self.index, step), :].astype(jnp.float32)
        total += self.from_core[step, 0].astype(jnp.float32)
        self.cross_copy(step).wait_recv()
        return total + self.from_cross[step].astype(jnp.float32)

    def send_gather(self, step, values):
        self.full[self.rows(self.index, step), :] = values
        self.gather_copy(step, 3).start()
        self.gather_copy(step, 4).start()

    def forward(self, step):
        self.gather_copy(step, 3).wait_recv()
        self.gather_copy(step, 5).start()

    def gathered(self, step):
        self.gather_copy(step, 4).wait_recv()
        self.gather_copy(step, 5).wait_recv()

    def finish(self, step, gather=True):
        for copy in self.core_copies(step):
            copy.wait_send()
        self.cross_copy(step).wait_send()
        if gather:
            for kind in (3, 4, 5):
                self.gather_copy(step, kind).wait_send()

    def take(self, ref, step):
        return jnp.concatenate([ref[self.rows(owner, step), :] for owner in range(NARROW)], axis=0)

    def put(self, ref, step, values):
        for owner in range(NARROW):
            ref[self.rows(owner, step), :] = values[owner * self.chunk : (owner + 1) * self.chunk]


def hop_scratch(own, chunk, width):
    steps = own // chunk
    return [
        pltpu.VMEM((steps, 2, chunk, width), jnp.bfloat16),
        pltpu.VMEM((steps, chunk, width), jnp.bfloat16),
        pltpu.VMEM((steps, chunk, width), jnp.bfloat16),
        pltpu.SemaphoreType.DMA((2, Hop.KINDS, steps)),
    ]


def stages(steps, work, ring=None, extra=None, ticks=0):
    ticks = max(ticks, steps + len(work) - 1)
    per_tick = 0 if ring is None else -(-2 * (ring.count - 1) // ticks)

    def body(tick, carry):
        for delay, stage in enumerate(work):
            step = tick - delay

            @pl.when((step >= 0) & (step < steps))
            def _():
                stage(step)

            unit = (delay + 1) * Ring.UNITS // len(work) - 1
            if per_tick and unit != delay * Ring.UNITS // len(work) - 1:
                if per_tick == 1:
                    ring.serve(tick, unit)
                else:
                    lax.fori_loop(0, per_tick, lambda i, c: (ring.serve(tick * per_tick + i, unit), c)[1], 0)
        if extra is not None:
            extra(tick)
        return carry

    lax.fori_loop(0, ticks, body, 0)


def middle_kernel(
    all_units, text_lens, c1, text, gains, shifts, biases, bias, so_w, cq_w, kv_w, co_w,
    h2, h3, q2, c2, kv2, x1, x2,
    units, own_sem, part1, part2, core1, tox1, fromx1, sem1, core2, tox2, fromx2, sem2,
):
    steps, chunk, width = tox1.shape
    cols = q2.shape[1]
    slots = text_lens.shape[0]
    texts = text.shape[0] // slots
    fetch = own_copy(all_units, units, own_sem)
    fetch.start()
    greet()
    one = Hop(part1, core1, tox1, fromx1, h2, sem1, chunk)
    two = Hop(part2, core2, tox2, fromx2, h3, sem2, chunk)
    scale = jnp.bfloat16(HEAD_DIM**-0.5)

    fetch.wait()

    def project(step):
        one.put(part1, step, dot_nn(one.take(c1, step), so_w[...]).astype(jnp.bfloat16))
        one.send_core(step)

        @pl.when(step == 1)
        def _():
            both = dot_nn(text[...], kv_w[...])
            kv2[:, :cols] = both[:, :cols].astype(jnp.bfloat16)
            kv2[:, cols:] = (both[:, cols:] + bias[1:2, :]).astype(jnp.bfloat16)

    def norm_one(step):
        rows = one.own_rows(step)
        resid = units[rows, :].astype(jnp.float32) + one.result(step) + biases[0:1, :]
        x1[rows, :] = resid
        one.send_gather(step, norm_forward(resid, gains[1:2, :], shifts[1:2, :])[0].astype(jnp.bfloat16))

    def cross(step):
        one.gathered(step)
        queries = (dot_nn(one.take(h2, step), cq_w[...]) + bias[0:1, :]).astype(jnp.bfloat16)
        one.put(q2, step, queries)
        scaled = queries * scale
        count = queries.shape[0] // slots
        place_of = lax.broadcasted_iota(jnp.int32, (count, texts), 1)
        context = []
        for slot in range(slots):
            mine = scaled[slot * count : (slot + 1) * count]
            keys = kv2[slot * texts : (slot + 1) * texts, :cols]
            values = kv2[slot * texts : (slot + 1) * texts, cols:]
            total = jnp.zeros((count, cols), jnp.float32)
            for head in range(cols // HEAD_DIM):
                scores = dot_nt(pick_head(mine, head), keys)
                scores = jnp.where(place_of < text_lens[slot], scores, MASKED_SCORE)
                weights = jnp.exp(scores - jnp.max(scores, axis=1, keepdims=True))
                weights = weights * (1.0 / jnp.sum(weights, axis=1, keepdims=True))
                total += dot_nn(weights.astype(jnp.bfloat16), pick_head(values, head))
            context.append(total.astype(jnp.bfloat16))
        context = jnp.concatenate(context, axis=0)
        one.put(c2, step, context)
        two.put(part2, step, dot_nn(context, co_w[...]).astype(jnp.bfloat16))
        two.send_core(step)

    def norm_two(step):
        rows = one.own_rows(step)
        resid = x1[rows, :] + two.result(step) + biases[1:2, :]
        x2[rows, :] = resid
        two.send_gather(step, norm_forward(resid, gains[2:3, :], shifts[2:3, :])[0].astype(jnp.bfloat16))

    stages(
        steps,
        [
            project, one.send_cross, norm_one, one.forward, cross,
            two.send_cross, norm_two, two.forward, two.gathered,
        ],
    )

    def finish(step, carry):
        one.finish(step)
        two.finish(step)
        return carry

    lax.fori_loop(0, steps, finish, 0)


def middle(units, text_lens, c1, text, gains, shifts, biases, bias, so_w, cq_w, kv_w, co_w):
    rows, cols = c1.shape
    own, width = rows // NARROW, units.shape[1]
    chunk = own // STEPS
    bf, f32 = jnp.bfloat16, jnp.float32
    shape = jax.ShapeDtypeStruct
    vmem = pl.BlockSpec(memory_space=pltpu.VMEM)
    hop = hop_scratch(own, chunk, width)
    return pl.pallas_call(
        middle_kernel,
        in_specs=[pl.BlockSpec(memory_space=pl.ANY), pl.BlockSpec(memory_space=pltpu.SMEM)] + [vmem] * 10,
        out_specs=[vmem] * 7,
        out_shape=[
            shape((rows, width), bf),
            shape((rows, width), bf),
            shape((rows, cols), bf),
            shape((rows, cols), bf),
            shape((text.shape[0], 2 * cols), bf),
            shape((own, width), f32),
            shape((own, width), f32),
        ],
        scratch_shapes=[pltpu.VMEM((own, width), bf), pltpu.SemaphoreType.DMA]
        + [pltpu.VMEM((rows, width), bf)] * 2
        + hop
        + hop,
        compiler_params=pltpu.CompilerParams(collective_id=0, has_side_effects=True, vmem_limit_bytes=58 * MIB),
        cost_estimate=pl.CostEstimate(flops=100 * 10**9, bytes_accessed=24 * MIB, transcendentals=4 * MIB),
        name="middle",
    )(units, text_lens, c1, text, gains, shifts, biases, bias, so_w, cq_w, kv_w, co_w)


def ffn_kernel(lens, h_ref, e_ref, wi_ref, b_ref, wo_ref, a_ref, d_ref, gi_ref, go_ref, gb_ref, gi_acc, go_acc):
    block = pl.program_id(0)
    per_slot = pl.num_programs(0) // lens.shape[0]
    length = lens[block // per_slot]

    @pl.when(block == 0)
    def _():
        gi_acc[...] = jnp.zeros_like(gi_acc)
        go_acc[...] = jnp.zeros_like(go_acc)
        gb_ref[...] = jnp.zeros_like(gb_ref)

    live = (block % per_slot) * BLOCK < length

    @pl.when(live)
    def _():
        rows, grads = h_ref[...], e_ref[...]
        out = jnp.zeros(a_ref.shape, jnp.float32)
        back_out = jnp.zeros(d_ref.shape, jnp.float32)
        hidden_count = wo_ref.shape[0]
        for first in range(0, hidden_count, HIDDEN):
            part = slice(first, first + HIDDEN)
            pre = dot_nn(rows, wi_ref[:, part]) + b_ref[:, part]
            cdf = 0.5 + 0.5 * lax.erf(pre * (0.5**0.5))
            pdf = jnp.exp(-0.5 * pre * pre) * 0.3989422804014327
            hidden = (pre * cdf).astype(jnp.bfloat16)
            slope = cdf + pre * pdf
            pre_grad = slope * dot_nt(grads, wo_ref[part, :])
            pre_low = pre_grad.astype(jnp.bfloat16)
            gb_ref[:, part] += jnp.sum(pre_low.astype(jnp.float32), axis=0, keepdims=True)
            out += dot_nn(hidden, wo_ref[part, :])
            back_out += dot_nt(pre_low, wi_ref[:, part])
            go_acc[part, :] += dot_tn(hidden, grads)
            gi_acc[:, part] += dot_tn(rows, pre_low)
        a_ref[...] = out.astype(jnp.bfloat16)
        d_ref[...] = back_out.astype(jnp.bfloat16)

    @pl.when(jnp.logical_not(live))
    def _():
        a_ref[...] = jnp.zeros_like(a_ref)
        d_ref[...] = jnp.zeros_like(d_ref)

    @pl.when(block == pl.num_programs(0) - 1)
    def _():
        gi_ref[...] = gi_acc[...].astype(jnp.bfloat16)
        go_ref[...] = go_acc[...].astype(jnp.bfloat16)


def ffn(lengths, rows_in, grads, w_in, b_in, w_out):
    rows, width = rows_in.shape
    count = w_out.shape[0]
    bf, f32 = jnp.bfloat16, jnp.float32
    shape = jax.ShapeDtypeStruct
    block = pl.BlockSpec((BLOCK, width), lambda i, *_: (i, 0))
    whole = lambda a, b: pl.BlockSpec((a, b), lambda i, *_: (0, 0), pipeline_mode=pl.Buffered(1))
    return pl.pallas_call(
        ffn_kernel,
        grid_spec=pltpu.PrefetchScalarGridSpec(
            num_scalar_prefetch=1,
            grid=(rows // BLOCK,),
            in_specs=[block, block, whole(width, count), whole(1, count), whole(count, width)],
            out_specs=[block, block, whole(width, count), whole(count, width), whole(1, count)],
            scratch_shapes=[pltpu.VMEM((width, count), f32), pltpu.VMEM((count, width), f32)],
        ),
        out_shape=[
            shape((rows, width), bf),
            shape((rows, width), bf),
            shape((width, count), bf),
            shape((count, width), bf),
            shape((1, count), f32),
        ],
        compiler_params=pltpu.CompilerParams(vmem_limit_bytes=58 * MIB),
        cost_estimate=pl.CostEstimate(flops=60 * 10**9, bytes_accessed=32 * MIB, transcendentals=8 * MIB),
        name="ffn",
    )(lengths, rows_in, grads, w_in, b_in.reshape(1, -1), w_out)


class FarHop(Hop):
    def fetch(self, mine, theirs, sems):
        self.mine, self.theirs = mine, theirs
        rows = lambda owner: pl.ds(pl.multiple_of(owner * self.own, self.own), self.own)
        self.fetches = [
            pltpu.make_async_copy(self.part.at[rows(owner)], ref, sems.at[slot])
            for slot, (owner, ref) in enumerate(((self.index, mine), (self.cross, theirs)))
        ]
        for copy in self.fetches:
            copy.start()

    def fetched(self):
        for copy in self.fetches:
            copy.wait()

    def cross_copy(self, step):
        return remote(
            self.theirs.at[self.own_rows(step)], self.from_cross.at[step], self.sems, 2, step, self.cross
        )

    def send_cross(self, step):
        for copy in self.core_copies(step):
            copy.wait_recv()
        total = self.theirs[self.own_rows(step), :].astype(jnp.float32)
        total += self.from_core[step, 1].astype(jnp.float32)
        self.theirs[self.own_rows(step), :] = total.astype(jnp.bfloat16)
        self.cross_copy(step).start()

    def result(self, step):
        total = self.mine[self.own_rows(step), :].astype(jnp.float32)
        total += self.from_core[step, 0].astype(jnp.float32)
        self.cross_copy(step).wait_recv()
        return total + self.from_cross[step].astype(jnp.float32)


def left_here(lens, own, rows):
    first = lax.axis_index("narrow") * own
    slot_rows = rows // lens.shape[0]
    return lens[first // slot_rows] - first % slot_rows


def row_of(step, chunk, width):
    return lax.broadcasted_iota(jnp.int32, (chunk, width), 0) + step * chunk


def turn_kernel(
    third, in_g, out_g, out_grad, lens, text_lens, x1, x2, h2, q2, c2, kv2, c1, gains, co_w, cq_w, so_w,
    in_sum, out_sum, g0, g1, dx1, dc1, dkv, bias_g, stats,
    co_g, cq_g, so_g, give_sem, e_own, own_sem, mine3, theirs3, core3, fromx3, sem3,
    part5, core5, tox5, fromx5, sem5, full3, full5, dx2, co_acc, cq_acc, so_acc, dkv_acc, fetch_sem,
    *ring_refs, count,
):
    steps, chunk, width = tox5.shape
    cols = q2.shape[1]
    slots = bias_g.shape[0]
    texts = kv2.shape[0] // slots

    def ring_view(ref, way, half, shard):
        high = width // count
        if way == 0:
            return ref.at[pl.ds(pl.multiple_of(shard * high, high), high), pl.ds(half * width, width)]
        return ref.at[pl.ds(pl.multiple_of(shard * 2 * high + half * high, high), high), :]

    ring = Ring(count, (in_g, out_g), (in_sum, out_sum), ring_view, *ring_refs)
    fetch = own_copy(out_grad, e_own, own_sem)
    fetch.start()
    greet(*ring.peers)
    ring.start()
    three = FarHop(third, core3, None, fromx3, full3, sem3, chunk)
    five = Hop(part5, core5, tox5, fromx5, full5, sem5, chunk)
    three.fetch(mine3, theirs3, fetch_sem)

    def start(step, carry):
        three.send_core(step)
        return carry

    lax.fori_loop(0, steps, start, 0)
    for ref in (co_acc, cq_acc, so_acc, dkv_acc, bias_g, stats):
        ref[...] = jnp.zeros_like(ref)
    three.fetched()
    fetch.wait()
    valid_rows = left_here(lens, x1.shape[0], h2.shape[0])
    scale = jnp.bfloat16(HEAD_DIM**-0.5)

    def norm_three(step):
        rows = three.own_rows(step)
        grad_in = three.result(step)
        _, normed, inv_std = norm_forward(x2[rows, :], gains[2:3, :], gains[2:3, :])
        stats[0:1, :] += column_sum(grad_in * normed)
        stats[1:2, :] += column_sum(grad_in)
        above = jnp.where(row_of(step, chunk, width) < valid_rows, e_own[rows, :].astype(jnp.float32), 0.0)
        total = above + norm_backward(grad_in, normed, inv_std, gains[2:3, :])
        stats[2:3, :] += column_sum(above)
        stats[3:4, :] += column_sum(total)
        dx2[rows, :] = total
        three.send_gather(step, total.astype(jnp.bfloat16))

    def cross(step):
        three.gathered(step)
        grads = three.take(full3, step)
        co_acc[...] += dot_tn(three.take(c2, step), grads)
        context = dot_nt(grads, co_w[...]).astype(jnp.bfloat16)
        queries = three.take(q2, step) * scale
        count = queries.shape[0] // slots
        place_of = lax.broadcasted_iota(jnp.int32, (texts, count), 0)
        q_grad = []
        for slot in range(slots):
            rows = slice(slot * count, (slot + 1) * count)
            texts_here = slice(slot * texts, (slot + 1) * texts)
            keys, values = kv2[texts_here, :cols], kv2[texts_here, cols:]
            total = jnp.zeros((count, cols), jnp.float32)
            for head in range(cols // HEAD_DIM):
                q_head, g_head = pick_head(queries[rows], head), pick_head(context[rows], head)
                scores = jnp.where(place_of < text_lens[slot], dot_nt(keys, q_head), MASKED_SCORE)
                weights = jnp.exp(scores - jnp.max(scores, axis=0, keepdims=True))
                weights = weights * (1.0 / jnp.sum(weights, axis=0, keepdims=True))
                dkv_acc[texts_here, cols:] += dot_nn(weights.astype(jnp.bfloat16), g_head)
                weight_grad = dot_nt(values, g_head)
                inner = jnp.sum(weights * weight_grad, axis=0, keepdims=True)
                score_grad = (weights * (weight_grad - inner)).astype(jnp.bfloat16)
                dkv_acc[texts_here, :cols] += dot_nn(score_grad, q_head)
                total += dot_tn(score_grad, pick_head(keys, head))
            q_grad.append((total * HEAD_DIM**-0.5).astype(jnp.bfloat16))
        q_grad = jnp.concatenate(q_grad, axis=0)
        five.put(part5, step, dot_nt(q_grad, cq_w[...]).astype(jnp.bfloat16))
        five.send_core(step)
        bias_g[0:1, :] += column_sum(q_grad.astype(jnp.float32))
        cq_acc[...] += dot_tn(five.take(h2, step), q_grad)

    def norm_two(step):
        rows = five.own_rows(step)
        grad_in = five.result(step)
        _, normed, inv_std = norm_forward(x1[rows, :], gains[1:2, :], gains[1:2, :])
        stats[4:5, :] += column_sum(grad_in * normed)
        stats[5:6, :] += column_sum(grad_in)
        total = dx2[rows, :] + norm_backward(grad_in, normed, inv_std, gains[1:2, :])
        stats[6:7, :] += column_sum(total)
        dx1[rows, :] = total
        five.send_gather(step, total.astype(jnp.bfloat16))

    def last(step):
        five.gathered(step)
        grads = five.take(full5, step)
        dc1_rows = dot_nt(grads, so_w[...]).astype(jnp.bfloat16)
        five.put(dc1, step, dc1_rows)
        so_acc[...] += dot_tn(five.take(c1, step), grads)

    stages(
        steps,
        [
            three.send_cross, norm_three, three.forward, cross,
            five.send_cross, norm_two, five.forward, last,
        ],
        ring,
    )
    dkv[...] = dkv_acc[...].astype(jnp.bfloat16)
    bias_g[1:2, :] = column_sum(dkv[:, cols:].astype(jnp.float32))
    co_g[...] = co_acc[...].astype(jnp.bfloat16)
    cq_g[...] = cq_acc[...].astype(jnp.bfloat16)
    so_g[...] = so_acc[...].astype(jnp.bfloat16)
    gives = [
        pltpu.make_async_copy(cq_g, g0.at[:, pl.ds(width - cols, cols)], give_sem.at[0]),
        pltpu.make_async_copy(co_g, g1.at[pl.ds(0, cols), :], give_sem.at[1]),
        pltpu.make_async_copy(so_g, g1.at[pl.ds(cols, cols), :], give_sem.at[2]),
    ]
    for give in gives:
        give.start()

    def finish(step, carry):
        three.finish(step)
        five.finish(step)
        return carry

    lax.fori_loop(0, steps, finish, 0)
    ring.finish()
    for give in gives:
        give.wait()


def turn(count, third, in_g, out_g, out_grad, lens, text_lens, x1, x2, h2, q2, c2, kv2, c1, gains, co_w, cq_w, so_w):
    rows, cols = c1.shape
    own, width = x1.shape
    chunk = own // STEPS
    bf, f32 = jnp.bfloat16, jnp.float32
    shape = jax.ShapeDtypeStruct
    vmem = pl.BlockSpec(memory_space=pltpu.VMEM)
    hbm = pl.BlockSpec(memory_space=pl.ANY)
    hop = hop_scratch(own, chunk, width)
    far = [pltpu.VMEM((own, width), bf)] * 2 + [hop[0], hop[2], hop[3]]
    return pl.pallas_call(
        functools.partial(turn_kernel, count=count),
        in_specs=[hbm] * 4 + [pl.BlockSpec(memory_space=pltpu.SMEM)] * 2 + [vmem] * 11,
        out_specs=[hbm] * 4 + [vmem] * 5,
        out_shape=[
            pltpu.HBM(in_g.shape, bf),
            pltpu.HBM(out_g.shape, bf),
            pltpu.HBM((width, width), bf),
            pltpu.HBM((width, width), bf),
            shape((own, width), f32),
            shape((rows, cols), bf),
            shape(kv2.shape, bf),
            shape((2, cols), f32),
            shape((8, width), f32),
        ],
        scratch_shapes=[
            pltpu.VMEM((cols, width), bf),
            pltpu.VMEM((width, cols), bf),
            pltpu.VMEM((cols, width), bf),
            pltpu.SemaphoreType.DMA((3,)),
            pltpu.VMEM((own, width), bf),
            pltpu.SemaphoreType.DMA,
        ]
        + far
        + [pltpu.VMEM((rows, width), bf)]
        + hop
        + [pltpu.VMEM((rows, width), bf)] * 2
        + [
            pltpu.VMEM((own, width), f32),
            pltpu.VMEM((cols, width), f32),
            pltpu.VMEM((width, cols), f32),
            pltpu.VMEM((cols, width), f32),
            pltpu.VMEM(kv2.shape, f32),
            pltpu.SemaphoreType.DMA((2,)),
        ]
        + ring_scratch(count, (width // count, width)),
        compiler_params=pltpu.CompilerParams(collective_id=1, has_side_effects=True, vmem_limit_bytes=60 * MIB),
        cost_estimate=pl.CostEstimate(flops=100 * 10**9, bytes_accessed=24 * MIB, transcendentals=4 * MIB),
        name="turn",
    )(third, in_g, out_g, out_grad, lens, text_lens, x1, x2, h2, q2, c2, kv2, c1, gains, co_w, cq_w, so_w)


SMALL = 16
NORM_ROWS = 9


class Small:
    def __init__(self, count, block, near, far, sems):
        self.count, self.mine, self.near, self.far, self.sems = count, block, near, far, sems
        self.index, self.core, self.cross, _ = place()
        self.spot, *self.peers = ring_place(count)

    def near_copy(self, kind):
        owner = self.cross if kind == 2 else self.index
        return remote(self.near.at[owner], self.near.at[owner], self.sems, 0, kind, (self.cross, self.core, self.core)[kind])

    def far_copy(self, way, step):
        block = self.far.at[(self.spot + (2 * way - 1) * step + self.count) % self.count]
        return remote(block, block, self.sems, 1 + way, step, self.peers[way], "wide")

    def begin(self):
        self.near[self.index] = self.mine[...]
        self.near_copy(0).start()
        self.near_copy(1).start()

    def forward(self):
        self.near_copy(0).wait_recv()
        self.near_copy(2).start()

    def launch(self):
        self.near_copy(1).wait_recv()
        self.near_copy(2).wait_recv()
        both = self.near[0]
        for owner in range(1, NARROW):
            both += self.near[owner]
        row = lax.broadcasted_iota(jnp.int32, both.shape, 0)
        self.far[self.spot] = jnp.where(row < SMALL - NORM_ROWS, self.mine[...], both)
        self.far_copy(0, 0).start()
        self.far_copy(1, 0).start()

    def rotate(self, step):
        for way in range(2):
            steps = self.count // 2 - way

            @pl.when(step < steps)
            def _():
                self.far_copy(way, step).wait_recv()

            @pl.when(step < steps - 1)
            def _():
                self.far_copy(way, step + 1).start()

    def finish(self, out):
        for kind in range(3):
            self.near_copy(kind).wait_send()

        for way in range(2):

            def body(step, carry):
                self.far_copy(way, step).wait_send()
                return carry

            lax.fori_loop(0, self.count // 2 - way, body, 0)
        out[...] = jnp.zeros_like(out)

        def add(spot, carry):
            out[...] += self.far[spot]
            return carry

        lax.fori_loop(0, self.count, add, 0)


def last_kernel(
    ffn_part, g0, g1, all_units, lens, dqkv, dkv, dx1, x2, self_b, cross_b, ffn_b, stats, gains, biases, qkv_w, kv_w,
    sum0, sum1, y, units_g, text_g, small_sum,
    units, own_sem, mine4, theirs4, core4, fromx4, sem4,
    part6, core6, tox6, fromx6, sem6, part7, core7, tox7, fromx7, sem7,
    fetch_sem, block, near, far, small_sem, *ring_refs, count,
):
    steps, chunk, width = tox6.shape
    text_steps = tox7.shape[0]

    def ring_view(ref, way, half, shard):
        high = width // count
        return ref.at[pl.ds(pl.multiple_of(shard * high, high), high), pl.ds(half * (width // 2), width // 2)]

    ring = Ring(count, (g0, g1), (sum0, sum1), ring_view, *ring_refs)
    small = Small(count, block, near, far, small_sem)
    fetch = own_copy(all_units, units, own_sem)
    fetch.start()
    greet(*ring.peers)
    ring.start()
    four = FarHop(ffn_part, core4, None, fromx4, None, sem4, chunk)
    six = Hop(part6, core6, tox6, fromx6, None, sem6, chunk)
    seven = Hop(part7, core7, tox7, fromx7, None, sem7, chunk)
    four.fetch(mine4, theirs4, fetch_sem)
    four.fetched()
    fetch.wait()
    block[...] = jnp.zeros_like(block)
    cols = self_b.shape[1]
    for row in range(2):
        block[0:1, row * cols : (row + 1) * cols] = self_b[row : row + 1, :]
        block[0:1, (2 + row) * cols : (3 + row) * cols] = cross_b[row : row + 1, :]
        block[1 + row : 2 + row, :] = ffn_b[:, row * width : (row + 1) * width]
    block[SMALL - NORM_ROWS : SMALL - 2, :] = stats[:7, :]
    valid_rows = left_here(lens, x2.shape[0], dqkv.shape[0])
    gain = gains[0:1, :]

    def project(step):
        grads = six.take(dqkv, step)
        total = dot_nt(grads[:, :cols], qkv_w[0]) + dot_nt(grads[:, cols : 2 * cols], qkv_w[1])
        six.put(part6, step, (total + dot_nt(grads[:, 2 * cols :], qkv_w[2])).astype(jnp.bfloat16))
        six.send_core(step)
        four.send_core(step)

    def norm_one(step):
        rows = six.own_rows(step)
        grad_in = six.result(step)
        _, normed, inv_std = norm_forward(units[rows, :].astype(jnp.float32), gain, gain)
        block[SMALL - 2 : SMALL - 1, :] += column_sum(grad_in * normed)
        block[SMALL - 1 : SMALL, :] += column_sum(grad_in)
        units_g[rows, :] = dx1[rows, :] + norm_backward(grad_in, normed, inv_std, gain)

    def text_only(work):
        def stage(step):
            @pl.when(step < text_steps)
            def _():
                work(step)

        return stage

    def text_project(step):
        seven.put(part7, step, dot_nt(seven.take(dkv, step), kv_w[...]).astype(jnp.bfloat16))
        seven.send_core(step)

    def text_result(step):
        text_g[seven.own_rows(step), :] = seven.result(step)

    def output(step):
        rows = four.own_rows(step)
        total = x2[rows, :] + four.result(step) + biases[2:3, :]
        y[rows, :] = jnp.where(row_of(step, chunk, width) < valid_rows, total, 0.0).astype(jnp.bfloat16)

    ready = steps + 1

    def extra(tick):
        for when, work in enumerate((small.begin, small.forward, small.launch)):
            pl.when(tick == ready + when)(work)
        step = tick - ready - 3

        @pl.when((step >= 0) & (step < count // 2))
        def _():
            small.rotate(step)

    stages(
        steps,
        [
            project, six.send_cross, norm_one, four.send_cross, output,
            text_only(text_project), text_only(seven.send_cross), text_only(text_result),
        ],
        ring,
        extra,
        ready + 3 + count // 2,
    )

    def finish(step, carry):
        four.finish(step, False)
        six.finish(step, False)
        text_only(lambda s: seven.finish(s, False))(step)
        return carry

    lax.fori_loop(0, steps, finish, 0)
    ring.finish()
    small.finish(small_sum)


def last(count, ffn_part, g0, g1, units, lens, dqkv, dkv, dx1, x2, *rest):
    rows = dqkv.shape[0]
    own, width = dx1.shape
    chunk = own // STEPS
    text_own = dkv.shape[0] // NARROW
    bf, f32 = jnp.bfloat16, jnp.float32
    shape = jax.ShapeDtypeStruct
    vmem = pl.BlockSpec(memory_space=pltpu.VMEM)
    hbm = pl.BlockSpec(memory_space=pl.ANY)
    hop = hop_scratch(own, chunk, width)
    far = [pltpu.VMEM((own, width), bf)] * 2 + [hop[0], hop[2], hop[3]]
    return pl.pallas_call(
        functools.partial(last_kernel, count=count),
        in_specs=[hbm] * 4 + [pl.BlockSpec(memory_space=pltpu.SMEM)] + [vmem] * (4 + len(rest)),
        out_specs=[hbm] * 2 + [vmem] * 4,
        out_shape=[
            pltpu.HBM(g0.shape, bf),
            pltpu.HBM(g1.shape, bf),
            shape((own, width), bf),
            shape((own, width), f32),
            shape((text_own, width), f32),
            shape((SMALL, width), f32),
        ],
        scratch_shapes=[pltpu.VMEM((own, width), bf), pltpu.SemaphoreType.DMA]
        + far
        + [pltpu.VMEM((rows, width), bf)]
        + hop
        + [pltpu.VMEM((dkv.shape[0], width), bf)]
        + hop_scratch(text_own, chunk, width)
        + [
            pltpu.SemaphoreType.DMA((2,)),
            pltpu.VMEM((SMALL, width), f32),
            pltpu.VMEM((NARROW, SMALL, width), f32),
            pltpu.VMEM((count, SMALL, width), f32),
            pltpu.SemaphoreType.DMA((2, 3, max(count // 2, 3))),
        ]
        + ring_scratch(count, (width // count, width // 2)),
        compiler_params=pltpu.CompilerParams(collective_id=2, has_side_effects=True, vmem_limit_bytes=58 * MIB),
        cost_estimate=pl.CostEstimate(flops=30 * 10**9, bytes_accessed=16 * MIB, transcendentals=0),
        name="last",
    )(ffn_part, g0, g1, units, lens, dqkv, dkv, dx1, x2, *rest)


def unpack_kernel(sum0, sum1, small, qkv_g, cq_g, co_g, so_g, kv_g, gain_g, shift_g, bias_g, self_b, cross_b, ffn_b):
    cols = cq_g.shape[1]
    for part in range(3):
        qkv_g[part] = sum0[:, part * cols : (part + 1) * cols].astype(jnp.float32)
    cq_g[...] = sum0[:, 3 * cols :].astype(jnp.float32)
    co_g[...] = sum1[:cols, :].astype(jnp.float32)
    so_g[...] = sum1[cols : 2 * cols, :].astype(jnp.float32)
    half = kv_g.shape[1] // 2
    for side in range(2):
        for part in range(2):
            first = (2 * side + part) * cols
            kv_g[part, side * half : (side + 1) * half, :] = sum1[2 * cols :, first : first + cols].astype(jnp.float32)
    norms = small[SMALL - NORM_ROWS :, :]
    for ref, order in ((gain_g, (7, 4, 0)), (shift_g, (8, 5, 1)), (bias_g, (6, 3, 2))):
        for row, source in enumerate(order):
            ref[row : row + 1, :] = norms[source : source + 1, :]
    width = small.shape[1]
    for row in range(2):
        self_b[row : row + 1, :] = small[0:1, row * cols : (row + 1) * cols]
        cross_b[row : row + 1, :] = small[0:1, (2 + row) * cols : (3 + row) * cols]
        ffn_b[:, row * width : (row + 1) * width] = small[1 + row : 2 + row, :]


def unpack(sum0, sum1, small, cols, hidden):
    width = sum0.shape[0]
    shape = lambda *dims: jax.ShapeDtypeStruct(dims, jnp.float32)
    vmem = pl.BlockSpec(memory_space=pltpu.VMEM)
    return pl.pallas_call(
        unpack_kernel,
        in_specs=[vmem] * 3,
        out_specs=[vmem] * 11,
        out_shape=[
            shape(3, width, cols), shape(width, cols), shape(cols, width), shape(cols, width), shape(2, width, cols),
            shape(3, width), shape(3, width), shape(3, width), shape(2, cols), shape(2, cols), shape(1, hidden),
        ],
        compiler_params=pltpu.CompilerParams(vmem_limit_bytes=40 * MIB),
        name="unpack",
    )(sum0, sum1, small)


def local(
    units,
    text,
    out_grad,
    unit_lengths,
    text_lengths,
    bucket_counts,
    norm_gain,
    norm_shift,
    self_qkv,
    self_bias,
    self_out,
    cross_q,
    cross_kv,
    cross_bias,
    cross_out,
    ffn_in,
    ffn_in_bias,
    ffn_out,
    out_bias,
):
    slot_live = jnp.arange(unit_lengths.shape[0], dtype=jnp.int32) < bucket_counts[0]
    lengths = jnp.where(slot_live, unit_lengths, 0)
    qkv_weights = jnp.transpose(self_qkv, (1, 0, 2))
    kv_weights = cross_kv.reshape(cross_kv.shape[0], -1)
    count = lax.axis_size("wide")
    first_in, queries, key_rows, value_rows, self_context = front(
        lengths, units, norm_gain, norm_shift, qkv_weights, self_bias
    )
    second_all, third_all, cross_queries, cross_context, text_kv, resid_one, resid_two = middle(
        units,
        text_lengths,
        self_context,
        text,
        norm_gain,
        norm_shift,
        out_bias,
        cross_bias,
        self_out,
        cross_q,
        kv_weights,
        cross_out,
    )
    ffn_part, third_part, ffn_in_grad, ffn_out_grad, ffn_bias_sum = ffn(
        lengths, third_all, out_grad, ffn_in, ffn_in_bias, ffn_out
    )
    in_sum, out_sum, grads_one, grads_two, resid_one_grad, context_grad, text_kv_grad, cross_bias_sum, stats = turn(
        count,
        third_part,
        ffn_in_grad,
        ffn_out_grad,
        out_grad,
        lengths,
        text_lengths,
        resid_one,
        resid_two,
        second_all,
        cross_queries,
        cross_context,
        text_kv,
        self_context,
        norm_gain,
        cross_out,
        cross_q,
        self_out,
    )
    qkv_grad, grads_one, grads_two, self_bias_sum, ffn_in_grad, ffn_out_grad = back(
        lengths,
        queries,
        key_rows,
        value_rows,
        context_grad,
        first_in,
        text,
        text_kv_grad,
        in_sum,
        out_sum,
        grads_one,
        grads_two,
    )
    summed_one, summed_two, output, units_grad, text_grad, small = last(
        count,
        ffn_part,
        grads_one,
        grads_two,
        units,
        lengths,
        qkv_grad,
        text_kv_grad,
        resid_one_grad,
        resid_two,
        self_bias_sum,
        cross_bias_sum,
        ffn_bias_sum,
        stats,
        norm_gain,
        out_bias,
        qkv_weights,
        kv_weights,
    )
    (
        self_qkv_grad,
        cross_q_grad,
        cross_out_grad,
        self_out_grad,
        cross_kv_grad,
        gain_grad,
        shift_grad,
        bias_grad,
        self_bias_grad,
        cross_bias_grad,
        ffn_in_bias_grad,
    ) = unpack(summed_one, summed_two, small, queries.shape[1], ffn_in_bias.shape[0])
    self_qkv_grad = jnp.transpose(self_qkv_grad, (1, 0, 2))
    cross_kv_grad = jnp.transpose(cross_kv_grad, (1, 0, 2))
    ffn_in_bias_grad = ffn_in_bias_grad.reshape(-1)
    return (
        output,
        units_grad,
        text_grad,
        gain_grad,
        shift_grad,
        self_qkv_grad,
        self_bias_grad,
        self_out_grad,
        cross_q_grad,
        cross_kv_grad,
        cross_bias_grad,
        cross_out_grad,
        ffn_in_grad,
        ffn_in_bias_grad,
        ffn_out_grad,
        bias_grad,
    )


def solution(mesh):
    placed = (
        P("wide", None),
        P("wide", None),
        P("wide", None),
        P("wide"),
        P("wide"),
        P("wide"),
        P(),
        P(),
        P(None, None, "narrow"),
        P(None, "narrow"),
        P("narrow", None),
        P(None, "narrow"),
        P(None, None, "narrow"),
        P(None, "narrow"),
        P("narrow", None),
        P(None, "narrow"),
        P("narrow"),
        P("narrow", None),
        P(),
    )
    return jax.shard_map(
        local,
        mesh=mesh,
        in_specs=placed,
        out_specs=(
            P(("wide", "narrow"), None),
            P(("wide", "narrow"), None),
            P(("wide", "narrow"), None),
            P(),
            P(),
            P(None, None, "narrow"),
            P(None, "narrow"),
            P("narrow", None),
            P(None, "narrow"),
            P(None, None, "narrow"),
            P(None, "narrow"),
            P("narrow", None),
            P(None, "narrow"),
            P("narrow"),
            P("narrow", None),
            P(),
        ),
        check_vma=False,
    )
```

```python
import functools

import jax
import jax.numpy as jnp
from jax import lax
from jax.experimental import pallas as pl
from jax.experimental.pallas import tpu as pltpu
from jax.sharding import PartitionSpec as P

HEAD_DIM = 64


NORM_EPSILON = 1e-05
MASKED_SCORE = -1000000000.0
EXACT = lax.Precision.HIGHEST


def norm_forward(values, gain_vec, shift_vec):
    row_mean = jnp.mean(values, axis=-1, keepdims=True)
    centered = values - row_mean
    inv_std = lax.rsqrt(jnp.mean(centered * centered, axis=-1, keepdims=True) + NORM_EPSILON)
    normed = centered * inv_std
    return (normed * gain_vec + shift_vec, normed, inv_std)


def norm_backward(grad_in, normed, inv_std, gain_vec):
    scaled = grad_in * gain_vec
    inner_term = scaled - jnp.mean(scaled, axis=-1, keepdims=True)
    inner_term = inner_term - normed * jnp.mean(scaled * normed, axis=-1, keepdims=True)
    return inner_term * inv_std


BLOCK = 256
MIB = 1 << 20
NARROW = 4
STEPS = 8
HIDDEN = 512
MESH = pl.DeviceIdType.MESH


def head_mask(shape, head):
    lane = lax.broadcasted_iota(jnp.int32, shape, len(shape) - 1)
    return (lane >= head * HEAD_DIM) & (lane < (head + 1) * HEAD_DIM)


def pick_head(values, head):
    return jnp.where(head_mask(values.shape, head), values, jnp.zeros_like(values))


def dot_nt(a, b):
    return lax.dot_general(a, b, (((1,), (1,)), ((), ())), preferred_element_type=jnp.float32)


def dot_nn(a, b):
    return jnp.dot(a, b, preferred_element_type=jnp.float32)


def dot_tn(a, b):
    return lax.dot_general(a, b, (((0,), (0,)), ((), ())), preferred_element_type=jnp.float32)


def column_sum(values):
    return jnp.sum(values, axis=0, keepdims=True)


def front_kernel(
    lens, x_ref, t_ref, g_ref, s_ref, w_ref, b_ref, kvw_ref, vb_ref, h_ref, q_ref, k_ref, v_ref, kv_ref, c_ref
):
    length = lens[pl.program_id(0)]
    width = q_ref.shape[1]
    both = dot_nn(t_ref[...], kvw_ref[...])
    kv_ref[:, :width] = both[:, :width].astype(jnp.bfloat16)
    kv_ref[:, width:] = (both[:, width:] + vb_ref[1:2, :]).astype(jnp.bfloat16)
    for i in range(x_ref.shape[0] // BLOCK):
        rows = pl.ds(i * BLOCK, BLOCK)

        @pl.when(i * BLOCK < length)
        def _():
            normed, _, _ = norm_forward(x_ref[rows, :].astype(jnp.float32), g_ref[0:1, :], s_ref[0:1, :])
            h1 = normed.astype(jnp.bfloat16)
            h_ref[rows, :] = h1
            queries = (dot_nn(h1, w_ref[0]) + b_ref[0:1, :]).astype(jnp.bfloat16)
            q_ref[rows, :] = queries
            k_ref[rows, :] = dot_nn(h1, w_ref[1]).astype(jnp.bfloat16)
            v_ref[rows, :] = (dot_nn(h1, w_ref[2]) + b_ref[1:2, :]).astype(jnp.bfloat16)
            count = (i + 1) * BLOCK
            keys, values = k_ref[:count, :], v_ref[:count, :]
            scaled = queries * jnp.bfloat16(HEAD_DIM**-0.5)
            row = lax.broadcasted_iota(jnp.int32, (BLOCK, count), 0) + i * BLOCK
            allowed = lax.broadcasted_iota(jnp.int32, (BLOCK, count), 1) <= row
            total = jnp.zeros((BLOCK, width), jnp.float32)
            for head in range(width // HEAD_DIM):
                scores = jnp.where(allowed, dot_nt(pick_head(scaled, head), keys), MASKED_SCORE)
                weights = jnp.exp(scores - jnp.max(scores, axis=1, keepdims=True))
                weights = weights * (1.0 / jnp.sum(weights, axis=1, keepdims=True))
                total += dot_nn(weights.astype(jnp.bfloat16), pick_head(values, head))
            c_ref[rows, :] = total.astype(jnp.bfloat16)

        @pl.when(i * BLOCK >= length)
        def _():
            for ref in (h_ref, q_ref, k_ref, v_ref, c_ref):
                ref[rows, :] = jnp.zeros((BLOCK, ref.shape[1]), ref.dtype)


def front(lengths, units, text, gains, shifts, weights, bias, kv_w, cross_bias):
    rows, width = units.shape
    slots = lengths.shape[0]
    slot_rows = rows // slots
    cols = weights.shape[2]
    whole = lambda a: pl.BlockSpec(a.shape, lambda s, *_: (0,) * a.ndim)
    slot = lambda w: pl.BlockSpec((slot_rows, w), lambda s, *_: (s, 0))
    texts = lambda w: pl.BlockSpec((text.shape[0] // slots, w), lambda s, *_: (s, 0))
    shape = lambda w: jax.ShapeDtypeStruct((rows, w), jnp.bfloat16)
    far = lambda w: pltpu.HBM((rows, w), jnp.bfloat16)
    return pl.pallas_call(
        front_kernel,
        grid_spec=pltpu.PrefetchScalarGridSpec(
            num_scalar_prefetch=1,
            grid=(slots,),
            in_specs=[slot(width), texts(width)]
            + [whole(a) for a in (gains, shifts, weights, bias, kv_w, cross_bias)],
            out_specs=[slot(width), slot(cols), slot(cols), slot(cols), texts(2 * cols), slot(cols)],
        ),
        out_shape=[
            far(width),
            far(cols),
            far(cols),
            far(cols),
            jax.ShapeDtypeStruct((text.shape[0], 2 * cols), jnp.bfloat16),
            shape(cols),
        ],
        compiler_params=pltpu.CompilerParams(vmem_limit_bytes=48 * MIB),
        cost_estimate=pl.CostEstimate(flops=20 * 10**9, bytes_accessed=16 * MIB, transcendentals=8 * MIB),
        name="front",
    )(lengths, units, text, gains, shifts, weights, bias, kv_w, cross_bias)


def back_kernel(
    lens, q_ref, k_ref, v_ref, dc_ref, h_ref, text_ref, dkv_ref, in_ref, out_ref, _g0, _g1,
    o_ref, g0_ref, g1_ref, b_ref, in_f32, out_f32, dk_acc, dv_acc, w_acc,
):
    in_f32[...] = in_ref[...].astype(jnp.float32)
    out_f32[...] = out_ref[...].astype(jnp.float32)

    @pl.when(pl.program_id(0) == 0)
    def _():
        w_acc[...] = jnp.zeros_like(w_acc)
        b_ref[...] = jnp.zeros_like(b_ref)
        kv_grad = dot_tn(text_ref[...], dkv_ref[...]).astype(jnp.bfloat16)
        half, both = g1_ref.shape[0], dkv_ref.shape[1]
        g1_ref[:, :both] = kv_grad[:half]
        g1_ref[:, both:] = kv_grad[half:]

    length = lens[pl.program_id(0)]
    slot_rows, width = q_ref.shape
    dk_acc[...] = jnp.zeros_like(dk_acc)
    dv_acc[...] = jnp.zeros_like(dv_acc)
    for i in range(slot_rows // BLOCK):
        rows = pl.ds(i * BLOCK, BLOCK)

        @pl.when(i * BLOCK < length)
        def _():
            count = (i + 1) * BLOCK
            keys, values = k_ref[:count, :], v_ref[:count, :]
            scaled = q_ref[rows, :] * jnp.bfloat16(HEAD_DIM**-0.5)
            grads = dc_ref[rows, :]
            col = lax.broadcasted_iota(jnp.int32, (count, BLOCK), 1) + i * BLOCK
            allowed = lax.broadcasted_iota(jnp.int32, (count, BLOCK), 0) <= col
            total = jnp.zeros((BLOCK, width), jnp.float32)
            for head in range(width // HEAD_DIM):
                q_head, g_head = pick_head(scaled, head), pick_head(grads, head)
                scores = jnp.where(allowed, dot_nt(keys, q_head), MASKED_SCORE)
                weights = jnp.exp(scores - jnp.max(scores, axis=0, keepdims=True))
                weights = weights * (1.0 / jnp.sum(weights, axis=0, keepdims=True))
                dv_acc[:count, :] += dot_nn(weights.astype(jnp.bfloat16), g_head)
                weight_grad = dot_nt(values, g_head)
                inner = jnp.sum(weights * weight_grad, axis=0, keepdims=True)
                score_grad = (weights * (weight_grad - inner)).astype(jnp.bfloat16)
                dk_acc[:count, :] += dot_nn(score_grad, q_head)
                total += dot_tn(score_grad, pick_head(keys, head))
            o_ref[rows, :width] = (total * HEAD_DIM**-0.5).astype(jnp.bfloat16)

        @pl.when(i * BLOCK >= length)
        def _():
            o_ref[rows, :width] = jnp.zeros((BLOCK, width), jnp.bfloat16)

    o_ref[:, width : 2 * width] = dk_acc[...].astype(jnp.bfloat16)
    o_ref[:, 2 * width :] = dv_acc[...].astype(jnp.bfloat16)
    for i in range(slot_rows // BLOCK):
        rows = pl.ds(i * BLOCK, BLOCK)

        @pl.when(i * BLOCK < length)
        def _():
            grads = o_ref[rows, :]
            w_acc[...] += dot_tn(h_ref[rows, :], grads)
            sums = column_sum(grads.astype(jnp.float32))
            b_ref[0:1, :] += sums[:, :width]
            b_ref[1:2, :] += sums[:, 2 * width :]

    @pl.when(pl.program_id(0) == pl.num_programs(0) - 1)
    def _():
        g0_ref[...] = w_acc[...].astype(jnp.bfloat16)


def back(lengths, queries, keys, values, grads, rows_in, text, dkv, in_sum, out_sum, g0, g1):
    rows, cols = queries.shape
    width = rows_in.shape[1]
    slots = lengths.shape[0]
    bf, f32 = jnp.bfloat16, jnp.float32
    shape = jax.ShapeDtypeStruct
    slot = lambda a: pl.BlockSpec((a.shape[0] // slots, a.shape[1]), lambda s, *_: (s, 0))
    whole = lambda a: pl.BlockSpec(a.shape, lambda s, *_: (0, 0))
    hbm = pl.BlockSpec(memory_space=pl.ANY)
    half = text.shape[1] // 2
    return pl.pallas_call(
        back_kernel,
        grid_spec=pltpu.PrefetchScalarGridSpec(
            num_scalar_prefetch=1,
            grid=(slots,),
            in_specs=[slot(queries)] * 4
            + [slot(rows_in), whole(text), whole(dkv), slot(in_sum), slot(out_sum), hbm, hbm],
            out_specs=[
                pl.BlockSpec((rows // slots, 3 * cols), lambda s, *_: (s, 0)),
                pl.BlockSpec((width, 3 * cols), lambda s, *_: (0, 0)),
                pl.BlockSpec((half, width), lambda s, *_: (1, 0)),
                pl.BlockSpec((2, cols), lambda s, *_: (0, 0)),
                slot(in_sum),
                slot(out_sum),
            ],
            scratch_shapes=[pltpu.VMEM((rows // slots, cols), f32)] * 2 + [pltpu.VMEM((width, 3 * cols), f32)],
        ),
        out_shape=[
            shape((rows, 3 * cols), bf),
            pltpu.HBM(g0.shape, bf),
            pltpu.HBM(g1.shape, bf),
            shape((2, cols), f32),
            shape(in_sum.shape, f32),
            shape(out_sum.shape, f32),
        ],
        input_output_aliases={10: 1, 11: 2},
        compiler_params=pltpu.CompilerParams(vmem_limit_bytes=60 * MIB),
        cost_estimate=pl.CostEstimate(flops=30 * 10**9, bytes_accessed=40 * MIB, transcendentals=8 * MIB),
        name="back",
    )(lengths, queries, keys, values, grads, rows_in, text, dkv, in_sum, out_sum, g0, g1)


def place():
    index = lax.axis_index("narrow")
    core = index + 1 - 2 * (index % 2)
    return index, core, (index + 2) % NARROW, (core + 2) % NARROW


def greet(*wide_peers):
    _, core, cross, _ = place()
    barrier = pltpu.get_barrier_semaphore()
    for peer in (core, cross):
        pl.semaphore_signal(barrier, inc=1, device_id={"narrow": peer}, device_id_type=MESH)
    for peer in wide_peers:
        pl.semaphore_signal(barrier, inc=1, device_id={"wide": peer}, device_id_type=MESH)
    pl.semaphore_wait(barrier, 2 + len(wide_peers))


def remote(source, target, sems, kind, step, peer, axis="narrow"):
    return pltpu.make_async_remote_copy(
        src_ref=source,
        dst_ref=target,
        send_sem=sems.at[0, kind, step],
        recv_sem=sems.at[1, kind, step],
        device_id={axis: peer},
        device_id_type=MESH,
    )


def ring_place(count):
    wide = lax.axis_index("wide")
    odd, half = wide % 2, wide // 2
    spot = odd * (half + 1) + (1 - odd) * ((count - half) % count)

    def at(where):
        high = ((where + count - 1) % count) // (count // 2)
        return (1 - high) * (2 * where - 1) + high * ((2 * (count - where)) % (2 * count))

    return spot, at((spot + 1) % count), at((spot + count - 1) % count)


class Ring:
    UNITS = 4

    def __init__(self, count, sources, outs, view, arrived, held, sems, fetch_sems, keep_sems):
        self.count, self.sources, self.outs, self.view = count, sources, outs, view
        self.arrived, self.held, self.sems = arrived, held, sems
        self.fetch_sems, self.keep_sems = fetch_sems, keep_sems
        spot, following, previous = ring_place(count)
        self.spots = (spot, (count - spot) % count)
        self.peers = (following, previous)

    def block(self, refs, unit, back_by):
        shard = (self.spots[unit // 2] + 2 * self.count - back_by) % self.count
        return self.view(refs[unit // 2], unit // 2, unit % 2, shard)

    def send(self, source, target, kind, unit, step):
        return remote(source, target, self.sems, kind * self.UNITS + unit, step, self.peers[unit // 2], "wide")

    def sum_copy(self, unit, step, first=False):
        source = self.block(self.sources, unit, 0) if first else self.arrived.at[unit, jnp.maximum(step - 1, 0)]
        return self.send(source, self.arrived.at[unit, step], 0, unit, step)

    def fetch(self, unit, step):
        slot = step % 2
        return pltpu.make_async_copy(
            self.block(self.sources, unit, step + 1), self.held.at[unit, slot], self.fetch_sems.at[unit, slot]
        )

    def keep(self, unit):
        return pltpu.make_async_copy(
            self.arrived.at[unit, self.count - 2], self.block(self.outs, unit, self.count - 1), self.keep_sems.at[unit]
        )

    def spread_copy(self, unit, step, first=False):
        target = self.block(self.outs, unit, self.count - 1 + step)
        source = self.arrived.at[unit, self.count - 2] if first else target
        return self.send(source, target, 1, unit, step)

    def start(self):
        for unit in range(self.UNITS):
            self.sum_copy(unit, 0, True).start()
            self.fetch(unit, 0).start()
            self.fetch(unit, 1).start()

    def serve(self, turn, unit):
        last = self.count - 2

        @pl.when(turn <= last)
        def _():
            self.sum_copy(unit, turn).wait_recv()
            self.fetch(unit, turn).wait()
            total = self.held[unit, turn % 2].astype(jnp.float32) + self.arrived[unit, turn].astype(jnp.float32)
            self.arrived[unit, turn] = total.astype(jnp.bfloat16)

            @pl.when(turn < last)
            def _():
                self.sum_copy(unit, turn + 1).start()

            @pl.when(turn < last - 1)
            def _():
                self.fetch(unit, turn + 2).start()

            @pl.when(turn == last)
            def _():
                self.spread_copy(unit, 0, True).start()
                self.keep(unit).start()

        @pl.when((turn > last) & (turn <= 2 * last + 1))
        def _():
            step = turn - last - 1
            self.spread_copy(unit, step).wait_recv()

            @pl.when(step < last)
            def _():
                self.spread_copy(unit, step + 1).start()

    def finish(self):
        for unit in range(self.UNITS):
            self.keep(unit).wait()

        def body(step, carry):
            for unit in range(self.UNITS):
                self.sum_copy(unit, step).wait_send()
                self.spread_copy(unit, step).wait_send()
            return carry

        lax.fori_loop(0, self.count - 1, body, 0)


def ring_scratch(count, block):
    return [
        pltpu.VMEM((Ring.UNITS, count - 1) + block, jnp.bfloat16),
        pltpu.VMEM((Ring.UNITS, 2) + block, jnp.bfloat16),
        pltpu.SemaphoreType.DMA((2, 2 * Ring.UNITS, count - 1)),
        pltpu.SemaphoreType.DMA((Ring.UNITS, 2)),
        pltpu.SemaphoreType.DMA((Ring.UNITS,)),
    ]


def own_copy(whole, own, sem):
    size = own.shape[0]
    first = pl.multiple_of(lax.axis_index("narrow") * size, size)
    return pltpu.make_async_copy(whole.at[pl.ds(first, size), :], own, sem)


class Hop:
    KINDS = 6

    def __init__(self, part, from_core, from_cross, full, sems, chunk):
        self.part, self.from_core, self.from_cross = part, from_core, from_cross
        self.full, self.sems, self.chunk = full, sems, chunk
        self.own = part.shape[0] // NARROW
        self.index, self.core, self.cross, self.diagonal = place()

    def rows(self, owner, step):
        return pl.ds(pl.multiple_of(owner * self.own + step * self.chunk, self.chunk), self.chunk)

    def own_rows(self, step):
        return pl.ds(pl.multiple_of(step * self.chunk, self.chunk), self.chunk)

    def core_copies(self, step):
        return [
            remote(self.part.at[self.rows(owner, step)], self.from_core.at[step, slot], self.sems, slot, step, self.core)
            for slot, owner in enumerate((self.core, self.diagonal))
        ]

    def cross_copy(self, step):
        return remote(
            self.part.at[self.rows(self.cross, step)], self.from_cross.at[step], self.sems, 2, step, self.cross
        )

    def gather_copy(self, step, kind):
        owner = self.cross if kind == 5 else self.index
        rows = self.full.at[self.rows(owner, step)]
        return remote(rows, rows, self.sems, kind, step, self.cross if kind == 3 else self.core)

    def send_core(self, step):
        for copy in self.core_copies(step):
            copy.start()

    def send_cross(self, step):
        for copy in self.core_copies(step):
            copy.wait_recv()
        total = self.part[self.rows(self.cross, step), :].astype(jnp.float32)
        total += self.from_core[step, 1].astype(jnp.float32)
        self.part[self.rows(self.cross, step), :] = total.astype(jnp.bfloat16)
        self.cross_copy(step).start()

    def result(self, step):
        total = self.part[self.rows(self.index, step), :].astype(jnp.float32)
        total += self.from_core[step, 0].astype(jnp.float32)
        self.cross_copy(step).wait_recv()
        return total + self.from_cross[step].astype(jnp.float32)

    def send_gather(self, step, values):
        self.full[self.rows(self.index, step), :] = values
        self.gather_copy(step, 3).start()
        self.gather_copy(step, 4).start()

    def forward(self, step):
        self.gather_copy(step, 3).wait_recv()
        self.gather_copy(step, 5).start()

    def gathered(self, step):
        self.gather_copy(step, 4).wait_recv()
        self.gather_copy(step, 5).wait_recv()

    def sent(self, step):
        for copy in self.core_copies(step):
            copy.wait_send()
        self.cross_copy(step).wait_send()

    def finish(self, step, gather=True, parts=True):
        if parts:
            self.sent(step)
        if gather:
            for kind in (3, 4, 5):
                self.gather_copy(step, kind).wait_send()

    def take(self, ref, step):
        return jnp.concatenate([ref[self.rows(owner, step), :] for owner in range(NARROW)], axis=0)

    def put(self, ref, step, values):
        for owner in range(NARROW):
            ref[self.rows(owner, step), :] = values[owner * self.chunk : (owner + 1) * self.chunk]


def hop_scratch(own, chunk, width):
    steps = own // chunk
    return [
        pltpu.VMEM((steps, 2, chunk, width), jnp.bfloat16),
        pltpu.VMEM((steps, chunk, width), jnp.bfloat16),
        pltpu.SemaphoreType.DMA((2, Hop.KINDS, steps)),
    ]


def stages(steps, work, ring=None, extra=None, ticks=0):
    ticks = max(ticks, steps + len(work) - 1)
    per_tick = 0 if ring is None else -(-2 * (ring.count - 1) // ticks)

    def body(tick, carry):
        for delay, stage in enumerate(work):
            step = tick - delay

            @pl.when((step >= 0) & (step < steps))
            def _():
                stage(step)

            unit = (delay + 1) * Ring.UNITS // len(work) - 1
            if per_tick and unit != delay * Ring.UNITS // len(work) - 1:
                if per_tick == 1:
                    ring.serve(tick, unit)
                else:
                    lax.fori_loop(0, per_tick, lambda i, c: (ring.serve(tick * per_tick + i, unit), c)[1], 0)
        if extra is not None:
            extra(tick)
        return carry

    lax.fori_loop(0, ticks, body, 0)


def middle_kernel(
    all_units, out_grad, far_in, far_out, lens, text_lens, c1, kv2, gains, shifts, biases, bias, so_w, cq_w, co_w, b_in,
    ffn_part, third, in_g, out_g, h2, q2, c2, x1, x2, in_bias_g,
    units, own_sem, w_in, w_out, weight_sem, grads_in, grads_sem, give, give_sem, in_acc, out_acc,
    part, h3, core1, fromx1, sem1, core2, fromx2, sem2,
):
    steps, chunk, width = fromx1.shape
    cols = q2.shape[1]
    slots = text_lens.shape[0]
    texts = kv2.shape[0] // slots
    slot_rows = h2.shape[0] // slots
    hidden_count = w_out.shape[0]
    fetches = [
        own_copy(all_units, units, own_sem),
        pltpu.make_async_copy(far_in, w_in, weight_sem.at[0]),
        pltpu.make_async_copy(far_out, w_out, weight_sem.at[1]),
    ]
    for fetch in fetches:
        fetch.start()
    greet()
    one = Hop(part, core1, fromx1, h2, sem1, chunk)
    two = Hop(part, core2, fromx2, h3, sem2, chunk)
    scale = jnp.bfloat16(HEAD_DIM**-0.5)
    in_acc[...] = jnp.zeros_like(in_acc)
    out_acc[...] = jnp.zeros_like(out_acc)
    in_bias_g[...] = jnp.zeros_like(in_bias_g)

    def grad_copies(step):
        slot = step % 2
        return [
            pltpu.make_async_copy(
                out_grad.at[one.rows(owner, step), :],
                grads_in.at[slot, pl.ds(owner * chunk, chunk), :],
                grads_sem.at[slot, owner],
            )
            for owner in range(NARROW)
        ]

    def give_copies(step, kind):
        slot = step % 2
        return [
            pltpu.make_async_copy(
                give.at[kind, slot, pl.ds(owner * chunk, chunk), :],
                (ffn_part, third)[kind].at[one.rows(owner, step), :],
                give_sem.at[kind, slot, owner],
            )
            for owner in range(NARROW)
        ]

    def project(step):
        one.put(part, step, dot_nn(one.take(c1, step), so_w[...]).astype(jnp.bfloat16))
        one.send_core(step)

    def norm_one(step):
        @pl.when(step == 0)
        def _():
            fetches[0].wait()

        rows = one.own_rows(step)
        resid = units[rows, :].astype(jnp.float32) + one.result(step) + biases[0:1, :]
        x1[rows, :] = resid
        one.send_gather(step, norm_forward(resid, gains[1:2, :], shifts[1:2, :])[0].astype(jnp.bfloat16))

    def cross(step):
        one.gathered(step)
        queries = (dot_nn(one.take(h2, step), cq_w[...]) + bias[0:1, :]).astype(jnp.bfloat16)
        one.put(q2, step, queries)
        scaled = queries * scale
        count = queries.shape[0] // slots
        place_of = lax.broadcasted_iota(jnp.int32, (count, texts), 1)
        context = []
        for slot in range(slots):
            mine = scaled[slot * count : (slot + 1) * count]
            keys = kv2[slot * texts : (slot + 1) * texts, :cols]
            values = kv2[slot * texts : (slot + 1) * texts, cols:]
            total = jnp.zeros((count, cols), jnp.float32)
            for head in range(cols // HEAD_DIM):
                scores = dot_nt(pick_head(mine, head), keys)
                scores = jnp.where(place_of < text_lens[slot], scores, MASKED_SCORE)
                weights = jnp.exp(scores - jnp.max(scores, axis=1, keepdims=True))
                weights = weights * (1.0 / jnp.sum(weights, axis=1, keepdims=True))
                total += dot_nn(weights.astype(jnp.bfloat16), pick_head(values, head))
            context.append(total.astype(jnp.bfloat16))
        context = jnp.concatenate(context, axis=0)
        one.put(c2, step, context)
        one.sent(step)
        two.put(part, step, dot_nn(context, co_w[...]).astype(jnp.bfloat16))
        two.send_core(step)

    def norm_two(step):
        rows = one.own_rows(step)
        resid = x1[rows, :] + two.result(step) + biases[1:2, :]
        x2[rows, :] = resid
        two.send_gather(step, norm_forward(resid, gains[2:3, :], shifts[2:3, :])[0].astype(jnp.bfloat16))

    def forward_two(step):
        two.forward(step)
        for copy in grad_copies(step):
            copy.start()

    def ffn(step):
        @pl.when(step == 0)
        def _():
            fetches[1].wait()
            fetches[2].wait()

        two.gathered(step)
        for copy in grad_copies(step):
            copy.wait()
        rows = two.take(h3, step)
        place_in = lax.broadcasted_iota(jnp.int32, (chunk, width), 0) + step * chunk
        grads = []
        for owner in range(NARROW):
            first = owner * two.own
            valid = place_in < lens[first // slot_rows] - first % slot_rows
            values = grads_in[step % 2, owner * chunk : (owner + 1) * chunk, :]
            grads.append(jnp.where(valid, values.astype(jnp.float32), 0.0).astype(jnp.bfloat16))
        grads = jnp.concatenate(grads, axis=0)
        out = jnp.zeros(rows.shape, jnp.float32)
        back_out = jnp.zeros(rows.shape, jnp.float32)
        for begin in range(0, hidden_count, HIDDEN):
            some = slice(begin, begin + HIDDEN)
            pre = dot_nn(rows, w_in[:, some]) + b_in[:, some]
            cdf = 0.5 + 0.5 * lax.erf(pre * (0.5**0.5))
            pdf = jnp.exp(-0.5 * pre * pre) * 0.3989422804014327
            hidden = (pre * cdf).astype(jnp.bfloat16)
            pre_low = ((cdf + pre * pdf) * dot_nt(grads, w_out[some, :])).astype(jnp.bfloat16)
            in_bias_g[:, some] += column_sum(pre_low.astype(jnp.float32))
            out += dot_nn(hidden, w_out[some, :])
            back_out += dot_nt(pre_low, w_in[:, some])
            out_acc[some, :] += dot_tn(hidden, grads)
            side, place_at = divmod(begin, width)
            in_acc[side * width : (side + 1) * width, place_at : place_at + HIDDEN] += dot_tn(rows, pre_low)

        @pl.when(step >= 2)
        def _():
            for kind in range(2):
                for copy in give_copies(step - 2, kind):
                    copy.wait()

        give[0, step % 2] = out.astype(jnp.bfloat16)
        give[1, step % 2] = back_out.astype(jnp.bfloat16)
        for kind in range(2):
            for copy in give_copies(step, kind):
                copy.start()

    stages(
        steps,
        [project, one.send_cross, norm_one, one.forward, cross, two.send_cross, norm_two, forward_two, ffn],
    )

    def finish(step, carry):
        one.finish(step, True, False)
        two.finish(step)
        return carry

    lax.fori_loop(0, steps, finish, 0)
    part[...] = out_acc[...].astype(jnp.bfloat16)
    results = [pltpu.make_async_copy(part, out_g, weight_sem.at[0])]
    results[0].start()
    h3[...] = in_acc[...].astype(jnp.bfloat16)
    for side in range(hidden_count // width):
        here = pl.ds(side * width, width)
        results.append(pltpu.make_async_copy(h3.at[here, :], in_g.at[:, here], weight_sem.at[1 + side]))
        results[-1].start()
    for step in (steps - 2, steps - 1):
        for kind in range(2):
            for copy in give_copies(step, kind):
                copy.wait()
    for copy in results:
        copy.wait()


def middle(units, out_grad, w_in, w_out, lens, text_lens, c1, kv2, gains, shifts, biases, bias, so_w, cq_w, co_w, b_in):
    rows, cols = c1.shape
    own, width = rows // NARROW, units.shape[1]
    hidden_count = w_out.shape[0]
    chunk = own // STEPS
    bf, f32 = jnp.bfloat16, jnp.float32
    shape = jax.ShapeDtypeStruct
    vmem = pl.BlockSpec(memory_space=pltpu.VMEM)
    hbm = pl.BlockSpec(memory_space=pl.ANY)
    hop = hop_scratch(own, chunk, width)
    dma = pltpu.SemaphoreType.DMA
    return pl.pallas_call(
        middle_kernel,
        in_specs=[hbm] * 4 + [pl.BlockSpec(memory_space=pltpu.SMEM)] * 2 + [vmem] * 10,
        out_specs=[hbm] * 4 + [vmem] * 6,
        out_shape=[
            pltpu.HBM((rows, width), bf),
            pltpu.HBM((rows, width), bf),
            pltpu.HBM((width, hidden_count), bf),
            pltpu.HBM((hidden_count, width), bf),
            shape((rows, width), bf),
            shape((rows, cols), bf),
            shape((rows, cols), bf),
            shape((own, width), f32),
            shape((own, width), f32),
            shape((1, hidden_count), f32),
        ],
        scratch_shapes=[
            pltpu.VMEM((own, width), bf),
            dma,
            pltpu.VMEM((width, hidden_count), bf),
            pltpu.VMEM((hidden_count, width), bf),
            dma((1 + hidden_count // width,)),
            pltpu.VMEM((2, NARROW * chunk, width), bf),
            dma((2, NARROW)),
            pltpu.VMEM((2, 2, NARROW * chunk, width), bf),
            dma((2, 2, NARROW)),
            pltpu.VMEM((hidden_count, width), f32),
            pltpu.VMEM((hidden_count, width), f32),
            pltpu.VMEM((rows, width), bf),
            pltpu.VMEM((rows, width), bf),
        ]
        + hop
        + hop,
        compiler_params=pltpu.CompilerParams(collective_id=0, has_side_effects=True, vmem_limit_bytes=60 * MIB),
        cost_estimate=pl.CostEstimate(flops=100 * 10**9, bytes_accessed=48 * MIB, transcendentals=8 * MIB),
        name="middle",
    )(
        units, out_grad, w_in, w_out, lens, text_lens, c1, kv2, gains, shifts, biases, bias, so_w, cq_w, co_w,
        b_in.reshape(1, -1),
    )


class FarHop(Hop):
    def fetch(self, mine, theirs, sems):
        self.mine, self.theirs = mine, theirs
        rows = lambda owner: pl.ds(pl.multiple_of(owner * self.own, self.own), self.own)
        self.fetches = [
            pltpu.make_async_copy(self.part.at[rows(owner)], ref, sems.at[slot])
            for slot, (owner, ref) in enumerate(((self.index, mine), (self.cross, theirs)))
        ]
        for copy in self.fetches:
            copy.start()

    def fetched(self):
        for copy in self.fetches:
            copy.wait()

    def cross_copy(self, step):
        return remote(
            self.theirs.at[self.own_rows(step)], self.from_cross.at[step], self.sems, 2, step, self.cross
        )

    def send_cross(self, step):
        for copy in self.core_copies(step):
            copy.wait_recv()
        total = self.theirs[self.own_rows(step), :].astype(jnp.float32)
        total += self.from_core[step, 1].astype(jnp.float32)
        self.theirs[self.own_rows(step), :] = total.astype(jnp.bfloat16)
        self.cross_copy(step).start()

    def result(self, step):
        total = self.mine[self.own_rows(step), :].astype(jnp.float32)
        total += self.from_core[step, 0].astype(jnp.float32)
        self.cross_copy(step).wait_recv()
        return total + self.from_cross[step].astype(jnp.float32)


def left_here(lens, own, rows):
    first = lax.axis_index("narrow") * own
    slot_rows = rows // lens.shape[0]
    return lens[first // slot_rows] - first % slot_rows


def row_of(step, chunk, width):
    return lax.broadcasted_iota(jnp.int32, (chunk, width), 0) + step * chunk


def turn_kernel(
    third, in_g, out_g, out_grad, lens, text_lens, x1, x2, h2, q2, c2, kv2, c1, gains, co_w, cq_w, so_w,
    in_sum, out_sum, g0, g1, dx1, dc1, dkv, bias_g, stats,
    co_g, cq_g, so_g, give_sem, e_own, own_sem, mine3, theirs3, core3, fromx3, sem3,
    part5, core5, fromx5, sem5, full3, full5, dx2, co_acc, cq_acc, so_acc, dkv_acc, fetch_sem,
    *ring_refs, count,
):
    steps, chunk, width = fromx5.shape
    cols = q2.shape[1]
    slots = bias_g.shape[0]
    texts = kv2.shape[0] // slots

    def ring_view(ref, way, half, shard):
        high = width // count
        if way == 0:
            return ref.at[pl.ds(pl.multiple_of(shard * high, high), high), pl.ds(half * width, width)]
        return ref.at[pl.ds(pl.multiple_of(shard * 2 * high + half * high, high), high), :]

    ring = Ring(count, (in_g, out_g), (in_sum, out_sum), ring_view, *ring_refs)
    fetch = own_copy(out_grad, e_own, own_sem)
    fetch.start()
    greet(*ring.peers)
    ring.start()
    three = FarHop(third, core3, fromx3, full3, sem3, chunk)
    five = Hop(part5, core5, fromx5, full5, sem5, chunk)
    three.fetch(mine3, theirs3, fetch_sem)

    def start(step, carry):
        three.send_core(step)
        return carry

    lax.fori_loop(0, steps, start, 0)
    for ref in (co_acc, cq_acc, so_acc, dkv_acc, bias_g, stats):
        ref[...] = jnp.zeros_like(ref)
    three.fetched()
    fetch.wait()
    valid_rows = left_here(lens, x1.shape[0], h2.shape[0])
    scale = jnp.bfloat16(HEAD_DIM**-0.5)

    def norm_three(step):
        rows = three.own_rows(step)
        grad_in = three.result(step)
        _, normed, inv_std = norm_forward(x2[rows, :], gains[2:3, :], gains[2:3, :])
        stats[0:1, :] += column_sum(grad_in * normed)
        stats[1:2, :] += column_sum(grad_in)
        above = jnp.where(row_of(step, chunk, width) < valid_rows, e_own[rows, :].astype(jnp.float32), 0.0)
        total = above + norm_backward(grad_in, normed, inv_std, gains[2:3, :])
        stats[2:3, :] += column_sum(above)
        stats[3:4, :] += column_sum(total)
        dx2[rows, :] = total
        three.send_gather(step, total.astype(jnp.bfloat16))

    def cross(step):
        three.gathered(step)
        grads = three.take(full3, step)
        co_acc[...] += dot_tn(three.take(c2, step), grads)
        context = dot_nt(grads, co_w[...]).astype(jnp.bfloat16)
        queries = three.take(q2, step) * scale
        count = queries.shape[0] // slots
        place_of = lax.broadcasted_iota(jnp.int32, (texts, count), 0)
        q_grad = []
        for slot in range(slots):
            rows = slice(slot * count, (slot + 1) * count)
            texts_here = slice(slot * texts, (slot + 1) * texts)
            keys, values = kv2[texts_here, :cols], kv2[texts_here, cols:]
            total = jnp.zeros((count, cols), jnp.float32)
            for head in range(cols // HEAD_DIM):
                q_head, g_head = pick_head(queries[rows], head), pick_head(context[rows], head)
                scores = jnp.where(place_of < text_lens[slot], dot_nt(keys, q_head), MASKED_SCORE)
                weights = jnp.exp(scores - jnp.max(scores, axis=0, keepdims=True))
                weights = weights * (1.0 / jnp.sum(weights, axis=0, keepdims=True))
                dkv_acc[texts_here, cols:] += dot_nn(weights.astype(jnp.bfloat16), g_head)
                weight_grad = dot_nt(values, g_head)
                inner = jnp.sum(weights * weight_grad, axis=0, keepdims=True)
                score_grad = (weights * (weight_grad - inner)).astype(jnp.bfloat16)
                dkv_acc[texts_here, :cols] += dot_nn(score_grad, q_head)
                total += dot_tn(score_grad, pick_head(keys, head))
            q_grad.append((total * HEAD_DIM**-0.5).astype(jnp.bfloat16))
        q_grad = jnp.concatenate(q_grad, axis=0)
        five.put(part5, step, dot_nt(q_grad, cq_w[...]).astype(jnp.bfloat16))
        five.send_core(step)
        bias_g[0:1, :] += column_sum(q_grad.astype(jnp.float32))
        cq_acc[...] += dot_tn(five.take(h2, step), q_grad)

    def norm_two(step):
        rows = five.own_rows(step)
        grad_in = five.result(step)
        _, normed, inv_std = norm_forward(x1[rows, :], gains[1:2, :], gains[1:2, :])
        stats[4:5, :] += column_sum(grad_in * normed)
        stats[5:6, :] += column_sum(grad_in)
        total = dx2[rows, :] + norm_backward(grad_in, normed, inv_std, gains[1:2, :])
        stats[6:7, :] += column_sum(total)
        dx1[rows, :] = total
        five.send_gather(step, total.astype(jnp.bfloat16))

    def last(step):
        five.gathered(step)
        grads = five.take(full5, step)
        dc1_rows = dot_nt(grads, so_w[...]).astype(jnp.bfloat16)
        five.put(dc1, step, dc1_rows)
        so_acc[...] += dot_tn(five.take(c1, step), grads)

    stages(
        steps,
        [
            three.send_cross, norm_three, three.forward, cross,
            five.send_cross, norm_two, five.forward, last,
        ],
        ring,
    )
    dkv[...] = dkv_acc[...].astype(jnp.bfloat16)
    bias_g[1:2, :] = column_sum(dkv[:, cols:].astype(jnp.float32))
    co_g[...] = co_acc[...].astype(jnp.bfloat16)
    cq_g[...] = cq_acc[...].astype(jnp.bfloat16)
    so_g[...] = so_acc[...].astype(jnp.bfloat16)
    gives = [
        pltpu.make_async_copy(cq_g, g0.at[:, pl.ds(width - cols, cols)], give_sem.at[0]),
        pltpu.make_async_copy(co_g, g1.at[pl.ds(0, cols), :], give_sem.at[1]),
        pltpu.make_async_copy(so_g, g1.at[pl.ds(cols, cols), :], give_sem.at[2]),
    ]
    for give in gives:
        give.start()

    def finish(step, carry):
        three.finish(step)
        five.finish(step)
        return carry

    lax.fori_loop(0, steps, finish, 0)
    ring.finish()
    for give in gives:
        give.wait()


def turn(count, third, in_g, out_g, out_grad, lens, text_lens, x1, x2, h2, q2, c2, kv2, c1, gains, co_w, cq_w, so_w):
    rows, cols = c1.shape
    own, width = x1.shape
    chunk = own // STEPS
    bf, f32 = jnp.bfloat16, jnp.float32
    shape = jax.ShapeDtypeStruct
    vmem = pl.BlockSpec(memory_space=pltpu.VMEM)
    hbm = pl.BlockSpec(memory_space=pl.ANY)
    hop = hop_scratch(own, chunk, width)
    far = [pltpu.VMEM((own, width), bf)] * 2 + hop
    return pl.pallas_call(
        functools.partial(turn_kernel, count=count),
        in_specs=[hbm] * 4 + [pl.BlockSpec(memory_space=pltpu.SMEM)] * 2 + [vmem] * 11,
        out_specs=[hbm] * 4 + [vmem] * 5,
        out_shape=[
            pltpu.HBM(in_g.shape, bf),
            pltpu.HBM(out_g.shape, bf),
            pltpu.HBM((width, width), bf),
            pltpu.HBM((width, width), bf),
            shape((own, width), f32),
            shape((rows, cols), bf),
            shape(kv2.shape, bf),
            shape((2, cols), f32),
            shape((8, width), f32),
        ],
        scratch_shapes=[
            pltpu.VMEM((cols, width), bf),
            pltpu.VMEM((width, cols), bf),
            pltpu.VMEM((cols, width), bf),
            pltpu.SemaphoreType.DMA((3,)),
            pltpu.VMEM((own, width), bf),
            pltpu.SemaphoreType.DMA,
        ]
        + far
        + [pltpu.VMEM((rows, width), bf)]
        + hop
        + [pltpu.VMEM((rows, width), bf)] * 2
        + [
            pltpu.VMEM((own, width), f32),
            pltpu.VMEM((cols, width), f32),
            pltpu.VMEM((width, cols), f32),
            pltpu.VMEM((cols, width), f32),
            pltpu.VMEM(kv2.shape, f32),
            pltpu.SemaphoreType.DMA((2,)),
        ]
        + ring_scratch(count, (width // count, width)),
        compiler_params=pltpu.CompilerParams(collective_id=1, has_side_effects=True, vmem_limit_bytes=60 * MIB),
        cost_estimate=pl.CostEstimate(flops=100 * 10**9, bytes_accessed=24 * MIB, transcendentals=4 * MIB),
        name="turn",
    )(third, in_g, out_g, out_grad, lens, text_lens, x1, x2, h2, q2, c2, kv2, c1, gains, co_w, cq_w, so_w)


SMALL = 16
NORM_ROWS = 9


class Small:
    def __init__(self, count, block, near, far, sems):
        self.count, self.mine, self.near, self.far, self.sems = count, block, near, far, sems
        self.index, self.core, self.cross, _ = place()
        self.spot, *self.peers = ring_place(count)

    def near_copy(self, kind):
        owner = self.cross if kind == 2 else self.index
        return remote(self.near.at[owner], self.near.at[owner], self.sems, 0, kind, (self.cross, self.core, self.core)[kind])

    def far_copy(self, way, step):
        block = self.far.at[(self.spot + (2 * way - 1) * step + self.count) % self.count]
        return remote(block, block, self.sems, 1 + way, step, self.peers[way], "wide")

    def begin(self):
        self.near[self.index] = self.mine[...]
        self.near_copy(0).start()
        self.near_copy(1).start()

    def forward(self):
        self.near_copy(0).wait_recv()
        self.near_copy(2).start()

    def launch(self):
        self.near_copy(1).wait_recv()
        self.near_copy(2).wait_recv()
        both = self.near[0]
        for owner in range(1, NARROW):
            both += self.near[owner]
        row = lax.broadcasted_iota(jnp.int32, both.shape, 0)
        self.far[self.spot] = jnp.where(row < SMALL - NORM_ROWS, self.mine[...], both)
        self.far_copy(0, 0).start()
        self.far_copy(1, 0).start()

    def rotate(self, step):
        for way in range(2):
            steps = self.count // 2 - way

            @pl.when(step < steps)
            def _():
                self.far_copy(way, step).wait_recv()

            @pl.when(step < steps - 1)
            def _():
                self.far_copy(way, step + 1).start()

    def finish(self, out):
        for kind in range(3):
            self.near_copy(kind).wait_send()

        for way in range(2):

            def body(step, carry):
                self.far_copy(way, step).wait_send()
                return carry

            lax.fori_loop(0, self.count // 2 - way, body, 0)
        out[...] = jnp.zeros_like(out)

        def add(spot, carry):
            out[...] += self.far[spot]
            return carry

        lax.fori_loop(0, self.count, add, 0)


def last_kernel(
    ffn_part, g0, g1, all_units, lens, dqkv, dkv, dx1, x2, self_b, cross_b, ffn_b, stats, gains, biases, qkv_w, kv_w,
    sum0, sum1, y, units_g, text_g, small_sum,
    units, own_sem, mine4, theirs4, core4, fromx4, sem4,
    part6, core6, fromx6, sem6, part7, core7, fromx7, sem7,
    fetch_sem, block, near, far, small_sem, *ring_refs, count,
):
    steps, chunk, width = fromx6.shape
    text_steps = fromx7.shape[0]

    def ring_view(ref, way, half, shard):
        high = width // count
        return ref.at[pl.ds(pl.multiple_of(shard * high, high), high), pl.ds(half * (width // 2), width // 2)]

    ring = Ring(count, (g0, g1), (sum0, sum1), ring_view, *ring_refs)
    small = Small(count, block, near, far, small_sem)
    fetch = own_copy(all_units, units, own_sem)
    fetch.start()
    greet(*ring.peers)
    ring.start()
    four = FarHop(ffn_part, core4, fromx4, None, sem4, chunk)
    six = Hop(part6, core6, fromx6, None, sem6, chunk)
    seven = Hop(part7, core7, fromx7, None, sem7, chunk)
    four.fetch(mine4, theirs4, fetch_sem)
    four.fetched()
    fetch.wait()
    block[...] = jnp.zeros_like(block)
    cols = self_b.shape[1]
    for row in range(2):
        block[0:1, row * cols : (row + 1) * cols] = self_b[row : row + 1, :]
        block[0:1, (2 + row) * cols : (3 + row) * cols] = cross_b[row : row + 1, :]
        block[1 + row : 2 + row, :] = ffn_b[:, row * width : (row + 1) * width]
    block[SMALL - NORM_ROWS : SMALL - 2, :] = stats[:7, :]
    valid_rows = left_here(lens, x2.shape[0], dqkv.shape[0])
    gain = gains[0:1, :]

    def project(step):
        grads = six.take(dqkv, step)
        total = dot_nt(grads[:, :cols], qkv_w[0]) + dot_nt(grads[:, cols : 2 * cols], qkv_w[1])
        six.put(part6, step, (total + dot_nt(grads[:, 2 * cols :], qkv_w[2])).astype(jnp.bfloat16))
        six.send_core(step)
        four.send_core(step)

    def norm_one(step):
        rows = six.own_rows(step)
        grad_in = six.result(step)
        _, normed, inv_std = norm_forward(units[rows, :].astype(jnp.float32), gain, gain)
        block[SMALL - 2 : SMALL - 1, :] += column_sum(grad_in * normed)
        block[SMALL - 1 : SMALL, :] += column_sum(grad_in)
        units_g[rows, :] = dx1[rows, :] + norm_backward(grad_in, normed, inv_std, gain)

    def text_only(work):
        def stage(step):
            @pl.when(step < text_steps)
            def _():
                work(step)

        return stage

    def text_project(step):
        seven.put(part7, step, dot_nt(seven.take(dkv, step), kv_w[...]).astype(jnp.bfloat16))
        seven.send_core(step)

    def text_result(step):
        text_g[seven.own_rows(step), :] = seven.result(step)

    def output(step):
        rows = four.own_rows(step)
        total = x2[rows, :] + four.result(step) + biases[2:3, :]
        y[rows, :] = jnp.where(row_of(step, chunk, width) < valid_rows, total, 0.0).astype(jnp.bfloat16)

    ready = steps + 1

    def extra(tick):
        for when, work in enumerate((small.begin, small.forward, small.launch)):
            pl.when(tick == ready + when)(work)
        step = tick - ready - 3

        @pl.when((step >= 0) & (step < count // 2))
        def _():
            small.rotate(step)

    stages(
        steps,
        [
            project, six.send_cross, norm_one, four.send_cross, output,
            text_only(text_project), text_only(seven.send_cross), text_only(text_result),
        ],
        ring,
        extra,
        ready + 3 + count // 2,
    )

    def finish(step, carry):
        four.finish(step, False)
        six.finish(step, False)
        text_only(lambda s: seven.finish(s, False))(step)
        return carry

    lax.fori_loop(0, steps, finish, 0)
    ring.finish()
    small.finish(small_sum)


def last(count, ffn_part, g0, g1, units, lens, dqkv, dkv, dx1, x2, *rest):
    rows = dqkv.shape[0]
    own, width = dx1.shape
    chunk = own // STEPS
    text_own = dkv.shape[0] // NARROW
    bf, f32 = jnp.bfloat16, jnp.float32
    shape = jax.ShapeDtypeStruct
    vmem = pl.BlockSpec(memory_space=pltpu.VMEM)
    hbm = pl.BlockSpec(memory_space=pl.ANY)
    hop = hop_scratch(own, chunk, width)
    far = [pltpu.VMEM((own, width), bf)] * 2 + hop
    return pl.pallas_call(
        functools.partial(last_kernel, count=count),
        in_specs=[hbm] * 4 + [pl.BlockSpec(memory_space=pltpu.SMEM)] + [vmem] * (4 + len(rest)),
        out_specs=[hbm] * 2 + [vmem] * 4,
        out_shape=[
            pltpu.HBM(g0.shape, bf),
            pltpu.HBM(g1.shape, bf),
            shape((own, width), bf),
            shape((own, width), f32),
            shape((text_own, width), f32),
            shape((SMALL, width), f32),
        ],
        scratch_shapes=[pltpu.VMEM((own, width), bf), pltpu.SemaphoreType.DMA]
        + far
        + [pltpu.VMEM((rows, width), bf)]
        + hop
        + [pltpu.VMEM((dkv.shape[0], width), bf)]
        + hop_scratch(text_own, chunk, width)
        + [
            pltpu.SemaphoreType.DMA((2,)),
            pltpu.VMEM((SMALL, width), f32),
            pltpu.VMEM((NARROW, SMALL, width), f32),
            pltpu.VMEM((count, SMALL, width), f32),
            pltpu.SemaphoreType.DMA((2, 3, max(count // 2, 3))),
        ]
        + ring_scratch(count, (width // count, width // 2)),
        compiler_params=pltpu.CompilerParams(collective_id=2, has_side_effects=True, vmem_limit_bytes=58 * MIB),
        cost_estimate=pl.CostEstimate(flops=30 * 10**9, bytes_accessed=16 * MIB, transcendentals=0),
        name="last",
    )(ffn_part, g0, g1, units, lens, dqkv, dkv, dx1, x2, *rest)


def unpack_kernel(sum0, sum1, small, qkv_g, cq_g, co_g, so_g, kv_g, gain_g, shift_g, bias_g, self_b, cross_b, ffn_b):
    cols = cq_g.shape[1]
    for part in range(3):
        qkv_g[part] = sum0[:, part * cols : (part + 1) * cols].astype(jnp.float32)
    cq_g[...] = sum0[:, 3 * cols :].astype(jnp.float32)
    co_g[...] = sum1[:cols, :].astype(jnp.float32)
    so_g[...] = sum1[cols : 2 * cols, :].astype(jnp.float32)
    half = kv_g.shape[1] // 2
    for side in range(2):
        for part in range(2):
            first = (2 * side + part) * cols
            kv_g[part, side * half : (side + 1) * half, :] = sum1[2 * cols :, first : first + cols].astype(jnp.float32)
    norms = small[SMALL - NORM_ROWS :, :]
    for ref, order in ((gain_g, (7, 4, 0)), (shift_g, (8, 5, 1)), (bias_g, (6, 3, 2))):
        for row, source in enumerate(order):
            ref[row : row + 1, :] = norms[source : source + 1, :]
    width = small.shape[1]
    for row in range(2):
        self_b[row : row + 1, :] = small[0:1, row * cols : (row + 1) * cols]
        cross_b[row : row + 1, :] = small[0:1, (2 + row) * cols : (3 + row) * cols]
        ffn_b[:, row * width : (row + 1) * width] = small[1 + row : 2 + row, :]


def unpack(sum0, sum1, small, cols, hidden):
    width = sum0.shape[0]
    shape = lambda *dims: jax.ShapeDtypeStruct(dims, jnp.float32)
    vmem = pl.BlockSpec(memory_space=pltpu.VMEM)
    return pl.pallas_call(
        unpack_kernel,
        in_specs=[vmem] * 3,
        out_specs=[vmem] * 11,
        out_shape=[
            shape(3, width, cols), shape(width, cols), shape(cols, width), shape(cols, width), shape(2, width, cols),
            shape(3, width), shape(3, width), shape(3, width), shape(2, cols), shape(2, cols), shape(1, hidden),
        ],
        compiler_params=pltpu.CompilerParams(vmem_limit_bytes=40 * MIB),
        name="unpack",
    )(sum0, sum1, small)


def local(
    units,
    text,
    out_grad,
    unit_lengths,
    text_lengths,
    bucket_counts,
    norm_gain,
    norm_shift,
    self_qkv,
    self_bias,
    self_out,
    cross_q,
    cross_kv,
    cross_bias,
    cross_out,
    ffn_in,
    ffn_in_bias,
    ffn_out,
    out_bias,
):
    slot_live = jnp.arange(unit_lengths.shape[0], dtype=jnp.int32) < bucket_counts[0]
    lengths = jnp.where(slot_live, unit_lengths, 0)
    qkv_weights = jnp.transpose(self_qkv, (1, 0, 2))
    kv_weights = cross_kv.reshape(cross_kv.shape[0], -1)
    count = lax.axis_size("wide")
    first_in, queries, key_rows, value_rows, text_kv, self_context = front(
        lengths, units, text, norm_gain, norm_shift, qkv_weights, self_bias, kv_weights, cross_bias
    )
    (
        ffn_part,
        third_part,
        ffn_in_grad,
        ffn_out_grad,
        second_all,
        cross_queries,
        cross_context,
        resid_one,
        resid_two,
        ffn_bias_sum,
    ) = middle(
        units,
        out_grad,
        ffn_in,
        ffn_out,
        lengths,
        text_lengths,
        self_context,
        text_kv,
        norm_gain,
        norm_shift,
        out_bias,
        cross_bias,
        self_out,
        cross_q,
        cross_out,
        ffn_in_bias,
    )
    in_sum, out_sum, grads_one, grads_two, resid_one_grad, context_grad, text_kv_grad, cross_bias_sum, stats = turn(
        count,
        third_part,
        ffn_in_grad,
        ffn_out_grad,
        out_grad,
        lengths,
        text_lengths,
        resid_one,
        resid_two,
        second_all,
        cross_queries,
        cross_context,
        text_kv,
        self_context,
        norm_gain,
        cross_out,
        cross_q,
        self_out,
    )
    qkv_grad, grads_one, grads_two, self_bias_sum, ffn_in_grad, ffn_out_grad = back(
        lengths,
        queries,
        key_rows,
        value_rows,
        context_grad,
        first_in,
        text,
        text_kv_grad,
        in_sum,
        out_sum,
        grads_one,
        grads_two,
    )
    summed_one, summed_two, output, units_grad, text_grad, small = last(
        count,
        ffn_part,
        grads_one,
        grads_two,
        units,
        lengths,
        qkv_grad,
        text_kv_grad,
        resid_one_grad,
        resid_two,
        self_bias_sum,
        cross_bias_sum,
        ffn_bias_sum,
        stats,
        norm_gain,
        out_bias,
        qkv_weights,
        kv_weights,
    )
    (
        self_qkv_grad,
        cross_q_grad,
        cross_out_grad,
        self_out_grad,
        cross_kv_grad,
        gain_grad,
        shift_grad,
        bias_grad,
        self_bias_grad,
        cross_bias_grad,
        ffn_in_bias_grad,
    ) = unpack(summed_one, summed_two, small, queries.shape[1], ffn_in_bias.shape[0])
    self_qkv_grad = jnp.transpose(self_qkv_grad, (1, 0, 2))
    cross_kv_grad = jnp.transpose(cross_kv_grad, (1, 0, 2))
    ffn_in_bias_grad = ffn_in_bias_grad.reshape(-1)
    return (
        output,
        units_grad,
        text_grad,
        gain_grad,
        shift_grad,
        self_qkv_grad,
        self_bias_grad,
        self_out_grad,
        cross_q_grad,
        cross_kv_grad,
        cross_bias_grad,
        cross_out_grad,
        ffn_in_grad,
        ffn_in_bias_grad,
        ffn_out_grad,
        bias_grad,
    )


def solution(mesh):
    placed = (
        P("wide", None),
        P("wide", None),
        P("wide", None),
        P("wide"),
        P("wide"),
        P("wide"),
        P(),
        P(),
        P(None, None, "narrow"),
        P(None, "narrow"),
        P("narrow", None),
        P(None, "narrow"),
        P(None, None, "narrow"),
        P(None, "narrow"),
        P("narrow", None),
        P(None, "narrow"),
        P("narrow"),
        P("narrow", None),
        P(),
    )
    return jax.shard_map(
        local,
        mesh=mesh,
        in_specs=placed,
        out_specs=(
            P(("wide", "narrow"), None),
            P(("wide", "narrow"), None),
            P(("wide", "narrow"), None),
            P(),
            P(),
            P(None, None, "narrow"),
            P(None, "narrow"),
            P("narrow", None),
            P(None, "narrow"),
            P(None, None, "narrow"),
            P(None, "narrow"),
            P("narrow", None),
            P(None, "narrow"),
            P("narrow"),
            P("narrow", None),
            P(),
        ),
        check_vma=False,
    )
```

```python
import functools

import jax
import jax.numpy as jnp
from jax import lax
from jax.experimental import pallas as pl
from jax.experimental.pallas import tpu as pltpu
from jax.sharding import PartitionSpec as P

HEAD_DIM = 64


NORM_EPSILON = 1e-05
MASKED_SCORE = -1000000000.0
EXACT = lax.Precision.HIGHEST


def norm_forward(values, gain_vec, shift_vec):
    row_mean = jnp.mean(values, axis=-1, keepdims=True)
    centered = values - row_mean
    inv_std = lax.rsqrt(jnp.mean(centered * centered, axis=-1, keepdims=True) + NORM_EPSILON)
    normed = centered * inv_std
    return (normed * gain_vec + shift_vec, normed, inv_std)


def norm_backward(grad_in, normed, inv_std, gain_vec):
    scaled = grad_in * gain_vec
    inner_term = scaled - jnp.mean(scaled, axis=-1, keepdims=True)
    inner_term = inner_term - normed * jnp.mean(scaled * normed, axis=-1, keepdims=True)
    return inner_term * inv_std


BLOCK = 256
LANES = 128
MIB = 1 << 20
NARROW = 4
STEPS = 8
HIDDEN = 512
MESH = pl.DeviceIdType.MESH


def head_mask(shape, head):
    lane = lax.broadcasted_iota(jnp.int32, shape, len(shape) - 1)
    return (lane >= head * HEAD_DIM) & (lane < (head + 1) * HEAD_DIM)


def pick_head(values, head):
    return jnp.where(head_mask(values.shape, head), values, jnp.zeros_like(values))


def dot_nt(a, b):
    return lax.dot_general(a, b, (((1,), (1,)), ((), ())), preferred_element_type=jnp.float32)


def dot_nn(a, b):
    return jnp.dot(a, b, preferred_element_type=jnp.float32)


def dot_tn(a, b):
    return lax.dot_general(a, b, (((0,), (0,)), ((), ())), preferred_element_type=jnp.float32)


def column_sum(values):
    return jnp.sum(values, axis=0, keepdims=True)


def mask_diagonal(scores, axis):
    count = scores.shape[axis]
    parts = [scores] if count == BLOCK else jnp.split(scores, [count - BLOCK], axis=axis)
    keys = lax.broadcasted_iota(jnp.int32, (BLOCK, BLOCK), axis)
    queries = lax.broadcasted_iota(jnp.int32, (BLOCK, BLOCK), 1 - axis)
    parts[-1] = jnp.where(keys <= queries, parts[-1], MASKED_SCORE)
    return jnp.concatenate(parts, axis=axis)


def front_kernel(
    lens, x_ref, t_ref, g_ref, s_ref, w_ref, b_ref, kvw_ref, vb_ref, h_ref, q_ref, k_ref, v_ref, kv_ref, c_ref, log_ref
):
    length = lens[pl.program_id(0)]
    width = q_ref.shape[1]
    both = dot_nn(t_ref[...], kvw_ref[...])
    kv_ref[:, :width] = both[:, :width].astype(jnp.bfloat16)
    kv_ref[:, width:] = (both[:, width:] + vb_ref[1:2, :]).astype(jnp.bfloat16)
    for i in range(x_ref.shape[0] // BLOCK):
        rows = pl.ds(i * BLOCK, BLOCK)

        @pl.when(i * BLOCK < length)
        def _():
            normed, _, _ = norm_forward(x_ref[rows, :].astype(jnp.float32), g_ref[0:1, :], s_ref[0:1, :])
            h1 = normed.astype(jnp.bfloat16)
            h_ref[rows, :] = h1
            queries = (dot_nn(h1, w_ref[0]) + b_ref[0:1, :]).astype(jnp.bfloat16)
            q_ref[rows, :] = queries
            k_ref[rows, :] = dot_nn(h1, w_ref[1]).astype(jnp.bfloat16)
            v_ref[rows, :] = (dot_nn(h1, w_ref[2]) + b_ref[1:2, :]).astype(jnp.bfloat16)
            count = (i + 1) * BLOCK
            keys, values = k_ref[:count, :], v_ref[:count, :]
            scaled = queries * jnp.bfloat16(HEAD_DIM**-0.5)
            total = jnp.zeros((BLOCK, width), jnp.float32)
            logs = jnp.zeros((BLOCK, LANES), jnp.float32)
            lane = lax.broadcasted_iota(jnp.int32, logs.shape, 1)
            for head in range(width // HEAD_DIM):
                scores = mask_diagonal(dot_nt(pick_head(scaled, head), keys), 1)
                top = jnp.max(scores, axis=1, keepdims=True)
                weights = jnp.exp(scores - top)
                norm = jnp.sum(weights, axis=1, keepdims=True)
                total += dot_nn(weights.astype(jnp.bfloat16), pick_head(values, head)) * (1.0 / norm)
                logs = jnp.where(lane == head, top + jnp.log(norm), logs)
            log_ref[:, rows] = logs.T[: log_ref.shape[0], :]
            c_ref[rows, :] = total.astype(jnp.bfloat16)

        @pl.when(i * BLOCK >= length)
        def _():
            for ref in (h_ref, q_ref, k_ref, v_ref, c_ref):
                ref[rows, :] = jnp.zeros((BLOCK, ref.shape[1]), ref.dtype)
            log_ref[:, rows] = jnp.zeros((log_ref.shape[0], BLOCK), jnp.float32)


def front(lengths, units, text, gains, shifts, weights, bias, kv_w, cross_bias):
    rows, width = units.shape
    slots = lengths.shape[0]
    slot_rows = rows // slots
    cols = weights.shape[2]
    whole = lambda a: pl.BlockSpec(a.shape, lambda s, *_: (0,) * a.ndim)
    slot = lambda w: pl.BlockSpec((slot_rows, w), lambda s, *_: (s, 0))
    texts = lambda w: pl.BlockSpec((text.shape[0] // slots, w), lambda s, *_: (s, 0))
    logs = pl.BlockSpec((8, slot_rows), lambda s, *_: (0, s))
    shape = lambda w: jax.ShapeDtypeStruct((rows, w), jnp.bfloat16)
    far = lambda w: pltpu.HBM((rows, w), jnp.bfloat16)
    return pl.pallas_call(
        front_kernel,
        grid_spec=pltpu.PrefetchScalarGridSpec(
            num_scalar_prefetch=1,
            grid=(slots,),
            in_specs=[slot(width), texts(width)]
            + [whole(a) for a in (gains, shifts, weights, bias, kv_w, cross_bias)],
            out_specs=[slot(width), slot(cols), slot(cols), slot(cols), texts(2 * cols), slot(cols), logs],
        ),
        out_shape=[
            far(width),
            far(cols),
            far(cols),
            far(cols),
            jax.ShapeDtypeStruct((text.shape[0], 2 * cols), jnp.bfloat16),
            shape(cols),
            pltpu.HBM((8, rows), jnp.float32),
        ],
        compiler_params=pltpu.CompilerParams(vmem_limit_bytes=48 * MIB),
        cost_estimate=pl.CostEstimate(flops=20 * 10**9, bytes_accessed=16 * MIB, transcendentals=8 * MIB),
        name="front",
    )(lengths, units, text, gains, shifts, weights, bias, kv_w, cross_bias)


def back_kernel(
    lens, q_ref, k_ref, v_ref, dc_ref, c_ref, log_ref, h_ref, text_ref, dkv_ref, in_ref, out_ref, _g0, _g1,
    o_ref, g0_ref, g1_ref, b_ref, in_f32, out_f32, dk_acc, dv_acc, w_acc,
):
    in_f32[...] = in_ref[...].astype(jnp.float32)
    out_f32[...] = out_ref[...].astype(jnp.float32)

    @pl.when(pl.program_id(0) == 0)
    def _():
        w_acc[...] = jnp.zeros_like(w_acc)
        b_ref[...] = jnp.zeros_like(b_ref)
        kv_grad = dot_tn(text_ref[...], dkv_ref[...]).astype(jnp.bfloat16)
        half, both = g1_ref.shape[0], dkv_ref.shape[1]
        g1_ref[:, :both] = kv_grad[:half]
        g1_ref[:, both:] = kv_grad[half:]

    length = lens[pl.program_id(0)]
    slot_rows, width = q_ref.shape
    dk_acc[...] = jnp.zeros_like(dk_acc)
    dv_acc[...] = jnp.zeros_like(dv_acc)
    for i in range(slot_rows // BLOCK):
        rows = pl.ds(i * BLOCK, BLOCK)

        @pl.when(i * BLOCK < length)
        def _():
            count = (i + 1) * BLOCK
            keys, values = k_ref[:count, :], v_ref[:count, :]
            scaled = q_ref[rows, :] * jnp.bfloat16(HEAD_DIM**-0.5)
            grads = dc_ref[rows, :]
            total = jnp.zeros((BLOCK, width), jnp.float32)
            heads = lax.broadcasted_iota(jnp.int32, (8, width), 0)
            lanes = lax.broadcasted_iota(jnp.int32, (8, width), 1)
            inner = lax.dot_general(
                jnp.where((lanes >= heads * HEAD_DIM) & (lanes < (heads + 1) * HEAD_DIM), 1.0, 0.0),
                grads.astype(jnp.float32) * c_ref[rows, :].astype(jnp.float32),
                (((1,), (1,)), ((), ())),
                precision=EXACT,
                preferred_element_type=jnp.float32,
            )
            for head in range(width // HEAD_DIM):
                q_head, g_head = pick_head(scaled, head), pick_head(grads, head)
                scores = mask_diagonal(dot_nt(keys, q_head), 0)
                weights = jnp.exp(scores - log_ref[head : head + 1, rows])
                dv_acc[:count, :] += dot_nn(weights.astype(jnp.bfloat16), g_head)
                weight_grad = dot_nt(values, g_head)
                score_grad = (weights * (weight_grad - inner[head : head + 1, :])).astype(jnp.bfloat16)
                dk_acc[:count, :] += dot_nn(score_grad, q_head)
                total += dot_tn(score_grad, pick_head(keys, head))
            o_ref[rows, :width] = (total * HEAD_DIM**-0.5).astype(jnp.bfloat16)

        @pl.when(i * BLOCK >= length)
        def _():
            o_ref[rows, :width] = jnp.zeros((BLOCK, width), jnp.bfloat16)

    o_ref[:, width : 2 * width] = dk_acc[...].astype(jnp.bfloat16)
    o_ref[:, 2 * width :] = dv_acc[...].astype(jnp.bfloat16)
    for i in range(slot_rows // BLOCK):
        rows = pl.ds(i * BLOCK, BLOCK)

        @pl.when(i * BLOCK < length)
        def _():
            grads = o_ref[rows, :]
            w_acc[...] += dot_tn(h_ref[rows, :], grads)
            sums = column_sum(grads.astype(jnp.float32))
            b_ref[0:1, :] += sums[:, :width]
            b_ref[1:2, :] += sums[:, 2 * width :]

    @pl.when(pl.program_id(0) == pl.num_programs(0) - 1)
    def _():
        g0_ref[...] = w_acc[...].astype(jnp.bfloat16)


def back(lengths, queries, keys, values, grads, context, logs, rows_in, text, dkv, in_sum, out_sum, g0, g1):
    rows, cols = queries.shape
    width = rows_in.shape[1]
    slots = lengths.shape[0]
    bf, f32 = jnp.bfloat16, jnp.float32
    shape = jax.ShapeDtypeStruct
    slot = lambda a: pl.BlockSpec((a.shape[0] // slots, a.shape[1]), lambda s, *_: (s, 0))
    whole = lambda a: pl.BlockSpec(a.shape, lambda s, *_: (0, 0))
    hbm = pl.BlockSpec(memory_space=pl.ANY)
    half = text.shape[1] // 2
    return pl.pallas_call(
        back_kernel,
        grid_spec=pltpu.PrefetchScalarGridSpec(
            num_scalar_prefetch=1,
            grid=(slots,),
            in_specs=[slot(queries)] * 5
            + [pl.BlockSpec((8, rows // slots), lambda s, *_: (0, s))]
            + [slot(rows_in), whole(text), whole(dkv), slot(in_sum), slot(out_sum), hbm, hbm],
            out_specs=[
                pl.BlockSpec((rows // slots, 3 * cols), lambda s, *_: (s, 0)),
                pl.BlockSpec((width, 3 * cols), lambda s, *_: (0, 0)),
                pl.BlockSpec((half, width), lambda s, *_: (1, 0)),
                pl.BlockSpec((2, cols), lambda s, *_: (0, 0)),
                slot(in_sum),
                slot(out_sum),
            ],
            scratch_shapes=[pltpu.VMEM((rows // slots, cols), f32)] * 2 + [pltpu.VMEM((width, 3 * cols), f32)],
        ),
        out_shape=[
            shape((rows, 3 * cols), bf),
            pltpu.HBM(g0.shape, bf),
            pltpu.HBM(g1.shape, bf),
            shape((2, cols), f32),
            shape(in_sum.shape, f32),
            shape(out_sum.shape, f32),
        ],
        input_output_aliases={12: 1, 13: 2},
        compiler_params=pltpu.CompilerParams(vmem_limit_bytes=60 * MIB),
        cost_estimate=pl.CostEstimate(flops=30 * 10**9, bytes_accessed=40 * MIB, transcendentals=8 * MIB),
        name="back",
    )(lengths, queries, keys, values, grads, context, logs, rows_in, text, dkv, in_sum, out_sum, g0, g1)


def place():
    index = lax.axis_index("narrow")
    core = index + 1 - 2 * (index % 2)
    return index, core, (index + 2) % NARROW, (core + 2) % NARROW


def greet(*wide_peers):
    _, core, cross, _ = place()
    barrier = pltpu.get_barrier_semaphore()
    for peer in (core, cross):
        pl.semaphore_signal(barrier, inc=1, device_id={"narrow": peer}, device_id_type=MESH)
    for peer in wide_peers:
        pl.semaphore_signal(barrier, inc=1, device_id={"wide": peer}, device_id_type=MESH)
    pl.semaphore_wait(barrier, 2 + len(wide_peers))


def remote(source, target, sems, kind, step, peer, axis="narrow"):
    return pltpu.make_async_remote_copy(
        src_ref=source,
        dst_ref=target,
        send_sem=sems.at[0, kind, step],
        recv_sem=sems.at[1, kind, step],
        device_id={axis: peer},
        device_id_type=MESH,
    )


def ring_place(count):
    wide = lax.axis_index("wide")
    odd, half = wide % 2, wide // 2
    spot = odd * (half + 1) + (1 - odd) * ((count - half) % count)

    def at(where):
        high = ((where + count - 1) % count) // (count // 2)
        return (1 - high) * (2 * where - 1) + high * ((2 * (count - where)) % (2 * count))

    return spot, at((spot + 1) % count), at((spot + count - 1) % count)


class Ring:
    UNITS = 4

    def __init__(self, count, sources, outs, view, arrived, held, sems, fetch_sems, keep_sems):
        self.count, self.sources, self.outs, self.view = count, sources, outs, view
        self.arrived, self.held, self.sems = arrived, held, sems
        self.fetch_sems, self.keep_sems = fetch_sems, keep_sems
        spot, following, previous = ring_place(count)
        self.spots = (spot, (count - spot) % count)
        self.peers = (following, previous)

    def block(self, refs, unit, back_by):
        shard = (self.spots[unit // 2] + 2 * self.count - back_by) % self.count
        return self.view(refs[unit // 2], unit // 2, unit % 2, shard)

    def send(self, source, target, kind, unit, step):
        return remote(source, target, self.sems, kind * self.UNITS + unit, step, self.peers[unit // 2], "wide")

    def sum_copy(self, unit, step, first=False):
        source = self.block(self.sources, unit, 0) if first else self.arrived.at[unit, jnp.maximum(step - 1, 0)]
        return self.send(source, self.arrived.at[unit, step], 0, unit, step)

    def fetch(self, unit, step):
        slot = step % 2
        return pltpu.make_async_copy(
            self.block(self.sources, unit, step + 1), self.held.at[unit, slot], self.fetch_sems.at[unit, slot]
        )

    def keep(self, unit):
        return pltpu.make_async_copy(
            self.arrived.at[unit, self.count - 2], self.block(self.outs, unit, self.count - 1), self.keep_sems.at[unit]
        )

    def spread_copy(self, unit, step, first=False):
        target = self.block(self.outs, unit, self.count - 1 + step)
        source = self.arrived.at[unit, self.count - 2] if first else target
        return self.send(source, target, 1, unit, step)

    def start(self):
        for unit in range(self.UNITS):
            self.sum_copy(unit, 0, True).start()
            self.fetch(unit, 0).start()
            self.fetch(unit, 1).start()

    def serve(self, turn, unit):
        last = self.count - 2

        @pl.when(turn <= last)
        def _():
            self.sum_copy(unit, turn).wait_recv()
            self.fetch(unit, turn).wait()
            total = self.held[unit, turn % 2].astype(jnp.float32) + self.arrived[unit, turn].astype(jnp.float32)
            self.arrived[unit, turn] = total.astype(jnp.bfloat16)

            @pl.when(turn < last)
            def _():
                self.sum_copy(unit, turn + 1).start()

            @pl.when(turn < last - 1)
            def _():
                self.fetch(unit, turn + 2).start()

            @pl.when(turn == last)
            def _():
                self.spread_copy(unit, 0, True).start()
                self.keep(unit).start()

        @pl.when((turn > last) & (turn <= 2 * last + 1))
        def _():
            step = turn - last - 1
            self.spread_copy(unit, step).wait_recv()

            @pl.when(step < last)
            def _():
                self.spread_copy(unit, step + 1).start()

    def finish(self):
        for unit in range(self.UNITS):
            self.keep(unit).wait()

        def body(step, carry):
            for unit in range(self.UNITS):
                self.sum_copy(unit, step).wait_send()
                self.spread_copy(unit, step).wait_send()
            return carry

        lax.fori_loop(0, self.count - 1, body, 0)


def ring_scratch(count, block):
    return [
        pltpu.VMEM((Ring.UNITS, count - 1) + block, jnp.bfloat16),
        pltpu.VMEM((Ring.UNITS, 2) + block, jnp.bfloat16),
        pltpu.SemaphoreType.DMA((2, 2 * Ring.UNITS, count - 1)),
        pltpu.SemaphoreType.DMA((Ring.UNITS, 2)),
        pltpu.SemaphoreType.DMA((Ring.UNITS,)),
    ]


def own_copy(whole, own, sem):
    size = own.shape[0]
    first = pl.multiple_of(lax.axis_index("narrow") * size, size)
    return pltpu.make_async_copy(whole.at[pl.ds(first, size), :], own, sem)


class Hop:
    KINDS = 6

    def __init__(self, part, from_core, from_cross, full, sems, chunk):
        self.part, self.from_core, self.from_cross = part, from_core, from_cross
        self.full, self.sems, self.chunk = full, sems, chunk
        self.own = part.shape[0] // NARROW
        self.index, self.core, self.cross, self.diagonal = place()

    def rows(self, owner, step):
        return pl.ds(pl.multiple_of(owner * self.own + step * self.chunk, self.chunk), self.chunk)

    def own_rows(self, step):
        return pl.ds(pl.multiple_of(step * self.chunk, self.chunk), self.chunk)

    def core_copies(self, step):
        return [
            remote(self.part.at[self.rows(owner, step)], self.from_core.at[step, slot], self.sems, slot, step, self.core)
            for slot, owner in enumerate((self.core, self.diagonal))
        ]

    def cross_copy(self, step):
        return remote(
            self.part.at[self.rows(self.cross, step)], self.from_cross.at[step], self.sems, 2, step, self.cross
        )

    def gather_copy(self, step, kind):
        owner = self.cross if kind == 5 else self.index
        rows = self.full.at[self.rows(owner, step)]
        return remote(rows, rows, self.sems, kind, step, self.cross if kind == 3 else self.core)

    def send_core(self, step):
        for copy in self.core_copies(step):
            copy.start()

    def send_cross(self, step):
        for copy in self.core_copies(step):
            copy.wait_recv()
        total = self.part[self.rows(self.cross, step), :].astype(jnp.float32)
        total += self.from_core[step, 1].astype(jnp.float32)
        self.part[self.rows(self.cross, step), :] = total.astype(jnp.bfloat16)
        self.cross_copy(step).start()

    def result(self, step):
        total = self.part[self.rows(self.index, step), :].astype(jnp.float32)
        total += self.from_core[step, 0].astype(jnp.float32)
        self.cross_copy(step).wait_recv()
        return total + self.from_cross[step].astype(jnp.float32)

    def send_gather(self, step, values):
        self.full[self.rows(self.index, step), :] = values
        self.gather_copy(step, 3).start()
        self.gather_copy(step, 4).start()

    def forward(self, step):
        self.gather_copy(step, 3).wait_recv()
        self.gather_copy(step, 5).start()

    def gathered(self, step):
        self.gather_copy(step, 4).wait_recv()
        self.gather_copy(step, 5).wait_recv()

    def sent(self, step):
        for copy in self.core_copies(step):
            copy.wait_send()
        self.cross_copy(step).wait_send()

    def finish(self, step, gather=True, parts=True):
        if parts:
            self.sent(step)
        if gather:
            for kind in (3, 4, 5):
                self.gather_copy(step, kind).wait_send()

    def take(self, ref, step):
        return jnp.concatenate([ref[self.rows(owner, step), :] for owner in range(NARROW)], axis=0)

    def put(self, ref, step, values):
        for owner in range(NARROW):
            ref[self.rows(owner, step), :] = values[owner * self.chunk : (owner + 1) * self.chunk]


def hop_scratch(own, chunk, width):
    steps = own // chunk
    return [
        pltpu.VMEM((steps, 2, chunk, width), jnp.bfloat16),
        pltpu.VMEM((steps, chunk, width), jnp.bfloat16),
        pltpu.SemaphoreType.DMA((2, Hop.KINDS, steps)),
    ]


def stages(steps, work, ring=None, extra=None, ticks=0):
    ticks = max(ticks, steps + max(delay for delay, _ in work))
    per_tick = 0 if ring is None else -(-2 * (ring.count - 1) // ticks)

    def body(tick, carry):
        for number, (delay, stage) in enumerate(work):
            step = tick - delay

            @pl.when((step >= 0) & (step < steps))
            def _():
                stage(step)

            unit = (number + 1) * Ring.UNITS // len(work) - 1
            if per_tick and unit != number * Ring.UNITS // len(work) - 1:
                if per_tick == 1:
                    ring.serve(tick, unit)
                else:
                    lax.fori_loop(0, per_tick, lambda i, c: (ring.serve(tick * per_tick + i, unit), c)[1], 0)
        if extra is not None:
            extra(tick)
        return carry

    lax.fori_loop(0, ticks, body, 0)


def middle_kernel(
    all_units, out_grad, far_in, far_out, far_so, far_cq, far_co, lens, text_lens,
    c1, kv2, gains, shifts, biases, bias, b_in,
    ffn_part, third, in_g, out_g, h2, q2, c2, x1, x2, in_bias_g,
    units, own_sem, so_w, cq_w, co_w, small_sem, w_in, w_out, weight_sem, grads_in, grads_sem, give, give_sem, in_acc, out_acc,
    part, h3, core1, fromx1, sem1, core2, fromx2, sem2,
):
    steps, chunk, width = fromx1.shape
    cols = q2.shape[1]
    slots = text_lens.shape[0]
    texts = kv2.shape[0] // slots
    slot_rows = h2.shape[0] // slots
    hidden_count = w_out.shape[0]
    near = [
        pltpu.make_async_copy(source, target, small_sem.at[slot])
        for slot, (source, target) in enumerate(((far_so, so_w), (far_cq, cq_w), (far_co, co_w)))
    ]
    for fetch in near:
        fetch.start()
    fetches = [
        own_copy(all_units, units, own_sem),
        pltpu.make_async_copy(far_in, w_in, weight_sem.at[0]),
        pltpu.make_async_copy(far_out, w_out, weight_sem.at[1]),
    ]
    for fetch in fetches:
        fetch.start()
    greet()
    one = Hop(part, core1, fromx1, h2, sem1, chunk)
    two = Hop(part, core2, fromx2, h3, sem2, chunk)
    scale = jnp.bfloat16(HEAD_DIM**-0.5)
    in_acc[...] = jnp.zeros_like(in_acc)
    out_acc[...] = jnp.zeros_like(out_acc)
    in_bias_g[...] = jnp.zeros_like(in_bias_g)
    for fetch in near:
        fetch.wait()

    def grad_copies(step):
        slot = step % 2
        return [
            pltpu.make_async_copy(
                out_grad.at[one.rows(owner, step), :],
                grads_in.at[slot, pl.ds(owner * chunk, chunk), :],
                grads_sem.at[slot, owner],
            )
            for owner in range(NARROW)
        ]

    def give_copies(step, kind):
        slot = step % 2
        return [
            pltpu.make_async_copy(
                give.at[kind, slot, pl.ds(owner * chunk, chunk), :],
                (ffn_part, third)[kind].at[one.rows(owner, step), :],
                give_sem.at[kind, slot, owner],
            )
            for owner in range(NARROW)
        ]

    def project(step):
        one.put(part, step, dot_nn(one.take(c1, step), so_w[...]).astype(jnp.bfloat16))
        one.send_core(step)

    def norm_one(step):
        @pl.when(step == 0)
        def _():
            fetches[0].wait()

        rows = one.own_rows(step)
        resid = units[rows, :].astype(jnp.float32) + one.result(step) + biases[0:1, :]
        x1[rows, :] = resid
        one.send_gather(step, norm_forward(resid, gains[1:2, :], shifts[1:2, :])[0].astype(jnp.bfloat16))

    def cross(step):
        one.gathered(step)
        queries = (dot_nn(one.take(h2, step), cq_w[...]) + bias[0:1, :]).astype(jnp.bfloat16)
        one.put(q2, step, queries)
        scaled = queries * scale
        count = queries.shape[0] // slots
        place_of = lax.broadcasted_iota(jnp.int32, (count, texts), 1)
        context = []
        for slot in range(slots):
            mine = scaled[slot * count : (slot + 1) * count]
            keys = kv2[slot * texts : (slot + 1) * texts, :cols]
            values = kv2[slot * texts : (slot + 1) * texts, cols:]
            total = jnp.zeros((count, cols), jnp.float32)
            for head in range(cols // HEAD_DIM):
                scores = dot_nt(pick_head(mine, head), keys)
                scores = jnp.where(place_of < text_lens[slot], scores, MASKED_SCORE)
                weights = jnp.exp(scores - jnp.max(scores, axis=1, keepdims=True))
                weights = weights * (1.0 / jnp.sum(weights, axis=1, keepdims=True))
                total += dot_nn(weights.astype(jnp.bfloat16), pick_head(values, head))
            context.append(total.astype(jnp.bfloat16))
        context = jnp.concatenate(context, axis=0)
        one.put(c2, step, context)
        one.sent(step)
        two.put(part, step, dot_nn(context, co_w[...]).astype(jnp.bfloat16))
        two.send_core(step)

    def norm_two(step):
        rows = one.own_rows(step)
        resid = x1[rows, :] + two.result(step) + biases[1:2, :]
        x2[rows, :] = resid
        two.send_gather(step, norm_forward(resid, gains[2:3, :], shifts[2:3, :])[0].astype(jnp.bfloat16))

    def forward_two(step):
        two.forward(step)
        for copy in grad_copies(step):
            copy.start()

    def ffn(step):
        @pl.when(step == 0)
        def _():
            fetches[1].wait()
            fetches[2].wait()

        two.gathered(step)
        for copy in grad_copies(step):
            copy.wait()
        rows = two.take(h3, step)
        place_in = lax.broadcasted_iota(jnp.int32, (chunk, width), 0) + step * chunk
        grads = []
        for owner in range(NARROW):
            first = owner * two.own
            valid = place_in < lens[first // slot_rows] - first % slot_rows
            values = grads_in[step % 2, owner * chunk : (owner + 1) * chunk, :]
            grads.append(jnp.where(valid, values.astype(jnp.float32), 0.0).astype(jnp.bfloat16))
        grads = jnp.concatenate(grads, axis=0)
        out = jnp.zeros(rows.shape, jnp.float32)
        back_out = jnp.zeros(rows.shape, jnp.float32)
        for begin in range(0, hidden_count, HIDDEN):
            some = slice(begin, begin + HIDDEN)
            pre = dot_nn(rows, w_in[:, some]) + b_in[:, some]
            cdf = 0.5 + 0.5 * lax.erf(pre * (0.5**0.5))
            pdf = jnp.exp(-0.5 * pre * pre) * 0.3989422804014327
            hidden = (pre * cdf).astype(jnp.bfloat16)
            pre_low = ((cdf + pre * pdf) * dot_nt(grads, w_out[some, :])).astype(jnp.bfloat16)
            in_bias_g[:, some] += column_sum(pre_low.astype(jnp.float32))
            out += dot_nn(hidden, w_out[some, :])
            back_out += dot_nt(pre_low, w_in[:, some])
            out_acc[some, :] += dot_tn(hidden, grads)
            side, place_at = divmod(begin, width)
            in_acc[side * width : (side + 1) * width, place_at : place_at + HIDDEN] += dot_tn(rows, pre_low)

        @pl.when(step >= 2)
        def _():
            for kind in range(2):
                for copy in give_copies(step - 2, kind):
                    copy.wait()

        give[0, step % 2] = out.astype(jnp.bfloat16)
        give[1, step % 2] = back_out.astype(jnp.bfloat16)
        for kind in range(2):
            for copy in give_copies(step, kind):
                copy.start()

    stages(
        steps,
        [
            (0, project), (1, one.send_cross), (2, norm_one), (3, one.forward), (4, cross),
            (5, two.send_cross), (6, norm_two), (7, forward_two), (8, ffn),
        ],
    )

    def finish(step, carry):
        one.finish(step, True, False)
        two.finish(step)
        return carry

    lax.fori_loop(0, steps, finish, 0)
    part[...] = out_acc[...].astype(jnp.bfloat16)
    results = [pltpu.make_async_copy(part, out_g, weight_sem.at[0])]
    results[0].start()
    h3[...] = in_acc[...].astype(jnp.bfloat16)
    for side in range(hidden_count // width):
        here = pl.ds(side * width, width)
        results.append(pltpu.make_async_copy(h3.at[here, :], in_g.at[:, here], weight_sem.at[1 + side]))
        results[-1].start()
    for step in (steps - 2, steps - 1):
        for kind in range(2):
            for copy in give_copies(step, kind):
                copy.wait()
    for copy in results:
        copy.wait()


def middle(units, out_grad, w_in, w_out, so_w, cq_w, co_w, lens, text_lens, c1, kv2, gains, shifts, biases, bias, b_in):
    rows, cols = c1.shape
    own, width = rows // NARROW, units.shape[1]
    hidden_count = w_out.shape[0]
    chunk = own // STEPS
    bf, f32 = jnp.bfloat16, jnp.float32
    shape = jax.ShapeDtypeStruct
    vmem = pl.BlockSpec(memory_space=pltpu.VMEM)
    hbm = pl.BlockSpec(memory_space=pl.ANY)
    hop = hop_scratch(own, chunk, width)
    dma = pltpu.SemaphoreType.DMA
    return pl.pallas_call(
        middle_kernel,
        in_specs=[hbm] * 7 + [pl.BlockSpec(memory_space=pltpu.SMEM)] * 2 + [vmem] * 7,
        out_specs=[hbm] * 4 + [vmem] * 6,
        out_shape=[
            pltpu.HBM((rows, width), bf),
            pltpu.HBM((rows, width), bf),
            pltpu.HBM((width, hidden_count), bf),
            pltpu.HBM((hidden_count, width), bf),
            shape((rows, width), bf),
            shape((rows, cols), bf),
            shape((rows, cols), bf),
            shape((own, width), f32),
            shape((own, width), f32),
            shape((1, hidden_count), f32),
        ],
        scratch_shapes=[
            pltpu.VMEM((own, width), bf),
            dma,
            pltpu.VMEM(so_w.shape, bf),
            pltpu.VMEM(cq_w.shape, bf),
            pltpu.VMEM(co_w.shape, bf),
            dma((3,)),
            pltpu.VMEM((width, hidden_count), bf),
            pltpu.VMEM((hidden_count, width), bf),
            dma((1 + hidden_count // width,)),
            pltpu.VMEM((2, NARROW * chunk, width), bf),
            dma((2, NARROW)),
            pltpu.VMEM((2, 2, NARROW * chunk, width), bf),
            dma((2, 2, NARROW)),
            pltpu.VMEM((hidden_count, width), f32),
            pltpu.VMEM((hidden_count, width), f32),
            pltpu.VMEM((rows, width), bf),
            pltpu.VMEM((rows, width), bf),
        ]
        + hop
        + hop,
        compiler_params=pltpu.CompilerParams(collective_id=0, has_side_effects=True, vmem_limit_bytes=60 * MIB),
        cost_estimate=pl.CostEstimate(flops=100 * 10**9, bytes_accessed=48 * MIB, transcendentals=8 * MIB),
        name="middle",
    )(
        units, out_grad, w_in, w_out, so_w, cq_w, co_w, lens, text_lens, c1, kv2, gains, shifts, biases, bias,
        b_in.reshape(1, -1),
    )


class FarHop(Hop):
    def fetch(self, mine, theirs, sems):
        self.mine, self.theirs = mine, theirs
        rows = lambda owner: pl.ds(pl.multiple_of(owner * self.own, self.own), self.own)
        self.fetches = [
            pltpu.make_async_copy(self.part.at[rows(owner)], ref, sems.at[slot])
            for slot, (owner, ref) in enumerate(((self.index, mine), (self.cross, theirs)))
        ]
        for copy in self.fetches:
            copy.start()

    def fetched(self):
        for copy in self.fetches:
            copy.wait()

    def cross_copy(self, step):
        return remote(
            self.theirs.at[self.own_rows(step)], self.from_cross.at[step], self.sems, 2, step, self.cross
        )

    def send_cross(self, step):
        for copy in self.core_copies(step):
            copy.wait_recv()
        total = self.theirs[self.own_rows(step), :].astype(jnp.float32)
        total += self.from_core[step, 1].astype(jnp.float32)
        self.theirs[self.own_rows(step), :] = total.astype(jnp.bfloat16)
        self.cross_copy(step).start()

    def result(self, step):
        total = self.mine[self.own_rows(step), :].astype(jnp.float32)
        total += self.from_core[step, 0].astype(jnp.float32)
        self.cross_copy(step).wait_recv()
        return total + self.from_cross[step].astype(jnp.float32)


def left_here(lens, own, rows):
    first = lax.axis_index("narrow") * own
    slot_rows = rows // lens.shape[0]
    return lens[first // slot_rows] - first % slot_rows


def row_of(step, chunk, width):
    return lax.broadcasted_iota(jnp.int32, (chunk, width), 0) + step * chunk


def turn_kernel(
    third, in_g, out_g, out_grad, lens, text_lens, x1, x2, h2, q2, c2, kv2, c1, gains, co_w, cq_w, so_w,
    in_sum, out_sum, g0, g1, dx1, dc1, dkv, bias_g, stats,
    co_g, cq_g, so_g, give_sem, e_own, own_sem, mine3, theirs3, core3, fromx3, sem3,
    part5, core5, fromx5, sem5, full3, full5, dx2, co_acc, cq_acc, so_acc, dkv_acc, fetch_sem,
    *ring_refs, count,
):
    steps, chunk, width = fromx5.shape
    cols = q2.shape[1]
    slots = bias_g.shape[0]
    texts = kv2.shape[0] // slots

    def ring_view(ref, way, half, shard):
        high = width // count
        if way == 0:
            return ref.at[pl.ds(pl.multiple_of(shard * high, high), high), pl.ds(half * width, width)]
        return ref.at[pl.ds(pl.multiple_of(shard * 2 * high + half * high, high), high), :]

    ring = Ring(count, (in_g, out_g), (in_sum, out_sum), ring_view, *ring_refs)
    fetch = own_copy(out_grad, e_own, own_sem)
    fetch.start()
    greet(*ring.peers)
    ring.start()
    three = FarHop(third, core3, fromx3, full3, sem3, chunk)
    five = Hop(part5, core5, fromx5, full5, sem5, chunk)
    three.fetch(mine3, theirs3, fetch_sem)

    def start(step, carry):
        three.send_core(step)
        return carry

    lax.fori_loop(0, steps, start, 0)
    for ref in (co_acc, cq_acc, so_acc, dkv_acc, bias_g, stats):
        ref[...] = jnp.zeros_like(ref)
    three.fetched()
    fetch.wait()
    valid_rows = left_here(lens, x1.shape[0], h2.shape[0])
    scale = jnp.bfloat16(HEAD_DIM**-0.5)

    def norm_three(step):
        rows = three.own_rows(step)
        grad_in = three.result(step)
        _, normed, inv_std = norm_forward(x2[rows, :], gains[2:3, :], gains[2:3, :])
        stats[0:1, :] += column_sum(grad_in * normed)
        stats[1:2, :] += column_sum(grad_in)
        above = jnp.where(row_of(step, chunk, width) < valid_rows, e_own[rows, :].astype(jnp.float32), 0.0)
        total = above + norm_backward(grad_in, normed, inv_std, gains[2:3, :])
        stats[2:3, :] += column_sum(above)
        stats[3:4, :] += column_sum(total)
        dx2[rows, :] = total
        three.send_gather(step, total.astype(jnp.bfloat16))

    def cross(step):
        three.gathered(step)
        grads = three.take(full3, step)
        co_acc[...] += dot_tn(three.take(c2, step), grads)
        context = dot_nt(grads, co_w[...]).astype(jnp.bfloat16)
        queries = three.take(q2, step) * scale
        count = queries.shape[0] // slots
        place_of = lax.broadcasted_iota(jnp.int32, (texts, count), 0)
        q_grad = []
        for slot in range(slots):
            rows = slice(slot * count, (slot + 1) * count)
            texts_here = slice(slot * texts, (slot + 1) * texts)
            keys, values = kv2[texts_here, :cols], kv2[texts_here, cols:]
            total = jnp.zeros((count, cols), jnp.float32)
            for head in range(cols // HEAD_DIM):
                q_head, g_head = pick_head(queries[rows], head), pick_head(context[rows], head)
                scores = jnp.where(place_of < text_lens[slot], dot_nt(keys, q_head), MASKED_SCORE)
                weights = jnp.exp(scores - jnp.max(scores, axis=0, keepdims=True))
                weights = weights * (1.0 / jnp.sum(weights, axis=0, keepdims=True))
                dkv_acc[texts_here, cols:] += dot_nn(weights.astype(jnp.bfloat16), g_head)
                weight_grad = dot_nt(values, g_head)
                inner = jnp.sum(weights * weight_grad, axis=0, keepdims=True)
                score_grad = (weights * (weight_grad - inner)).astype(jnp.bfloat16)
                dkv_acc[texts_here, :cols] += dot_nn(score_grad, q_head)
                total += dot_tn(score_grad, pick_head(keys, head))
            q_grad.append((total * HEAD_DIM**-0.5).astype(jnp.bfloat16))
        q_grad = jnp.concatenate(q_grad, axis=0)
        five.put(part5, step, dot_nt(q_grad, cq_w[...]).astype(jnp.bfloat16))
        five.send_core(step)
        bias_g[0:1, :] += column_sum(q_grad.astype(jnp.float32))
        cq_acc[...] += dot_tn(five.take(h2, step), q_grad)

    def norm_two(step):
        rows = five.own_rows(step)
        grad_in = five.result(step)
        _, normed, inv_std = norm_forward(x1[rows, :], gains[1:2, :], gains[1:2, :])
        stats[4:5, :] += column_sum(grad_in * normed)
        stats[5:6, :] += column_sum(grad_in)
        total = dx2[rows, :] + norm_backward(grad_in, normed, inv_std, gains[1:2, :])
        stats[6:7, :] += column_sum(total)
        dx1[rows, :] = total
        five.send_gather(step, total.astype(jnp.bfloat16))

    def last(step):
        five.gathered(step)
        grads = five.take(full5, step)
        dc1_rows = dot_nt(grads, so_w[...]).astype(jnp.bfloat16)
        five.put(dc1, step, dc1_rows)
        so_acc[...] += dot_tn(five.take(c1, step), grads)

    stages(
        steps,
        list(
            enumerate(
                [
                    three.send_cross, norm_three, three.forward, cross,
                    five.send_cross, norm_two, five.forward, last,
                ]
            )
        ),
        ring,
    )
    dkv[...] = dkv_acc[...].astype(jnp.bfloat16)
    bias_g[1:2, :] = column_sum(dkv[:, cols:].astype(jnp.float32))
    co_g[...] = co_acc[...].astype(jnp.bfloat16)
    cq_g[...] = cq_acc[...].astype(jnp.bfloat16)
    so_g[...] = so_acc[...].astype(jnp.bfloat16)
    gives = [
        pltpu.make_async_copy(cq_g, g0.at[:, pl.ds(width - cols, cols)], give_sem.at[0]),
        pltpu.make_async_copy(co_g, g1.at[pl.ds(0, cols), :], give_sem.at[1]),
        pltpu.make_async_copy(so_g, g1.at[pl.ds(cols, cols), :], give_sem.at[2]),
    ]
    for give in gives:
        give.start()

    def finish(step, carry):
        three.finish(step)
        five.finish(step)
        return carry

    lax.fori_loop(0, steps, finish, 0)
    ring.finish()
    for give in gives:
        give.wait()


def turn(count, third, in_g, out_g, out_grad, lens, text_lens, x1, x2, h2, q2, c2, kv2, c1, gains, co_w, cq_w, so_w):
    rows, cols = c1.shape
    own, width = x1.shape
    chunk = own // STEPS
    bf, f32 = jnp.bfloat16, jnp.float32
    shape = jax.ShapeDtypeStruct
    vmem = pl.BlockSpec(memory_space=pltpu.VMEM)
    hbm = pl.BlockSpec(memory_space=pl.ANY)
    hop = hop_scratch(own, chunk, width)
    far = [pltpu.VMEM((own, width), bf)] * 2 + hop
    return pl.pallas_call(
        functools.partial(turn_kernel, count=count),
        in_specs=[hbm] * 4 + [pl.BlockSpec(memory_space=pltpu.SMEM)] * 2 + [vmem] * 11,
        out_specs=[hbm] * 4 + [vmem] * 5,
        out_shape=[
            pltpu.HBM(in_g.shape, bf),
            pltpu.HBM(out_g.shape, bf),
            pltpu.HBM((width, width), bf),
            pltpu.HBM((width, width), bf),
            shape((own, width), f32),
            shape((rows, cols), bf),
            shape(kv2.shape, bf),
            shape((2, cols), f32),
            shape((8, width), f32),
        ],
        scratch_shapes=[
            pltpu.VMEM((cols, width), bf),
            pltpu.VMEM((width, cols), bf),
            pltpu.VMEM((cols, width), bf),
            pltpu.SemaphoreType.DMA((3,)),
            pltpu.VMEM((own, width), bf),
            pltpu.SemaphoreType.DMA,
        ]
        + far
        + [pltpu.VMEM((rows, width), bf)]
        + hop
        + [pltpu.VMEM((rows, width), bf)] * 2
        + [
            pltpu.VMEM((own, width), f32),
            pltpu.VMEM((cols, width), f32),
            pltpu.VMEM((width, cols), f32),
            pltpu.VMEM((cols, width), f32),
            pltpu.VMEM(kv2.shape, f32),
            pltpu.SemaphoreType.DMA((2,)),
        ]
        + ring_scratch(count, (width // count, width)),
        compiler_params=pltpu.CompilerParams(collective_id=1, has_side_effects=True, vmem_limit_bytes=60 * MIB),
        cost_estimate=pl.CostEstimate(flops=100 * 10**9, bytes_accessed=24 * MIB, transcendentals=4 * MIB),
        name="turn",
    )(third, in_g, out_g, out_grad, lens, text_lens, x1, x2, h2, q2, c2, kv2, c1, gains, co_w, cq_w, so_w)


SMALL = 16
NORM_ROWS = 9


class Small:
    def __init__(self, count, block, near, far, sems):
        self.count, self.mine, self.near, self.far, self.sems = count, block, near, far, sems
        self.index, self.core, self.cross, _ = place()
        self.spot, *self.peers = ring_place(count)

    def near_copy(self, kind):
        owner = self.cross if kind == 2 else self.index
        return remote(self.near.at[owner], self.near.at[owner], self.sems, 0, kind, (self.cross, self.core, self.core)[kind])

    def far_copy(self, way, step):
        block = self.far.at[(self.spot + (2 * way - 1) * step + self.count) % self.count]
        return remote(block, block, self.sems, 1 + way, step, self.peers[way], "wide")

    def begin(self):
        self.near[self.index] = self.mine[...]
        self.near_copy(0).start()
        self.near_copy(1).start()

    def forward(self):
        self.near_copy(0).wait_recv()
        self.near_copy(2).start()

    def launch(self):
        self.near_copy(1).wait_recv()
        self.near_copy(2).wait_recv()
        both = self.near[0]
        for owner in range(1, NARROW):
            both += self.near[owner]
        row = lax.broadcasted_iota(jnp.int32, both.shape, 0)
        self.far[self.spot] = jnp.where(row < SMALL - NORM_ROWS, self.mine[...], both)
        self.far_copy(0, 0).start()
        self.far_copy(1, 0).start()

    def rotate(self, step):
        for way in range(2):
            steps = self.count // 2 - way

            @pl.when(step < steps)
            def _():
                self.far_copy(way, step).wait_recv()

            @pl.when(step < steps - 1)
            def _():
                self.far_copy(way, step + 1).start()

    def finish(self, out):
        for kind in range(3):
            self.near_copy(kind).wait_send()

        for way in range(2):

            def body(step, carry):
                self.far_copy(way, step).wait_send()
                return carry

            lax.fori_loop(0, self.count // 2 - way, body, 0)
        out[...] = jnp.zeros_like(out)

        def add(spot, carry):
            out[...] += self.far[spot]
            return carry

        lax.fori_loop(0, self.count, add, 0)


def last_kernel(
    ffn_part, g0, g1, all_units, lens, dqkv, dkv, dx1, x2, self_b, cross_b, ffn_b, stats, gains, biases, qkv_w, kv_w,
    sum0, sum1, y, units_g, text_g, small_sum,
    units, own_sem, mine4, theirs4, core4, fromx4, sem4,
    part6, core6, fromx6, sem6, part7, core7, fromx7, sem7,
    fetch_sem, block, near, far, small_sem, *ring_refs, count,
):
    steps, chunk, width = fromx6.shape
    text_steps = fromx7.shape[0]

    def ring_view(ref, way, half, shard):
        high = width // count
        return ref.at[pl.ds(pl.multiple_of(shard * high, high), high), pl.ds(half * (width // 2), width // 2)]

    ring = Ring(count, (g0, g1), (sum0, sum1), ring_view, *ring_refs)
    small = Small(count, block, near, far, small_sem)
    fetch = own_copy(all_units, units, own_sem)
    fetch.start()
    greet(*ring.peers)
    ring.start()
    four = FarHop(ffn_part, core4, fromx4, None, sem4, chunk)
    six = Hop(part6, core6, fromx6, None, sem6, chunk)
    seven = Hop(part7, core7, fromx7, None, sem7, chunk)
    four.fetch(mine4, theirs4, fetch_sem)
    four.fetched()
    fetch.wait()
    block[...] = jnp.zeros_like(block)
    cols = self_b.shape[1]
    for row in range(2):
        block[0:1, row * cols : (row + 1) * cols] = self_b[row : row + 1, :]
        block[0:1, (2 + row) * cols : (3 + row) * cols] = cross_b[row : row + 1, :]
        block[1 + row : 2 + row, :] = ffn_b[:, row * width : (row + 1) * width]
    block[SMALL - NORM_ROWS : SMALL - 2, :] = stats[:7, :]
    valid_rows = left_here(lens, x2.shape[0], dqkv.shape[0])
    gain = gains[0:1, :]

    def project(step):
        grads = six.take(dqkv, step)
        total = dot_nt(grads[:, :cols], qkv_w[0]) + dot_nt(grads[:, cols : 2 * cols], qkv_w[1])
        six.put(part6, step, (total + dot_nt(grads[:, 2 * cols :], qkv_w[2])).astype(jnp.bfloat16))
        six.send_core(step)
        four.send_core(step)

    def norm_one(step):
        rows = six.own_rows(step)
        grad_in = six.result(step)
        _, normed, inv_std = norm_forward(units[rows, :].astype(jnp.float32), gain, gain)
        block[SMALL - 2 : SMALL - 1, :] += column_sum(grad_in * normed)
        block[SMALL - 1 : SMALL, :] += column_sum(grad_in)
        units_g[rows, :] = dx1[rows, :] + norm_backward(grad_in, normed, inv_std, gain)

    def text_only(work):
        def stage(step):
            @pl.when(step < text_steps)
            def _():
                work(step)

        return stage

    def text_project(step):
        seven.put(part7, step, dot_nt(seven.take(dkv, step), kv_w[...]).astype(jnp.bfloat16))
        seven.send_core(step)

    def text_result(step):
        text_g[seven.own_rows(step), :] = seven.result(step)

    def output(step):
        rows = four.own_rows(step)
        total = x2[rows, :] + four.result(step) + biases[2:3, :]
        y[rows, :] = jnp.where(row_of(step, chunk, width) < valid_rows, total, 0.0).astype(jnp.bfloat16)

    ready = steps + 1

    def extra(tick):
        for when, work in enumerate((small.begin, small.forward, small.launch)):
            pl.when(tick == ready + when)(work)
        step = tick - ready - 3

        @pl.when((step >= 0) & (step < count // 2))
        def _():
            small.rotate(step)

    stages(
        steps,
        list(
            enumerate(
                [
                    project, six.send_cross, norm_one, four.send_cross, output,
                    text_only(text_project), text_only(seven.send_cross), text_only(text_result),
                ]
            )
        ),
        ring,
        extra,
        ready + 3 + count // 2,
    )

    def finish(step, carry):
        four.finish(step, False)
        six.finish(step, False)
        text_only(lambda s: seven.finish(s, False))(step)
        return carry

    lax.fori_loop(0, steps, finish, 0)
    ring.finish()
    small.finish(small_sum)


def last(count, ffn_part, g0, g1, units, lens, dqkv, dkv, dx1, x2, *rest):
    rows = dqkv.shape[0]
    own, width = dx1.shape
    chunk = own // STEPS
    text_own = dkv.shape[0] // NARROW
    bf, f32 = jnp.bfloat16, jnp.float32
    shape = jax.ShapeDtypeStruct
    vmem = pl.BlockSpec(memory_space=pltpu.VMEM)
    hbm = pl.BlockSpec(memory_space=pl.ANY)
    hop = hop_scratch(own, chunk, width)
    far = [pltpu.VMEM((own, width), bf)] * 2 + hop
    return pl.pallas_call(
        functools.partial(last_kernel, count=count),
        in_specs=[hbm] * 4 + [pl.BlockSpec(memory_space=pltpu.SMEM)] + [vmem] * (4 + len(rest)),
        out_specs=[hbm] * 2 + [vmem] * 4,
        out_shape=[
            pltpu.HBM(g0.shape, bf),
            pltpu.HBM(g1.shape, bf),
            shape((own, width), bf),
            shape((own, width), f32),
            shape((text_own, width), f32),
            shape((SMALL, width), f32),
        ],
        scratch_shapes=[pltpu.VMEM((own, width), bf), pltpu.SemaphoreType.DMA]
        + far
        + [pltpu.VMEM((rows, width), bf)]
        + hop
        + [pltpu.VMEM((dkv.shape[0], width), bf)]
        + hop_scratch(text_own, chunk, width)
        + [
            pltpu.SemaphoreType.DMA((2,)),
            pltpu.VMEM((SMALL, width), f32),
            pltpu.VMEM((NARROW, SMALL, width), f32),
            pltpu.VMEM((count, SMALL, width), f32),
            pltpu.SemaphoreType.DMA((2, 3, max(count // 2, 3))),
        ]
        + ring_scratch(count, (width // count, width // 2)),
        compiler_params=pltpu.CompilerParams(collective_id=2, has_side_effects=True, vmem_limit_bytes=58 * MIB),
        cost_estimate=pl.CostEstimate(flops=30 * 10**9, bytes_accessed=16 * MIB, transcendentals=0),
        name="last",
    )(ffn_part, g0, g1, units, lens, dqkv, dkv, dx1, x2, *rest)


def unpack_kernel(sum0, sum1, small, qkv_g, cq_g, co_g, so_g, kv_g, gain_g, shift_g, bias_g, self_b, cross_b, ffn_b):
    cols = cq_g.shape[1]
    for part in range(3):
        qkv_g[part] = sum0[:, part * cols : (part + 1) * cols].astype(jnp.float32)
    cq_g[...] = sum0[:, 3 * cols :].astype(jnp.float32)
    co_g[...] = sum1[:cols, :].astype(jnp.float32)
    so_g[...] = sum1[cols : 2 * cols, :].astype(jnp.float32)
    half = kv_g.shape[0] // 2
    for side in range(2):
        for part in range(2):
            first = (2 * side + part) * cols
            kv_g[side * half : (side + 1) * half, part, :] = sum1[2 * cols :, first : first + cols].astype(jnp.float32)
    norms = small[SMALL - NORM_ROWS :, :]
    for ref, order in ((gain_g, (7, 4, 0)), (shift_g, (8, 5, 1)), (bias_g, (6, 3, 2))):
        for row, source in enumerate(order):
            ref[row : row + 1, :] = norms[source : source + 1, :]
    width = small.shape[1]
    for row in range(2):
        self_b[row : row + 1, :] = small[0:1, row * cols : (row + 1) * cols]
        cross_b[row : row + 1, :] = small[0:1, (2 + row) * cols : (3 + row) * cols]
        ffn_b[:, row * width : (row + 1) * width] = small[1 + row : 2 + row, :]


def unpack(sum0, sum1, small, cols, hidden):
    width = sum0.shape[0]
    shape = lambda *dims: jax.ShapeDtypeStruct(dims, jnp.float32)
    vmem = pl.BlockSpec(memory_space=pltpu.VMEM)
    return pl.pallas_call(
        unpack_kernel,
        in_specs=[vmem] * 3,
        out_specs=[vmem] * 11,
        out_shape=[
            shape(3, width, cols), shape(width, cols), shape(cols, width), shape(cols, width), shape(width, 2, cols),
            shape(3, width), shape(3, width), shape(3, width), shape(2, cols), shape(2, cols), shape(1, hidden),
        ],
        compiler_params=pltpu.CompilerParams(vmem_limit_bytes=40 * MIB),
        name="unpack",
    )(sum0, sum1, small)


def local(
    units,
    text,
    out_grad,
    unit_lengths,
    text_lengths,
    bucket_counts,
    norm_gain,
    norm_shift,
    self_qkv,
    self_bias,
    self_out,
    cross_q,
    cross_kv,
    cross_bias,
    cross_out,
    ffn_in,
    ffn_in_bias,
    ffn_out,
    out_bias,
):
    slot_live = jnp.arange(unit_lengths.shape[0], dtype=jnp.int32) < bucket_counts[0]
    lengths = jnp.where(slot_live, unit_lengths, 0)
    qkv_weights = jnp.transpose(self_qkv, (1, 0, 2))
    kv_weights = cross_kv.reshape(cross_kv.shape[0], -1)
    count = lax.axis_size("wide")
    first_in, queries, key_rows, value_rows, text_kv, self_context, self_logs = front(
        lengths, units, text, norm_gain, norm_shift, qkv_weights, self_bias, kv_weights, cross_bias
    )
    (
        ffn_part,
        third_part,
        ffn_in_grad,
        ffn_out_grad,
        second_all,
        cross_queries,
        cross_context,
        resid_one,
        resid_two,
        ffn_bias_sum,
    ) = middle(
        units,
        out_grad,
        ffn_in,
        ffn_out,
        self_out,
        cross_q,
        cross_out,
        lengths,
        text_lengths,
        self_context,
        text_kv,
        norm_gain,
        norm_shift,
        out_bias,
        cross_bias,
        ffn_in_bias,
    )
    in_sum, out_sum, grads_one, grads_two, resid_one_grad, context_grad, text_kv_grad, cross_bias_sum, stats = turn(
        count,
        third_part,
        ffn_in_grad,
        ffn_out_grad,
        out_grad,
        lengths,
        text_lengths,
        resid_one,
        resid_two,
        second_all,
        cross_queries,
        cross_context,
        text_kv,
        self_context,
        norm_gain,
        cross_out,
        cross_q,
        self_out,
    )
    qkv_grad, grads_one, grads_two, self_bias_sum, ffn_in_grad, ffn_out_grad = back(
        lengths,
        queries,
        key_rows,
        value_rows,
        context_grad,
        self_context,
        self_logs,
        first_in,
        text,
        text_kv_grad,
        in_sum,
        out_sum,
        grads_one,
        grads_two,
    )
    summed_one, summed_two, output, units_grad, text_grad, small = last(
        count,
        ffn_part,
        grads_one,
        grads_two,
        units,
        lengths,
        qkv_grad,
        text_kv_grad,
        resid_one_grad,
        resid_two,
        self_bias_sum,
        cross_bias_sum,
        ffn_bias_sum,
        stats,
        norm_gain,
        out_bias,
        qkv_weights,
        kv_weights,
    )
    (
        self_qkv_grad,
        cross_q_grad,
        cross_out_grad,
        self_out_grad,
        cross_kv_grad,
        gain_grad,
        shift_grad,
        bias_grad,
        self_bias_grad,
        cross_bias_grad,
        ffn_in_bias_grad,
    ) = unpack(summed_one, summed_two, small, queries.shape[1], ffn_in_bias.shape[0])
    self_qkv_grad = jnp.transpose(self_qkv_grad, (1, 0, 2))
    ffn_in_bias_grad = ffn_in_bias_grad.reshape(-1)
    return (
        output,
        units_grad,
        text_grad,
        gain_grad,
        shift_grad,
        self_qkv_grad,
        self_bias_grad,
        self_out_grad,
        cross_q_grad,
        cross_kv_grad,
        cross_bias_grad,
        cross_out_grad,
        ffn_in_grad,
        ffn_in_bias_grad,
        ffn_out_grad,
        bias_grad,
    )


def solution(mesh):
    placed = (
        P("wide", None),
        P("wide", None),
        P("wide", None),
        P("wide"),
        P("wide"),
        P("wide"),
        P(),
        P(),
        P(None, None, "narrow"),
        P(None, "narrow"),
        P("narrow", None),
        P(None, "narrow"),
        P(None, None, "narrow"),
        P(None, "narrow"),
        P("narrow", None),
        P(None, "narrow"),
        P("narrow"),
        P("narrow", None),
        P(),
    )
    return jax.shard_map(
        local,
        mesh=mesh,
        in_specs=placed,
        out_specs=(
            P(("wide", "narrow"), None),
            P(("wide", "narrow"), None),
            P(("wide", "narrow"), None),
            P(),
            P(),
            P(None, None, "narrow"),
            P(None, "narrow"),
            P("narrow", None),
            P(None, "narrow"),
            P(None, None, "narrow"),
            P(None, "narrow"),
            P("narrow", None),
            P(None, "narrow"),
            P("narrow"),
            P("narrow", None),
            P(),
        ),
        check_vma=False,
    )
```

```python
import functools

import jax
import jax.numpy as jnp
from jax import lax
from jax.experimental import pallas as pl
from jax.experimental.pallas import tpu as pltpu
from jax.sharding import PartitionSpec as P

HEAD_DIM = 64


NORM_EPSILON = 1e-05
MASKED_SCORE = -1000000000.0
EXACT = lax.Precision.HIGHEST


def norm_forward(values, gain_vec, shift_vec):
    row_mean = jnp.mean(values, axis=-1, keepdims=True)
    centered = values - row_mean
    inv_std = lax.rsqrt(jnp.mean(centered * centered, axis=-1, keepdims=True) + NORM_EPSILON)
    normed = centered * inv_std
    return (normed * gain_vec + shift_vec, normed, inv_std)


def norm_backward(grad_in, normed, inv_std, gain_vec):
    scaled = grad_in * gain_vec
    inner_term = scaled - jnp.mean(scaled, axis=-1, keepdims=True)
    inner_term = inner_term - normed * jnp.mean(scaled * normed, axis=-1, keepdims=True)
    return inner_term * inv_std


BLOCK = 256
LANES = 128
MIB = 1 << 20
NARROW = 4
STEPS = 8
HIDDEN = 512
MESH = pl.DeviceIdType.MESH


def head_mask(shape, head):
    lane = lax.broadcasted_iota(jnp.int32, shape, len(shape) - 1)
    return (lane >= head * HEAD_DIM) & (lane < (head + 1) * HEAD_DIM)


def pick_head(values, head):
    return jnp.where(head_mask(values.shape, head), values, jnp.zeros_like(values))


def dot_nt(a, b):
    return lax.dot_general(a, b, (((1,), (1,)), ((), ())), preferred_element_type=jnp.float32)


def dot_nn(a, b):
    return jnp.dot(a, b, preferred_element_type=jnp.float32)


def dot_tn(a, b):
    return lax.dot_general(a, b, (((0,), (0,)), ((), ())), preferred_element_type=jnp.float32)


def column_sum(values):
    return jnp.sum(values, axis=0, keepdims=True)


def mask_diagonal(scores, axis):
    count = scores.shape[axis]
    parts = [scores] if count == BLOCK else jnp.split(scores, [count - BLOCK], axis=axis)
    keys = lax.broadcasted_iota(jnp.int32, (BLOCK, BLOCK), axis)
    queries = lax.broadcasted_iota(jnp.int32, (BLOCK, BLOCK), 1 - axis)
    parts[-1] = jnp.where(keys <= queries, parts[-1], MASKED_SCORE)
    return jnp.concatenate(parts, axis=axis)


def front_kernel(
    lens, x_ref, t_ref, g_ref, s_ref, w_ref, b_ref, kvw_ref, vb_ref, h_ref, q_ref, k_ref, v_ref, kv_ref, c_ref, log_ref
):
    length = lens[pl.program_id(0)]
    width = q_ref.shape[1]
    both = dot_nn(t_ref[...], kvw_ref[...])
    kv_ref[:, :width] = both[:, :width].astype(jnp.bfloat16)
    kv_ref[:, width:] = (both[:, width:] + vb_ref[1:2, :]).astype(jnp.bfloat16)
    for i in range(x_ref.shape[0] // BLOCK):
        rows = pl.ds(i * BLOCK, BLOCK)

        @pl.when(i * BLOCK < length)
        def _():
            normed, _, _ = norm_forward(x_ref[rows, :].astype(jnp.float32), g_ref[0:1, :], s_ref[0:1, :])
            h1 = normed.astype(jnp.bfloat16)
            h_ref[rows, :] = h1
            queries = (dot_nn(h1, w_ref[0]) + b_ref[0:1, :]).astype(jnp.bfloat16)
            q_ref[rows, :] = queries
            k_ref[rows, :] = dot_nn(h1, w_ref[1]).astype(jnp.bfloat16)
            v_ref[rows, :] = (dot_nn(h1, w_ref[2]) + b_ref[1:2, :]).astype(jnp.bfloat16)
            count = (i + 1) * BLOCK
            keys, values = k_ref[:count, :], v_ref[:count, :]
            scaled = queries * jnp.bfloat16(HEAD_DIM**-0.5)
            total = jnp.zeros((BLOCK, width), jnp.float32)
            logs = jnp.zeros((BLOCK, LANES), jnp.float32)
            lane = lax.broadcasted_iota(jnp.int32, logs.shape, 1)
            for head in range(width // HEAD_DIM):
                scores = mask_diagonal(dot_nt(pick_head(scaled, head), keys), 1)
                top = jnp.max(scores, axis=1, keepdims=True)
                weights = jnp.exp(scores - top)
                norm = jnp.sum(weights, axis=1, keepdims=True)
                total += dot_nn(weights.astype(jnp.bfloat16), pick_head(values, head)) * (1.0 / norm)
                logs = jnp.where(lane == head, top + jnp.log(norm), logs)
            log_ref[:, rows] = logs.T[: log_ref.shape[0], :]
            c_ref[rows, :] = total.astype(jnp.bfloat16)

        @pl.when(i * BLOCK >= length)
        def _():
            for ref in (h_ref, q_ref, k_ref, v_ref, c_ref):
                ref[rows, :] = jnp.zeros((BLOCK, ref.shape[1]), ref.dtype)
            log_ref[:, rows] = jnp.zeros((log_ref.shape[0], BLOCK), jnp.float32)


def front(lengths, units, text, gains, shifts, weights, bias, kv_w, cross_bias):
    rows, width = units.shape
    slots = lengths.shape[0]
    slot_rows = rows // slots
    cols = weights.shape[2]
    whole = lambda a: pl.BlockSpec(a.shape, lambda s, *_: (0,) * a.ndim)
    slot = lambda w: pl.BlockSpec((slot_rows, w), lambda s, *_: (s, 0))
    texts = lambda w: pl.BlockSpec((text.shape[0] // slots, w), lambda s, *_: (s, 0))
    logs = pl.BlockSpec((8, slot_rows), lambda s, *_: (0, s))
    shape = lambda w: jax.ShapeDtypeStruct((rows, w), jnp.bfloat16)
    far = lambda w: pltpu.HBM((rows, w), jnp.bfloat16)
    return pl.pallas_call(
        front_kernel,
        grid_spec=pltpu.PrefetchScalarGridSpec(
            num_scalar_prefetch=1,
            grid=(slots,),
            in_specs=[slot(width), texts(width)]
            + [whole(a) for a in (gains, shifts, weights, bias, kv_w, cross_bias)],
            out_specs=[slot(width), slot(cols), slot(cols), slot(cols), texts(2 * cols), slot(cols), logs],
        ),
        out_shape=[
            far(width),
            far(cols),
            far(cols),
            far(cols),
            jax.ShapeDtypeStruct((text.shape[0], 2 * cols), jnp.bfloat16),
            shape(cols),
            pltpu.HBM((8, rows), jnp.float32),
        ],
        compiler_params=pltpu.CompilerParams(vmem_limit_bytes=60 * MIB),
        cost_estimate=pl.CostEstimate(flops=20 * 10**9, bytes_accessed=16 * MIB, transcendentals=8 * MIB),
        name="front",
    )(lengths, units, text, gains, shifts, weights, bias, kv_w, cross_bias)


def back_kernel(
    lens, q_ref, k_ref, v_ref, dc_ref, c_ref, log_ref, h_ref, text_ref, dkv_ref, in_ref, out_ref, _g0, _g1,
    o_ref, g0_ref, g1_ref, b_ref, in_f32, out_f32, dk_acc, dv_acc, w_acc,
):
    in_f32[...] = in_ref[...].astype(jnp.float32)
    out_f32[...] = out_ref[...].astype(jnp.float32)

    @pl.when(pl.program_id(0) == 0)
    def _():
        w_acc[...] = jnp.zeros_like(w_acc)
        b_ref[...] = jnp.zeros_like(b_ref)
        kv_grad = dot_tn(text_ref[...], dkv_ref[...]).astype(jnp.bfloat16)
        half, both = g1_ref.shape[0], dkv_ref.shape[1]
        g1_ref[:, :both] = kv_grad[:half]
        g1_ref[:, both:] = kv_grad[half:]

    length = lens[pl.program_id(0)]
    slot_rows, width = q_ref.shape
    dk_acc[...] = jnp.zeros_like(dk_acc)
    dv_acc[...] = jnp.zeros_like(dv_acc)
    for i in range(slot_rows // BLOCK):
        rows = pl.ds(i * BLOCK, BLOCK)

        @pl.when(i * BLOCK < length)
        def _():
            count = (i + 1) * BLOCK
            keys, values = k_ref[:count, :], v_ref[:count, :]
            scaled = q_ref[rows, :] * jnp.bfloat16(HEAD_DIM**-0.5)
            grads = dc_ref[rows, :]
            total = jnp.zeros((BLOCK, width), jnp.float32)
            heads = lax.broadcasted_iota(jnp.int32, (8, width), 0)
            lanes = lax.broadcasted_iota(jnp.int32, (8, width), 1)
            inner = lax.dot_general(
                jnp.where((lanes >= heads * HEAD_DIM) & (lanes < (heads + 1) * HEAD_DIM), 1.0, 0.0),
                grads.astype(jnp.float32) * c_ref[rows, :].astype(jnp.float32),
                (((1,), (1,)), ((), ())),
                precision=EXACT,
                preferred_element_type=jnp.float32,
            )
            for head in range(width // HEAD_DIM):
                q_head, g_head = pick_head(scaled, head), pick_head(grads, head)
                scores = mask_diagonal(dot_nt(keys, q_head), 0)
                weights = jnp.exp(scores - log_ref[head : head + 1, rows])
                dv_acc[:count, :] += dot_nn(weights.astype(jnp.bfloat16), g_head)
                weight_grad = dot_nt(values, g_head)
                score_grad = (weights * (weight_grad - inner[head : head + 1, :])).astype(jnp.bfloat16)
                dk_acc[:count, :] += dot_nn(score_grad, q_head)
                total += dot_tn(score_grad, pick_head(keys, head))
            o_ref[rows, :width] = (total * HEAD_DIM**-0.5).astype(jnp.bfloat16)

        @pl.when(i * BLOCK >= length)
        def _():
            o_ref[rows, :width] = jnp.zeros((BLOCK, width), jnp.bfloat16)

    o_ref[:, width : 2 * width] = dk_acc[...].astype(jnp.bfloat16)
    o_ref[:, 2 * width :] = dv_acc[...].astype(jnp.bfloat16)
    for i in range(slot_rows // BLOCK):
        rows = pl.ds(i * BLOCK, BLOCK)

        @pl.when(i * BLOCK < length)
        def _():
            sums = column_sum(o_ref[rows, :].astype(jnp.float32))
            b_ref[0:1, :] += sums[:, :width]
            b_ref[1:2, :] += sums[:, 2 * width :]

    for first in range(0, h_ref.shape[1], BLOCK):
        w_acc[first : first + BLOCK, :] += dot_tn(h_ref[:, first : first + BLOCK], o_ref[...])

    @pl.when(pl.program_id(0) == pl.num_programs(0) - 1)
    def _():
        g0_ref[...] = w_acc[...].astype(jnp.bfloat16)


def back(lengths, queries, keys, values, grads, context, logs, rows_in, text, dkv, in_sum, out_sum, g0, g1):
    rows, cols = queries.shape
    width = rows_in.shape[1]
    slots = lengths.shape[0]
    bf, f32 = jnp.bfloat16, jnp.float32
    shape = jax.ShapeDtypeStruct
    slot = lambda a: pl.BlockSpec((a.shape[0] // slots, a.shape[1]), lambda s, *_: (s, 0))
    whole = lambda a: pl.BlockSpec(a.shape, lambda s, *_: (0, 0))
    hbm = pl.BlockSpec(memory_space=pl.ANY)
    half = text.shape[1] // 2
    return pl.pallas_call(
        back_kernel,
        grid_spec=pltpu.PrefetchScalarGridSpec(
            num_scalar_prefetch=1,
            grid=(slots,),
            in_specs=[slot(queries)] * 5
            + [pl.BlockSpec((8, rows // slots), lambda s, *_: (0, s))]
            + [slot(rows_in), whole(text), whole(dkv), slot(in_sum), slot(out_sum), hbm, hbm],
            out_specs=[
                pl.BlockSpec((rows // slots, 3 * cols), lambda s, *_: (s, 0)),
                pl.BlockSpec((width, 3 * cols), lambda s, *_: (0, 0)),
                pl.BlockSpec((half, width), lambda s, *_: (1, 0)),
                pl.BlockSpec((2, cols), lambda s, *_: (0, 0)),
                slot(in_sum),
                slot(out_sum),
            ],
            scratch_shapes=[pltpu.VMEM((rows // slots, cols), f32)] * 2 + [pltpu.VMEM((width, 3 * cols), f32)],
        ),
        out_shape=[
            shape((rows, 3 * cols), bf),
            pltpu.HBM(g0.shape, bf),
            pltpu.HBM(g1.shape, bf),
            shape((2, cols), f32),
            shape(in_sum.shape, f32),
            shape(out_sum.shape, f32),
        ],
        input_output_aliases={12: 1, 13: 2},
        compiler_params=pltpu.CompilerParams(vmem_limit_bytes=60 * MIB),
        cost_estimate=pl.CostEstimate(flops=30 * 10**9, bytes_accessed=40 * MIB, transcendentals=8 * MIB),
        name="back",
    )(lengths, queries, keys, values, grads, context, logs, rows_in, text, dkv, in_sum, out_sum, g0, g1)


def place():
    index = lax.axis_index("narrow")
    core = index + 1 - 2 * (index % 2)
    return index, core, (index + 2) % NARROW, (core + 2) % NARROW


def greet(*wide_peers):
    _, core, cross, _ = place()
    barrier = pltpu.get_barrier_semaphore()
    for peer in (core, cross):
        pl.semaphore_signal(barrier, inc=1, device_id={"narrow": peer}, device_id_type=MESH)
    for peer in wide_peers:
        pl.semaphore_signal(barrier, inc=1, device_id={"wide": peer}, device_id_type=MESH)
    pl.semaphore_wait(barrier, 2 + len(wide_peers))


def remote(source, target, sems, kind, step, peer, axis="narrow"):
    return pltpu.make_async_remote_copy(
        src_ref=source,
        dst_ref=target,
        send_sem=sems.at[0, kind, step],
        recv_sem=sems.at[1, kind, step],
        device_id={axis: peer},
        device_id_type=MESH,
    )


def ring_place(count):
    wide = lax.axis_index("wide")
    odd, half = wide % 2, wide // 2
    spot = odd * (half + 1) + (1 - odd) * ((count - half) % count)

    def at(where):
        high = ((where + count - 1) % count) // (count // 2)
        return (1 - high) * (2 * where - 1) + high * ((2 * (count - where)) % (2 * count))

    return spot, at((spot + 1) % count), at((spot + count - 1) % count)


class Ring:
    UNITS = 4

    def __init__(self, count, sources, outs, view, arrived, held, sems, fetch_sems, keep_sems):
        self.count, self.sources, self.outs, self.view = count, sources, outs, view
        self.arrived, self.held, self.sems = arrived, held, sems
        self.fetch_sems, self.keep_sems = fetch_sems, keep_sems
        spot, following, previous = ring_place(count)
        self.spots = (spot, (count - spot) % count)
        self.peers = (following, previous)

    def block(self, refs, unit, back_by):
        shard = (self.spots[unit // 2] + 2 * self.count - back_by) % self.count
        return self.view(refs[unit // 2], unit // 2, unit % 2, shard)

    def send(self, source, target, kind, unit, step):
        return remote(source, target, self.sems, kind * self.UNITS + unit, step, self.peers[unit // 2], "wide")

    def sum_copy(self, unit, step, first=False):
        source = self.block(self.sources, unit, 0) if first else self.arrived.at[unit, jnp.maximum(step - 1, 0)]
        return self.send(source, self.arrived.at[unit, step], 0, unit, step)

    def fetch(self, unit, step):
        slot = step % 2
        return pltpu.make_async_copy(
            self.block(self.sources, unit, step + 1), self.held.at[unit, slot], self.fetch_sems.at[unit, slot]
        )

    def keep(self, unit):
        return pltpu.make_async_copy(
            self.arrived.at[unit, self.count - 2], self.block(self.outs, unit, self.count - 1), self.keep_sems.at[unit]
        )

    def spread_copy(self, unit, step, first=False):
        target = self.block(self.outs, unit, self.count - 1 + step)
        source = self.arrived.at[unit, self.count - 2] if first else target
        return self.send(source, target, 1, unit, step)

    def start(self):
        for unit in range(self.UNITS):
            self.sum_copy(unit, 0, True).start()
            self.fetch(unit, 0).start()
            self.fetch(unit, 1).start()

    def serve(self, turn, unit):
        last = self.count - 2

        @pl.when(turn <= last)
        def _():
            self.sum_copy(unit, turn).wait_recv()
            self.fetch(unit, turn).wait()
            total = self.held[unit, turn % 2].astype(jnp.float32) + self.arrived[unit, turn].astype(jnp.float32)
            self.arrived[unit, turn] = total.astype(jnp.bfloat16)

            @pl.when(turn < last)
            def _():
                self.sum_copy(unit, turn + 1).start()

            @pl.when(turn < last - 1)
            def _():
                self.fetch(unit, turn + 2).start()

            @pl.when(turn == last)
            def _():
                self.spread_copy(unit, 0, True).start()
                self.keep(unit).start()

        @pl.when((turn > last) & (turn <= 2 * last + 1))
        def _():
            step = turn - last - 1
            self.spread_copy(unit, step).wait_recv()

            @pl.when(step < last)
            def _():
                self.spread_copy(unit, step + 1).start()

    def finish(self):
        for unit in range(self.UNITS):
            self.keep(unit).wait()

        def body(step, carry):
            for unit in range(self.UNITS):
                self.sum_copy(unit, step).wait_send()
                self.spread_copy(unit, step).wait_send()
            return carry

        lax.fori_loop(0, self.count - 1, body, 0)


def ring_scratch(count, block):
    return [
        pltpu.VMEM((Ring.UNITS, count - 1) + block, jnp.bfloat16),
        pltpu.VMEM((Ring.UNITS, 2) + block, jnp.bfloat16),
        pltpu.SemaphoreType.DMA((2, 2 * Ring.UNITS, count - 1)),
        pltpu.SemaphoreType.DMA((Ring.UNITS, 2)),
        pltpu.SemaphoreType.DMA((Ring.UNITS,)),
    ]


def own_copy(whole, own, sem):
    size = own.shape[0]
    first = pl.multiple_of(lax.axis_index("narrow") * size, size)
    return pltpu.make_async_copy(whole.at[pl.ds(first, size), :], own, sem)


def moves(sources, targets, sems):
    pairs = list(zip(sources, targets, strict=True))
    return [pltpu.make_async_copy(a, b, sems.at[slot]) for slot, (a, b) in enumerate(pairs)]


class Hop:
    KINDS = 6

    def __init__(self, part, from_core, from_cross, full, sems, chunk):
        self.part, self.from_core, self.from_cross = part, from_core, from_cross
        self.full, self.sems, self.chunk = full, sems, chunk
        self.own = part.shape[0] // NARROW
        self.index, self.core, self.cross, self.diagonal = place()

    def rows(self, owner, step):
        return pl.ds(pl.multiple_of(owner * self.own + step * self.chunk, self.chunk), self.chunk)

    def own_rows(self, step):
        return pl.ds(pl.multiple_of(step * self.chunk, self.chunk), self.chunk)

    def core_copies(self, step):
        return [
            remote(self.part.at[self.rows(owner, step)], self.from_core.at[step, slot], self.sems, slot, step, self.core)
            for slot, owner in enumerate((self.core, self.diagonal))
        ]

    def cross_copy(self, step):
        return remote(
            self.part.at[self.rows(self.cross, step)], self.from_cross.at[step], self.sems, 2, step, self.cross
        )

    def gather_copy(self, step, kind):
        owner = self.cross if kind == 5 else self.index
        rows = self.full.at[self.rows(owner, step)]
        return remote(rows, rows, self.sems, kind, step, self.cross if kind == 3 else self.core)

    def send_core(self, step):
        for copy in self.core_copies(step):
            copy.start()

    def send_cross(self, step):
        for copy in self.core_copies(step):
            copy.wait_recv()
        total = self.part[self.rows(self.cross, step), :].astype(jnp.float32)
        total += self.from_core[step, 1].astype(jnp.float32)
        self.part[self.rows(self.cross, step), :] = total.astype(jnp.bfloat16)
        self.cross_copy(step).start()

    def result(self, step):
        total = self.part[self.rows(self.index, step), :].astype(jnp.float32)
        total += self.from_core[step, 0].astype(jnp.float32)
        self.cross_copy(step).wait_recv()
        return total + self.from_cross[step].astype(jnp.float32)

    def send_gather(self, step, values):
        self.full[self.rows(self.index, step), :] = values
        self.gather_copy(step, 3).start()
        self.gather_copy(step, 4).start()

    def forward(self, step):
        self.gather_copy(step, 3).wait_recv()
        self.gather_copy(step, 5).start()

    def gathered(self, step):
        self.gather_copy(step, 4).wait_recv()
        self.gather_copy(step, 5).wait_recv()

    def sent(self, step):
        for copy in self.core_copies(step):
            copy.wait_send()
        self.cross_copy(step).wait_send()

    def finish(self, step, gather=True, parts=True):
        if parts:
            self.sent(step)
        if gather:
            for kind in (3, 4, 5):
                self.gather_copy(step, kind).wait_send()

    def take(self, ref, step):
        return jnp.concatenate([ref[self.rows(owner, step), :] for owner in range(NARROW)], axis=0)

    def put(self, ref, step, values):
        for owner in range(NARROW):
            ref[self.rows(owner, step), :] = values[owner * self.chunk : (owner + 1) * self.chunk]


def hop_scratch(own, chunk, width):
    steps = own // chunk
    return [
        pltpu.VMEM((steps, 2, chunk, width), jnp.bfloat16),
        pltpu.VMEM((steps, chunk, width), jnp.bfloat16),
        pltpu.SemaphoreType.DMA((2, Hop.KINDS, steps)),
    ]


def stages(steps, work, ring=None, extra=None, ticks=0):
    ticks = max(ticks, steps + max(delay for delay, _ in work))
    per_tick = 0 if ring is None else -(-2 * (ring.count - 1) // ticks)

    def body(tick, carry):
        for number, (delay, stage) in enumerate(work):
            step = tick - delay

            @pl.when((step >= 0) & (step < steps))
            def _():
                stage(step)

            unit = (number + 1) * Ring.UNITS // len(work) - 1
            if per_tick and unit != number * Ring.UNITS // len(work) - 1:
                if per_tick == 1:
                    ring.serve(tick, unit)
                else:
                    lax.fori_loop(0, per_tick, lambda i, c: (ring.serve(tick * per_tick + i, unit), c)[1], 0)
        if extra is not None:
            extra(tick)
        return carry

    lax.fori_loop(0, ticks, body, 0)


def middle_kernel(
    all_units, out_grad, far_in, far_out, far_so, far_cq, far_co, lens, text_lens,
    c1, kv2, gains, shifts, biases, bias, b_in,
    ffn_part, third, in_g, out_g, far_h2, far_q2, far_c2, far_x1, far_x2, in_bias_g,
    h2, q2, c2, x1, x2, leave_sem, units, own_sem, so_w, cq_w, co_w, small_sem, w_in, w_out, weight_sem, grads_in, grads_sem, give, give_sem, in_acc, out_acc,
    part, h3, core1, fromx1, sem1, core2, fromx2, sem2,
):
    steps, chunk, width = fromx1.shape
    cols = q2.shape[1]
    slots = text_lens.shape[0]
    texts = kv2.shape[0] // slots
    slot_rows = h2.shape[0] // slots
    hidden_count = w_out.shape[0]
    near = [
        pltpu.make_async_copy(source, target, small_sem.at[slot])
        for slot, (source, target) in enumerate(((far_so, so_w), (far_cq, cq_w), (far_co, co_w)))
    ]
    for fetch in near:
        fetch.start()
    fetches = [
        own_copy(all_units, units, own_sem),
        pltpu.make_async_copy(far_in, w_in, weight_sem.at[0]),
        pltpu.make_async_copy(far_out, w_out, weight_sem.at[1]),
    ]
    for fetch in fetches:
        fetch.start()
    greet()
    one = Hop(part, core1, fromx1, h2, sem1, chunk)
    two = Hop(part, core2, fromx2, h3, sem2, chunk)
    scale = jnp.bfloat16(HEAD_DIM**-0.5)
    in_acc[...] = jnp.zeros_like(in_acc)
    out_acc[...] = jnp.zeros_like(out_acc)
    in_bias_g[...] = jnp.zeros_like(in_bias_g)
    for fetch in near:
        fetch.wait()

    def grad_copies(step):
        slot = step % 2
        return [
            pltpu.make_async_copy(
                out_grad.at[one.rows(owner, step), :],
                grads_in.at[slot, pl.ds(owner * chunk, chunk), :],
                grads_sem.at[slot, owner],
            )
            for owner in range(NARROW)
        ]

    def give_copies(step, kind):
        slot = step % 2
        return [
            pltpu.make_async_copy(
                give.at[kind, slot, pl.ds(owner * chunk, chunk), :],
                (ffn_part, third)[kind].at[one.rows(owner, step), :],
                give_sem.at[kind, slot, owner],
            )
            for owner in range(NARROW)
        ]

    def project(step):
        one.put(part, step, dot_nn(one.take(c1, step), so_w[...]).astype(jnp.bfloat16))
        one.send_core(step)

    def norm_one(step):
        @pl.when(step == 0)
        def _():
            fetches[0].wait()

        rows = one.own_rows(step)
        resid = units[rows, :].astype(jnp.float32) + one.result(step) + biases[0:1, :]
        x1[rows, :] = resid
        one.send_gather(step, norm_forward(resid, gains[1:2, :], shifts[1:2, :])[0].astype(jnp.bfloat16))

    def cross(step):
        one.gathered(step)
        queries = (dot_nn(one.take(h2, step), cq_w[...]) + bias[0:1, :]).astype(jnp.bfloat16)
        one.put(q2, step, queries)
        scaled = queries * scale
        count = queries.shape[0] // slots
        place_of = lax.broadcasted_iota(jnp.int32, (count * (cols // HEAD_DIM), texts), 1)
        context = []
        for slot in range(slots):
            mine = scaled[slot * count : (slot + 1) * count]
            keys = kv2[slot * texts : (slot + 1) * texts, :cols]
            values = kv2[slot * texts : (slot + 1) * texts, cols:]
            heads = range(cols // HEAD_DIM)
            scores = dot_nt(jnp.concatenate([pick_head(mine, head) for head in heads], axis=0), keys)
            scores = jnp.where(place_of < text_lens[slot], scores, MASKED_SCORE)
            weights = jnp.exp(scores - jnp.max(scores, axis=1, keepdims=True))
            norm = jnp.sum(weights, axis=1, keepdims=True)
            mixed = dot_nn(weights.astype(jnp.bfloat16), values) * (1.0 / norm)
            total = jnp.zeros((count, cols), jnp.float32)
            for head in heads:
                total += pick_head(mixed[head * count : (head + 1) * count], head)
            context.append(total.astype(jnp.bfloat16))
        context = jnp.concatenate(context, axis=0)
        one.put(c2, step, context)
        one.sent(step)
        two.put(part, step, dot_nn(context, co_w[...]).astype(jnp.bfloat16))
        two.send_core(step)

    def norm_two(step):
        rows = one.own_rows(step)
        resid = x1[rows, :] + two.result(step) + biases[1:2, :]
        x2[rows, :] = resid
        two.send_gather(step, norm_forward(resid, gains[2:3, :], shifts[2:3, :])[0].astype(jnp.bfloat16))

    def forward_two(step):
        two.forward(step)
        for copy in grad_copies(step):
            copy.start()

    def ffn(step):
        @pl.when(step == 0)
        def _():
            fetches[1].wait()
            fetches[2].wait()

        two.gathered(step)
        for copy in grad_copies(step):
            copy.wait()
        rows = two.take(h3, step)
        place_in = lax.broadcasted_iota(jnp.int32, (chunk, width), 0) + step * chunk
        grads = []
        for owner in range(NARROW):
            first = owner * two.own
            valid = place_in < lens[first // slot_rows] - first % slot_rows
            values = grads_in[step % 2, owner * chunk : (owner + 1) * chunk, :]
            grads.append(jnp.where(valid, values.astype(jnp.float32), 0.0).astype(jnp.bfloat16))
        grads = jnp.concatenate(grads, axis=0)
        out = jnp.zeros(rows.shape, jnp.float32)
        back_out = jnp.zeros(rows.shape, jnp.float32)
        for begin in range(0, hidden_count, HIDDEN):
            some = slice(begin, begin + HIDDEN)
            pre = dot_nn(rows, w_in[:, some]) + b_in[:, some]
            cdf = 0.5 + 0.5 * lax.erf(pre * (0.5**0.5))
            pdf = jnp.exp(-0.5 * pre * pre) * 0.3989422804014327
            hidden = (pre * cdf).astype(jnp.bfloat16)
            pre_low = ((cdf + pre * pdf) * dot_nt(grads, w_out[some, :])).astype(jnp.bfloat16)
            in_bias_g[:, some] += column_sum(pre_low.astype(jnp.float32))
            out += dot_nn(hidden, w_out[some, :])
            back_out += dot_nt(pre_low, w_in[:, some])
            out_acc[some, :] += dot_tn(hidden, grads)
            side, place_at = divmod(begin, width)
            in_acc[side * width : (side + 1) * width, place_at : place_at + HIDDEN] += dot_tn(rows, pre_low)

        @pl.when(step >= 2)
        def _():
            for kind in range(2):
                for copy in give_copies(step - 2, kind):
                    copy.wait()

        give[0, step % 2] = out.astype(jnp.bfloat16)
        give[1, step % 2] = back_out.astype(jnp.bfloat16)
        for kind in range(2):
            for copy in give_copies(step, kind):
                copy.start()

    stages(
        steps,
        [
            (0, project), (1, one.send_cross), (2, norm_one), (3, one.forward), (4, cross),
            (5, two.send_cross), (6, norm_two), (7, forward_two), (8, ffn),
        ],
    )

    def finish(step, carry):
        one.finish(step, True, False)
        two.finish(step)
        return carry

    lax.fori_loop(0, steps, finish, 0)
    leaving = moves((h2, q2, c2, x1, x2), (far_h2, far_q2, far_c2, far_x1, far_x2), leave_sem)
    for copy in leaving:
        copy.start()
    part[...] = out_acc[...].astype(jnp.bfloat16)
    results = [pltpu.make_async_copy(part, out_g, weight_sem.at[0])]
    results[0].start()
    h3[...] = in_acc[...].astype(jnp.bfloat16)
    for side in range(hidden_count // width):
        here = pl.ds(side * width, width)
        results.append(pltpu.make_async_copy(h3.at[here, :], in_g.at[:, here], weight_sem.at[1 + side]))
        results[-1].start()
    for step in (steps - 2, steps - 1):
        for kind in range(2):
            for copy in give_copies(step, kind):
                copy.wait()
    for copy in results + leaving:
        copy.wait()


def middle(units, out_grad, w_in, w_out, so_w, cq_w, co_w, lens, text_lens, c1, kv2, gains, shifts, biases, bias, b_in):
    rows, cols = c1.shape
    own, width = rows // NARROW, units.shape[1]
    hidden_count = w_out.shape[0]
    chunk = own // STEPS
    bf, f32 = jnp.bfloat16, jnp.float32
    shape = jax.ShapeDtypeStruct
    vmem = pl.BlockSpec(memory_space=pltpu.VMEM)
    hbm = pl.BlockSpec(memory_space=pl.ANY)
    hop = hop_scratch(own, chunk, width)
    dma = pltpu.SemaphoreType.DMA
    return pl.pallas_call(
        middle_kernel,
        in_specs=[hbm] * 7 + [pl.BlockSpec(memory_space=pltpu.SMEM)] * 2 + [vmem] * 7,
        out_specs=[hbm] * 9 + [vmem],
        out_shape=[
            pltpu.HBM((rows, width), bf),
            pltpu.HBM((rows, width), bf),
            pltpu.HBM((width, hidden_count), bf),
            pltpu.HBM((hidden_count, width), bf),
            pltpu.HBM((rows, width), bf),
            pltpu.HBM((rows, cols), bf),
            pltpu.HBM((rows, cols), bf),
            pltpu.HBM((own, width), f32),
            pltpu.HBM((own, width), f32),
            shape((1, hidden_count), f32),
        ],
        scratch_shapes=[
            pltpu.VMEM((rows, width), bf),
            pltpu.VMEM((rows, cols), bf),
            pltpu.VMEM((rows, cols), bf),
            pltpu.VMEM((own, width), f32),
            pltpu.VMEM((own, width), f32),
            dma((5,)),
            pltpu.VMEM((own, width), bf),
            dma,
            pltpu.VMEM(so_w.shape, bf),
            pltpu.VMEM(cq_w.shape, bf),
            pltpu.VMEM(co_w.shape, bf),
            dma((3,)),
            pltpu.VMEM((width, hidden_count), bf),
            pltpu.VMEM((hidden_count, width), bf),
            dma((1 + hidden_count // width,)),
            pltpu.VMEM((2, NARROW * chunk, width), bf),
            dma((2, NARROW)),
            pltpu.VMEM((2, 2, NARROW * chunk, width), bf),
            dma((2, 2, NARROW)),
            pltpu.VMEM((hidden_count, width), f32),
            pltpu.VMEM((hidden_count, width), f32),
            pltpu.VMEM((rows, width), bf),
            pltpu.VMEM((rows, width), bf),
        ]
        + hop
        + hop,
        compiler_params=pltpu.CompilerParams(collective_id=0, has_side_effects=True, vmem_limit_bytes=60 * MIB),
        cost_estimate=pl.CostEstimate(flops=100 * 10**9, bytes_accessed=48 * MIB, transcendentals=8 * MIB),
        name="middle",
    )(
        units, out_grad, w_in, w_out, so_w, cq_w, co_w, lens, text_lens, c1, kv2, gains, shifts, biases, bias,
        b_in.reshape(1, -1),
    )


class FarHop(Hop):
    def fetch(self, mine, theirs, sems):
        self.mine, self.theirs = mine, theirs
        rows = lambda owner: pl.ds(pl.multiple_of(owner * self.own, self.own), self.own)
        self.fetches = [
            pltpu.make_async_copy(self.part.at[rows(owner)], ref, sems.at[slot])
            for slot, (owner, ref) in enumerate(((self.index, mine), (self.cross, theirs)))
        ]
        for copy in self.fetches:
            copy.start()

    def fetched(self):
        for copy in self.fetches:
            copy.wait()

    def cross_copy(self, step):
        return remote(
            self.theirs.at[self.own_rows(step)], self.from_cross.at[step], self.sems, 2, step, self.cross
        )

    def send_cross(self, step):
        for copy in self.core_copies(step):
            copy.wait_recv()
        total = self.theirs[self.own_rows(step), :].astype(jnp.float32)
        total += self.from_core[step, 1].astype(jnp.float32)
        self.theirs[self.own_rows(step), :] = total.astype(jnp.bfloat16)
        self.cross_copy(step).start()

    def result(self, step):
        total = self.mine[self.own_rows(step), :].astype(jnp.float32)
        total += self.from_core[step, 0].astype(jnp.float32)
        self.cross_copy(step).wait_recv()
        return total + self.from_cross[step].astype(jnp.float32)


def left_here(lens, own, rows):
    first = lax.axis_index("narrow") * own
    slot_rows = rows // lens.shape[0]
    return lens[first // slot_rows] - first % slot_rows


def row_of(step, chunk, width):
    return lax.broadcasted_iota(jnp.int32, (chunk, width), 0) + step * chunk


def turn_kernel(
    third, ffn_part, in_g, out_g, out_grad, lens, text_lens,
    far_x1, far_x2, far_h2, far_q2, far_c2, far_kv2, far_c1, gains, biases, far_co, far_cq, far_so,
    in_sum, out_sum, g0, g1, y, dx1, dc1, dkv, bias_g, stats,
    x1, x2, h2, q2, c2, kv2, c1, co_w, cq_w, so_w, arrive_sem, cq_g, give_sem, e_own, own_sem, mine3, theirs3, core3, fromx3, sem3, mine4, theirs4, core4, fromx4, sem4,
    part5, core5, fromx5, sem5, full3, full5, co_acc, cq_acc, so_acc, dkv_acc, fetch_sem,
    *ring_refs, count,
):
    steps, chunk, width = fromx5.shape
    cols = q2.shape[1]
    slots = bias_g.shape[0]
    texts = kv2.shape[0] // slots

    def ring_view(ref, way, half, shard):
        high = width // count
        if way == 0:
            return ref.at[pl.ds(pl.multiple_of(shard * high, high), high), pl.ds(half * width, width)]
        return ref.at[pl.ds(pl.multiple_of(shard * 2 * high + half * high, high), high), :]

    ring = Ring(count, (in_g, out_g), (in_sum, out_sum), ring_view, *ring_refs)
    fetch = own_copy(out_grad, e_own, own_sem)
    fetch.start()
    greet(*ring.peers)
    ring.start()
    three = FarHop(third, core3, fromx3, full3, sem3, chunk)
    four = FarHop(ffn_part, core4, fromx4, None, sem4, chunk)
    five = Hop(part5, core5, fromx5, full5, sem5, chunk)
    arriving = moves(
        (far_x2, far_x1, far_h2, far_q2, far_c2, far_kv2, far_c1, far_co, far_cq, far_so),
        (x2, x1, h2, q2, c2, kv2, c1, co_w, cq_w, so_w),
        arrive_sem,
    )
    three.fetch(mine3, theirs3, fetch_sem.at[0])
    for copy in arriving:
        copy.start()
    four.fetch(mine4, theirs4, fetch_sem.at[1])

    def start(step, carry):
        three.send_core(step)
        four.send_core(step)
        return carry

    lax.fori_loop(0, steps, start, 0)
    for ref in (co_acc, cq_acc, so_acc, dkv_acc, bias_g, stats):
        ref[...] = jnp.zeros_like(ref)
    three.fetched()
    four.fetched()
    fetch.wait()
    for copy in arriving:
        copy.wait()
    valid_rows = left_here(lens, x1.shape[0], h2.shape[0])
    scale = jnp.bfloat16(HEAD_DIM**-0.5)

    def norm_three(step):
        rows = three.own_rows(step)
        grad_in = three.result(step)
        _, normed, inv_std = norm_forward(x2[rows, :], gains[2:3, :], gains[2:3, :])
        stats[0:1, :] += column_sum(grad_in * normed)
        stats[1:2, :] += column_sum(grad_in)
        above = jnp.where(row_of(step, chunk, width) < valid_rows, e_own[rows, :].astype(jnp.float32), 0.0)
        total = above + norm_backward(grad_in, normed, inv_std, gains[2:3, :])
        stats[2:3, :] += column_sum(above)
        stats[3:4, :] += column_sum(total)
        dx1[rows, :] = total
        three.send_gather(step, total.astype(jnp.bfloat16))

    def cross(step):
        three.gathered(step)
        grads = three.take(full3, step)
        co_acc[...] += dot_tn(three.take(c2, step), grads)
        context = dot_nt(grads, co_w[...]).astype(jnp.bfloat16)
        queries = three.take(q2, step) * scale
        count = queries.shape[0] // slots
        place_of = lax.broadcasted_iota(jnp.int32, (texts, count), 0)
        q_grad = []
        for slot in range(slots):
            rows = slice(slot * count, (slot + 1) * count)
            texts_here = slice(slot * texts, (slot + 1) * texts)
            keys, values = kv2[texts_here, :cols], kv2[texts_here, cols:]
            total = jnp.zeros((count, cols), jnp.float32)
            for head in range(cols // HEAD_DIM):
                q_head, g_head = pick_head(queries[rows], head), pick_head(context[rows], head)
                scores = jnp.where(place_of < text_lens[slot], dot_nt(keys, q_head), MASKED_SCORE)
                weights = jnp.exp(scores - jnp.max(scores, axis=0, keepdims=True))
                weights = weights * (1.0 / jnp.sum(weights, axis=0, keepdims=True))
                dkv_acc[texts_here, cols:] += dot_nn(weights.astype(jnp.bfloat16), g_head)
                weight_grad = dot_nt(values, g_head)
                inner = jnp.sum(weights * weight_grad, axis=0, keepdims=True)
                score_grad = (weights * (weight_grad - inner)).astype(jnp.bfloat16)
                dkv_acc[texts_here, :cols] += dot_nn(score_grad, q_head)
                total += dot_tn(score_grad, pick_head(keys, head))
            q_grad.append((total * HEAD_DIM**-0.5).astype(jnp.bfloat16))
        q_grad = jnp.concatenate(q_grad, axis=0)
        five.put(part5, step, dot_nt(q_grad, cq_w[...]).astype(jnp.bfloat16))
        five.send_core(step)
        bias_g[0:1, :] += column_sum(q_grad.astype(jnp.float32))
        cq_acc[...] += dot_tn(five.take(h2, step), q_grad)

    def norm_two(step):
        rows = five.own_rows(step)
        grad_in = five.result(step)
        _, normed, inv_std = norm_forward(x1[rows, :], gains[1:2, :], gains[1:2, :])
        stats[4:5, :] += column_sum(grad_in * normed)
        stats[5:6, :] += column_sum(grad_in)
        total = dx1[rows, :] + norm_backward(grad_in, normed, inv_std, gains[1:2, :])
        stats[6:7, :] += column_sum(total)
        dx1[rows, :] = total
        five.send_gather(step, total.astype(jnp.bfloat16))

    def last(step):
        five.gathered(step)
        grads = five.take(full5, step)
        dc1_rows = dot_nt(grads, so_w[...]).astype(jnp.bfloat16)
        five.put(dc1, step, dc1_rows)
        so_acc[...] += dot_tn(five.take(c1, step), grads)

    def output(step):
        rows = four.own_rows(step)
        total = x2[rows, :] + four.result(step) + biases[2:3, :]
        y[rows, :] = jnp.where(row_of(step, chunk, width) < valid_rows, total, 0.0).astype(jnp.bfloat16)

    half = steps // 2
    late = steps + 2

    def side(tick):
        for begin, first in ((0, 0), (late, half)):
            for ahead, work in ((1, output), (0, four.send_cross)):
                step = tick - begin - ahead

                @pl.when((step >= 0) & (step < half))
                def _():
                    work(first + step)

    stages(
        steps,
        list(
            enumerate(
                [
                    three.send_cross, norm_three, three.forward, cross,
                    five.send_cross, norm_two, five.forward, last,
                ]
            )
        ),
        ring,
        side,
        late + half + 1,
    )
    dkv[...] = dkv_acc[...].astype(jnp.bfloat16)
    bias_g[1:2, :] = column_sum(dkv[:, cols:].astype(jnp.float32))
    mine4[:cols, :] = co_acc[...].astype(jnp.bfloat16)
    cq_g[...] = cq_acc[...].astype(jnp.bfloat16)
    mine4[cols : 2 * cols, :] = so_acc[...].astype(jnp.bfloat16)
    gives = [
        pltpu.make_async_copy(cq_g, g0.at[:, pl.ds(width - cols, cols)], give_sem.at[0]),
        pltpu.make_async_copy(mine4.at[pl.ds(0, 2 * cols), :], g1.at[pl.ds(0, 2 * cols), :], give_sem.at[1]),
    ]
    for give in gives:
        give.start()

    def finish(step, carry):
        three.finish(step)
        four.finish(step, False)
        five.finish(step)
        return carry

    lax.fori_loop(0, steps, finish, 0)
    ring.finish()
    for give in gives:
        give.wait()


def turn(
    count, third, ffn_part, in_g, out_g, out_grad, lens, text_lens,
    x1, x2, h2, q2, c2, kv2, c1, gains, biases, co_w, cq_w, so_w,
):
    rows, cols = c1.shape
    own, width = x1.shape
    chunk = own // STEPS
    bf, f32 = jnp.bfloat16, jnp.float32
    shape = jax.ShapeDtypeStruct
    vmem = pl.BlockSpec(memory_space=pltpu.VMEM)
    hbm = pl.BlockSpec(memory_space=pl.ANY)
    hop = hop_scratch(own, chunk, width)
    far = [pltpu.VMEM((own, width), bf)] * 2 + hop
    return pl.pallas_call(
        functools.partial(turn_kernel, count=count),
        in_specs=[hbm] * 5 + [pl.BlockSpec(memory_space=pltpu.SMEM)] * 2 + [hbm] * 7 + [vmem] * 2 + [hbm] * 3,
        out_specs=[hbm] * 4 + [vmem] * 6,
        out_shape=[
            pltpu.HBM(in_g.shape, bf),
            pltpu.HBM(out_g.shape, bf),
            pltpu.HBM((width, width), bf),
            pltpu.HBM((width, width), bf),
            shape((own, width), bf),
            shape((own, width), f32),
            shape((rows, cols), bf),
            shape(kv2.shape, bf),
            shape((2, cols), f32),
            shape((8, width), f32),
        ],
        scratch_shapes=[pltpu.VMEM(a.shape, a.dtype) for a in (x1, x2, h2, q2, c2, kv2, c1, co_w, cq_w, so_w)]
        + [
            pltpu.SemaphoreType.DMA((10,)),
            pltpu.VMEM((width, cols), bf),
            pltpu.SemaphoreType.DMA((2,)),
            pltpu.VMEM((own, width), bf),
            pltpu.SemaphoreType.DMA,
        ]
        + far
        + far
        + [pltpu.VMEM((rows, width), bf)]
        + hop
        + [pltpu.VMEM((rows, width), bf)] * 2
        + [
            pltpu.VMEM((cols, width), f32),
            pltpu.VMEM((width, cols), f32),
            pltpu.VMEM((cols, width), f32),
            pltpu.VMEM(kv2.shape, f32),
            pltpu.SemaphoreType.DMA((2, 2)),
        ]
        + ring_scratch(count, (width // count, width)),
        compiler_params=pltpu.CompilerParams(collective_id=1, has_side_effects=True, vmem_limit_bytes=60 * MIB),
        cost_estimate=pl.CostEstimate(flops=100 * 10**9, bytes_accessed=24 * MIB, transcendentals=4 * MIB),
        name="turn",
    )(
        third, ffn_part, in_g, out_g, out_grad, lens, text_lens,
        x1, x2, h2, q2, c2, kv2, c1, gains, biases, co_w, cq_w, so_w,
    )


SMALL = 16
NORM_ROWS = 9


class Small:
    def __init__(self, count, block, near, far, sems):
        self.count, self.mine, self.near, self.far, self.sems = count, block, near, far, sems
        self.index, self.core, self.cross, _ = place()
        self.spot, *self.peers = ring_place(count)

    def near_copy(self, kind):
        owner = self.cross if kind == 2 else self.index
        return remote(self.near.at[owner], self.near.at[owner], self.sems, 0, kind, (self.cross, self.core, self.core)[kind])

    def far_copy(self, way, step):
        block = self.far.at[(self.spot + (2 * way - 1) * step + self.count) % self.count]
        return remote(block, block, self.sems, 1 + way, step, self.peers[way], "wide")

    def begin(self):
        self.near[self.index] = self.mine[...]
        self.near_copy(0).start()
        self.near_copy(1).start()

    def forward(self):
        self.near_copy(0).wait_recv()
        self.near_copy(2).start()

    def launch(self):
        self.near_copy(1).wait_recv()
        self.near_copy(2).wait_recv()
        both = self.near[0]
        for owner in range(1, NARROW):
            both += self.near[owner]
        row = lax.broadcasted_iota(jnp.int32, both.shape, 0)
        self.far[self.spot] = jnp.where(row < SMALL - NORM_ROWS, self.mine[...], both)
        self.far_copy(0, 0).start()
        self.far_copy(1, 0).start()

    def rotate(self, step):
        for way in range(2):
            steps = self.count // 2 - way

            @pl.when(step < steps)
            def _():
                self.far_copy(way, step).wait_recv()

            @pl.when(step < steps - 1)
            def _():
                self.far_copy(way, step + 1).start()

    def finish(self, out):
        for kind in range(3):
            self.near_copy(kind).wait_send()

        for way in range(2):

            def body(step, carry):
                self.far_copy(way, step).wait_send()
                return carry

            lax.fori_loop(0, self.count // 2 - way, body, 0)
        out[...] = jnp.zeros_like(out)

        def add(spot, carry):
            out[...] += self.far[spot]
            return carry

        lax.fori_loop(0, self.count, add, 0)


def last_kernel(
    g0, g1, all_units, far_dqkv, far_dkv, far_dx1, far_qkv, far_kv, self_b, cross_b, ffn_b, stats, gains,
    sum0, sum1, units_g, text_g, small_sum,
    dqkv, dkv, dx1, qkv_w, kv_w, arrive_sem, units, own_sem, part6, core6, fromx6, sem6, part7, core7, fromx7, sem7,
    block, near, far, small_sem, *ring_refs, count,
):
    steps, chunk, width = fromx6.shape
    text_steps = fromx7.shape[0]

    def ring_view(ref, way, half, shard):
        high = width // count
        return ref.at[pl.ds(pl.multiple_of(shard * high, high), high), pl.ds(half * (width // 2), width // 2)]

    ring = Ring(count, (g0, g1), (sum0, sum1), ring_view, *ring_refs)
    small = Small(count, block, near, far, small_sem)
    fetch = own_copy(all_units, units, own_sem)
    fetch.start()
    greet(*ring.peers)
    ring.start()
    arriving = moves(
        (far_dqkv, far_dkv, far_dx1, far_qkv, far_kv), (dqkv, dkv, dx1, qkv_w, kv_w), arrive_sem
    )
    for copy in arriving:
        copy.start()
    six = Hop(part6, core6, fromx6, None, sem6, chunk)
    seven = Hop(part7, core7, fromx7, None, sem7, chunk)
    fetch.wait()
    for copy in arriving:
        copy.wait()
    block[...] = jnp.zeros_like(block)
    cols = self_b.shape[1]
    for row in range(2):
        block[0:1, row * cols : (row + 1) * cols] = self_b[row : row + 1, :]
        block[0:1, (2 + row) * cols : (3 + row) * cols] = cross_b[row : row + 1, :]
        block[1 + row : 2 + row, :] = ffn_b[:, row * width : (row + 1) * width]
    block[SMALL - NORM_ROWS : SMALL - 2, :] = stats[:7, :]
    gain = gains[0:1, :]

    def project(step):
        grads = six.take(dqkv, step)
        total = dot_nt(grads[:, :cols], qkv_w[0]) + dot_nt(grads[:, cols : 2 * cols], qkv_w[1])
        six.put(part6, step, (total + dot_nt(grads[:, 2 * cols :], qkv_w[2])).astype(jnp.bfloat16))
        six.send_core(step)

    def norm_one(step):
        rows = six.own_rows(step)
        grad_in = six.result(step)
        _, normed, inv_std = norm_forward(units[rows, :].astype(jnp.float32), gain, gain)
        block[SMALL - 2 : SMALL - 1, :] += column_sum(grad_in * normed)
        block[SMALL - 1 : SMALL, :] += column_sum(grad_in)
        units_g[rows, :] = dx1[rows, :] + norm_backward(grad_in, normed, inv_std, gain)

    def text_only(work):
        def stage(step):
            @pl.when(step < text_steps)
            def _():
                work(step)

        return stage

    def text_project(step):
        seven.put(part7, step, dot_nt(seven.take(dkv, step), kv_w[...]).astype(jnp.bfloat16))
        seven.send_core(step)

    def text_result(step):
        text_g[seven.own_rows(step), :] = seven.result(step)

    ready = steps + 1

    def extra(tick):
        for when, work in enumerate((small.begin, small.forward, small.launch)):
            pl.when(tick == ready + when)(work)
        step = tick - ready - 3

        @pl.when((step >= 0) & (step < count // 2))
        def _():
            small.rotate(step)

    stages(
        steps,
        list(
            enumerate(
                [
                    project, six.send_cross, norm_one, text_only(text_project), text_only(seven.send_cross), text_only(text_result),
                ]
            )
        ),
        ring,
        extra,
        ready + 3 + count // 2,
    )

    def finish(step, carry):
        six.finish(step, False)
        text_only(lambda s: seven.finish(s, False))(step)
        return carry

    lax.fori_loop(0, steps, finish, 0)
    ring.finish()
    small.finish(small_sum)


def last(count, g0, g1, units, dqkv, dkv, dx1, qkv_w, kv_w, *rest):
    rows = dqkv.shape[0]
    own, width = dx1.shape
    chunk = own // STEPS
    text_own = dkv.shape[0] // NARROW
    bf, f32 = jnp.bfloat16, jnp.float32
    shape = jax.ShapeDtypeStruct
    vmem = pl.BlockSpec(memory_space=pltpu.VMEM)
    hbm = pl.BlockSpec(memory_space=pl.ANY)
    hop = hop_scratch(own, chunk, width)
    return pl.pallas_call(
        functools.partial(last_kernel, count=count),
        in_specs=[hbm] * 8 + [vmem] * len(rest),
        out_specs=[hbm] * 2 + [vmem] * 3,
        out_shape=[
            pltpu.HBM(g0.shape, bf),
            pltpu.HBM(g1.shape, bf),
            shape((own, width), f32),
            shape((text_own, width), f32),
            shape((SMALL, width), f32),
        ],
        scratch_shapes=[pltpu.VMEM(a.shape, a.dtype) for a in (dqkv, dkv, dx1, qkv_w, kv_w)]
        + [pltpu.SemaphoreType.DMA((5,)), pltpu.VMEM((own, width), bf), pltpu.SemaphoreType.DMA]
        + [pltpu.VMEM((rows, width), bf)]
        + hop
        + [pltpu.VMEM((dkv.shape[0], width), bf)]
        + hop_scratch(text_own, chunk, width)
        + [
            pltpu.VMEM((SMALL, width), f32),
            pltpu.VMEM((NARROW, SMALL, width), f32),
            pltpu.VMEM((count, SMALL, width), f32),
            pltpu.SemaphoreType.DMA((2, 3, max(count // 2, 3))),
        ]
        + ring_scratch(count, (width // count, width // 2)),
        compiler_params=pltpu.CompilerParams(collective_id=2, has_side_effects=True, vmem_limit_bytes=58 * MIB),
        cost_estimate=pl.CostEstimate(flops=30 * 10**9, bytes_accessed=16 * MIB, transcendentals=0),
        name="last",
    )(g0, g1, units, dqkv, dkv, dx1, qkv_w, kv_w, *rest)


def unpack_kernel(
    sum0, sum1, small, y_in, units_in, text_in,
    qkv_g, cq_g, co_g, so_g, kv_g, gain_g, shift_g, bias_g, self_b, cross_b, ffn_b, y, units_g, text_g,
):
    cols = cq_g.shape[1]
    step = pl.program_id(0)
    y[...] = y_in[...]
    units_g[...] = units_in[...]
    text_g[...] = text_in[...]
    for part in range(3):
        qkv_g[part] = sum0[:, part * cols : (part + 1) * cols].astype(jnp.float32)
    cq_g[...] = sum0[:, 3 * cols :].astype(jnp.float32)
    for when, ref in enumerate((co_g, so_g)):

        @pl.when(step == when)
        def _():
            ref[...] = sum1[...].astype(jnp.float32)

    half = kv_g.shape[0] // 2
    for when in range(half // cols):

        @pl.when(step == 2 + when)
        def _():
            for side in range(2):
                rows = slice(side * half + when * cols, side * half + (when + 1) * cols)
                for part in range(2):
                    first = (2 * side + part) * cols
                    kv_g[rows, part, :] = sum1[:, first : first + cols].astype(jnp.float32)

    @pl.when(step == 0)
    def _():
        norms = small[SMALL - NORM_ROWS :, :]
        for ref, order in ((gain_g, (7, 4, 0)), (shift_g, (8, 5, 1)), (bias_g, (6, 3, 2))):
            for row, source in enumerate(order):
                ref[row : row + 1, :] = norms[source : source + 1, :]
        width = small.shape[1]
        for row in range(2):
            self_b[row : row + 1, :] = small[0:1, row * cols : (row + 1) * cols]
            cross_b[row : row + 1, :] = small[0:1, (2 + row) * cols : (3 + row) * cols]
            ffn_b[:, row * width : (row + 1) * width] = small[1 + row : 2 + row, :]


def unpack(sum0, sum1, small, cols, hidden, *row_outs):
    width = sum0.shape[0]
    steps = width // cols
    f32 = jnp.float32
    block = lambda a: pl.BlockSpec((a.shape[0] // steps,) + a.shape[1:], lambda i: (i, 0))
    whole = lambda a: pl.BlockSpec(a.shape, lambda i: (0,) * len(a.shape))
    fixed = [
        jax.ShapeDtypeStruct(dims, f32)
        for dims in (
            (cols, width), (cols, width), (width, 2, cols),
            (3, width), (3, width), (3, width), (2, cols), (2, cols), (1, hidden),
        )
    ]
    moving = [jax.ShapeDtypeStruct((3, width, cols), f32), jax.ShapeDtypeStruct((width, cols), f32)]
    return pl.pallas_call(
        unpack_kernel,
        grid=(steps,),
        in_specs=[block(sum0), block(sum1), whole(small)] + [block(a) for a in row_outs],
        out_specs=[pl.BlockSpec((3, cols, cols), lambda i: (0, i, 0)), block(moving[1])]
        + [whole(a) for a in fixed]
        + [block(a) for a in row_outs],
        out_shape=moving + fixed + [jax.ShapeDtypeStruct(a.shape, a.dtype) for a in row_outs],
        compiler_params=pltpu.CompilerParams(vmem_limit_bytes=60 * MIB),
        name="unpack",
    )(sum0, sum1, small, *row_outs)


def local(
    units,
    text,
    out_grad,
    unit_lengths,
    text_lengths,
    bucket_counts,
    norm_gain,
    norm_shift,
    self_qkv,
    self_bias,
    self_out,
    cross_q,
    cross_kv,
    cross_bias,
    cross_out,
    ffn_in,
    ffn_in_bias,
    ffn_out,
    out_bias,
):
    slot_live = jnp.arange(unit_lengths.shape[0], dtype=jnp.int32) < bucket_counts[0]
    lengths = jnp.where(slot_live, unit_lengths, 0)
    qkv_weights = jnp.transpose(self_qkv, (1, 0, 2))
    kv_weights = cross_kv.reshape(cross_kv.shape[0], -1)
    count = lax.axis_size("wide")
    first_in, queries, key_rows, value_rows, text_kv, self_context, self_logs = front(
        lengths, units, text, norm_gain, norm_shift, qkv_weights, self_bias, kv_weights, cross_bias
    )
    (
        ffn_part,
        third_part,
        ffn_in_grad,
        ffn_out_grad,
        second_all,
        cross_queries,
        cross_context,
        resid_one,
        resid_two,
        ffn_bias_sum,
    ) = middle(
        units,
        out_grad,
        ffn_in,
        ffn_out,
        self_out,
        cross_q,
        cross_out,
        lengths,
        text_lengths,
        self_context,
        text_kv,
        norm_gain,
        norm_shift,
        out_bias,
        cross_bias,
        ffn_in_bias,
    )
    in_sum, out_sum, grads_one, grads_two, output, resid_one_grad, context_grad, text_kv_grad, cross_bias_sum, stats = turn(
        count,
        third_part,
        ffn_part,
        ffn_in_grad,
        ffn_out_grad,
        out_grad,
        lengths,
        text_lengths,
        resid_one,
        resid_two,
        second_all,
        cross_queries,
        cross_context,
        text_kv,
        self_context,
        norm_gain,
        out_bias,
        cross_out,
        cross_q,
        self_out,
    )
    qkv_grad, grads_one, grads_two, self_bias_sum, ffn_in_grad, ffn_out_grad = back(
        lengths,
        queries,
        key_rows,
        value_rows,
        context_grad,
        self_context,
        self_logs,
        first_in,
        text,
        text_kv_grad,
        in_sum,
        out_sum,
        grads_one,
        grads_two,
    )
    summed_one, summed_two, units_grad, text_grad, small = last(
        count,
        grads_one,
        grads_two,
        units,
        qkv_grad,
        text_kv_grad,
        resid_one_grad,
        qkv_weights,
        kv_weights,
        self_bias_sum,
        cross_bias_sum,
        ffn_bias_sum,
        stats,
        norm_gain,
    )
    (
        self_qkv_grad,
        cross_q_grad,
        cross_out_grad,
        self_out_grad,
        cross_kv_grad,
        gain_grad,
        shift_grad,
        bias_grad,
        self_bias_grad,
        cross_bias_grad,
        ffn_in_bias_grad,
        output,
        units_grad,
        text_grad,
    ) = unpack(
        summed_one, summed_two, small, queries.shape[1], ffn_in_bias.shape[0], output, units_grad, text_grad
    )
    self_qkv_grad = jnp.transpose(self_qkv_grad, (1, 0, 2))
    ffn_in_bias_grad = ffn_in_bias_grad.reshape(-1)
    return (
        output,
        units_grad,
        text_grad,
        gain_grad,
        shift_grad,
        self_qkv_grad,
        self_bias_grad,
        self_out_grad,
        cross_q_grad,
        cross_kv_grad,
        cross_bias_grad,
        cross_out_grad,
        ffn_in_grad,
        ffn_in_bias_grad,
        ffn_out_grad,
        bias_grad,
    )


def solution(mesh):
    placed = (
        P("wide", None),
        P("wide", None),
        P("wide", None),
        P("wide"),
        P("wide"),
        P("wide"),
        P(),
        P(),
        P(None, None, "narrow"),
        P(None, "narrow"),
        P("narrow", None),
        P(None, "narrow"),
        P(None, None, "narrow"),
        P(None, "narrow"),
        P("narrow", None),
        P(None, "narrow"),
        P("narrow"),
        P("narrow", None),
        P(),
    )
    return jax.shard_map(
        local,
        mesh=mesh,
        in_specs=placed,
        out_specs=(
            P(("wide", "narrow"), None),
            P(("wide", "narrow"), None),
            P(("wide", "narrow"), None),
            P(),
            P(),
            P(None, None, "narrow"),
            P(None, "narrow"),
            P("narrow", None),
            P(None, "narrow"),
            P(None, None, "narrow"),
            P(None, "narrow"),
            P("narrow", None),
            P(None, "narrow"),
            P("narrow"),
            P("narrow", None),
            P(),
        ),
        check_vma=False,
    )
```

```python
import functools

import jax
import jax.numpy as jnp
from jax import lax
from jax.experimental import pallas as pl
from jax.experimental.pallas import tpu as pltpu
from jax.sharding import PartitionSpec as P

HEAD_DIM = 64


NORM_EPSILON = 1e-05
MASKED_SCORE = -1000000000.0
EXACT = lax.Precision.HIGHEST


def norm_forward(values, gain_vec, shift_vec):
    row_mean = jnp.mean(values, axis=-1, keepdims=True)
    centered = values - row_mean
    inv_std = lax.rsqrt(jnp.mean(centered * centered, axis=-1, keepdims=True) + NORM_EPSILON)
    normed = centered * inv_std
    return (normed * gain_vec + shift_vec, normed, inv_std)


def norm_backward(grad_in, normed, inv_std, gain_vec):
    scaled = grad_in * gain_vec
    inner_term = scaled - jnp.mean(scaled, axis=-1, keepdims=True)
    inner_term = inner_term - normed * jnp.mean(scaled * normed, axis=-1, keepdims=True)
    return inner_term * inv_std


BLOCK = 256
LANES = 128
MIB = 1 << 20
NARROW = 4
STEPS = 8
HIDDEN = 512
MESH = pl.DeviceIdType.MESH


def head_mask(shape, head):
    lane = lax.broadcasted_iota(jnp.int32, shape, len(shape) - 1)
    return (lane >= head * HEAD_DIM) & (lane < (head + 1) * HEAD_DIM)


def pick_head(values, head):
    return jnp.where(head_mask(values.shape, head), values, jnp.zeros_like(values))


def dot_nt(a, b):
    return lax.dot_general(a, b, (((1,), (1,)), ((), ())), preferred_element_type=jnp.float32)


def dot_nn(a, b):
    return jnp.dot(a, b, preferred_element_type=jnp.float32)


def dot_tn(a, b):
    return lax.dot_general(a, b, (((0,), (0,)), ((), ())), preferred_element_type=jnp.float32)


def column_sum(values):
    return jnp.sum(values, axis=0, keepdims=True)


def mask_diagonal(scores, axis):
    count = scores.shape[axis]
    parts = [scores] if count == BLOCK else jnp.split(scores, [count - BLOCK], axis=axis)
    keys = lax.broadcasted_iota(jnp.int32, (BLOCK, BLOCK), axis)
    queries = lax.broadcasted_iota(jnp.int32, (BLOCK, BLOCK), 1 - axis)
    parts[-1] = jnp.where(keys <= queries, parts[-1], MASKED_SCORE)
    return jnp.concatenate(parts, axis=axis)


def front_kernel(
    lens, x_ref, t_ref, g_ref, s_ref, w_ref, b_ref, kvw_ref, vb_ref, h_ref, q_ref, k_ref, v_ref, kv_ref, c_ref, log_ref
):
    length = lens[pl.program_id(0)]
    width = q_ref.shape[1]
    both = dot_nn(t_ref[...], kvw_ref[...])
    kv_ref[:, :width] = both[:, :width].astype(jnp.bfloat16)
    kv_ref[:, width:] = (both[:, width:] + vb_ref[1:2, :]).astype(jnp.bfloat16)
    for i in range(x_ref.shape[0] // BLOCK):
        rows = pl.ds(i * BLOCK, BLOCK)

        @pl.when(i * BLOCK < length)
        def _():
            normed, _, _ = norm_forward(x_ref[rows, :].astype(jnp.float32), g_ref[0:1, :], s_ref[0:1, :])
            h1 = normed.astype(jnp.bfloat16)
            h_ref[rows, :] = h1
            queries = (dot_nn(h1, w_ref[0]) + b_ref[0:1, :]).astype(jnp.bfloat16)
            q_ref[rows, :] = queries
            k_ref[rows, :] = dot_nn(h1, w_ref[1]).astype(jnp.bfloat16)
            v_ref[rows, :] = (dot_nn(h1, w_ref[2]) + b_ref[1:2, :]).astype(jnp.bfloat16)
            count = (i + 1) * BLOCK
            keys, values = k_ref[:count, :], v_ref[:count, :]
            scaled = queries * jnp.bfloat16(HEAD_DIM**-0.5)
            total = jnp.zeros((BLOCK, width), jnp.float32)
            logs = jnp.zeros((BLOCK, LANES), jnp.float32)
            lane = lax.broadcasted_iota(jnp.int32, logs.shape, 1)
            for head in range(width // HEAD_DIM):
                scores = mask_diagonal(dot_nt(pick_head(scaled, head), keys), 1)
                top = jnp.max(scores, axis=1, keepdims=True)
                weights = jnp.exp(scores - top)
                norm = jnp.sum(weights, axis=1, keepdims=True)
                total += dot_nn(weights.astype(jnp.bfloat16), pick_head(values, head)) * (1.0 / norm)
                logs = jnp.where(lane == head, top + jnp.log(norm), logs)
            log_ref[:, rows] = logs.T[: log_ref.shape[0], :]
            c_ref[rows, :] = total.astype(jnp.bfloat16)

        @pl.when(i * BLOCK >= length)
        def _():
            for ref in (h_ref, q_ref, k_ref, v_ref, c_ref):
                ref[rows, :] = jnp.zeros((BLOCK, ref.shape[1]), ref.dtype)
            log_ref[:, rows] = jnp.zeros((log_ref.shape[0], BLOCK), jnp.float32)


def front(lengths, units, text, gains, shifts, weights, bias, kv_w, cross_bias):
    rows, width = units.shape
    slots = lengths.shape[0]
    slot_rows = rows // slots
    cols = weights.shape[2]
    whole = lambda a: pl.BlockSpec(a.shape, lambda s, *_: (0,) * a.ndim)
    slot = lambda w: pl.BlockSpec((slot_rows, w), lambda s, *_: (s, 0))
    texts = lambda w: pl.BlockSpec((text.shape[0] // slots, w), lambda s, *_: (s, 0))
    logs = pl.BlockSpec((8, slot_rows), lambda s, *_: (0, s))
    shape = lambda w: jax.ShapeDtypeStruct((rows, w), jnp.bfloat16)
    far = lambda w: pltpu.HBM((rows, w), jnp.bfloat16)
    return pl.pallas_call(
        front_kernel,
        grid_spec=pltpu.PrefetchScalarGridSpec(
            num_scalar_prefetch=1,
            grid=(slots,),
            in_specs=[slot(width), texts(width)]
            + [whole(a) for a in (gains, shifts, weights, bias, kv_w, cross_bias)],
            out_specs=[slot(width), slot(cols), slot(cols), slot(cols), texts(2 * cols), slot(cols), logs],
        ),
        out_shape=[
            far(width),
            far(cols),
            far(cols),
            far(cols),
            jax.ShapeDtypeStruct((text.shape[0], 2 * cols), jnp.bfloat16),
            shape(cols),
            pltpu.HBM((8, rows), jnp.float32),
        ],
        compiler_params=pltpu.CompilerParams(vmem_limit_bytes=60 * MIB),
        cost_estimate=pl.CostEstimate(flops=20 * 10**9, bytes_accessed=16 * MIB, transcendentals=8 * MIB),
        name="front",
    )(lengths, units, text, gains, shifts, weights, bias, kv_w, cross_bias)


def back_kernel(
    lens, q_ref, k_ref, v_ref, dc_ref, c_ref, log_ref, h_ref, text_ref, dkv_ref, in_ref, out_ref, _g0, _g1,
    o_ref, g0_ref, g1_ref, b_ref, in_f32, out_f32, dk_acc, dv_acc, w_acc,
):
    in_f32[...] = in_ref[...].astype(jnp.float32)
    out_f32[...] = out_ref[...].astype(jnp.float32)

    @pl.when(pl.program_id(0) == 0)
    def _():
        w_acc[...] = jnp.zeros_like(w_acc)
        b_ref[...] = jnp.zeros_like(b_ref)
        kv_grad = dot_tn(text_ref[...], dkv_ref[...]).astype(jnp.bfloat16)
        half, both = g1_ref.shape[0], dkv_ref.shape[1]
        g1_ref[:, :both] = kv_grad[:half]
        g1_ref[:, both:] = kv_grad[half:]

    length = lens[pl.program_id(0)]
    slot_rows, width = q_ref.shape
    dk_acc[...] = jnp.zeros_like(dk_acc)
    dv_acc[...] = jnp.zeros_like(dv_acc)
    for i in range(slot_rows // BLOCK):
        rows = pl.ds(i * BLOCK, BLOCK)

        @pl.when(i * BLOCK < length)
        def _():
            count = (i + 1) * BLOCK
            keys, values = k_ref[:count, :], v_ref[:count, :]
            scaled = q_ref[rows, :] * jnp.bfloat16(HEAD_DIM**-0.5)
            grads = dc_ref[rows, :]
            total = jnp.zeros((BLOCK, width), jnp.float32)
            heads = lax.broadcasted_iota(jnp.int32, (8, width), 0)
            lanes = lax.broadcasted_iota(jnp.int32, (8, width), 1)
            inner = lax.dot_general(
                jnp.where((lanes >= heads * HEAD_DIM) & (lanes < (heads + 1) * HEAD_DIM), 1.0, 0.0),
                grads.astype(jnp.float32) * c_ref[rows, :].astype(jnp.float32),
                (((1,), (1,)), ((), ())),
                precision=EXACT,
                preferred_element_type=jnp.float32,
            )
            for head in range(width // HEAD_DIM):
                q_head, g_head = pick_head(scaled, head), pick_head(grads, head)
                scores = mask_diagonal(dot_nt(keys, q_head), 0)
                weights = jnp.exp(scores - log_ref[head : head + 1, rows])
                dv_acc[:count, :] += dot_nn(weights.astype(jnp.bfloat16), g_head)
                weight_grad = dot_nt(values, g_head)
                score_grad = (weights * (weight_grad - inner[head : head + 1, :])).astype(jnp.bfloat16)
                dk_acc[:count, :] += dot_nn(score_grad, q_head)
                total += dot_tn(score_grad, pick_head(keys, head))
            o_ref[rows, :width] = (total * HEAD_DIM**-0.5).astype(jnp.bfloat16)

        @pl.when(i * BLOCK >= length)
        def _():
            o_ref[rows, :width] = jnp.zeros((BLOCK, width), jnp.bfloat16)

    o_ref[:, width : 2 * width] = dk_acc[...].astype(jnp.bfloat16)
    o_ref[:, 2 * width :] = dv_acc[...].astype(jnp.bfloat16)
    for i in range(slot_rows // BLOCK):
        rows = pl.ds(i * BLOCK, BLOCK)

        @pl.when(i * BLOCK < length)
        def _():
            sums = column_sum(o_ref[rows, :].astype(jnp.float32))
            b_ref[0:1, :] += sums[:, :width]
            b_ref[1:2, :] += sums[:, 2 * width :]

    for first in range(0, h_ref.shape[1], BLOCK):
        w_acc[first : first + BLOCK, :] += dot_tn(h_ref[:, first : first + BLOCK], o_ref[...])

    @pl.when(pl.program_id(0) == pl.num_programs(0) - 1)
    def _():
        g0_ref[...] = w_acc[...].astype(jnp.bfloat16)


def back(lengths, queries, keys, values, grads, context, logs, rows_in, text, dkv, in_sum, out_sum, g0, g1):
    rows, cols = queries.shape
    width = rows_in.shape[1]
    slots = lengths.shape[0]
    bf, f32 = jnp.bfloat16, jnp.float32
    shape = jax.ShapeDtypeStruct
    slot = lambda a: pl.BlockSpec((a.shape[0] // slots, a.shape[1]), lambda s, *_: (s, 0))
    whole = lambda a: pl.BlockSpec(a.shape, lambda s, *_: (0, 0))
    hbm = pl.BlockSpec(memory_space=pl.ANY)
    half = text.shape[1] // 2
    return pl.pallas_call(
        back_kernel,
        grid_spec=pltpu.PrefetchScalarGridSpec(
            num_scalar_prefetch=1,
            grid=(slots,),
            in_specs=[slot(queries)] * 5
            + [pl.BlockSpec((8, rows // slots), lambda s, *_: (0, s))]
            + [slot(rows_in), whole(text), whole(dkv), slot(in_sum), slot(out_sum), hbm, hbm],
            out_specs=[
                pl.BlockSpec((rows // slots, 3 * cols), lambda s, *_: (s, 0)),
                pl.BlockSpec((width, 3 * cols), lambda s, *_: (0, 0)),
                pl.BlockSpec((half, width), lambda s, *_: (1, 0)),
                pl.BlockSpec((2, cols), lambda s, *_: (0, 0)),
                slot(in_sum),
                slot(out_sum),
            ],
            scratch_shapes=[pltpu.VMEM((rows // slots, cols), f32)] * 2 + [pltpu.VMEM((width, 3 * cols), f32)],
        ),
        out_shape=[
            shape((rows, 3 * cols), bf),
            pltpu.HBM(g0.shape, bf),
            pltpu.HBM(g1.shape, bf),
            shape((2, cols), f32),
            shape(in_sum.shape, f32),
            shape(out_sum.shape, f32),
        ],
        input_output_aliases={12: 1, 13: 2},
        compiler_params=pltpu.CompilerParams(vmem_limit_bytes=60 * MIB),
        cost_estimate=pl.CostEstimate(flops=30 * 10**9, bytes_accessed=40 * MIB, transcendentals=8 * MIB),
        name="back",
    )(lengths, queries, keys, values, grads, context, logs, rows_in, text, dkv, in_sum, out_sum, g0, g1)


def place():
    index = lax.axis_index("narrow")
    core = index + 1 - 2 * (index % 2)
    return index, core, (index + 2) % NARROW, (core + 2) % NARROW


def greet(*wide_peers):
    _, core, cross, _ = place()
    barrier = pltpu.get_barrier_semaphore()
    for peer in (core, cross):
        pl.semaphore_signal(barrier, inc=1, device_id={"narrow": peer}, device_id_type=MESH)
    for peer in wide_peers:
        pl.semaphore_signal(barrier, inc=1, device_id={"wide": peer}, device_id_type=MESH)
    pl.semaphore_wait(barrier, 2 + len(wide_peers))


def remote(source, target, sems, kind, step, peer, axis="narrow"):
    return pltpu.make_async_remote_copy(
        src_ref=source,
        dst_ref=target,
        send_sem=sems.at[0, kind, step],
        recv_sem=sems.at[1, kind, step],
        device_id={axis: peer},
        device_id_type=MESH,
    )


def ring_place(count):
    wide = lax.axis_index("wide")
    odd, half = wide % 2, wide // 2
    spot = odd * (half + 1) + (1 - odd) * ((count - half) % count)

    def at(where):
        high = ((where + count - 1) % count) // (count // 2)
        return (1 - high) * (2 * where - 1) + high * ((2 * (count - where)) % (2 * count))

    return spot, at((spot + 1) % count), at((spot + count - 1) % count)


class Ring:
    UNITS = 4

    def __init__(self, count, sources, outs, view, arrived, held, sems, fetch_sems, keep_sems):
        self.count, self.sources, self.outs, self.view = count, sources, outs, view
        self.arrived, self.held, self.sems = arrived, held, sems
        self.fetch_sems, self.keep_sems = fetch_sems, keep_sems
        spot, following, previous = ring_place(count)
        self.spots = (spot, (count - spot) % count)
        self.peers = (following, previous)

    def block(self, refs, unit, back_by):
        shard = (self.spots[unit // 2] + 2 * self.count - back_by) % self.count
        return self.view(refs[unit // 2], unit // 2, unit % 2, shard)

    def send(self, source, target, kind, unit, step):
        return remote(source, target, self.sems, kind * self.UNITS + unit, step, self.peers[unit // 2], "wide")

    def sum_copy(self, unit, step, first=False):
        source = self.block(self.sources, unit, 0) if first else self.arrived.at[unit, jnp.maximum(step - 1, 0)]
        return self.send(source, self.arrived.at[unit, step], 0, unit, step)

    def fetch(self, unit, step):
        slot = step % 2
        return pltpu.make_async_copy(
            self.block(self.sources, unit, step + 1), self.held.at[unit, slot], self.fetch_sems.at[unit, slot]
        )

    def keep(self, unit):
        return pltpu.make_async_copy(
            self.arrived.at[unit, self.count - 2], self.block(self.outs, unit, self.count - 1), self.keep_sems.at[unit]
        )

    def spread_copy(self, unit, step, first=False):
        target = self.block(self.outs, unit, self.count - 1 + step)
        source = self.arrived.at[unit, self.count - 2] if first else target
        return self.send(source, target, 1, unit, step)

    def start(self):
        for unit in range(self.UNITS):
            self.sum_copy(unit, 0, True).start()
            self.fetch(unit, 0).start()
            self.fetch(unit, 1).start()

    def serve(self, turn, unit):
        last = self.count - 2

        @pl.when(turn <= last)
        def _():
            self.sum_copy(unit, turn).wait_recv()
            self.fetch(unit, turn).wait()
            total = self.held[unit, turn % 2].astype(jnp.float32) + self.arrived[unit, turn].astype(jnp.float32)
            self.arrived[unit, turn] = total.astype(jnp.bfloat16)

            @pl.when(turn < last)
            def _():
                self.sum_copy(unit, turn + 1).start()

            @pl.when(turn < last - 1)
            def _():
                self.fetch(unit, turn + 2).start()

            @pl.when(turn == last)
            def _():
                self.spread_copy(unit, 0, True).start()
                self.keep(unit).start()

        @pl.when((turn > last) & (turn <= 2 * last + 1))
        def _():
            step = turn - last - 1
            self.spread_copy(unit, step).wait_recv()

            @pl.when(step < last)
            def _():
                self.spread_copy(unit, step + 1).start()

    def finish(self):
        for unit in range(self.UNITS):
            self.keep(unit).wait()

        def body(step, carry):
            for unit in range(self.UNITS):
                self.sum_copy(unit, step).wait_send()
                self.spread_copy(unit, step).wait_send()
            return carry

        lax.fori_loop(0, self.count - 1, body, 0)


def ring_scratch(count, block):
    return [
        pltpu.VMEM((Ring.UNITS, count - 1) + block, jnp.bfloat16),
        pltpu.VMEM((Ring.UNITS, 2) + block, jnp.bfloat16),
        pltpu.SemaphoreType.DMA((2, 2 * Ring.UNITS, count - 1)),
        pltpu.SemaphoreType.DMA((Ring.UNITS, 2)),
        pltpu.SemaphoreType.DMA((Ring.UNITS,)),
    ]


def own_copy(whole, own, sem):
    size = own.shape[0]
    first = pl.multiple_of(lax.axis_index("narrow") * size, size)
    return pltpu.make_async_copy(whole.at[pl.ds(first, size), :], own, sem)


def moves(sources, targets, sems):
    pairs = list(zip(sources, targets, strict=True))
    return [pltpu.make_async_copy(a, b, sems.at[slot]) for slot, (a, b) in enumerate(pairs)]


class Hop:
    KINDS = 6

    def __init__(self, part, from_core, from_cross, full, sems, chunk):
        self.part, self.from_core, self.from_cross = part, from_core, from_cross
        self.full, self.sems, self.chunk = full, sems, chunk
        self.own = part.shape[0] // NARROW
        self.index, self.core, self.cross, self.diagonal = place()

    def rows(self, owner, step):
        return pl.ds(pl.multiple_of(owner * self.own + step * self.chunk, self.chunk), self.chunk)

    def own_rows(self, step):
        return pl.ds(pl.multiple_of(step * self.chunk, self.chunk), self.chunk)

    def core_copies(self, step):
        return [
            remote(self.part.at[self.rows(owner, step)], self.from_core.at[step, slot], self.sems, slot, step, self.core)
            for slot, owner in enumerate((self.core, self.diagonal))
        ]

    def cross_copy(self, step):
        return remote(
            self.part.at[self.rows(self.cross, step)], self.from_cross.at[step], self.sems, 2, step, self.cross
        )

    def gather_copy(self, step, kind):
        owner = self.cross if kind == 5 else self.index
        rows = self.full.at[self.rows(owner, step)]
        return remote(rows, rows, self.sems, kind, step, self.cross if kind == 3 else self.core)

    def send_core(self, step):
        for copy in self.core_copies(step):
            copy.start()

    def send_cross(self, step):
        for copy in self.core_copies(step):
            copy.wait_recv()
        total = self.part[self.rows(self.cross, step), :].astype(jnp.float32)
        total += self.from_core[step, 1].astype(jnp.float32)
        self.part[self.rows(self.cross, step), :] = total.astype(jnp.bfloat16)
        self.cross_copy(step).start()

    def result(self, step):
        total = self.part[self.rows(self.index, step), :].astype(jnp.float32)
        total += self.from_core[step, 0].astype(jnp.float32)
        self.cross_copy(step).wait_recv()
        return total + self.from_cross[step].astype(jnp.float32)

    def send_gather(self, step, values):
        self.full[self.rows(self.index, step), :] = values
        self.gather_copy(step, 3).start()
        self.gather_copy(step, 4).start()

    def forward(self, step):
        self.gather_copy(step, 3).wait_recv()
        self.gather_copy(step, 5).start()

    def gathered(self, step):
        self.gather_copy(step, 4).wait_recv()
        self.gather_copy(step, 5).wait_recv()

    def sent(self, step):
        for copy in self.core_copies(step):
            copy.wait_send()
        self.cross_copy(step).wait_send()

    def finish(self, step, gather=True, parts=True):
        if parts:
            self.sent(step)
        if gather:
            for kind in (3, 4, 5):
                self.gather_copy(step, kind).wait_send()

    def take(self, ref, step):
        return jnp.concatenate([ref[self.rows(owner, step), :] for owner in range(NARROW)], axis=0)

    def put(self, ref, step, values):
        for owner in range(NARROW):
            ref[self.rows(owner, step), :] = values[owner * self.chunk : (owner + 1) * self.chunk]


def hop_scratch(own, chunk, width):
    steps = own // chunk
    return [
        pltpu.VMEM((steps, 2, chunk, width), jnp.bfloat16),
        pltpu.VMEM((steps, chunk, width), jnp.bfloat16),
        pltpu.SemaphoreType.DMA((2, Hop.KINDS, steps)),
    ]


def stages(steps, work, ring=None, extra=None, ticks=0):
    ticks = max(ticks, steps + max(delay for delay, _ in work))
    per_tick = 0 if ring is None else -(-2 * (ring.count - 1) // ticks)

    def body(tick, carry):
        for number, (delay, stage) in enumerate(work):
            step = tick - delay

            @pl.when((step >= 0) & (step < steps))
            def _():
                stage(step)

            unit = (number + 1) * Ring.UNITS // len(work) - 1
            if per_tick and unit != number * Ring.UNITS // len(work) - 1:
                if per_tick == 1:
                    ring.serve(tick, unit)
                else:
                    lax.fori_loop(0, per_tick, lambda i, c: (ring.serve(tick * per_tick + i, unit), c)[1], 0)
            if extra is not None and number in (len(work) // 2, len(work) - 1):
                extra(2 * tick + (number == len(work) - 1))
        return carry

    lax.fori_loop(0, ticks, body, 0)


def middle_kernel(
    all_units, out_grad, far_in, far_out, far_so, far_cq, far_co, lens, text_lens,
    c1, kv2, gains, shifts, biases, bias, b_in,
    ffn_part, third, in_g, out_g, far_h2, far_q2, far_c2, far_x1, far_x2, in_bias_g,
    h2, q2, c2, x1, x2, leave_sem, units, own_sem, so_w, cq_w, co_w, small_sem, w_in, w_out, weight_sem, grads_in, grads_sem, give, give_sem, in_acc, out_acc,
    part, h3, core1, fromx1, sem1, core2, fromx2, sem2,
):
    steps, chunk, width = fromx1.shape
    cols = q2.shape[1]
    slots = text_lens.shape[0]
    texts = kv2.shape[0] // slots
    slot_rows = h2.shape[0] // slots
    hidden_count = w_out.shape[0]
    near = [
        pltpu.make_async_copy(source, target, small_sem.at[slot])
        for slot, (source, target) in enumerate(((far_so, so_w), (far_cq, cq_w), (far_co, co_w)))
    ]
    for fetch in near:
        fetch.start()
    fetches = [
        own_copy(all_units, units, own_sem),
        pltpu.make_async_copy(far_in, w_in, weight_sem.at[0]),
        pltpu.make_async_copy(far_out, w_out, weight_sem.at[1]),
    ]
    fetches[0].start()
    greet()
    one = Hop(part, core1, fromx1, h2, sem1, chunk)
    two = Hop(part, core2, fromx2, h3, sem2, chunk)
    scale = jnp.bfloat16(HEAD_DIM**-0.5)
    in_bias_g[...] = jnp.zeros_like(in_bias_g)
    for fetch in near:
        fetch.wait()

    leaving = moves((h2, q2, c2, x1, x2), (far_h2, far_q2, far_c2, far_x1, far_x2), leave_sem)

    def grad_copies(step):
        slot = step % 2
        return [
            pltpu.make_async_copy(
                out_grad.at[one.rows(owner, step), :],
                grads_in.at[slot, pl.ds(owner * chunk, chunk), :],
                grads_sem.at[slot, owner],
            )
            for owner in range(NARROW)
        ]

    def give_copies(step, kind):
        slot = step % 2
        return [
            pltpu.make_async_copy(
                give.at[kind, slot, pl.ds(owner * chunk, chunk), :],
                (ffn_part, third)[kind].at[one.rows(owner, step), :],
                give_sem.at[kind, slot, owner],
            )
            for owner in range(NARROW)
        ]

    def project(step):
        one.put(part, step, dot_nn(one.take(c1, step), so_w[...]).astype(jnp.bfloat16))
        one.send_core(step)
        for when, ref in ((1, in_acc), (2, out_acc)):

            @pl.when(step == when)
            def _():
                fetches[when].start()
                ref[...] = jnp.zeros_like(ref)

    def norm_one(step):
        @pl.when(step == 0)
        def _():
            fetches[0].wait()

        rows = one.own_rows(step)
        resid = units[rows, :].astype(jnp.float32) + one.result(step) + biases[0:1, :]
        x1[rows, :] = resid
        one.send_gather(step, norm_forward(resid, gains[1:2, :], shifts[1:2, :])[0].astype(jnp.bfloat16))

    def cross(step):
        one.gathered(step)
        queries = (dot_nn(one.take(h2, step), cq_w[...]) + bias[0:1, :]).astype(jnp.bfloat16)
        one.put(q2, step, queries)
        scaled = queries * scale
        count = queries.shape[0] // slots
        place_of = lax.broadcasted_iota(jnp.int32, (count * (cols // HEAD_DIM), texts), 1)
        context = []
        for slot in range(slots):
            mine = scaled[slot * count : (slot + 1) * count]
            keys = kv2[slot * texts : (slot + 1) * texts, :cols]
            values = kv2[slot * texts : (slot + 1) * texts, cols:]
            heads = range(cols // HEAD_DIM)
            scores = dot_nt(jnp.concatenate([pick_head(mine, head) for head in heads], axis=0), keys)
            scores = jnp.where(place_of < text_lens[slot], scores, MASKED_SCORE)
            weights = jnp.exp(scores - jnp.max(scores, axis=1, keepdims=True))
            norm = jnp.sum(weights, axis=1, keepdims=True)
            mixed = dot_nn(weights.astype(jnp.bfloat16), values) * (1.0 / norm)
            total = jnp.zeros((count, cols), jnp.float32)
            for head in heads:
                total += pick_head(mixed[head * count : (head + 1) * count], head)
            context.append(total.astype(jnp.bfloat16))
        context = jnp.concatenate(context, axis=0)
        one.put(c2, step, context)
        one.sent(step)
        two.put(part, step, dot_nn(context, co_w[...]).astype(jnp.bfloat16))
        two.send_core(step)

    def norm_two(step):
        rows = one.own_rows(step)
        resid = x1[rows, :] + two.result(step) + biases[1:2, :]
        x2[rows, :] = resid
        two.send_gather(step, norm_forward(resid, gains[2:3, :], shifts[2:3, :])[0].astype(jnp.bfloat16))

    def forward_two(step):
        two.forward(step)
        for copy in grad_copies(step):
            copy.start()

    def ffn(step):
        @pl.when(step == 0)
        def _():
            fetches[1].wait()
            fetches[2].wait()

        @pl.when(step == steps - 3)
        def _():
            for copy in leaving:
                copy.start()

        two.gathered(step)
        for copy in grad_copies(step):
            copy.wait()
        rows = two.take(h3, step)
        place_in = lax.broadcasted_iota(jnp.int32, (chunk, width), 0) + step * chunk
        grads = []
        for owner in range(NARROW):
            first = owner * two.own
            valid = place_in < lens[first // slot_rows] - first % slot_rows
            values = grads_in[step % 2, owner * chunk : (owner + 1) * chunk, :]
            grads.append(jnp.where(valid, values.astype(jnp.float32), 0.0).astype(jnp.bfloat16))
        grads = jnp.concatenate(grads, axis=0)
        out = jnp.zeros(rows.shape, jnp.float32)
        back_out = jnp.zeros(rows.shape, jnp.float32)
        for begin in range(0, hidden_count, HIDDEN):
            some = slice(begin, begin + HIDDEN)
            pre = dot_nn(rows, w_in[:, some]) + b_in[:, some]
            cdf = 0.5 + 0.5 * lax.erf(pre * (0.5**0.5))
            pdf = jnp.exp(-0.5 * pre * pre) * 0.3989422804014327
            hidden = (pre * cdf).astype(jnp.bfloat16)
            pre_low = ((cdf + pre * pdf) * dot_nt(grads, w_out[some, :])).astype(jnp.bfloat16)
            in_bias_g[:, some] += column_sum(pre_low.astype(jnp.float32))
            out += dot_nn(hidden, w_out[some, :])
            back_out += dot_nt(pre_low, w_in[:, some])
            out_acc[some, :] += dot_tn(hidden, grads)
            side, place_at = divmod(begin, width)
            in_acc[side * width : (side + 1) * width, place_at : place_at + HIDDEN] += dot_tn(rows, pre_low)

        @pl.when(step >= 2)
        def _():
            for kind in range(2):
                for copy in give_copies(step - 2, kind):
                    copy.wait()

        give[0, step % 2] = out.astype(jnp.bfloat16)
        give[1, step % 2] = back_out.astype(jnp.bfloat16)
        for kind in range(2):
            for copy in give_copies(step, kind):
                copy.start()

    stages(
        steps,
        [
            (0, project), (1, one.send_cross), (2, norm_one), (3, one.forward), (4, cross),
            (5, two.send_cross), (6, norm_two), (7, forward_two), (8, ffn),
        ],
    )

    def finish(step, carry):
        one.finish(step, True, False)
        two.finish(step)
        return carry

    lax.fori_loop(0, steps, finish, 0)
    part[...] = out_acc[...].astype(jnp.bfloat16)
    results = [pltpu.make_async_copy(part, out_g, weight_sem.at[0])]
    results[0].start()
    h3[...] = in_acc[...].astype(jnp.bfloat16)
    for side in range(hidden_count // width):
        here = pl.ds(side * width, width)
        results.append(pltpu.make_async_copy(h3.at[here, :], in_g.at[:, here], weight_sem.at[1 + side]))
        results[-1].start()
    for step in (steps - 2, steps - 1):
        for kind in range(2):
            for copy in give_copies(step, kind):
                copy.wait()
    for copy in results + leaving:
        copy.wait()


def middle(units, out_grad, w_in, w_out, so_w, cq_w, co_w, lens, text_lens, c1, kv2, gains, shifts, biases, bias, b_in):
    rows, cols = c1.shape
    own, width = rows // NARROW, units.shape[1]
    hidden_count = w_out.shape[0]
    chunk = own // STEPS
    bf, f32 = jnp.bfloat16, jnp.float32
    shape = jax.ShapeDtypeStruct
    vmem = pl.BlockSpec(memory_space=pltpu.VMEM)
    hbm = pl.BlockSpec(memory_space=pl.ANY)
    hop = hop_scratch(own, chunk, width)
    dma = pltpu.SemaphoreType.DMA
    return pl.pallas_call(
        middle_kernel,
        in_specs=[hbm] * 7 + [pl.BlockSpec(memory_space=pltpu.SMEM)] * 2 + [vmem] * 7,
        out_specs=[hbm] * 9 + [vmem],
        out_shape=[
            pltpu.HBM((rows, width), bf),
            pltpu.HBM((rows, width), bf),
            pltpu.HBM((width, hidden_count), bf),
            pltpu.HBM((hidden_count, width), bf),
            pltpu.HBM((rows, width), bf),
            pltpu.HBM((rows, cols), bf),
            pltpu.HBM((rows, cols), bf),
            pltpu.HBM((own, width), f32),
            pltpu.HBM((own, width), f32),
            shape((1, hidden_count), f32),
        ],
        scratch_shapes=[
            pltpu.VMEM((rows, width), bf),
            pltpu.VMEM((rows, cols), bf),
            pltpu.VMEM((rows, cols), bf),
            pltpu.VMEM((own, width), f32),
            pltpu.VMEM((own, width), f32),
            dma((5,)),
            pltpu.VMEM((own, width), bf),
            dma,
            pltpu.VMEM(so_w.shape, bf),
            pltpu.VMEM(cq_w.shape, bf),
            pltpu.VMEM(co_w.shape, bf),
            dma((3,)),
            pltpu.VMEM((width, hidden_count), bf),
            pltpu.VMEM((hidden_count, width), bf),
            dma((1 + hidden_count // width,)),
            pltpu.VMEM((2, NARROW * chunk, width), bf),
            dma((2, NARROW)),
            pltpu.VMEM((2, 2, NARROW * chunk, width), bf),
            dma((2, 2, NARROW)),
            pltpu.VMEM((hidden_count, width), f32),
            pltpu.VMEM((hidden_count, width), f32),
            pltpu.VMEM((rows, width), bf),
            pltpu.VMEM((rows, width), bf),
        ]
        + hop
        + hop,
        compiler_params=pltpu.CompilerParams(collective_id=0, has_side_effects=True, vmem_limit_bytes=60 * MIB),
        cost_estimate=pl.CostEstimate(flops=100 * 10**9, bytes_accessed=48 * MIB, transcendentals=8 * MIB),
        name="middle",
    )(
        units, out_grad, w_in, w_out, so_w, cq_w, co_w, lens, text_lens, c1, kv2, gains, shifts, biases, bias,
        b_in.reshape(1, -1),
    )


class FarHop(Hop):
    def fetch(self, mine, theirs, sems):
        self.mine, self.theirs = mine, theirs
        rows = lambda owner: pl.ds(pl.multiple_of(owner * self.own, self.own), self.own)
        self.fetches = [
            pltpu.make_async_copy(self.part.at[rows(owner)], ref, sems.at[slot])
            for slot, (owner, ref) in enumerate(((self.index, mine), (self.cross, theirs)))
        ]
        for copy in self.fetches:
            copy.start()

    def fetched(self):
        for copy in self.fetches:
            copy.wait()

    def cross_copy(self, step):
        return remote(
            self.theirs.at[self.own_rows(step)], self.from_cross.at[step], self.sems, 2, step, self.cross
        )

    def send_cross(self, step):
        for copy in self.core_copies(step):
            copy.wait_recv()
        total = self.theirs[self.own_rows(step), :].astype(jnp.float32)
        total += self.from_core[step, 1].astype(jnp.float32)
        self.theirs[self.own_rows(step), :] = total.astype(jnp.bfloat16)
        self.cross_copy(step).start()

    def result(self, step):
        total = self.mine[self.own_rows(step), :].astype(jnp.float32)
        total += self.from_core[step, 0].astype(jnp.float32)
        self.cross_copy(step).wait_recv()
        return total + self.from_cross[step].astype(jnp.float32)


def left_here(lens, own, rows):
    first = lax.axis_index("narrow") * own
    slot_rows = rows // lens.shape[0]
    return lens[first // slot_rows] - first % slot_rows


def row_of(step, chunk, width):
    return lax.broadcasted_iota(jnp.int32, (chunk, width), 0) + step * chunk


def turn_kernel(
    third, ffn_part, in_g, out_g, out_grad, lens, text_lens,
    far_x1, far_x2, far_h2, far_q2, far_c2, far_kv2, far_c1, gains, biases, far_co, far_cq, far_so,
    in_sum, out_sum, g0, g1, y, dx1, dc1, dkv, bias_g, stats,
    x1, x2, h2, q2, c2, kv2, c1, co_w, cq_w, so_w, arrive_sem, cq_g, give_sem, e_own, own_sem, mine3, theirs3, core3, fromx3, sem3, mine4, theirs4, core4, fromx4, sem4,
    part5, core5, fromx5, sem5, full3, full5, co_acc, cq_acc, so_acc, dkv_acc, fetch_sem,
    *ring_refs, count,
):
    steps, chunk, width = fromx5.shape
    cols = q2.shape[1]
    slots = bias_g.shape[0]
    texts = kv2.shape[0] // slots

    def ring_view(ref, way, half, shard):
        high = width // count
        if way == 0:
            return ref.at[pl.ds(pl.multiple_of(shard * high, high), high), pl.ds(half * width, width)]
        return ref.at[pl.ds(pl.multiple_of(shard * 2 * high + half * high, high), high), :]

    ring = Ring(count, (in_g, out_g), (in_sum, out_sum), ring_view, *ring_refs)
    fetch = own_copy(out_grad, e_own, own_sem)
    fetch.start()
    greet(*ring.peers)
    ring.start()
    three = FarHop(third, core3, fromx3, full3, sem3, chunk)
    four = FarHop(ffn_part, core4, fromx4, None, sem4, chunk)
    five = Hop(part5, core5, fromx5, full5, sem5, chunk)
    arriving = moves(
        (far_x2, far_x1, far_h2, far_q2, far_c2, far_kv2, far_c1, far_co, far_cq, far_so),
        (x2, x1, h2, q2, c2, kv2, c1, co_w, cq_w, so_w),
        arrive_sem,
    )
    three.fetch(mine3, theirs3, fetch_sem.at[0])
    for copy in arriving:
        copy.start()
    four.fetch(mine4, theirs4, fetch_sem.at[1])

    def start(step, carry):
        three.send_core(step)
        four.send_core(step)
        return carry

    lax.fori_loop(0, steps, start, 0)
    for ref in (co_acc, cq_acc, so_acc, dkv_acc, bias_g, stats):
        ref[...] = jnp.zeros_like(ref)
    three.fetched()
    four.fetched()
    fetch.wait()
    for copy in arriving:
        copy.wait()
    valid_rows = left_here(lens, x1.shape[0], h2.shape[0])
    scale = jnp.bfloat16(HEAD_DIM**-0.5)

    def norm_three(step):
        rows = three.own_rows(step)
        grad_in = three.result(step)
        _, normed, inv_std = norm_forward(x2[rows, :], gains[2:3, :], gains[2:3, :])
        stats[0:1, :] += column_sum(grad_in * normed)
        stats[1:2, :] += column_sum(grad_in)
        above = jnp.where(row_of(step, chunk, width) < valid_rows, e_own[rows, :].astype(jnp.float32), 0.0)
        total = above + norm_backward(grad_in, normed, inv_std, gains[2:3, :])
        stats[2:3, :] += column_sum(above)
        stats[3:4, :] += column_sum(total)
        dx1[rows, :] = total
        three.send_gather(step, total.astype(jnp.bfloat16))

    def cross(step):
        three.gathered(step)
        grads = three.take(full3, step)
        co_acc[...] += dot_tn(three.take(c2, step), grads)
        context = dot_nt(grads, co_w[...]).astype(jnp.bfloat16)
        queries = three.take(q2, step) * scale
        count = queries.shape[0] // slots
        place_of = lax.broadcasted_iota(jnp.int32, (texts, count), 0)
        q_grad = []
        for slot in range(slots):
            rows = slice(slot * count, (slot + 1) * count)
            texts_here = slice(slot * texts, (slot + 1) * texts)
            keys, values = kv2[texts_here, :cols], kv2[texts_here, cols:]
            total = jnp.zeros((count, cols), jnp.float32)
            for head in range(cols // HEAD_DIM):
                q_head, g_head = pick_head(queries[rows], head), pick_head(context[rows], head)
                scores = jnp.where(place_of < text_lens[slot], dot_nt(keys, q_head), MASKED_SCORE)
                weights = jnp.exp(scores - jnp.max(scores, axis=0, keepdims=True))
                weights = weights * (1.0 / jnp.sum(weights, axis=0, keepdims=True))
                dkv_acc[texts_here, cols:] += dot_nn(weights.astype(jnp.bfloat16), g_head)
                weight_grad = dot_nt(values, g_head)
                inner = jnp.sum(weights * weight_grad, axis=0, keepdims=True)
                score_grad = (weights * (weight_grad - inner)).astype(jnp.bfloat16)
                dkv_acc[texts_here, :cols] += dot_nn(score_grad, q_head)
                total += dot_tn(score_grad, pick_head(keys, head))
            q_grad.append((total * HEAD_DIM**-0.5).astype(jnp.bfloat16))
        q_grad = jnp.concatenate(q_grad, axis=0)
        five.put(part5, step, dot_nt(q_grad, cq_w[...]).astype(jnp.bfloat16))
        five.send_core(step)
        bias_g[0:1, :] += column_sum(q_grad.astype(jnp.float32))
        cq_acc[...] += dot_tn(five.take(h2, step), q_grad)

    def norm_two(step):
        rows = five.own_rows(step)
        grad_in = five.result(step)
        _, normed, inv_std = norm_forward(x1[rows, :], gains[1:2, :], gains[1:2, :])
        stats[4:5, :] += column_sum(grad_in * normed)
        stats[5:6, :] += column_sum(grad_in)
        total = dx1[rows, :] + norm_backward(grad_in, normed, inv_std, gains[1:2, :])
        stats[6:7, :] += column_sum(total)
        dx1[rows, :] = total
        five.send_gather(step, total.astype(jnp.bfloat16))

    def last(step):
        five.gathered(step)
        grads = five.take(full5, step)
        dc1_rows = dot_nt(grads, so_w[...]).astype(jnp.bfloat16)
        five.put(dc1, step, dc1_rows)
        so_acc[...] += dot_tn(five.take(c1, step), grads)

    def output(step):
        rows = four.own_rows(step)
        total = x2[rows, :] + four.result(step) + biases[2:3, :]
        y[rows, :] = jnp.where(row_of(step, chunk, width) < valid_rows, total, 0.0).astype(jnp.bfloat16)

    half = steps // 2
    late = steps + 2

    def side(half_tick):
        tick = half_tick // 2
        for begin, first in ((0, 0), (late, half)):
            for ahead, work in ((1, output), (0, four.send_cross)):
                step = tick - begin - ahead

                @pl.when((step >= 0) & (step < half) & (half_tick % 2 == 1))
                def _():
                    work(first + step)

    stages(
        steps,
        list(
            enumerate(
                [
                    three.send_cross, norm_three, three.forward, cross,
                    five.send_cross, norm_two, five.forward, last,
                ]
            )
        ),
        ring,
        side,
        late + half + 1,
    )
    dkv[...] = dkv_acc[...].astype(jnp.bfloat16)
    bias_g[1:2, :] = column_sum(dkv[:, cols:].astype(jnp.float32))
    mine4[:cols, :] = co_acc[...].astype(jnp.bfloat16)
    cq_g[...] = cq_acc[...].astype(jnp.bfloat16)
    mine4[cols : 2 * cols, :] = so_acc[...].astype(jnp.bfloat16)
    gives = [
        pltpu.make_async_copy(cq_g, g0.at[:, pl.ds(width - cols, cols)], give_sem.at[0]),
        pltpu.make_async_copy(mine4.at[pl.ds(0, 2 * cols), :], g1.at[pl.ds(0, 2 * cols), :], give_sem.at[1]),
    ]
    for give in gives:
        give.start()

    def finish(step, carry):
        three.finish(step)
        four.finish(step, False)
        five.finish(step)
        return carry

    lax.fori_loop(0, steps, finish, 0)
    ring.finish()
    for give in gives:
        give.wait()


def turn(
    count, third, ffn_part, in_g, out_g, out_grad, lens, text_lens,
    x1, x2, h2, q2, c2, kv2, c1, gains, biases, co_w, cq_w, so_w,
):
    rows, cols = c1.shape
    own, width = x1.shape
    chunk = own // STEPS
    bf, f32 = jnp.bfloat16, jnp.float32
    shape = jax.ShapeDtypeStruct
    vmem = pl.BlockSpec(memory_space=pltpu.VMEM)
    hbm = pl.BlockSpec(memory_space=pl.ANY)
    hop = hop_scratch(own, chunk, width)
    far = [pltpu.VMEM((own, width), bf)] * 2 + hop
    return pl.pallas_call(
        functools.partial(turn_kernel, count=count),
        in_specs=[hbm] * 5 + [pl.BlockSpec(memory_space=pltpu.SMEM)] * 2 + [hbm] * 7 + [vmem] * 2 + [hbm] * 3,
        out_specs=[hbm] * 4 + [vmem] * 6,
        out_shape=[
            pltpu.HBM(in_g.shape, bf),
            pltpu.HBM(out_g.shape, bf),
            pltpu.HBM((width, width), bf),
            pltpu.HBM((width, width), bf),
            shape((own, width), bf),
            shape((own, width), f32),
            shape((rows, cols), bf),
            shape(kv2.shape, bf),
            shape((2, cols), f32),
            shape((8, width), f32),
        ],
        scratch_shapes=[pltpu.VMEM(a.shape, a.dtype) for a in (x1, x2, h2, q2, c2, kv2, c1, co_w, cq_w, so_w)]
        + [
            pltpu.SemaphoreType.DMA((10,)),
            pltpu.VMEM((width, cols), bf),
            pltpu.SemaphoreType.DMA((2,)),
            pltpu.VMEM((own, width), bf),
            pltpu.SemaphoreType.DMA,
        ]
        + far
        + far
        + [pltpu.VMEM((rows, width), bf)]
        + hop
        + [pltpu.VMEM((rows, width), bf)] * 2
        + [
            pltpu.VMEM((cols, width), f32),
            pltpu.VMEM((width, cols), f32),
            pltpu.VMEM((cols, width), f32),
            pltpu.VMEM(kv2.shape, f32),
            pltpu.SemaphoreType.DMA((2, 2)),
        ]
        + ring_scratch(count, (width // count, width)),
        compiler_params=pltpu.CompilerParams(collective_id=1, has_side_effects=True, vmem_limit_bytes=60 * MIB),
        cost_estimate=pl.CostEstimate(flops=100 * 10**9, bytes_accessed=24 * MIB, transcendentals=4 * MIB),
        name="turn",
    )(
        third, ffn_part, in_g, out_g, out_grad, lens, text_lens,
        x1, x2, h2, q2, c2, kv2, c1, gains, biases, co_w, cq_w, so_w,
    )


SMALL = 16
NORM_ROWS = 9


class Small:
    def __init__(self, count, block, near, far, sems):
        self.count, self.mine, self.near, self.far, self.sems = count, block, near, far, sems
        self.index, self.core, self.cross, _ = place()
        self.spot, *self.peers = ring_place(count)

    def near_copy(self, kind):
        owner = self.cross if kind == 2 else self.index
        return remote(self.near.at[owner], self.near.at[owner], self.sems, 0, kind, (self.cross, self.core, self.core)[kind])

    def far_copy(self, way, step):
        block = self.far.at[(self.spot + (2 * way - 1) * step + self.count) % self.count]
        return remote(block, block, self.sems, 1 + way, step, self.peers[way], "wide")

    def begin(self):
        self.near[self.index] = self.mine[...]
        self.near_copy(0).start()
        self.near_copy(1).start()

    def forward(self):
        self.near_copy(0).wait_recv()
        self.near_copy(2).start()

    def launch(self):
        self.near_copy(1).wait_recv()
        self.near_copy(2).wait_recv()
        both = self.near[0]
        for owner in range(1, NARROW):
            both += self.near[owner]
        row = lax.broadcasted_iota(jnp.int32, both.shape, 0)
        self.far[self.spot] = jnp.where(row < SMALL - NORM_ROWS, self.mine[...], both)
        self.far_copy(0, 0).start()
        self.far_copy(1, 0).start()

    def rotate(self, step):
        for way in range(2):
            steps = self.count // 2 - way

            @pl.when(step < steps)
            def _():
                self.far_copy(way, step).wait_recv()

            @pl.when(step < steps - 1)
            def _():
                self.far_copy(way, step + 1).start()

    def finish(self, out):
        for kind in range(3):
            self.near_copy(kind).wait_send()

        for way in range(2):

            def body(step, carry):
                self.far_copy(way, step).wait_send()
                return carry

            lax.fori_loop(0, self.count // 2 - way, body, 0)
        out[...] = jnp.zeros_like(out)

        def add(spot, carry):
            out[...] += self.far[spot]
            return carry

        lax.fori_loop(0, self.count, add, 0)


def last_kernel(
    g0, g1, all_units, far_dqkv, far_dkv, far_dx1, far_qkv, far_kv, self_b, cross_b, ffn_b, stats, gains,
    sum0, sum1, units_g, text_g, small_sum,
    dqkv, dkv, dx1, qkv_w, kv_w, arrive_sem, units, own_sem, part6, core6, fromx6, sem6, part7, core7, fromx7, sem7,
    block, near, far, small_sem, *ring_refs, count,
):
    steps, chunk, width = fromx6.shape
    text_steps = fromx7.shape[0]

    def ring_view(ref, way, half, shard):
        high = width // count
        return ref.at[pl.ds(pl.multiple_of(shard * high, high), high), pl.ds(half * (width // 2), width // 2)]

    ring = Ring(count, (g0, g1), (sum0, sum1), ring_view, *ring_refs)
    small = Small(count, block, near, far, small_sem)
    fetch = own_copy(all_units, units, own_sem)
    fetch.start()
    greet(*ring.peers)
    ring.start()
    arriving = moves(
        (far_dqkv, far_dkv, far_dx1, far_qkv, far_kv), (dqkv, dkv, dx1, qkv_w, kv_w), arrive_sem
    )
    for copy in arriving:
        copy.start()
    six = Hop(part6, core6, fromx6, None, sem6, chunk)
    seven = Hop(part7, core7, fromx7, None, sem7, chunk)
    fetch.wait()
    for copy in arriving:
        copy.wait()
    block[...] = jnp.zeros_like(block)
    cols = self_b.shape[1]
    for row in range(2):
        block[0:1, row * cols : (row + 1) * cols] = self_b[row : row + 1, :]
        block[0:1, (2 + row) * cols : (3 + row) * cols] = cross_b[row : row + 1, :]
        block[1 + row : 2 + row, :] = ffn_b[:, row * width : (row + 1) * width]
    block[SMALL - NORM_ROWS : SMALL - 2, :] = stats[:7, :]
    gain = gains[0:1, :]

    def project(step):
        grads = six.take(dqkv, step)
        total = dot_nt(grads[:, :cols], qkv_w[0]) + dot_nt(grads[:, cols : 2 * cols], qkv_w[1])
        six.put(part6, step, (total + dot_nt(grads[:, 2 * cols :], qkv_w[2])).astype(jnp.bfloat16))
        six.send_core(step)

    def norm_one(step):
        rows = six.own_rows(step)
        grad_in = six.result(step)
        _, normed, inv_std = norm_forward(units[rows, :].astype(jnp.float32), gain, gain)
        block[SMALL - 2 : SMALL - 1, :] += column_sum(grad_in * normed)
        block[SMALL - 1 : SMALL, :] += column_sum(grad_in)
        units_g[rows, :] = dx1[rows, :] + norm_backward(grad_in, normed, inv_std, gain)

    def text_only(work):
        def stage(step):
            @pl.when(step < text_steps)
            def _():
                work(step)

        return stage

    def text_project(step):
        seven.put(part7, step, dot_nt(seven.take(dkv, step), kv_w[...]).astype(jnp.bfloat16))
        seven.send_core(step)

    def text_result(step):
        text_g[seven.own_rows(step), :] = seven.result(step)

    ready = 2 * (steps + 1)

    def extra(half_tick):
        for when, work in enumerate((small.begin, small.forward, small.launch)):
            pl.when(half_tick == ready + when)(work)
        step = half_tick - ready - 3

        @pl.when((step >= 0) & (step < count // 2))
        def _():
            small.rotate(step)

    stages(
        steps,
        list(
            enumerate(
                [
                    project, six.send_cross, norm_one, text_only(text_project), text_only(seven.send_cross), text_only(text_result),
                ]
            )
        ),
        ring,
        extra,
        max((ready + 4 + count // 2) // 2, 2 * (count - 1)),
    )

    def finish(step, carry):
        six.finish(step, False)
        text_only(lambda s: seven.finish(s, False))(step)
        return carry

    lax.fori_loop(0, steps, finish, 0)
    ring.finish()
    small.finish(small_sum)


def last(count, g0, g1, units, dqkv, dkv, dx1, qkv_w, kv_w, *rest):
    rows = dqkv.shape[0]
    own, width = dx1.shape
    chunk = own // STEPS
    text_own = dkv.shape[0] // NARROW
    bf, f32 = jnp.bfloat16, jnp.float32
    shape = jax.ShapeDtypeStruct
    vmem = pl.BlockSpec(memory_space=pltpu.VMEM)
    hbm = pl.BlockSpec(memory_space=pl.ANY)
    hop = hop_scratch(own, chunk, width)
    return pl.pallas_call(
        functools.partial(last_kernel, count=count),
        in_specs=[hbm] * 8 + [vmem] * len(rest),
        out_specs=[hbm] * 2 + [vmem] * 3,
        out_shape=[
            pltpu.HBM(g0.shape, bf),
            pltpu.HBM(g1.shape, bf),
            shape((own, width), f32),
            shape((text_own, width), f32),
            shape((SMALL, width), f32),
        ],
        scratch_shapes=[pltpu.VMEM(a.shape, a.dtype) for a in (dqkv, dkv, dx1, qkv_w, kv_w)]
        + [pltpu.SemaphoreType.DMA((5,)), pltpu.VMEM((own, width), bf), pltpu.SemaphoreType.DMA]
        + [pltpu.VMEM((rows, width), bf)]
        + hop
        + [pltpu.VMEM((dkv.shape[0], width), bf)]
        + hop_scratch(text_own, chunk, width)
        + [
            pltpu.VMEM((SMALL, width), f32),
            pltpu.VMEM((NARROW, SMALL, width), f32),
            pltpu.VMEM((count, SMALL, width), f32),
            pltpu.SemaphoreType.DMA((2, 3, max(count // 2, 3))),
        ]
        + ring_scratch(count, (width // count, width // 2)),
        compiler_params=pltpu.CompilerParams(collective_id=2, has_side_effects=True, vmem_limit_bytes=58 * MIB),
        cost_estimate=pl.CostEstimate(flops=30 * 10**9, bytes_accessed=16 * MIB, transcendentals=0),
        name="last",
    )(g0, g1, units, dqkv, dkv, dx1, qkv_w, kv_w, *rest)


def unpack_kernel(
    sum0, sum1, small, y_in, units_in, text_in,
    qkv_g, cq_g, co_g, so_g, kv_g, gain_g, shift_g, bias_g, self_b, cross_b, ffn_b, y, units_g, text_g,
):
    cols = cq_g.shape[1]
    step = pl.program_id(0)
    y[...] = y_in[...]
    units_g[...] = units_in[...]
    text_g[...] = text_in[...]
    for part in range(3):
        qkv_g[part] = sum0[:, part * cols : (part + 1) * cols].astype(jnp.float32)
    cq_g[...] = sum0[:, 3 * cols :].astype(jnp.float32)
    for when, ref in enumerate((co_g, so_g)):

        @pl.when(step == when)
        def _():
            ref[...] = sum1[...].astype(jnp.float32)

    half = kv_g.shape[0] // 2
    for when in range(half // cols):

        @pl.when(step == 2 + when)
        def _():
            for side in range(2):
                rows = slice(side * half + when * cols, side * half + (when + 1) * cols)
                for part in range(2):
                    first = (2 * side + part) * cols
                    kv_g[rows, part, :] = sum1[:, first : first + cols].astype(jnp.float32)

    @pl.when(step == 0)
    def _():
        norms = small[SMALL - NORM_ROWS :, :]
        for ref, order in ((gain_g, (7, 4, 0)), (shift_g, (8, 5, 1)), (bias_g, (6, 3, 2))):
            for row, source in enumerate(order):
                ref[row : row + 1, :] = norms[source : source + 1, :]
        width = small.shape[1]
        for row in range(2):
            self_b[row : row + 1, :] = small[0:1, row * cols : (row + 1) * cols]
            cross_b[row : row + 1, :] = small[0:1, (2 + row) * cols : (3 + row) * cols]
            ffn_b[:, row * width : (row + 1) * width] = small[1 + row : 2 + row, :]


def unpack(sum0, sum1, small, cols, hidden, *row_outs):
    width = sum0.shape[0]
    steps = width // cols
    f32 = jnp.float32
    block = lambda a: pl.BlockSpec((a.shape[0] // steps,) + a.shape[1:], lambda i: (i, 0))
    whole = lambda a: pl.BlockSpec(a.shape, lambda i: (0,) * len(a.shape))
    fixed = [
        jax.ShapeDtypeStruct(dims, f32)
        for dims in (
            (cols, width), (cols, width), (width, 2, cols),
            (3, width), (3, width), (3, width), (2, cols), (2, cols), (1, hidden),
        )
    ]
    moving = [jax.ShapeDtypeStruct((3, width, cols), f32), jax.ShapeDtypeStruct((width, cols), f32)]
    return pl.pallas_call(
        unpack_kernel,
        grid=(steps,),
        in_specs=[block(sum0), block(sum1), whole(small)] + [block(a) for a in row_outs],
        out_specs=[pl.BlockSpec((3, cols, cols), lambda i: (0, i, 0)), block(moving[1])]
        + [whole(a) for a in fixed]
        + [block(a) for a in row_outs],
        out_shape=moving + fixed + [jax.ShapeDtypeStruct(a.shape, a.dtype) for a in row_outs],
        compiler_params=pltpu.CompilerParams(vmem_limit_bytes=60 * MIB),
        name="unpack",
    )(sum0, sum1, small, *row_outs)


def local(
    units,
    text,
    out_grad,
    unit_lengths,
    text_lengths,
    bucket_counts,
    norm_gain,
    norm_shift,
    self_qkv,
    self_bias,
    self_out,
    cross_q,
    cross_kv,
    cross_bias,
    cross_out,
    ffn_in,
    ffn_in_bias,
    ffn_out,
    out_bias,
):
    slot_live = jnp.arange(unit_lengths.shape[0], dtype=jnp.int32) < bucket_counts[0]
    lengths = jnp.where(slot_live, unit_lengths, 0)
    qkv_weights = jnp.transpose(self_qkv, (1, 0, 2))
    kv_weights = cross_kv.reshape(cross_kv.shape[0], -1)
    count = lax.axis_size("wide")
    first_in, queries, key_rows, value_rows, text_kv, self_context, self_logs = front(
        lengths, units, text, norm_gain, norm_shift, qkv_weights, self_bias, kv_weights, cross_bias
    )
    (
        ffn_part,
        third_part,
        ffn_in_grad,
        ffn_out_grad,
        second_all,
        cross_queries,
        cross_context,
        resid_one,
        resid_two,
        ffn_bias_sum,
    ) = middle(
        units,
        out_grad,
        ffn_in,
        ffn_out,
        self_out,
        cross_q,
        cross_out,
        lengths,
        text_lengths,
        self_context,
        text_kv,
        norm_gain,
        norm_shift,
        out_bias,
        cross_bias,
        ffn_in_bias,
    )
    in_sum, out_sum, grads_one, grads_two, output, resid_one_grad, context_grad, text_kv_grad, cross_bias_sum, stats = turn(
        count,
        third_part,
        ffn_part,
        ffn_in_grad,
        ffn_out_grad,
        out_grad,
        lengths,
        text_lengths,
        resid_one,
        resid_two,
        second_all,
        cross_queries,
        cross_context,
        text_kv,
        self_context,
        norm_gain,
        out_bias,
        cross_out,
        cross_q,
        self_out,
    )
    qkv_grad, grads_one, grads_two, self_bias_sum, ffn_in_grad, ffn_out_grad = back(
        lengths,
        queries,
        key_rows,
        value_rows,
        context_grad,
        self_context,
        self_logs,
        first_in,
        text,
        text_kv_grad,
        in_sum,
        out_sum,
        grads_one,
        grads_two,
    )
    summed_one, summed_two, units_grad, text_grad, small = last(
        count,
        grads_one,
        grads_two,
        units,
        qkv_grad,
        text_kv_grad,
        resid_one_grad,
        qkv_weights,
        kv_weights,
        self_bias_sum,
        cross_bias_sum,
        ffn_bias_sum,
        stats,
        norm_gain,
    )
    (
        self_qkv_grad,
        cross_q_grad,
        cross_out_grad,
        self_out_grad,
        cross_kv_grad,
        gain_grad,
        shift_grad,
        bias_grad,
        self_bias_grad,
        cross_bias_grad,
        ffn_in_bias_grad,
        output,
        units_grad,
        text_grad,
    ) = unpack(
        summed_one, summed_two, small, queries.shape[1], ffn_in_bias.shape[0], output, units_grad, text_grad
    )
    self_qkv_grad = jnp.transpose(self_qkv_grad, (1, 0, 2))
    ffn_in_bias_grad = ffn_in_bias_grad.reshape(-1)
    return (
        output,
        units_grad,
        text_grad,
        gain_grad,
        shift_grad,
        self_qkv_grad,
        self_bias_grad,
        self_out_grad,
        cross_q_grad,
        cross_kv_grad,
        cross_bias_grad,
        cross_out_grad,
        ffn_in_grad,
        ffn_in_bias_grad,
        ffn_out_grad,
        bias_grad,
    )


def solution(mesh):
    placed = (
        P("wide", None),
        P("wide", None),
        P("wide", None),
        P("wide"),
        P("wide"),
        P("wide"),
        P(),
        P(),
        P(None, None, "narrow"),
        P(None, "narrow"),
        P("narrow", None),
        P(None, "narrow"),
        P(None, None, "narrow"),
        P(None, "narrow"),
        P("narrow", None),
        P(None, "narrow"),
        P("narrow"),
        P("narrow", None),
        P(),
    )
    return jax.shard_map(
        local,
        mesh=mesh,
        in_specs=placed,
        out_specs=(
            P(("wide", "narrow"), None),
            P(("wide", "narrow"), None),
            P(("wide", "narrow"), None),
            P(),
            P(),
            P(None, None, "narrow"),
            P(None, "narrow"),
            P("narrow", None),
            P(None, "narrow"),
            P(None, None, "narrow"),
            P(None, "narrow"),
            P("narrow", None),
            P(None, "narrow"),
            P("narrow"),
            P("narrow", None),
            P(),
        ),
        check_vma=False,
    )
```

```python
import functools

import jax
import jax.numpy as jnp
from jax import lax
from jax.experimental import pallas as pl
from jax.experimental.pallas import tpu as pltpu
from jax.sharding import PartitionSpec as P

HEAD_DIM = 64


NORM_EPSILON = 1e-05
MASKED_SCORE = -1000000000.0
EXACT = lax.Precision.HIGHEST


def norm_forward(values, gain_vec, shift_vec):
    row_mean = jnp.mean(values, axis=-1, keepdims=True)
    centered = values - row_mean
    inv_std = lax.rsqrt(jnp.mean(centered * centered, axis=-1, keepdims=True) + NORM_EPSILON)
    normed = centered * inv_std
    return (normed * gain_vec + shift_vec, normed, inv_std)


def norm_backward(grad_in, normed, inv_std, gain_vec):
    scaled = grad_in * gain_vec
    inner_term = scaled - jnp.mean(scaled, axis=-1, keepdims=True)
    inner_term = inner_term - normed * jnp.mean(scaled * normed, axis=-1, keepdims=True)
    return inner_term * inv_std


BLOCK = 256
LANES = 128
MIB = 1 << 20
NARROW = 4
STEPS = 8
HIDDEN = 512
MESH = pl.DeviceIdType.MESH


def head_mask(shape, head):
    lane = lax.broadcasted_iota(jnp.int32, shape, len(shape) - 1)
    return (lane >= head * HEAD_DIM) & (lane < (head + 1) * HEAD_DIM)


def pick_head(values, head):
    return jnp.where(head_mask(values.shape, head), values, jnp.zeros_like(values))


def dot_nt(a, b):
    return lax.dot_general(a, b, (((1,), (1,)), ((), ())), preferred_element_type=jnp.float32)


def dot_nn(a, b):
    return jnp.dot(a, b, preferred_element_type=jnp.float32)


def dot_tn(a, b):
    return lax.dot_general(a, b, (((0,), (0,)), ((), ())), preferred_element_type=jnp.float32)


def column_sum(values):
    return jnp.sum(values, axis=0, keepdims=True)


def mask_diagonal(scores, axis):
    count = scores.shape[axis]
    parts = [scores] if count == BLOCK else jnp.split(scores, [count - BLOCK], axis=axis)
    keys = lax.broadcasted_iota(jnp.int32, parts[-1].shape, axis)
    queries = lax.broadcasted_iota(jnp.int32, keys.shape, 1 - axis) & (BLOCK - 1)
    parts[-1] = jnp.where(keys <= queries, parts[-1], MASKED_SCORE)
    return jnp.concatenate(parts, axis=axis)


def front_kernel(
    lens, x_ref, t_ref, g_ref, s_ref, w_ref, b_ref, kvw_ref, vb_ref, h_ref, q_ref, k_ref, v_ref, kv_ref, c_ref, log_ref
):
    length = lens[pl.program_id(0)]
    width = q_ref.shape[1]
    both = dot_nn(t_ref[...], kvw_ref[...])
    kv_ref[:, :width] = both[:, :width].astype(jnp.bfloat16)
    kv_ref[:, width:] = (both[:, width:] + vb_ref[1:2, :]).astype(jnp.bfloat16)
    for i in range(x_ref.shape[0] // BLOCK):
        rows = pl.ds(i * BLOCK, BLOCK)

        @pl.when(i * BLOCK < length)
        def _():
            normed, _, _ = norm_forward(x_ref[rows, :].astype(jnp.float32), g_ref[0:1, :], s_ref[0:1, :])
            h1 = normed.astype(jnp.bfloat16)
            h_ref[rows, :] = h1
            queries = (dot_nn(h1, w_ref[0]) + b_ref[0:1, :]).astype(jnp.bfloat16)
            q_ref[rows, :] = queries
            k_ref[rows, :] = dot_nn(h1, w_ref[1]).astype(jnp.bfloat16)
            v_ref[rows, :] = (dot_nn(h1, w_ref[2]) + b_ref[1:2, :]).astype(jnp.bfloat16)
            count = (i + 1) * BLOCK
            keys, values = k_ref[:count, :], v_ref[:count, :]
            scaled = queries * jnp.bfloat16(HEAD_DIM**-0.5)
            total = jnp.zeros((BLOCK, width), jnp.float32)
            logs = jnp.zeros((BLOCK, LANES), jnp.float32)
            lane = lax.broadcasted_iota(jnp.int32, logs.shape, 1)
            for head in range(width // HEAD_DIM):
                scores = mask_diagonal(dot_nt(pick_head(scaled, head), keys), 1)
                top = jnp.max(scores, axis=1, keepdims=True)
                weights = jnp.exp(scores - top)
                norm = jnp.sum(weights, axis=1, keepdims=True)
                total += dot_nn(weights.astype(jnp.bfloat16), pick_head(values, head)) * (1.0 / norm)
                logs = jnp.where(lane == head, top + jnp.log(norm), logs)
            log_ref[:, rows] = logs.T[: log_ref.shape[0], :]
            c_ref[rows, :] = total.astype(jnp.bfloat16)

        @pl.when(i * BLOCK >= length)
        def _():
            for ref in (h_ref, q_ref, k_ref, v_ref, c_ref):
                ref[rows, :] = jnp.zeros((BLOCK, ref.shape[1]), ref.dtype)
            log_ref[:, rows] = jnp.zeros((log_ref.shape[0], BLOCK), jnp.float32)


def front(lengths, units, text, gains, shifts, weights, bias, kv_w, cross_bias):
    rows, width = units.shape
    slots = lengths.shape[0]
    slot_rows = rows // slots
    cols = weights.shape[2]
    whole = lambda a: pl.BlockSpec(a.shape, lambda s, *_: (0,) * a.ndim)
    slot = lambda w: pl.BlockSpec((slot_rows, w), lambda s, *_: (s, 0))
    texts = lambda w: pl.BlockSpec((text.shape[0] // slots, w), lambda s, *_: (s, 0))
    logs = pl.BlockSpec((8, slot_rows), lambda s, *_: (0, s))
    shape = lambda w: jax.ShapeDtypeStruct((rows, w), jnp.bfloat16)
    far = lambda w: pltpu.HBM((rows, w), jnp.bfloat16)
    return pl.pallas_call(
        front_kernel,
        grid_spec=pltpu.PrefetchScalarGridSpec(
            num_scalar_prefetch=1,
            grid=(slots,),
            in_specs=[slot(width), texts(width)]
            + [whole(a) for a in (gains, shifts, weights, bias, kv_w, cross_bias)],
            out_specs=[slot(width), slot(cols), slot(cols), slot(cols), texts(2 * cols), slot(cols), logs],
        ),
        out_shape=[
            far(width),
            far(cols),
            far(cols),
            far(cols),
            jax.ShapeDtypeStruct((text.shape[0], 2 * cols), jnp.bfloat16),
            shape(cols),
            pltpu.HBM((8, rows), jnp.float32),
        ],
        compiler_params=pltpu.CompilerParams(vmem_limit_bytes=60 * MIB),
        cost_estimate=pl.CostEstimate(flops=20 * 10**9, bytes_accessed=16 * MIB, transcendentals=8 * MIB),
        name="front",
    )(lengths, units, text, gains, shifts, weights, bias, kv_w, cross_bias)


def back_kernel(
    lens, q_ref, k_ref, v_ref, dc_ref, c_ref, log_ref, h_ref, text_ref, dkv_ref, in_ref, out_ref, _g0, _g1,
    o_ref, g0_ref, g1_ref, b_ref, in_f32, out_f32, dk_acc, dv_acc, w_acc,
):
    in_f32[...] = in_ref[...].astype(jnp.float32)
    out_f32[...] = out_ref[...].astype(jnp.float32)
    slot, turn_now = pl.program_id(0), pl.program_id(1)
    slot_rows, width = q_ref.shape
    heads = range(width // HEAD_DIM)

    @pl.when((slot == 0) & (turn_now == 0))
    def _():
        w_acc[...] = jnp.zeros_like(w_acc)
        b_ref[...] = jnp.zeros_like(b_ref)
        kv_grad = dot_tn(text_ref[...], dkv_ref[...]).astype(jnp.bfloat16)
        half, both = g1_ref.shape[0], dkv_ref.shape[1]
        g1_ref[:, :both] = kv_grad[:half]
        g1_ref[:, both:] = kv_grad[half:]

    @pl.when(turn_now == 0)
    def _():
        dk_acc[...] = jnp.zeros_like(dk_acc)
        dv_acc[...] = jnp.zeros_like(dv_acc)
        o_ref[:, :width] = jnp.zeros((slot_rows, width), jnp.bfloat16)

    def stack(values):
        return jnp.concatenate([pick_head(values, head) for head in heads], axis=0)

    def side_by_side(values):
        return jnp.concatenate([values[head : head + 1, :] for head in heads], axis=1)

    for i in range(slot_rows // BLOCK):
        rows = pl.ds(i * BLOCK, BLOCK)

        @pl.when((turn_now == i) & (i * BLOCK < lens[slot]))
        def _():
            count = (i + 1) * BLOCK
            keys, values = k_ref[:count, :], v_ref[:count, :]
            grads = dc_ref[rows, :]
            q_heads, g_heads = stack(q_ref[rows, :] * jnp.bfloat16(HEAD_DIM**-0.5)), stack(grads)
            owners = lax.broadcasted_iota(jnp.int32, (8, width), 0)
            lanes = lax.broadcasted_iota(jnp.int32, (8, width), 1)
            inner = lax.dot_general(
                jnp.where((lanes >= owners * HEAD_DIM) & (lanes < (owners + 1) * HEAD_DIM), 1.0, 0.0),
                grads.astype(jnp.float32) * c_ref[rows, :].astype(jnp.float32),
                (((1,), (1,)), ((), ())),
                precision=EXACT,
                preferred_element_type=jnp.float32,
            )
            weights = jnp.exp(mask_diagonal(dot_nt(keys, q_heads), 0) - side_by_side(log_ref[:, rows]))
            dv_acc[:count, :] += dot_nn(weights.astype(jnp.bfloat16), g_heads)
            score_grad = (weights * (dot_nt(values, g_heads) - side_by_side(inner))).astype(jnp.bfloat16)
            dk_acc[:count, :] += dot_nn(score_grad, q_heads)
            total = jnp.zeros((BLOCK, width), jnp.float32)
            for head in heads:
                total += dot_tn(score_grad[:, head * BLOCK : (head + 1) * BLOCK], pick_head(keys, head))
            q_grad = (total * HEAD_DIM**-0.5).astype(jnp.bfloat16)
            o_ref[rows, :width] = q_grad
            b_ref[0:1, :] += column_sum(q_grad.astype(jnp.float32))

    @pl.when(turn_now == pl.num_programs(1) - 1)
    def _():
        v_grad = dv_acc[...].astype(jnp.bfloat16)
        o_ref[:, width : 2 * width] = dk_acc[...].astype(jnp.bfloat16)
        o_ref[:, 2 * width :] = v_grad
        b_ref[1:2, :] += column_sum(v_grad.astype(jnp.float32))
        for first in range(0, h_ref.shape[1], BLOCK):
            w_acc[first : first + BLOCK, :] += dot_tn(h_ref[:, first : first + BLOCK], o_ref[...])

        @pl.when(slot == pl.num_programs(0) - 1)
        def _():
            g0_ref[...] = w_acc[...].astype(jnp.bfloat16)


def back(lengths, queries, keys, values, grads, context, logs, rows_in, text, dkv, in_sum, out_sum, g0, g1):
    rows, cols = queries.shape
    width = rows_in.shape[1]
    slots = lengths.shape[0]
    bf, f32 = jnp.bfloat16, jnp.float32
    shape = jax.ShapeDtypeStruct
    slot = lambda a: pl.BlockSpec((a.shape[0] // slots, a.shape[1]), lambda s, i, *_: (s, 0))
    blocks = rows // slots // BLOCK
    piece = lambda a: pl.BlockSpec((a.shape[0] // (slots * blocks), a.shape[1]), lambda s, i, *_: (s * blocks + i, 0))
    whole = lambda a: pl.BlockSpec(a.shape, lambda s, i, *_: (0, 0))
    hbm = pl.BlockSpec(memory_space=pl.ANY)
    half = text.shape[1] // 2
    return pl.pallas_call(
        back_kernel,
        grid_spec=pltpu.PrefetchScalarGridSpec(
            num_scalar_prefetch=1,
            grid=(slots, blocks),
            in_specs=[slot(queries)] * 5
            + [pl.BlockSpec((8, rows // slots), lambda s, i, *_: (0, s))]
            + [slot(rows_in), whole(text), whole(dkv), piece(in_sum), piece(out_sum), hbm, hbm],
            out_specs=[
                pl.BlockSpec((rows // slots, 3 * cols), lambda s, i, *_: (s, 0)),
                pl.BlockSpec((width, 3 * cols), lambda s, i, *_: (0, 0)),
                pl.BlockSpec((half, width), lambda s, i, *_: (1, 0)),
                pl.BlockSpec((2, cols), lambda s, i, *_: (0, 0)),
                piece(in_sum),
                piece(out_sum),
            ],
            scratch_shapes=[pltpu.VMEM((rows // slots, cols), f32)] * 2 + [pltpu.VMEM((width, 3 * cols), f32)],
        ),
        out_shape=[
            shape((rows, 3 * cols), bf),
            pltpu.HBM(g0.shape, bf),
            pltpu.HBM(g1.shape, bf),
            shape((2, cols), f32),
            shape(in_sum.shape, f32),
            shape(out_sum.shape, f32),
        ],
        input_output_aliases={12: 1, 13: 2},
        compiler_params=pltpu.CompilerParams(vmem_limit_bytes=60 * MIB),
        cost_estimate=pl.CostEstimate(flops=30 * 10**9, bytes_accessed=40 * MIB, transcendentals=8 * MIB),
        name="back",
    )(lengths, queries, keys, values, grads, context, logs, rows_in, text, dkv, in_sum, out_sum, g0, g1)


def place():
    index = lax.axis_index("narrow")
    core = index + 1 - 2 * (index % 2)
    return index, core, (index + 2) % NARROW, (core + 2) % NARROW


def greet(*wide_peers):
    _, core, cross, _ = place()
    barrier = pltpu.get_barrier_semaphore()
    for peer in (core, cross):
        pl.semaphore_signal(barrier, inc=1, device_id={"narrow": peer}, device_id_type=MESH)
    for peer in wide_peers:
        pl.semaphore_signal(barrier, inc=1, device_id={"wide": peer}, device_id_type=MESH)
    pl.semaphore_wait(barrier, 2 + len(wide_peers))


def remote(source, target, sems, kind, step, peer, axis="narrow"):
    return pltpu.make_async_remote_copy(
        src_ref=source,
        dst_ref=target,
        send_sem=sems.at[0, kind, step],
        recv_sem=sems.at[1, kind, step],
        device_id={axis: peer},
        device_id_type=MESH,
    )


def ring_place(count):
    wide = lax.axis_index("wide")
    odd, half = wide % 2, wide // 2
    spot = odd * (half + 1) + (1 - odd) * ((count - half) % count)

    def at(where):
        high = ((where + count - 1) % count) // (count // 2)
        return (1 - high) * (2 * where - 1) + high * ((2 * (count - where)) % (2 * count))

    return spot, at((spot + 1) % count), at((spot + count - 1) % count)


class Ring:
    UNITS = 4

    def __init__(self, count, sources, outs, view, arrived, held, sems, fetch_sems, keep_sems):
        self.count, self.sources, self.outs, self.view = count, sources, outs, view
        self.arrived, self.held, self.sems = arrived, held, sems
        self.fetch_sems, self.keep_sems = fetch_sems, keep_sems
        spot, following, previous = ring_place(count)
        self.spots = (spot, (count - spot) % count)
        self.peers = (following, previous)

    def block(self, refs, unit, back_by):
        shard = (self.spots[unit // 2] + 2 * self.count - back_by) % self.count
        return self.view(refs[unit // 2], unit // 2, unit % 2, shard)

    def send(self, source, target, kind, unit, step):
        return remote(source, target, self.sems, kind * self.UNITS + unit, step, self.peers[unit // 2], "wide")

    def sum_copy(self, unit, step, first=False):
        source = self.block(self.sources, unit, 0) if first else self.arrived.at[unit, jnp.maximum(step - 1, 0)]
        return self.send(source, self.arrived.at[unit, step], 0, unit, step)

    def fetch(self, unit, step):
        slot = step % 2
        return pltpu.make_async_copy(
            self.block(self.sources, unit, step + 1), self.held.at[unit, slot], self.fetch_sems.at[unit, slot]
        )

    def keep(self, unit):
        return pltpu.make_async_copy(
            self.arrived.at[unit, self.count - 2], self.block(self.outs, unit, self.count - 1), self.keep_sems.at[unit]
        )

    def spread_copy(self, unit, step, first=False):
        target = self.block(self.outs, unit, self.count - 1 + step)
        source = self.arrived.at[unit, self.count - 2] if first else target
        return self.send(source, target, 1, unit, step)

    def start(self):
        for unit in range(self.UNITS):
            self.sum_copy(unit, 0, True).start()
            self.fetch(unit, 0).start()
            self.fetch(unit, 1).start()

    def serve(self, turn, unit):
        last = self.count - 2

        @pl.when(turn <= last)
        def _():
            self.sum_copy(unit, turn).wait_recv()
            self.fetch(unit, turn).wait()
            total = self.held[unit, turn % 2].astype(jnp.float32) + self.arrived[unit, turn].astype(jnp.float32)
            self.arrived[unit, turn] = total.astype(jnp.bfloat16)

            @pl.when(turn < last)
            def _():
                self.sum_copy(unit, turn + 1).start()

            @pl.when(turn < last - 1)
            def _():
                self.fetch(unit, turn + 2).start()

            @pl.when(turn == last)
            def _():
                self.spread_copy(unit, 0, True).start()
                self.keep(unit).start()

        @pl.when((turn > last) & (turn <= 2 * last + 1))
        def _():
            step = turn - last - 1
            self.spread_copy(unit, step).wait_recv()

            @pl.when(step < last)
            def _():
                self.spread_copy(unit, step + 1).start()

    def finish(self):
        for unit in range(self.UNITS):
            self.keep(unit).wait()

        def body(step, carry):
            for unit in range(self.UNITS):
                self.sum_copy(unit, step).wait_send()
                self.spread_copy(unit, step).wait_send()
            return carry

        lax.fori_loop(0, self.count - 1, body, 0)


def ring_scratch(count, block):
    return [
        pltpu.VMEM((Ring.UNITS, count - 1) + block, jnp.bfloat16),
        pltpu.VMEM((Ring.UNITS, 2) + block, jnp.bfloat16),
        pltpu.SemaphoreType.DMA((2, 2 * Ring.UNITS, count - 1)),
        pltpu.SemaphoreType.DMA((Ring.UNITS, 2)),
        pltpu.SemaphoreType.DMA((Ring.UNITS,)),
    ]


def own_copy(whole, own, sem):
    size = own.shape[0]
    first = pl.multiple_of(lax.axis_index("narrow") * size, size)
    return pltpu.make_async_copy(whole.at[pl.ds(first, size), :], own, sem)


def moves(sources, targets, sems):
    pairs = list(zip(sources, targets, strict=True))
    return [pltpu.make_async_copy(a, b, sems.at[slot]) for slot, (a, b) in enumerate(pairs)]


class Hop:
    KINDS = 6

    def __init__(self, part, from_core, from_cross, full, sems, chunk):
        self.part, self.from_core, self.from_cross = part, from_core, from_cross
        self.full, self.sems, self.chunk = full, sems, chunk
        self.own = part.shape[0] // NARROW
        self.index, self.core, self.cross, self.diagonal = place()

    def rows(self, owner, step):
        return pl.ds(pl.multiple_of(owner * self.own + step * self.chunk, self.chunk), self.chunk)

    def own_rows(self, step):
        return pl.ds(pl.multiple_of(step * self.chunk, self.chunk), self.chunk)

    def core_copies(self, step):
        return [
            remote(self.part.at[self.rows(owner, step)], self.from_core.at[step, slot], self.sems, slot, step, self.core)
            for slot, owner in enumerate((self.core, self.diagonal))
        ]

    def cross_copy(self, step):
        return remote(
            self.part.at[self.rows(self.cross, step)], self.from_cross.at[step], self.sems, 2, step, self.cross
        )

    def gather_copy(self, step, kind):
        owner = self.cross if kind == 5 else self.index
        rows = self.full.at[self.rows(owner, step)]
        return remote(rows, rows, self.sems, kind, step, self.cross if kind == 3 else self.core)

    def send_core(self, step):
        for copy in self.core_copies(step):
            copy.start()

    def send_cross(self, step):
        for copy in self.core_copies(step):
            copy.wait_recv()
        total = self.part[self.rows(self.cross, step), :].astype(jnp.float32)
        total += self.from_core[step, 1].astype(jnp.float32)
        self.part[self.rows(self.cross, step), :] = total.astype(jnp.bfloat16)
        self.cross_copy(step).start()

    def result(self, step):
        total = self.part[self.rows(self.index, step), :].astype(jnp.float32)
        total += self.from_core[step, 0].astype(jnp.float32)
        self.cross_copy(step).wait_recv()
        return total + self.from_cross[step].astype(jnp.float32)

    def send_gather(self, step, values):
        self.full[self.rows(self.index, step), :] = values
        self.gather_copy(step, 3).start()
        self.gather_copy(step, 4).start()

    def forward(self, step):
        self.gather_copy(step, 3).wait_recv()
        self.gather_copy(step, 5).start()

    def gathered(self, step):
        self.gather_copy(step, 4).wait_recv()
        self.gather_copy(step, 5).wait_recv()

    def sent(self, step):
        for copy in self.core_copies(step):
            copy.wait_send()
        self.cross_copy(step).wait_send()

    def finish(self, step, gather=True, parts=True):
        if parts:
            self.sent(step)
        if gather:
            for kind in (3, 4, 5):
                self.gather_copy(step, kind).wait_send()

    def take(self, ref, step):
        return jnp.concatenate([ref[self.rows(owner, step), :] for owner in range(NARROW)], axis=0)

    def put(self, ref, step, values):
        for owner in range(NARROW):
            ref[self.rows(owner, step), :] = values[owner * self.chunk : (owner + 1) * self.chunk]


def hop_scratch(own, chunk, width):
    steps = own // chunk
    return [
        pltpu.VMEM((steps, 2, chunk, width), jnp.bfloat16),
        pltpu.VMEM((steps, chunk, width), jnp.bfloat16),
        pltpu.SemaphoreType.DMA((2, Hop.KINDS, steps)),
    ]


def stages(steps, work, ring=None, extra=None, ticks=0):
    ticks = max(ticks, steps + max(delay for delay, _ in work))
    per_tick = 0 if ring is None else -(-2 * (ring.count - 1) // ticks)

    def body(tick, carry):
        for number, (delay, stage) in enumerate(work):
            step = tick - delay

            @pl.when((step >= 0) & (step < steps))
            def _():
                stage(step)

            unit = (number + 1) * Ring.UNITS // len(work) - 1
            if per_tick and unit != number * Ring.UNITS // len(work) - 1:
                if per_tick == 1:
                    ring.serve(tick, unit)
                else:
                    lax.fori_loop(0, per_tick, lambda i, c: (ring.serve(tick * per_tick + i, unit), c)[1], 0)
            if extra is not None and number in (len(work) // 2, len(work) - 1):
                extra(2 * tick + (number == len(work) - 1))
        return carry

    lax.fori_loop(0, ticks, body, 0)


def middle_kernel(
    all_units, out_grad, far_in, far_out, far_so, far_cq, far_co, lens, text_lens,
    c1, kv2, gains, shifts, biases, bias, b_in,
    ffn_part, third, in_g, out_g, far_h2, far_q2, far_c2, far_x1, far_x2, in_bias_g,
    h2, q2, c2, x1, x2, leave_sem, units, own_sem, so_w, cq_w, co_w, small_sem, w_in, w_out, weight_sem, grads_in, grads_sem, give, give_sem, in_acc, out_acc,
    part, h3, core1, fromx1, sem1, core2, fromx2, sem2,
):
    steps, chunk, width = fromx1.shape
    cols = q2.shape[1]
    slots = text_lens.shape[0]
    texts = kv2.shape[0] // slots
    slot_rows = h2.shape[0] // slots
    hidden_count = w_out.shape[0]
    near = [
        pltpu.make_async_copy(source, target, small_sem.at[slot])
        for slot, (source, target) in enumerate(((far_so, so_w), (far_cq, cq_w), (far_co, co_w)))
    ]
    for fetch in near:
        fetch.start()
    fetches = [
        own_copy(all_units, units, own_sem),
        pltpu.make_async_copy(far_in, w_in, weight_sem.at[0]),
        pltpu.make_async_copy(far_out, w_out, weight_sem.at[1]),
    ]
    fetches[0].start()
    greet()
    one = Hop(part, core1, fromx1, h2, sem1, chunk)
    two = Hop(part, core2, fromx2, h3, sem2, chunk)
    scale = jnp.bfloat16(HEAD_DIM**-0.5)
    in_bias_g[...] = jnp.zeros_like(in_bias_g)
    for fetch in near:
        fetch.wait()

    leaving = moves((h2, q2, c2, x1, x2), (far_h2, far_q2, far_c2, far_x1, far_x2), leave_sem)

    def grad_copies(step):
        slot = step % 2
        return [
            pltpu.make_async_copy(
                out_grad.at[one.rows(owner, step), :],
                grads_in.at[slot, pl.ds(owner * chunk, chunk), :],
                grads_sem.at[slot, owner],
            )
            for owner in range(NARROW)
        ]

    def give_copies(step, kind):
        slot = step % 2
        return [
            pltpu.make_async_copy(
                give.at[kind, slot, pl.ds(owner * chunk, chunk), :],
                (ffn_part, third)[kind].at[one.rows(owner, step), :],
                give_sem.at[kind, slot, owner],
            )
            for owner in range(NARROW)
        ]

    def project(step):
        one.put(part, step, dot_nn(one.take(c1, step), so_w[...]).astype(jnp.bfloat16))
        one.send_core(step)
        for when, ref in ((1, in_acc), (2, out_acc)):

            @pl.when(step == when)
            def _():
                fetches[when].start()
                ref[...] = jnp.zeros_like(ref)

    def norm_one(step):
        @pl.when(step == 0)
        def _():
            fetches[0].wait()

        rows = one.own_rows(step)
        resid = units[rows, :].astype(jnp.float32) + one.result(step) + biases[0:1, :]
        x1[rows, :] = resid
        one.send_gather(step, norm_forward(resid, gains[1:2, :], shifts[1:2, :])[0].astype(jnp.bfloat16))

    def cross(step):
        one.gathered(step)
        queries = (dot_nn(one.take(h2, step), cq_w[...]) + bias[0:1, :]).astype(jnp.bfloat16)
        one.put(q2, step, queries)
        scaled = queries * scale
        count = queries.shape[0] // slots
        place_of = lax.broadcasted_iota(jnp.int32, (count * (cols // HEAD_DIM), texts), 1)
        context = []
        for slot in range(slots):
            mine = scaled[slot * count : (slot + 1) * count]
            keys = kv2[slot * texts : (slot + 1) * texts, :cols]
            values = kv2[slot * texts : (slot + 1) * texts, cols:]
            heads = range(cols // HEAD_DIM)
            scores = dot_nt(jnp.concatenate([pick_head(mine, head) for head in heads], axis=0), keys)
            scores = jnp.where(place_of < text_lens[slot], scores, MASKED_SCORE)
            weights = jnp.exp(scores - jnp.max(scores, axis=1, keepdims=True))
            norm = jnp.sum(weights, axis=1, keepdims=True)
            mixed = dot_nn(weights.astype(jnp.bfloat16), values) * (1.0 / norm)
            total = jnp.zeros((count, cols), jnp.float32)
            for head in heads:
                total += pick_head(mixed[head * count : (head + 1) * count], head)
            context.append(total.astype(jnp.bfloat16))
        context = jnp.concatenate(context, axis=0)
        one.put(c2, step, context)
        one.sent(step)
        two.put(part, step, dot_nn(context, co_w[...]).astype(jnp.bfloat16))
        two.send_core(step)

    def norm_two(step):
        rows = one.own_rows(step)
        resid = x1[rows, :] + two.result(step) + biases[1:2, :]
        x2[rows, :] = resid
        two.send_gather(step, norm_forward(resid, gains[2:3, :], shifts[2:3, :])[0].astype(jnp.bfloat16))

    def forward_two(step):
        two.forward(step)
        for copy in grad_copies(step):
            copy.start()

    def ffn(step):
        @pl.when(step == 0)
        def _():
            fetches[1].wait()
            fetches[2].wait()

        @pl.when(step == steps - 3)
        def _():
            for copy in leaving:
                copy.start()

        two.gathered(step)
        for copy in grad_copies(step):
            copy.wait()
        rows = two.take(h3, step)
        place_in = lax.broadcasted_iota(jnp.int32, (chunk, width), 0) + step * chunk
        grads = []
        for owner in range(NARROW):
            first = owner * two.own
            valid = place_in < lens[first // slot_rows] - first % slot_rows
            values = grads_in[step % 2, owner * chunk : (owner + 1) * chunk, :]
            grads.append(jnp.where(valid, values.astype(jnp.float32), 0.0).astype(jnp.bfloat16))
        grads = jnp.concatenate(grads, axis=0)
        out = jnp.zeros(rows.shape, jnp.float32)
        back_out = jnp.zeros(rows.shape, jnp.float32)
        for begin in range(0, hidden_count, HIDDEN):
            some = slice(begin, begin + HIDDEN)
            pre = dot_nn(rows, w_in[:, some]) + b_in[:, some]
            cdf = 0.5 + 0.5 * lax.erf(pre * (0.5**0.5))
            pdf = jnp.exp(-0.5 * pre * pre) * 0.3989422804014327
            hidden = (pre * cdf).astype(jnp.bfloat16)
            pre_low = ((cdf + pre * pdf) * dot_nt(grads, w_out[some, :])).astype(jnp.bfloat16)
            in_bias_g[:, some] += column_sum(pre_low.astype(jnp.float32))
            out += dot_nn(hidden, w_out[some, :])
            back_out += dot_nt(pre_low, w_in[:, some])
            out_acc[some, :] += dot_tn(hidden, grads)
            side, place_at = divmod(begin, width)
            in_acc[side * width : (side + 1) * width, place_at : place_at + HIDDEN] += dot_tn(rows, pre_low)

        @pl.when(step >= 2)
        def _():
            for kind in range(2):
                for copy in give_copies(step - 2, kind):
                    copy.wait()

        give[0, step % 2] = out.astype(jnp.bfloat16)
        give[1, step % 2] = back_out.astype(jnp.bfloat16)
        for kind in range(2):
            for copy in give_copies(step, kind):
                copy.start()

    stages(
        steps,
        [
            (0, project), (1, one.send_cross), (2, norm_one), (3, one.forward), (4, cross),
            (5, two.send_cross), (6, norm_two), (7, forward_two), (8, ffn),
        ],
    )

    def finish(step, carry):
        one.finish(step, True, False)
        two.finish(step)
        return carry

    lax.fori_loop(0, steps, finish, 0)
    part[...] = out_acc[...].astype(jnp.bfloat16)
    results = [pltpu.make_async_copy(part, out_g, weight_sem.at[0])]
    results[0].start()
    h3[...] = in_acc[...].astype(jnp.bfloat16)
    for side in range(hidden_count // width):
        here = pl.ds(side * width, width)
        results.append(pltpu.make_async_copy(h3.at[here, :], in_g.at[:, here], weight_sem.at[1 + side]))
        results[-1].start()
    for step in (steps - 2, steps - 1):
        for kind in range(2):
            for copy in give_copies(step, kind):
                copy.wait()
    for copy in results + leaving:
        copy.wait()


def middle(units, out_grad, w_in, w_out, so_w, cq_w, co_w, lens, text_lens, c1, kv2, gains, shifts, biases, bias, b_in):
    rows, cols = c1.shape
    own, width = rows // NARROW, units.shape[1]
    hidden_count = w_out.shape[0]
    chunk = own // STEPS
    bf, f32 = jnp.bfloat16, jnp.float32
    shape = jax.ShapeDtypeStruct
    vmem = pl.BlockSpec(memory_space=pltpu.VMEM)
    hbm = pl.BlockSpec(memory_space=pl.ANY)
    hop = hop_scratch(own, chunk, width)
    dma = pltpu.SemaphoreType.DMA
    return pl.pallas_call(
        middle_kernel,
        in_specs=[hbm] * 7 + [pl.BlockSpec(memory_space=pltpu.SMEM)] * 2 + [vmem] * 7,
        out_specs=[hbm] * 9 + [vmem],
        out_shape=[
            pltpu.HBM((rows, width), bf),
            pltpu.HBM((rows, width), bf),
            pltpu.HBM((width, hidden_count), bf),
            pltpu.HBM((hidden_count, width), bf),
            pltpu.HBM((rows, width), bf),
            pltpu.HBM((rows, cols), bf),
            pltpu.HBM((rows, cols), bf),
            pltpu.HBM((own, width), f32),
            pltpu.HBM((own, width), f32),
            shape((1, hidden_count), f32),
        ],
        scratch_shapes=[
            pltpu.VMEM((rows, width), bf),
            pltpu.VMEM((rows, cols), bf),
            pltpu.VMEM((rows, cols), bf),
            pltpu.VMEM((own, width), f32),
            pltpu.VMEM((own, width), f32),
            dma((5,)),
            pltpu.VMEM((own, width), bf),
            dma,
            pltpu.VMEM(so_w.shape, bf),
            pltpu.VMEM(cq_w.shape, bf),
            pltpu.VMEM(co_w.shape, bf),
            dma((3,)),
            pltpu.VMEM((width, hidden_count), bf),
            pltpu.VMEM((hidden_count, width), bf),
            dma((1 + hidden_count // width,)),
            pltpu.VMEM((2, NARROW * chunk, width), bf),
            dma((2, NARROW)),
            pltpu.VMEM((2, 2, NARROW * chunk, width), bf),
            dma((2, 2, NARROW)),
            pltpu.VMEM((hidden_count, width), f32),
            pltpu.VMEM((hidden_count, width), f32),
            pltpu.VMEM((rows, width), bf),
            pltpu.VMEM((rows, width), bf),
        ]
        + hop
        + hop,
        compiler_params=pltpu.CompilerParams(collective_id=0, has_side_effects=True, vmem_limit_bytes=60 * MIB),
        cost_estimate=pl.CostEstimate(flops=100 * 10**9, bytes_accessed=48 * MIB, transcendentals=8 * MIB),
        name="middle",
    )(
        units, out_grad, w_in, w_out, so_w, cq_w, co_w, lens, text_lens, c1, kv2, gains, shifts, biases, bias,
        b_in.reshape(1, -1),
    )


class FarHop(Hop):
    def fetch(self, mine, theirs, sems):
        self.mine, self.theirs = mine, theirs
        rows = lambda owner: pl.ds(pl.multiple_of(owner * self.own, self.own), self.own)
        self.fetches = [
            pltpu.make_async_copy(self.part.at[rows(owner)], ref, sems.at[slot])
            for slot, (owner, ref) in enumerate(((self.index, mine), (self.cross, theirs)))
        ]
        for copy in self.fetches:
            copy.start()

    def fetched(self):
        for copy in self.fetches:
            copy.wait()

    def cross_copy(self, step):
        return remote(
            self.theirs.at[self.own_rows(step)], self.from_cross.at[step], self.sems, 2, step, self.cross
        )

    def send_cross(self, step):
        for copy in self.core_copies(step):
            copy.wait_recv()
        total = self.theirs[self.own_rows(step), :].astype(jnp.float32)
        total += self.from_core[step, 1].astype(jnp.float32)
        self.theirs[self.own_rows(step), :] = total.astype(jnp.bfloat16)
        self.cross_copy(step).start()

    def result(self, step):
        total = self.mine[self.own_rows(step), :].astype(jnp.float32)
        total += self.from_core[step, 0].astype(jnp.float32)
        self.cross_copy(step).wait_recv()
        return total + self.from_cross[step].astype(jnp.float32)


def left_here(lens, own, rows):
    first = lax.axis_index("narrow") * own
    slot_rows = rows // lens.shape[0]
    return lens[first // slot_rows] - first % slot_rows


def row_of(step, chunk, width):
    return lax.broadcasted_iota(jnp.int32, (chunk, width), 0) + step * chunk


def turn_kernel(
    third, ffn_part, in_g, out_g, out_grad, lens, text_lens,
    far_x1, far_x2, far_h2, far_q2, far_c2, far_kv2, far_c1, gains, biases, far_co, far_cq, far_so,
    in_sum, out_sum, g0, g1, y, dx1, dc1, dkv, bias_g, stats,
    x1, x2, h2, q2, c2, kv2, c1, co_w, cq_w, so_w, arrive_sem, cq_g, give_sem, e_own, own_sem, mine3, theirs3, core3, fromx3, sem3, mine4, theirs4, core4, fromx4, sem4,
    part5, core5, fromx5, sem5, full3, full5, co_acc, cq_acc, so_acc, dkv_acc, fetch_sem,
    *ring_refs, count,
):
    steps, chunk, width = fromx5.shape
    cols = q2.shape[1]
    slots = bias_g.shape[0]
    texts = kv2.shape[0] // slots

    def ring_view(ref, way, half, shard):
        high = width // count
        if way == 0:
            return ref.at[pl.ds(pl.multiple_of(shard * high, high), high), pl.ds(half * width, width)]
        return ref.at[pl.ds(pl.multiple_of(shard * 2 * high + half * high, high), high), :]

    ring = Ring(count, (in_g, out_g), (in_sum, out_sum), ring_view, *ring_refs)
    fetch = own_copy(out_grad, e_own, own_sem)
    fetch.start()
    greet(*ring.peers)
    ring.start()
    three = FarHop(third, core3, fromx3, full3, sem3, chunk)
    four = FarHop(ffn_part, core4, fromx4, None, sem4, chunk)
    five = Hop(part5, core5, fromx5, full5, sem5, chunk)
    arriving = moves(
        (far_x2, far_x1, far_h2, far_q2, far_c2, far_kv2, far_c1, far_co, far_cq, far_so),
        (x2, x1, h2, q2, c2, kv2, c1, co_w, cq_w, so_w),
        arrive_sem,
    )
    three.fetch(mine3, theirs3, fetch_sem.at[0])
    for copy in arriving:
        copy.start()
    four.fetch(mine4, theirs4, fetch_sem.at[1])

    def start(step, carry):
        three.send_core(step)
        four.send_core(step)
        return carry

    lax.fori_loop(0, steps, start, 0)
    for ref in (co_acc, cq_acc, so_acc, dkv_acc, bias_g, stats):
        ref[...] = jnp.zeros_like(ref)
    three.fetched()
    four.fetched()
    fetch.wait()
    for copy in arriving:
        copy.wait()
    valid_rows = left_here(lens, x1.shape[0], h2.shape[0])
    scale = jnp.bfloat16(HEAD_DIM**-0.5)

    def norm_three(step):
        rows = three.own_rows(step)
        grad_in = three.result(step)
        _, normed, inv_std = norm_forward(x2[rows, :], gains[2:3, :], gains[2:3, :])
        stats[0:1, :] += column_sum(grad_in * normed)
        stats[1:2, :] += column_sum(grad_in)
        above = jnp.where(row_of(step, chunk, width) < valid_rows, e_own[rows, :].astype(jnp.float32), 0.0)
        total = above + norm_backward(grad_in, normed, inv_std, gains[2:3, :])
        stats[2:3, :] += column_sum(above)
        stats[3:4, :] += column_sum(total)
        dx1[rows, :] = total
        three.send_gather(step, total.astype(jnp.bfloat16))

    def cross(step):
        three.gathered(step)
        grads = three.take(full3, step)
        co_acc[...] += dot_tn(three.take(c2, step), grads)
        context = dot_nt(grads, co_w[...]).astype(jnp.bfloat16)
        queries = three.take(q2, step) * scale
        count = queries.shape[0] // slots
        place_of = lax.broadcasted_iota(jnp.int32, (texts, count), 0)
        q_grad = []
        for slot in range(slots):
            rows = slice(slot * count, (slot + 1) * count)
            texts_here = slice(slot * texts, (slot + 1) * texts)
            keys, values = kv2[texts_here, :cols], kv2[texts_here, cols:]
            total = jnp.zeros((count, cols), jnp.float32)
            for head in range(cols // HEAD_DIM):
                q_head, g_head = pick_head(queries[rows], head), pick_head(context[rows], head)
                scores = jnp.where(place_of < text_lens[slot], dot_nt(keys, q_head), MASKED_SCORE)
                weights = jnp.exp(scores - jnp.max(scores, axis=0, keepdims=True))
                weights = weights * (1.0 / jnp.sum(weights, axis=0, keepdims=True))
                dkv_acc[texts_here, cols:] += dot_nn(weights.astype(jnp.bfloat16), g_head)
                weight_grad = dot_nt(values, g_head)
                inner = jnp.sum(weights * weight_grad, axis=0, keepdims=True)
                score_grad = (weights * (weight_grad - inner)).astype(jnp.bfloat16)
                dkv_acc[texts_here, :cols] += dot_nn(score_grad, q_head)
                total += dot_tn(score_grad, pick_head(keys, head))
            q_grad.append((total * HEAD_DIM**-0.5).astype(jnp.bfloat16))
        q_grad = jnp.concatenate(q_grad, axis=0)
        five.put(part5, step, dot_nt(q_grad, cq_w[...]).astype(jnp.bfloat16))
        five.send_core(step)
        bias_g[0:1, :] += column_sum(q_grad.astype(jnp.float32))
        cq_acc[...] += dot_tn(five.take(h2, step), q_grad)

    def norm_two(step):
        rows = five.own_rows(step)
        grad_in = five.result(step)
        _, normed, inv_std = norm_forward(x1[rows, :], gains[1:2, :], gains[1:2, :])
        stats[4:5, :] += column_sum(grad_in * normed)
        stats[5:6, :] += column_sum(grad_in)
        total = dx1[rows, :] + norm_backward(grad_in, normed, inv_std, gains[1:2, :])
        stats[6:7, :] += column_sum(total)
        dx1[rows, :] = total
        five.send_gather(step, total.astype(jnp.bfloat16))

    def last(step):
        five.gathered(step)
        grads = five.take(full5, step)
        dc1_rows = dot_nt(grads, so_w[...]).astype(jnp.bfloat16)
        five.put(dc1, step, dc1_rows)
        so_acc[...] += dot_tn(five.take(c1, step), grads)

    def output(step):
        rows = four.own_rows(step)
        total = x2[rows, :] + four.result(step) + biases[2:3, :]
        y[rows, :] = jnp.where(row_of(step, chunk, width) < valid_rows, total, 0.0).astype(jnp.bfloat16)

    half = steps // 2
    late = steps + 2

    def side(half_tick):
        tick = half_tick // 2
        for begin, first in ((0, 0), (late, half)):
            for ahead, work in ((1, output), (0, four.send_cross)):
                step = tick - begin - ahead

                @pl.when((step >= 0) & (step < half) & (half_tick % 2 == 1))
                def _():
                    work(first + step)

    stages(
        steps,
        list(
            enumerate(
                [
                    three.send_cross, norm_three, three.forward, cross,
                    five.send_cross, norm_two, five.forward, last,
                ]
            )
        ),
        ring,
        side,
        late + half + 1,
    )
    dkv[...] = dkv_acc[...].astype(jnp.bfloat16)
    bias_g[1:2, :] = column_sum(dkv[:, cols:].astype(jnp.float32))
    mine4[:cols, :] = co_acc[...].astype(jnp.bfloat16)
    cq_g[...] = cq_acc[...].astype(jnp.bfloat16)
    mine4[cols : 2 * cols, :] = so_acc[...].astype(jnp.bfloat16)
    gives = [
        pltpu.make_async_copy(cq_g, g0.at[:, pl.ds(width - cols, cols)], give_sem.at[0]),
        pltpu.make_async_copy(mine4.at[pl.ds(0, 2 * cols), :], g1.at[pl.ds(0, 2 * cols), :], give_sem.at[1]),
    ]
    for give in gives:
        give.start()

    def finish(step, carry):
        three.finish(step)
        four.finish(step, False)
        five.finish(step)
        return carry

    lax.fori_loop(0, steps, finish, 0)
    ring.finish()
    for give in gives:
        give.wait()


def turn(
    count, third, ffn_part, in_g, out_g, out_grad, lens, text_lens,
    x1, x2, h2, q2, c2, kv2, c1, gains, biases, co_w, cq_w, so_w,
):
    rows, cols = c1.shape
    own, width = x1.shape
    chunk = own // STEPS
    bf, f32 = jnp.bfloat16, jnp.float32
    shape = jax.ShapeDtypeStruct
    vmem = pl.BlockSpec(memory_space=pltpu.VMEM)
    hbm = pl.BlockSpec(memory_space=pl.ANY)
    hop = hop_scratch(own, chunk, width)
    far = [pltpu.VMEM((own, width), bf)] * 2 + hop
    return pl.pallas_call(
        functools.partial(turn_kernel, count=count),
        in_specs=[hbm] * 5 + [pl.BlockSpec(memory_space=pltpu.SMEM)] * 2 + [hbm] * 7 + [vmem] * 2 + [hbm] * 3,
        out_specs=[hbm] * 4 + [vmem] * 6,
        out_shape=[
            pltpu.HBM(in_g.shape, bf),
            pltpu.HBM(out_g.shape, bf),
            pltpu.HBM((width, width), bf),
            pltpu.HBM((width, width), bf),
            shape((own, width), bf),
            shape((own, width), f32),
            shape((rows, cols), bf),
            shape(kv2.shape, bf),
            shape((2, cols), f32),
            shape((8, width), f32),
        ],
        scratch_shapes=[pltpu.VMEM(a.shape, a.dtype) for a in (x1, x2, h2, q2, c2, kv2, c1, co_w, cq_w, so_w)]
        + [
            pltpu.SemaphoreType.DMA((10,)),
            pltpu.VMEM((width, cols), bf),
            pltpu.SemaphoreType.DMA((2,)),
            pltpu.VMEM((own, width), bf),
            pltpu.SemaphoreType.DMA,
        ]
        + far
        + far
        + [pltpu.VMEM((rows, width), bf)]
        + hop
        + [pltpu.VMEM((rows, width), bf)] * 2
        + [
            pltpu.VMEM((cols, width), f32),
            pltpu.VMEM((width, cols), f32),
            pltpu.VMEM((cols, width), f32),
            pltpu.VMEM(kv2.shape, f32),
            pltpu.SemaphoreType.DMA((2, 2)),
        ]
        + ring_scratch(count, (width // count, width)),
        compiler_params=pltpu.CompilerParams(collective_id=1, has_side_effects=True, vmem_limit_bytes=60 * MIB),
        cost_estimate=pl.CostEstimate(flops=100 * 10**9, bytes_accessed=24 * MIB, transcendentals=4 * MIB),
        name="turn",
    )(
        third, ffn_part, in_g, out_g, out_grad, lens, text_lens,
        x1, x2, h2, q2, c2, kv2, c1, gains, biases, co_w, cq_w, so_w,
    )


SMALL = 16
NORM_ROWS = 9


class Small:
    def __init__(self, count, block, near, far, sems):
        self.count, self.mine, self.near, self.far, self.sems = count, block, near, far, sems
        self.index, self.core, self.cross, _ = place()
        self.spot, *self.peers = ring_place(count)

    def near_copy(self, kind):
        owner = self.cross if kind == 2 else self.index
        return remote(self.near.at[owner], self.near.at[owner], self.sems, 0, kind, (self.cross, self.core, self.core)[kind])

    def far_copy(self, way, step):
        block = self.far.at[(self.spot + (2 * way - 1) * step + self.count) % self.count]
        return remote(block, block, self.sems, 1 + way, step, self.peers[way], "wide")

    def begin(self):
        self.near[self.index] = self.mine[...]
        self.near_copy(0).start()
        self.near_copy(1).start()

    def forward(self):
        self.near_copy(0).wait_recv()
        self.near_copy(2).start()

    def launch(self):
        self.near_copy(1).wait_recv()
        self.near_copy(2).wait_recv()
        both = self.near[0]
        for owner in range(1, NARROW):
            both += self.near[owner]
        row = lax.broadcasted_iota(jnp.int32, both.shape, 0)
        self.far[self.spot] = jnp.where(row < SMALL - NORM_ROWS, self.mine[...], both)
        self.far_copy(0, 0).start()
        self.far_copy(1, 0).start()

    def rotate(self, step):
        for way in range(2):
            steps = self.count // 2 - way

            @pl.when(step < steps)
            def _():
                self.far_copy(way, step).wait_recv()

            @pl.when(step < steps - 1)
            def _():
                self.far_copy(way, step + 1).start()

    def finish(self, out):
        for kind in range(3):
            self.near_copy(kind).wait_send()

        for way in range(2):

            def body(step, carry):
                self.far_copy(way, step).wait_send()
                return carry

            lax.fori_loop(0, self.count // 2 - way, body, 0)
        out[...] = jnp.zeros_like(out)

        def add(spot, carry):
            out[...] += self.far[spot]
            return carry

        lax.fori_loop(0, self.count, add, 0)


def last_kernel(
    g0, g1, all_units, far_dqkv, far_dkv, far_dx1, far_qkv, far_kv, self_b, cross_b, ffn_b, stats, gains,
    sum0, sum1, units_g, text_g, small_sum,
    dqkv, dkv, dx1, qkv_w, kv_w, arrive_sem, units, own_sem, part6, core6, fromx6, sem6, part7, core7, fromx7, sem7,
    block, near, far, small_sem, *ring_refs, count,
):
    steps, chunk, width = fromx6.shape
    text_steps = fromx7.shape[0]

    def ring_view(ref, way, half, shard):
        high = width // count
        return ref.at[pl.ds(pl.multiple_of(shard * high, high), high), pl.ds(half * (width // 2), width // 2)]

    ring = Ring(count, (g0, g1), (sum0, sum1), ring_view, *ring_refs)
    small = Small(count, block, near, far, small_sem)
    fetch = own_copy(all_units, units, own_sem)
    fetch.start()
    greet(*ring.peers)
    ring.start()
    arriving = moves(
        (far_dqkv, far_dkv, far_dx1, far_qkv, far_kv), (dqkv, dkv, dx1, qkv_w, kv_w), arrive_sem
    )
    for copy in arriving:
        copy.start()
    six = Hop(part6, core6, fromx6, None, sem6, chunk)
    seven = Hop(part7, core7, fromx7, None, sem7, chunk)
    fetch.wait()
    for copy in arriving:
        copy.wait()
    block[...] = jnp.zeros_like(block)
    cols = self_b.shape[1]
    for row in range(2):
        block[0:1, row * cols : (row + 1) * cols] = self_b[row : row + 1, :]
        block[0:1, (2 + row) * cols : (3 + row) * cols] = cross_b[row : row + 1, :]
        block[1 + row : 2 + row, :] = ffn_b[:, row * width : (row + 1) * width]
    block[SMALL - NORM_ROWS : SMALL - 2, :] = stats[:7, :]
    gain = gains[0:1, :]

    def project(step):
        grads = six.take(dqkv, step)
        total = dot_nt(grads[:, :cols], qkv_w[0]) + dot_nt(grads[:, cols : 2 * cols], qkv_w[1])
        six.put(part6, step, (total + dot_nt(grads[:, 2 * cols :], qkv_w[2])).astype(jnp.bfloat16))
        six.send_core(step)

    def norm_one(step):
        rows = six.own_rows(step)
        grad_in = six.result(step)
        _, normed, inv_std = norm_forward(units[rows, :].astype(jnp.float32), gain, gain)
        block[SMALL - 2 : SMALL - 1, :] += column_sum(grad_in * normed)
        block[SMALL - 1 : SMALL, :] += column_sum(grad_in)
        units_g[rows, :] = dx1[rows, :] + norm_backward(grad_in, normed, inv_std, gain)

    def text_only(work):
        def stage(step):
            @pl.when(step < text_steps)
            def _():
                work(step)

        return stage

    def text_project(step):
        seven.put(part7, step, dot_nt(seven.take(dkv, step), kv_w[...]).astype(jnp.bfloat16))
        seven.send_core(step)

    def text_result(step):
        text_g[seven.own_rows(step), :] = seven.result(step)

    ready = 2 * (steps + 1)

    def extra(half_tick):
        for when, work in enumerate((small.begin, small.forward, small.launch)):
            pl.when(half_tick == ready + when)(work)
        step = half_tick - ready - 3

        @pl.when((step >= 0) & (step < count // 2))
        def _():
            small.rotate(step)

    stages(
        steps,
        list(
            enumerate(
                [
                    project, six.send_cross, norm_one, text_only(text_project), text_only(seven.send_cross), text_only(text_result),
                ]
            )
        ),
        ring,
        extra,
        max((ready + 4 + count // 2) // 2, 2 * (count - 1)),
    )

    def finish(step, carry):
        six.finish(step, False)
        text_only(lambda s: seven.finish(s, False))(step)
        return carry

    lax.fori_loop(0, steps, finish, 0)
    ring.finish()
    small.finish(small_sum)


def last(count, g0, g1, units, dqkv, dkv, dx1, qkv_w, kv_w, *rest):
    rows = dqkv.shape[0]
    own, width = dx1.shape
    chunk = own // STEPS
    text_own = dkv.shape[0] // NARROW
    bf, f32 = jnp.bfloat16, jnp.float32
    shape = jax.ShapeDtypeStruct
    vmem = pl.BlockSpec(memory_space=pltpu.VMEM)
    hbm = pl.BlockSpec(memory_space=pl.ANY)
    hop = hop_scratch(own, chunk, width)
    return pl.pallas_call(
        functools.partial(last_kernel, count=count),
        in_specs=[hbm] * 8 + [vmem] * len(rest),
        out_specs=[hbm] * 2 + [vmem] * 3,
        out_shape=[
            pltpu.HBM(g0.shape, bf),
            pltpu.HBM(g1.shape, bf),
            shape((own, width), f32),
            shape((text_own, width), f32),
            shape((SMALL, width), f32),
        ],
        scratch_shapes=[pltpu.VMEM(a.shape, a.dtype) for a in (dqkv, dkv, dx1, qkv_w, kv_w)]
        + [pltpu.SemaphoreType.DMA((5,)), pltpu.VMEM((own, width), bf), pltpu.SemaphoreType.DMA]
        + [pltpu.VMEM((rows, width), bf)]
        + hop
        + [pltpu.VMEM((dkv.shape[0], width), bf)]
        + hop_scratch(text_own, chunk, width)
        + [
            pltpu.VMEM((SMALL, width), f32),
            pltpu.VMEM((NARROW, SMALL, width), f32),
            pltpu.VMEM((count, SMALL, width), f32),
            pltpu.SemaphoreType.DMA((2, 3, max(count // 2, 3))),
        ]
        + ring_scratch(count, (width // count, width // 2)),
        compiler_params=pltpu.CompilerParams(collective_id=2, has_side_effects=True, vmem_limit_bytes=58 * MIB),
        cost_estimate=pl.CostEstimate(flops=30 * 10**9, bytes_accessed=16 * MIB, transcendentals=0),
        name="last",
    )(g0, g1, units, dqkv, dkv, dx1, qkv_w, kv_w, *rest)


def unpack_kernel(
    sum0, sum1, small, y_in, units_in, text_in,
    qkv_g, cq_g, co_g, so_g, kv_g, gain_g, shift_g, bias_g, self_b, cross_b, ffn_b, y, units_g, text_g,
):
    cols = cq_g.shape[1]
    step = pl.program_id(0)
    y[...] = y_in[...]
    units_g[...] = units_in[...]
    text_g[...] = text_in[...]
    for part in range(3):
        qkv_g[part] = sum0[:, part * cols : (part + 1) * cols].astype(jnp.float32)
    cq_g[...] = sum0[:, 3 * cols :].astype(jnp.float32)
    for when, ref in enumerate((co_g, so_g)):

        @pl.when(step == when)
        def _():
            ref[...] = sum1[...].astype(jnp.float32)

    half = kv_g.shape[0] // 2
    for when in range(half // cols):

        @pl.when(step == 2 + when)
        def _():
            for side in range(2):
                rows = slice(side * half + when * cols, side * half + (when + 1) * cols)
                for part in range(2):
                    first = (2 * side + part) * cols
                    kv_g[rows, part, :] = sum1[:, first : first + cols].astype(jnp.float32)

    @pl.when(step == 0)
    def _():
        norms = small[SMALL - NORM_ROWS :, :]
        for ref, order in ((gain_g, (7, 4, 0)), (shift_g, (8, 5, 1)), (bias_g, (6, 3, 2))):
            for row, source in enumerate(order):
                ref[row : row + 1, :] = norms[source : source + 1, :]
        width = small.shape[1]
        for row in range(2):
            self_b[row : row + 1, :] = small[0:1, row * cols : (row + 1) * cols]
            cross_b[row : row + 1, :] = small[0:1, (2 + row) * cols : (3 + row) * cols]
            ffn_b[:, row * width : (row + 1) * width] = small[1 + row : 2 + row, :]


def unpack(sum0, sum1, small, cols, hidden, *row_outs):
    width = sum0.shape[0]
    steps = width // cols
    f32 = jnp.float32
    block = lambda a: pl.BlockSpec((a.shape[0] // steps,) + a.shape[1:], lambda i: (i, 0))
    whole = lambda a: pl.BlockSpec(a.shape, lambda i: (0,) * len(a.shape))
    fixed = [
        jax.ShapeDtypeStruct(dims, f32)
        for dims in (
            (cols, width), (cols, width), (width, 2, cols),
            (3, width), (3, width), (3, width), (2, cols), (2, cols), (1, hidden),
        )
    ]
    moving = [jax.ShapeDtypeStruct((3, width, cols), f32), jax.ShapeDtypeStruct((width, cols), f32)]
    return pl.pallas_call(
        unpack_kernel,
        grid=(steps,),
        in_specs=[block(sum0), block(sum1), whole(small)] + [block(a) for a in row_outs],
        out_specs=[pl.BlockSpec((3, cols, cols), lambda i: (0, i, 0)), block(moving[1])]
        + [whole(a) for a in fixed]
        + [block(a) for a in row_outs],
        out_shape=moving + fixed + [jax.ShapeDtypeStruct(a.shape, a.dtype) for a in row_outs],
        compiler_params=pltpu.CompilerParams(vmem_limit_bytes=60 * MIB),
        name="unpack",
    )(sum0, sum1, small, *row_outs)


def local(
    units,
    text,
    out_grad,
    unit_lengths,
    text_lengths,
    bucket_counts,
    norm_gain,
    norm_shift,
    self_qkv,
    self_bias,
    self_out,
    cross_q,
    cross_kv,
    cross_bias,
    cross_out,
    ffn_in,
    ffn_in_bias,
    ffn_out,
    out_bias,
):
    slot_live = jnp.arange(unit_lengths.shape[0], dtype=jnp.int32) < bucket_counts[0]
    lengths = jnp.where(slot_live, unit_lengths, 0)
    qkv_weights = jnp.transpose(self_qkv, (1, 0, 2))
    kv_weights = cross_kv.reshape(cross_kv.shape[0], -1)
    count = lax.axis_size("wide")
    first_in, queries, key_rows, value_rows, text_kv, self_context, self_logs = front(
        lengths, units, text, norm_gain, norm_shift, qkv_weights, self_bias, kv_weights, cross_bias
    )
    (
        ffn_part,
        third_part,
        ffn_in_grad,
        ffn_out_grad,
        second_all,
        cross_queries,
        cross_context,
        resid_one,
        resid_two,
        ffn_bias_sum,
    ) = middle(
        units,
        out_grad,
        ffn_in,
        ffn_out,
        self_out,
        cross_q,
        cross_out,
        lengths,
        text_lengths,
        self_context,
        text_kv,
        norm_gain,
        norm_shift,
        out_bias,
        cross_bias,
        ffn_in_bias,
    )
    in_sum, out_sum, grads_one, grads_two, output, resid_one_grad, context_grad, text_kv_grad, cross_bias_sum, stats = turn(
        count,
        third_part,
        ffn_part,
        ffn_in_grad,
        ffn_out_grad,
        out_grad,
        lengths,
        text_lengths,
        resid_one,
        resid_two,
        second_all,
        cross_queries,
        cross_context,
        text_kv,
        self_context,
        norm_gain,
        out_bias,
        cross_out,
        cross_q,
        self_out,
    )
    qkv_grad, grads_one, grads_two, self_bias_sum, ffn_in_grad, ffn_out_grad = back(
        lengths,
        queries,
        key_rows,
        value_rows,
        context_grad,
        self_context,
        self_logs,
        first_in,
        text,
        text_kv_grad,
        in_sum,
        out_sum,
        grads_one,
        grads_two,
    )
    summed_one, summed_two, units_grad, text_grad, small = last(
        count,
        grads_one,
        grads_two,
        units,
        qkv_grad,
        text_kv_grad,
        resid_one_grad,
        qkv_weights,
        kv_weights,
        self_bias_sum,
        cross_bias_sum,
        ffn_bias_sum,
        stats,
        norm_gain,
    )
    (
        self_qkv_grad,
        cross_q_grad,
        cross_out_grad,
        self_out_grad,
        cross_kv_grad,
        gain_grad,
        shift_grad,
        bias_grad,
        self_bias_grad,
        cross_bias_grad,
        ffn_in_bias_grad,
        output,
        units_grad,
        text_grad,
    ) = unpack(
        summed_one, summed_two, small, queries.shape[1], ffn_in_bias.shape[0], output, units_grad, text_grad
    )
    self_qkv_grad = jnp.transpose(self_qkv_grad, (1, 0, 2))
    ffn_in_bias_grad = ffn_in_bias_grad.reshape(-1)
    return (
        output,
        units_grad,
        text_grad,
        gain_grad,
        shift_grad,
        self_qkv_grad,
        self_bias_grad,
        self_out_grad,
        cross_q_grad,
        cross_kv_grad,
        cross_bias_grad,
        cross_out_grad,
        ffn_in_grad,
        ffn_in_bias_grad,
        ffn_out_grad,
        bias_grad,
    )


def solution(mesh):
    placed = (
        P("wide", None),
        P("wide", None),
        P("wide", None),
        P("wide"),
        P("wide"),
        P("wide"),
        P(),
        P(),
        P(None, None, "narrow"),
        P(None, "narrow"),
        P("narrow", None),
        P(None, "narrow"),
        P(None, None, "narrow"),
        P(None, "narrow"),
        P("narrow", None),
        P(None, "narrow"),
        P("narrow"),
        P("narrow", None),
        P(),
    )
    return jax.shard_map(
        local,
        mesh=mesh,
        in_specs=placed,
        out_specs=(
            P(("wide", "narrow"), None),
            P(("wide", "narrow"), None),
            P(("wide", "narrow"), None),
            P(),
            P(),
            P(None, None, "narrow"),
            P(None, "narrow"),
            P("narrow", None),
            P(None, "narrow"),
            P(None, None, "narrow"),
            P(None, "narrow"),
            P("narrow", None),
            P(None, "narrow"),
            P("narrow"),
            P("narrow", None),
            P(),
        ),
        check_vma=False,
    )
```

```python
import functools

import jax
import jax.numpy as jnp
from jax import lax
from jax.experimental import pallas as pl
from jax.experimental.pallas import tpu as pltpu
from jax.sharding import PartitionSpec as P

HEAD_DIM = 64


NORM_EPSILON = 1e-05
MASKED_SCORE = -1000000000.0
EXACT = lax.Precision.HIGHEST


def norm_forward(values, gain_vec, shift_vec):
    row_mean = jnp.mean(values, axis=-1, keepdims=True)
    centered = values - row_mean
    inv_std = lax.rsqrt(jnp.mean(centered * centered, axis=-1, keepdims=True) + NORM_EPSILON)
    normed = centered * inv_std
    return (normed * gain_vec + shift_vec, normed, inv_std)


def norm_backward(grad_in, normed, inv_std, gain_vec):
    scaled = grad_in * gain_vec
    inner_term = scaled - jnp.mean(scaled, axis=-1, keepdims=True)
    inner_term = inner_term - normed * jnp.mean(scaled * normed, axis=-1, keepdims=True)
    return inner_term * inv_std


BLOCK = 256
LANES = 128
MIB = 1 << 20
NARROW = 4
STEPS = 8
HIDDEN = 512
MESH = pl.DeviceIdType.MESH


def head_mask(shape, head):
    lane = lax.broadcasted_iota(jnp.int32, shape, len(shape) - 1)
    return (lane >= head * HEAD_DIM) & (lane < (head + 1) * HEAD_DIM)


def pick_head(values, head):
    return jnp.where(head_mask(values.shape, head), values, jnp.zeros_like(values))


def dot_nt(a, b):
    return lax.dot_general(a, b, (((1,), (1,)), ((), ())), preferred_element_type=jnp.float32)


def dot_nn(a, b):
    return jnp.dot(a, b, preferred_element_type=jnp.float32)


def dot_tn(a, b):
    return lax.dot_general(a, b, (((0,), (0,)), ((), ())), preferred_element_type=jnp.float32)


def column_sum(values):
    return jnp.sum(values, axis=0, keepdims=True)


def mask_diagonal(scores, axis):
    count = scores.shape[axis]
    parts = [scores] if count == BLOCK else jnp.split(scores, [count - BLOCK], axis=axis)
    keys = lax.broadcasted_iota(jnp.int32, parts[-1].shape, axis)
    queries = lax.broadcasted_iota(jnp.int32, keys.shape, 1 - axis) & (BLOCK - 1)
    parts[-1] = jnp.where(keys <= queries, parts[-1], MASKED_SCORE)
    return jnp.concatenate(parts, axis=axis)


def front_kernel(
    lens, x_ref, t_ref, g_ref, s_ref, w_ref, b_ref, kvw_ref, vb_ref, h_ref, q_ref, k_ref, v_ref, kv_ref, c_ref, log_ref
):
    length = lens[pl.program_id(0)]
    width = q_ref.shape[1]
    turn_now = pl.program_id(1)

    @pl.when(turn_now == 0)
    def _():
        both = dot_nn(t_ref[...], kvw_ref[...])
        kv_ref[:, :width] = both[:, :width].astype(jnp.bfloat16)
        kv_ref[:, width:] = (both[:, width:] + vb_ref[1:2, :]).astype(jnp.bfloat16)

    for i in range(q_ref.shape[0] // BLOCK):
        rows = pl.ds(i * BLOCK, BLOCK)

        @pl.when((turn_now == i) & (i * BLOCK < length))
        def _():
            normed, _, _ = norm_forward(x_ref[...].astype(jnp.float32), g_ref[0:1, :], s_ref[0:1, :])
            h1 = normed.astype(jnp.bfloat16)
            h_ref[...] = h1
            queries = (dot_nn(h1, w_ref[0]) + b_ref[0:1, :]).astype(jnp.bfloat16)
            q_ref[rows, :] = queries
            k_ref[rows, :] = dot_nn(h1, w_ref[1]).astype(jnp.bfloat16)
            v_ref[rows, :] = (dot_nn(h1, w_ref[2]) + b_ref[1:2, :]).astype(jnp.bfloat16)
            count = (i + 1) * BLOCK
            keys, values = k_ref[:count, :], v_ref[:count, :]
            scaled = queries * jnp.bfloat16(HEAD_DIM**-0.5)
            total = jnp.zeros((BLOCK, width), jnp.float32)
            logs = jnp.zeros((BLOCK, LANES), jnp.float32)
            lane = lax.broadcasted_iota(jnp.int32, logs.shape, 1)
            for head in range(width // HEAD_DIM):
                scores = mask_diagonal(dot_nt(pick_head(scaled, head), keys), 1)
                top = jnp.max(scores, axis=1, keepdims=True)
                weights = jnp.exp(scores - top)
                norm = jnp.sum(weights, axis=1, keepdims=True)
                total += dot_nn(weights.astype(jnp.bfloat16), pick_head(values, head)) * (1.0 / norm)
                logs = jnp.where(lane == head, top + jnp.log(norm), logs)
            log_ref[:, rows] = logs.T[: log_ref.shape[0], :]
            c_ref[rows, :] = total.astype(jnp.bfloat16)

        @pl.when((turn_now == i) & (i * BLOCK >= length))
        def _():
            h_ref[...] = jnp.zeros_like(h_ref)
            for ref in (q_ref, k_ref, v_ref, c_ref):
                ref[rows, :] = jnp.zeros((BLOCK, ref.shape[1]), ref.dtype)
            log_ref[:, rows] = jnp.zeros((log_ref.shape[0], BLOCK), jnp.float32)


def front(lengths, units, text, gains, shifts, weights, bias, kv_w, cross_bias):
    rows, width = units.shape
    slots = lengths.shape[0]
    slot_rows = rows // slots
    cols = weights.shape[2]
    whole = lambda a: pl.BlockSpec(a.shape, lambda s, i, *_: (0,) * a.ndim)
    slot = lambda w: pl.BlockSpec((slot_rows, w), lambda s, i, *_: (s, 0))
    texts = lambda w: pl.BlockSpec((text.shape[0] // slots, w), lambda s, i, *_: (s, 0))
    logs = pl.BlockSpec((8, slot_rows), lambda s, i, *_: (0, s))
    blocks = slot_rows // BLOCK
    piece = pl.BlockSpec((BLOCK, width), lambda s, i, *_: (s * blocks + i, 0))
    shape = lambda w: jax.ShapeDtypeStruct((rows, w), jnp.bfloat16)
    far = lambda w: pltpu.HBM((rows, w), jnp.bfloat16)
    return pl.pallas_call(
        front_kernel,
        grid_spec=pltpu.PrefetchScalarGridSpec(
            num_scalar_prefetch=1,
            grid=(slots, blocks),
            in_specs=[piece, texts(width)]
            + [whole(a) for a in (gains, shifts, weights, bias, kv_w, cross_bias)],
            out_specs=[piece, slot(cols), slot(cols), slot(cols), texts(2 * cols), slot(cols), logs],
        ),
        out_shape=[
            far(width),
            far(cols),
            far(cols),
            far(cols),
            jax.ShapeDtypeStruct((text.shape[0], 2 * cols), jnp.bfloat16),
            shape(cols),
            pltpu.HBM((8, rows), jnp.float32),
        ],
        compiler_params=pltpu.CompilerParams(vmem_limit_bytes=60 * MIB),
        cost_estimate=pl.CostEstimate(flops=20 * 10**9, bytes_accessed=16 * MIB, transcendentals=8 * MIB),
        name="front",
    )(lengths, units, text, gains, shifts, weights, bias, kv_w, cross_bias)


def back_kernel(
    lens, q_ref, k_ref, v_ref, dc_ref, c_ref, log_ref, h_ref, text_ref, dkv_ref, in_ref, out_ref, _g0, _g1,
    o_ref, g0_ref, g1_ref, b_ref, in_f32, out_f32, dk_acc, dv_acc, w_acc,
):
    in_f32[...] = in_ref[...].astype(jnp.float32)
    out_f32[...] = out_ref[...].astype(jnp.float32)
    slot, turn_now = pl.program_id(0), pl.program_id(1)
    slot_rows, width = q_ref.shape
    heads = range(width // HEAD_DIM)

    @pl.when((slot == 0) & (turn_now == 0))
    def _():
        w_acc[...] = jnp.zeros_like(w_acc)
        b_ref[...] = jnp.zeros_like(b_ref)
        kv_grad = dot_tn(text_ref[...], dkv_ref[...]).astype(jnp.bfloat16)
        half, both = g1_ref.shape[0], dkv_ref.shape[1]
        g1_ref[:, :both] = kv_grad[:half]
        g1_ref[:, both:] = kv_grad[half:]

    @pl.when(turn_now == 0)
    def _():
        dk_acc[...] = jnp.zeros_like(dk_acc)
        dv_acc[...] = jnp.zeros_like(dv_acc)
        o_ref[:, :width] = jnp.zeros((slot_rows, width), jnp.bfloat16)

    def stack(values):
        return jnp.concatenate([pick_head(values, head) for head in heads], axis=0)

    def side_by_side(values):
        return jnp.concatenate([values[head : head + 1, :] for head in heads], axis=1)

    for i in range(slot_rows // BLOCK):
        rows = pl.ds(i * BLOCK, BLOCK)

        @pl.when((turn_now == i) & (i * BLOCK < lens[slot]))
        def _():
            count = (i + 1) * BLOCK
            keys, values = k_ref[:count, :], v_ref[:count, :]
            grads = dc_ref[rows, :]
            q_heads, g_heads = stack(q_ref[rows, :] * jnp.bfloat16(HEAD_DIM**-0.5)), stack(grads)
            owners = lax.broadcasted_iota(jnp.int32, (8, width), 0)
            lanes = lax.broadcasted_iota(jnp.int32, (8, width), 1)
            inner = lax.dot_general(
                jnp.where((lanes >= owners * HEAD_DIM) & (lanes < (owners + 1) * HEAD_DIM), 1.0, 0.0),
                grads.astype(jnp.float32) * c_ref[rows, :].astype(jnp.float32),
                (((1,), (1,)), ((), ())),
                precision=EXACT,
                preferred_element_type=jnp.float32,
            )
            weights = jnp.exp(mask_diagonal(dot_nt(keys, q_heads), 0) - side_by_side(log_ref[:, rows]))
            dv_acc[:count, :] += dot_nn(weights.astype(jnp.bfloat16), g_heads)
            score_grad = (weights * (dot_nt(values, g_heads) - side_by_side(inner))).astype(jnp.bfloat16)
            dk_acc[:count, :] += dot_nn(score_grad, q_heads)
            total = jnp.zeros((BLOCK, width), jnp.float32)
            for head in heads:
                total += dot_tn(score_grad[:, head * BLOCK : (head + 1) * BLOCK], pick_head(keys, head))
            q_grad = (total * HEAD_DIM**-0.5).astype(jnp.bfloat16)
            o_ref[rows, :width] = q_grad
            b_ref[0:1, :] += column_sum(q_grad.astype(jnp.float32))

    @pl.when(turn_now == pl.num_programs(1) - 1)
    def _():
        v_grad = dv_acc[...].astype(jnp.bfloat16)
        o_ref[:, width : 2 * width] = dk_acc[...].astype(jnp.bfloat16)
        o_ref[:, 2 * width :] = v_grad
        b_ref[1:2, :] += column_sum(v_grad.astype(jnp.float32))
        for first in range(0, h_ref.shape[1], BLOCK):
            w_acc[first : first + BLOCK, :] += dot_tn(h_ref[:, first : first + BLOCK], o_ref[...])

        @pl.when(slot == pl.num_programs(0) - 1)
        def _():
            g0_ref[...] = w_acc[...].astype(jnp.bfloat16)


def back(lengths, queries, keys, values, grads, context, logs, rows_in, text, dkv, in_sum, out_sum, g0, g1):
    rows, cols = queries.shape
    width = rows_in.shape[1]
    slots = lengths.shape[0]
    bf, f32 = jnp.bfloat16, jnp.float32
    shape = jax.ShapeDtypeStruct
    slot = lambda a: pl.BlockSpec((a.shape[0] // slots, a.shape[1]), lambda s, i, *_: (s, 0))
    blocks = rows // slots // BLOCK
    piece = lambda a: pl.BlockSpec((a.shape[0] // (slots * blocks), a.shape[1]), lambda s, i, *_: (s * blocks + i, 0))
    whole = lambda a: pl.BlockSpec(a.shape, lambda s, i, *_: (0, 0))
    hbm = pl.BlockSpec(memory_space=pl.ANY)
    half = text.shape[1] // 2
    return pl.pallas_call(
        back_kernel,
        grid_spec=pltpu.PrefetchScalarGridSpec(
            num_scalar_prefetch=1,
            grid=(slots, blocks),
            in_specs=[slot(queries)] * 5
            + [pl.BlockSpec((8, rows // slots), lambda s, i, *_: (0, s))]
            + [slot(rows_in), whole(text), whole(dkv), piece(in_sum), piece(out_sum), hbm, hbm],
            out_specs=[
                pl.BlockSpec((rows // slots, 3 * cols), lambda s, i, *_: (s, 0)),
                pl.BlockSpec((width, 3 * cols), lambda s, i, *_: (0, 0)),
                pl.BlockSpec((half, width), lambda s, i, *_: (1, 0)),
                pl.BlockSpec((2, cols), lambda s, i, *_: (0, 0)),
                piece(in_sum),
                piece(out_sum),
            ],
            scratch_shapes=[pltpu.VMEM((rows // slots, cols), f32)] * 2 + [pltpu.VMEM((width, 3 * cols), f32)],
        ),
        out_shape=[
            shape((rows, 3 * cols), bf),
            pltpu.HBM(g0.shape, bf),
            pltpu.HBM(g1.shape, bf),
            shape((2, cols), f32),
            shape(in_sum.shape, f32),
            shape(out_sum.shape, f32),
        ],
        input_output_aliases={12: 1, 13: 2},
        compiler_params=pltpu.CompilerParams(vmem_limit_bytes=60 * MIB),
        cost_estimate=pl.CostEstimate(flops=30 * 10**9, bytes_accessed=40 * MIB, transcendentals=8 * MIB),
        name="back",
    )(lengths, queries, keys, values, grads, context, logs, rows_in, text, dkv, in_sum, out_sum, g0, g1)


def place():
    index = lax.axis_index("narrow")
    core = index + 1 - 2 * (index % 2)
    return index, core, (index + 2) % NARROW, (core + 2) % NARROW


def greet(*wide_peers):
    _, core, cross, _ = place()
    barrier = pltpu.get_barrier_semaphore()
    for peer in (core, cross):
        pl.semaphore_signal(barrier, inc=1, device_id={"narrow": peer}, device_id_type=MESH)
    for peer in wide_peers:
        pl.semaphore_signal(barrier, inc=1, device_id={"wide": peer}, device_id_type=MESH)
    pl.semaphore_wait(barrier, 2 + len(wide_peers))


def remote(source, target, sems, kind, step, peer, axis="narrow"):
    return pltpu.make_async_remote_copy(
        src_ref=source,
        dst_ref=target,
        send_sem=sems.at[0, kind, step],
        recv_sem=sems.at[1, kind, step],
        device_id={axis: peer},
        device_id_type=MESH,
    )


def ring_place(count):
    wide = lax.axis_index("wide")
    odd, half = wide % 2, wide // 2
    spot = odd * (half + 1) + (1 - odd) * ((count - half) % count)

    def at(where):
        high = ((where + count - 1) % count) // (count // 2)
        return (1 - high) * (2 * where - 1) + high * ((2 * (count - where)) % (2 * count))

    return spot, at((spot + 1) % count), at((spot + count - 1) % count)


class Ring:
    UNITS = 4

    def __init__(self, count, sources, outs, view, arrived, held, sems, fetch_sems, keep_sems):
        self.count, self.sources, self.outs, self.view = count, sources, outs, view
        self.arrived, self.held, self.sems = arrived, held, sems
        self.fetch_sems, self.keep_sems = fetch_sems, keep_sems
        spot, following, previous = ring_place(count)
        self.spots = (spot, (count - spot) % count)
        self.peers = (following, previous)

    def block(self, refs, unit, back_by):
        shard = (self.spots[unit // 2] + 2 * self.count - back_by) % self.count
        return self.view(refs[unit // 2], unit // 2, unit % 2, shard)

    def send(self, source, target, kind, unit, step):
        return remote(source, target, self.sems, kind * self.UNITS + unit, step, self.peers[unit // 2], "wide")

    def sum_copy(self, unit, step, first=False):
        source = self.block(self.sources, unit, 0) if first else self.arrived.at[unit, jnp.maximum(step - 1, 0)]
        return self.send(source, self.arrived.at[unit, step], 0, unit, step)

    def fetch(self, unit, step):
        slot = step % 2
        return pltpu.make_async_copy(
            self.block(self.sources, unit, step + 1), self.held.at[unit, slot], self.fetch_sems.at[unit, slot]
        )

    def keep(self, unit):
        return pltpu.make_async_copy(
            self.arrived.at[unit, self.count - 2], self.block(self.outs, unit, self.count - 1), self.keep_sems.at[unit]
        )

    def spread_copy(self, unit, step, first=False):
        target = self.block(self.outs, unit, self.count - 1 + step)
        source = self.arrived.at[unit, self.count - 2] if first else target
        return self.send(source, target, 1, unit, step)

    def start(self):
        for unit in range(self.UNITS):
            self.sum_copy(unit, 0, True).start()
            self.fetch(unit, 0).start()
            self.fetch(unit, 1).start()

    def serve(self, turn, unit):
        last = self.count - 2

        @pl.when(turn <= last)
        def _():
            self.sum_copy(unit, turn).wait_recv()
            self.fetch(unit, turn).wait()
            total = self.held[unit, turn % 2].astype(jnp.float32) + self.arrived[unit, turn].astype(jnp.float32)
            self.arrived[unit, turn] = total.astype(jnp.bfloat16)

            @pl.when(turn < last)
            def _():
                self.sum_copy(unit, turn + 1).start()

            @pl.when(turn < last - 1)
            def _():
                self.fetch(unit, turn + 2).start()

            @pl.when(turn == last)
            def _():
                self.spread_copy(unit, 0, True).start()
                self.keep(unit).start()

        @pl.when((turn > last) & (turn <= 2 * last + 1))
        def _():
            step = turn - last - 1
            self.spread_copy(unit, step).wait_recv()

            @pl.when(step < last)
            def _():
                self.spread_copy(unit, step + 1).start()

    def finish(self):
        for unit in range(self.UNITS):
            self.keep(unit).wait()

        def body(step, carry):
            for unit in range(self.UNITS):
                self.sum_copy(unit, step).wait_send()
                self.spread_copy(unit, step).wait_send()
            return carry

        lax.fori_loop(0, self.count - 1, body, 0)


def ring_scratch(count, block):
    return [
        pltpu.VMEM((Ring.UNITS, count - 1) + block, jnp.bfloat16),
        pltpu.VMEM((Ring.UNITS, 2) + block, jnp.bfloat16),
        pltpu.SemaphoreType.DMA((2, 2 * Ring.UNITS, count - 1)),
        pltpu.SemaphoreType.DMA((Ring.UNITS, 2)),
        pltpu.SemaphoreType.DMA((Ring.UNITS,)),
    ]


def own_copy(whole, own, sem):
    size = own.shape[0]
    first = pl.multiple_of(lax.axis_index("narrow") * size, size)
    return pltpu.make_async_copy(whole.at[pl.ds(first, size), :], own, sem)


def moves(sources, targets, sems):
    pairs = list(zip(sources, targets, strict=True))
    return [pltpu.make_async_copy(a, b, sems.at[slot]) for slot, (a, b) in enumerate(pairs)]


class Hop:
    KINDS = 6

    def __init__(self, part, from_core, from_cross, full, sems, chunk):
        self.part, self.from_core, self.from_cross = part, from_core, from_cross
        self.full, self.sems, self.chunk = full, sems, chunk
        self.own = part.shape[0] // NARROW
        self.index, self.core, self.cross, self.diagonal = place()

    def rows(self, owner, step):
        return pl.ds(pl.multiple_of(owner * self.own + step * self.chunk, self.chunk), self.chunk)

    def own_rows(self, step):
        return pl.ds(pl.multiple_of(step * self.chunk, self.chunk), self.chunk)

    def core_copies(self, step):
        return [
            remote(self.part.at[self.rows(owner, step)], self.from_core.at[step, slot], self.sems, slot, step, self.core)
            for slot, owner in enumerate((self.core, self.diagonal))
        ]

    def cross_copy(self, step):
        return remote(
            self.part.at[self.rows(self.cross, step)], self.from_cross.at[step], self.sems, 2, step, self.cross
        )

    def gather_copy(self, step, kind):
        owner = self.cross if kind == 5 else self.index
        rows = self.full.at[self.rows(owner, step)]
        return remote(rows, rows, self.sems, kind, step, self.cross if kind == 3 else self.core)

    def send_core(self, step):
        for copy in self.core_copies(step):
            copy.start()

    def send_cross(self, step):
        for copy in self.core_copies(step):
            copy.wait_recv()
        total = self.part[self.rows(self.cross, step), :].astype(jnp.float32)
        total += self.from_core[step, 1].astype(jnp.float32)
        self.part[self.rows(self.cross, step), :] = total.astype(jnp.bfloat16)
        self.cross_copy(step).start()

    def result(self, step):
        total = self.part[self.rows(self.index, step), :].astype(jnp.float32)
        total += self.from_core[step, 0].astype(jnp.float32)
        self.cross_copy(step).wait_recv()
        return total + self.from_cross[step].astype(jnp.float32)

    def send_gather(self, step, values):
        self.full[self.rows(self.index, step), :] = values
        self.gather_copy(step, 3).start()
        self.gather_copy(step, 4).start()

    def forward(self, step):
        self.gather_copy(step, 3).wait_recv()
        self.gather_copy(step, 5).start()

    def gathered(self, step):
        self.gather_copy(step, 4).wait_recv()
        self.gather_copy(step, 5).wait_recv()

    def sent(self, step):
        for copy in self.core_copies(step):
            copy.wait_send()
        self.cross_copy(step).wait_send()

    def finish(self, step, gather=True, parts=True):
        if parts:
            self.sent(step)
        if gather:
            for kind in (3, 4, 5):
                self.gather_copy(step, kind).wait_send()

    def take(self, ref, step):
        return jnp.concatenate([ref[self.rows(owner, step), :] for owner in range(NARROW)], axis=0)

    def put(self, ref, step, values):
        for owner in range(NARROW):
            ref[self.rows(owner, step), :] = values[owner * self.chunk : (owner + 1) * self.chunk]


def hop_scratch(own, chunk, width):
    steps = own // chunk
    return [
        pltpu.VMEM((steps, 2, chunk, width), jnp.bfloat16),
        pltpu.VMEM((steps, chunk, width), jnp.bfloat16),
        pltpu.SemaphoreType.DMA((2, Hop.KINDS, steps)),
    ]


def stages(steps, work, ring=None, extra=None, ticks=0):
    ticks = max(ticks, steps + max(delay for delay, _ in work))
    per_tick = 0 if ring is None else -(-2 * (ring.count - 1) // ticks)

    def body(tick, carry):
        for number, (delay, stage) in enumerate(work):
            step = tick - delay

            @pl.when((step >= 0) & (step < steps))
            def _():
                stage(step)

            unit = (number + 1) * Ring.UNITS // len(work) - 1
            if per_tick and unit != number * Ring.UNITS // len(work) - 1:
                if per_tick == 1:
                    ring.serve(tick, unit)
                else:
                    lax.fori_loop(0, per_tick, lambda i, c: (ring.serve(tick * per_tick + i, unit), c)[1], 0)
            if extra is not None and number in (len(work) // 2, len(work) - 1):
                extra(2 * tick + (number == len(work) - 1))
        return carry

    lax.fori_loop(0, ticks, body, 0)


def middle_kernel(
    all_units, out_grad, far_in, far_out, far_so, far_cq, far_co, lens, text_lens,
    c1, kv2, gains, shifts, biases, bias, b_in,
    ffn_part, third, in_g, out_g, far_h2, far_q2, far_c2, far_x1, far_x2, in_bias_g,
    h2, q2, c2, x1, x2, leave_sem, units, own_sem, so_w, cq_w, co_w, small_sem, w_in, w_out, weight_sem, grads_in, grads_sem, give, give_sem, in_acc, out_acc,
    part, h3, core1, fromx1, sem1, core2, fromx2, sem2,
):
    steps, chunk, width = fromx1.shape
    cols = q2.shape[1]
    slots = text_lens.shape[0]
    texts = kv2.shape[0] // slots
    slot_rows = h2.shape[0] // slots
    hidden_count = w_out.shape[0]
    near = [
        pltpu.make_async_copy(source, target, small_sem.at[slot])
        for slot, (source, target) in enumerate(((far_so, so_w), (far_cq, cq_w), (far_co, co_w)))
    ]
    for fetch in near:
        fetch.start()
    fetches = [
        own_copy(all_units, units, own_sem),
        pltpu.make_async_copy(far_in, w_in, weight_sem.at[0]),
        pltpu.make_async_copy(far_out, w_out, weight_sem.at[1]),
    ]
    fetches[0].start()
    greet()
    one = Hop(part, core1, fromx1, h2, sem1, chunk)
    two = Hop(part, core2, fromx2, h3, sem2, chunk)
    scale = jnp.bfloat16(HEAD_DIM**-0.5)
    in_bias_g[...] = jnp.zeros_like(in_bias_g)
    for fetch in near:
        fetch.wait()

    leaving = moves((h2, q2, c2, x1, x2), (far_h2, far_q2, far_c2, far_x1, far_x2), leave_sem)

    def grad_copies(step):
        slot = step % 2
        return [
            pltpu.make_async_copy(
                out_grad.at[one.rows(owner, step), :],
                grads_in.at[slot, pl.ds(owner * chunk, chunk), :],
                grads_sem.at[slot, owner],
            )
            for owner in range(NARROW)
        ]

    def give_copies(step, kind):
        slot = step % 2
        return [
            pltpu.make_async_copy(
                give.at[kind, slot, pl.ds(owner * chunk, chunk), :],
                (ffn_part, third)[kind].at[one.rows(owner, step), :],
                give_sem.at[kind, slot, owner],
            )
            for owner in range(NARROW)
        ]

    def project(step):
        one.put(part, step, dot_nn(one.take(c1, step), so_w[...]).astype(jnp.bfloat16))
        one.send_core(step)
        for when, ref in ((1, in_acc), (2, out_acc)):

            @pl.when(step == when)
            def _():
                fetches[when].start()
                ref[...] = jnp.zeros_like(ref)

    def norm_one(step):
        @pl.when(step == 0)
        def _():
            fetches[0].wait()

        rows = one.own_rows(step)
        resid = units[rows, :].astype(jnp.float32) + one.result(step) + biases[0:1, :]
        x1[rows, :] = resid
        one.send_gather(step, norm_forward(resid, gains[1:2, :], shifts[1:2, :])[0].astype(jnp.bfloat16))

    def cross(step):
        one.gathered(step)
        queries = (dot_nn(one.take(h2, step), cq_w[...]) + bias[0:1, :]).astype(jnp.bfloat16)
        one.put(q2, step, queries)
        scaled = queries * scale
        count = queries.shape[0] // slots
        place_of = lax.broadcasted_iota(jnp.int32, (count * (cols // HEAD_DIM), texts), 1)
        context = []
        for slot in range(slots):
            mine = scaled[slot * count : (slot + 1) * count]
            keys = kv2[slot * texts : (slot + 1) * texts, :cols]
            values = kv2[slot * texts : (slot + 1) * texts, cols:]
            heads = range(cols // HEAD_DIM)
            scores = dot_nt(jnp.concatenate([pick_head(mine, head) for head in heads], axis=0), keys)
            scores = jnp.where(place_of < text_lens[slot], scores, MASKED_SCORE)
            weights = jnp.exp(scores - jnp.max(scores, axis=1, keepdims=True))
            norm = jnp.sum(weights, axis=1, keepdims=True)
            mixed = dot_nn(weights.astype(jnp.bfloat16), values) * (1.0 / norm)
            total = jnp.zeros((count, cols), jnp.float32)
            for head in heads:
                total += pick_head(mixed[head * count : (head + 1) * count], head)
            context.append(total.astype(jnp.bfloat16))
        context = jnp.concatenate(context, axis=0)
        one.put(c2, step, context)
        one.sent(step)
        two.put(part, step, dot_nn(context, co_w[...]).astype(jnp.bfloat16))
        two.send_core(step)

    def norm_two(step):
        rows = one.own_rows(step)
        resid = x1[rows, :] + two.result(step) + biases[1:2, :]
        x2[rows, :] = resid
        two.send_gather(step, norm_forward(resid, gains[2:3, :], shifts[2:3, :])[0].astype(jnp.bfloat16))

    def forward_two(step):
        two.forward(step)
        for copy in grad_copies(step):
            copy.start()

    def ffn(step):
        @pl.when(step == 0)
        def _():
            fetches[1].wait()
            fetches[2].wait()

        @pl.when(step == steps - 3)
        def _():
            for copy in leaving:
                copy.start()

        two.gathered(step)
        for copy in grad_copies(step):
            copy.wait()
        rows = two.take(h3, step)
        place_in = lax.broadcasted_iota(jnp.int32, (chunk, width), 0) + step * chunk
        grads = []
        for owner in range(NARROW):
            first = owner * two.own
            valid = place_in < lens[first // slot_rows] - first % slot_rows
            values = grads_in[step % 2, owner * chunk : (owner + 1) * chunk, :]
            grads.append(jnp.where(valid, values.astype(jnp.float32), 0.0).astype(jnp.bfloat16))
        grads = jnp.concatenate(grads, axis=0)
        out = jnp.zeros(rows.shape, jnp.float32)
        back_out = jnp.zeros(rows.shape, jnp.float32)
        for begin in range(0, hidden_count, HIDDEN):
            some = slice(begin, begin + HIDDEN)
            pre = dot_nn(rows, w_in[:, some]) + b_in[:, some]
            cdf = 0.5 + 0.5 * lax.erf(pre * (0.5**0.5))
            pdf = jnp.exp(-0.5 * pre * pre) * 0.3989422804014327
            hidden = (pre * cdf).astype(jnp.bfloat16)
            pre_low = ((cdf + pre * pdf) * dot_nt(grads, w_out[some, :])).astype(jnp.bfloat16)
            in_bias_g[:, some] += column_sum(pre_low.astype(jnp.float32))
            out += dot_nn(hidden, w_out[some, :])
            back_out += dot_nt(pre_low, w_in[:, some])
            out_acc[some, :] += dot_tn(hidden, grads)
            side, place_at = divmod(begin, width)
            in_acc[side * width : (side + 1) * width, place_at : place_at + HIDDEN] += dot_tn(rows, pre_low)

        @pl.when(step >= 2)
        def _():
            for kind in range(2):
                for copy in give_copies(step - 2, kind):
                    copy.wait()

        give[0, step % 2] = out.astype(jnp.bfloat16)
        give[1, step % 2] = back_out.astype(jnp.bfloat16)
        for kind in range(2):
            for copy in give_copies(step, kind):
                copy.start()

    stages(
        steps,
        [
            (0, project), (1, one.send_cross), (2, norm_one), (3, one.forward), (4, cross),
            (5, two.send_cross), (6, norm_two), (7, forward_two), (8, ffn),
        ],
    )

    def finish(step, carry):
        one.finish(step, True, False)
        two.finish(step)
        return carry

    lax.fori_loop(0, steps, finish, 0)
    part[...] = out_acc[...].astype(jnp.bfloat16)
    results = [pltpu.make_async_copy(part, out_g, weight_sem.at[0])]
    results[0].start()
    h3[...] = in_acc[...].astype(jnp.bfloat16)
    for side in range(hidden_count // width):
        here = pl.ds(side * width, width)
        results.append(pltpu.make_async_copy(h3.at[here, :], in_g.at[:, here], weight_sem.at[1 + side]))
        results[-1].start()
    for step in (steps - 2, steps - 1):
        for kind in range(2):
            for copy in give_copies(step, kind):
                copy.wait()
    for copy in results + leaving:
        copy.wait()


def middle(units, out_grad, w_in, w_out, so_w, cq_w, co_w, lens, text_lens, c1, kv2, gains, shifts, biases, bias, b_in):
    rows, cols = c1.shape
    own, width = rows // NARROW, units.shape[1]
    hidden_count = w_out.shape[0]
    chunk = own // STEPS
    bf, f32 = jnp.bfloat16, jnp.float32
    shape = jax.ShapeDtypeStruct
    vmem = pl.BlockSpec(memory_space=pltpu.VMEM)
    hbm = pl.BlockSpec(memory_space=pl.ANY)
    hop = hop_scratch(own, chunk, width)
    dma = pltpu.SemaphoreType.DMA
    return pl.pallas_call(
        middle_kernel,
        in_specs=[hbm] * 7 + [pl.BlockSpec(memory_space=pltpu.SMEM)] * 2 + [vmem] * 7,
        out_specs=[hbm] * 9 + [vmem],
        out_shape=[
            pltpu.HBM((rows, width), bf),
            pltpu.HBM((rows, width), bf),
            pltpu.HBM((width, hidden_count), bf),
            pltpu.HBM((hidden_count, width), bf),
            pltpu.HBM((rows, width), bf),
            pltpu.HBM((rows, cols), bf),
            pltpu.HBM((rows, cols), bf),
            pltpu.HBM((own, width), f32),
            pltpu.HBM((own, width), f32),
            shape((1, hidden_count), f32),
        ],
        scratch_shapes=[
            pltpu.VMEM((rows, width), bf),
            pltpu.VMEM((rows, cols), bf),
            pltpu.VMEM((rows, cols), bf),
            pltpu.VMEM((own, width), f32),
            pltpu.VMEM((own, width), f32),
            dma((5,)),
            pltpu.VMEM((own, width), bf),
            dma,
            pltpu.VMEM(so_w.shape, bf),
            pltpu.VMEM(cq_w.shape, bf),
            pltpu.VMEM(co_w.shape, bf),
            dma((3,)),
            pltpu.VMEM((width, hidden_count), bf),
            pltpu.VMEM((hidden_count, width), bf),
            dma((1 + hidden_count // width,)),
            pltpu.VMEM((2, NARROW * chunk, width), bf),
            dma((2, NARROW)),
            pltpu.VMEM((2, 2, NARROW * chunk, width), bf),
            dma((2, 2, NARROW)),
            pltpu.VMEM((hidden_count, width), f32),
            pltpu.VMEM((hidden_count, width), f32),
            pltpu.VMEM((rows, width), bf),
            pltpu.VMEM((rows, width), bf),
        ]
        + hop
        + hop,
        compiler_params=pltpu.CompilerParams(collective_id=0, has_side_effects=True, vmem_limit_bytes=60 * MIB),
        cost_estimate=pl.CostEstimate(flops=100 * 10**9, bytes_accessed=48 * MIB, transcendentals=8 * MIB),
        name="middle",
    )(
        units, out_grad, w_in, w_out, so_w, cq_w, co_w, lens, text_lens, c1, kv2, gains, shifts, biases, bias,
        b_in.reshape(1, -1),
    )


class FarHop(Hop):
    def fetch(self, mine, theirs, sems):
        self.mine, self.theirs = mine, theirs
        rows = lambda owner: pl.ds(pl.multiple_of(owner * self.own, self.own), self.own)
        self.fetches = [
            pltpu.make_async_copy(self.part.at[rows(owner)], ref, sems.at[slot])
            for slot, (owner, ref) in enumerate(((self.index, mine), (self.cross, theirs)))
        ]
        for copy in self.fetches:
            copy.start()

    def fetched(self):
        for copy in self.fetches:
            copy.wait()

    def cross_copy(self, step):
        return remote(
            self.theirs.at[self.own_rows(step)], self.from_cross.at[step], self.sems, 2, step, self.cross
        )

    def send_cross(self, step):
        for copy in self.core_copies(step):
            copy.wait_recv()
        total = self.theirs[self.own_rows(step), :].astype(jnp.float32)
        total += self.from_core[step, 1].astype(jnp.float32)
        self.theirs[self.own_rows(step), :] = total.astype(jnp.bfloat16)
        self.cross_copy(step).start()

    def result(self, step):
        total = self.mine[self.own_rows(step), :].astype(jnp.float32)
        total += self.from_core[step, 0].astype(jnp.float32)
        self.cross_copy(step).wait_recv()
        return total + self.from_cross[step].astype(jnp.float32)


def left_here(lens, own, rows):
    first = lax.axis_index("narrow") * own
    slot_rows = rows // lens.shape[0]
    return lens[first // slot_rows] - first % slot_rows


def row_of(step, chunk, width):
    return lax.broadcasted_iota(jnp.int32, (chunk, width), 0) + step * chunk


def turn_kernel(
    third, ffn_part, in_g, out_g, out_grad, lens, text_lens,
    far_x1, far_x2, far_h2, far_q2, far_c2, far_kv2, far_c1, gains, biases, far_co, far_cq, far_so,
    in_sum, out_sum, g0, g1, y, dx1, dc1, dkv, bias_g, stats,
    x1, x2, h2, q2, c2, kv2, c1, co_w, cq_w, so_w, arrive_sem, cq_g, give_sem, e_own, own_sem, mine3, theirs3, core3, fromx3, sem3, mine4, theirs4, core4, fromx4, sem4,
    part5, core5, fromx5, sem5, full3, full5, co_acc, cq_acc, so_acc, dkv_acc, fetch_sem,
    *ring_refs, count,
):
    steps, chunk, width = fromx5.shape
    cols = q2.shape[1]
    slots = bias_g.shape[0]
    texts = kv2.shape[0] // slots

    def ring_view(ref, way, half, shard):
        high = width // count
        if way == 0:
            return ref.at[pl.ds(pl.multiple_of(shard * high, high), high), pl.ds(half * width, width)]
        return ref.at[pl.ds(pl.multiple_of(shard * 2 * high + half * high, high), high), :]

    ring = Ring(count, (in_g, out_g), (in_sum, out_sum), ring_view, *ring_refs)
    fetch = own_copy(out_grad, e_own, own_sem)
    fetch.start()
    greet(*ring.peers)
    ring.start()
    three = FarHop(third, core3, fromx3, full3, sem3, chunk)
    four = FarHop(ffn_part, core4, fromx4, None, sem4, chunk)
    five = Hop(part5, core5, fromx5, full5, sem5, chunk)
    arriving = moves(
        (far_x2, far_x1, far_h2, far_q2, far_c2, far_kv2, far_c1, far_co, far_cq, far_so),
        (x2, x1, h2, q2, c2, kv2, c1, co_w, cq_w, so_w),
        arrive_sem,
    )
    three.fetch(mine3, theirs3, fetch_sem.at[0])
    for copy in arriving:
        copy.start()
    four.fetch(mine4, theirs4, fetch_sem.at[1])

    def start(step, carry):
        three.send_core(step)
        four.send_core(step)
        return carry

    lax.fori_loop(0, steps, start, 0)
    for ref in (co_acc, cq_acc, so_acc, dkv_acc, bias_g, stats):
        ref[...] = jnp.zeros_like(ref)
    three.fetched()
    four.fetched()
    fetch.wait()
    for copy in arriving:
        copy.wait()
    valid_rows = left_here(lens, x1.shape[0], h2.shape[0])
    scale = jnp.bfloat16(HEAD_DIM**-0.5)

    def norm_three(step):
        rows = three.own_rows(step)
        grad_in = three.result(step)
        _, normed, inv_std = norm_forward(x2[rows, :], gains[2:3, :], gains[2:3, :])
        stats[0:1, :] += column_sum(grad_in * normed)
        stats[1:2, :] += column_sum(grad_in)
        above = jnp.where(row_of(step, chunk, width) < valid_rows, e_own[rows, :].astype(jnp.float32), 0.0)
        total = above + norm_backward(grad_in, normed, inv_std, gains[2:3, :])
        stats[2:3, :] += column_sum(above)
        stats[3:4, :] += column_sum(total)
        dx1[rows, :] = total
        three.send_gather(step, total.astype(jnp.bfloat16))

    def cross(step):
        three.gathered(step)
        grads = three.take(full3, step)
        co_acc[...] += dot_tn(three.take(c2, step), grads)
        context = dot_nt(grads, co_w[...]).astype(jnp.bfloat16)
        queries = three.take(q2, step) * scale
        count = queries.shape[0] // slots
        place_of = lax.broadcasted_iota(jnp.int32, (texts, count), 0)
        q_grad = []
        for slot in range(slots):
            rows = slice(slot * count, (slot + 1) * count)
            texts_here = slice(slot * texts, (slot + 1) * texts)
            keys, values = kv2[texts_here, :cols], kv2[texts_here, cols:]
            total = jnp.zeros((count, cols), jnp.float32)
            for head in range(cols // HEAD_DIM):
                q_head, g_head = pick_head(queries[rows], head), pick_head(context[rows], head)
                scores = jnp.where(place_of < text_lens[slot], dot_nt(keys, q_head), MASKED_SCORE)
                weights = jnp.exp(scores - jnp.max(scores, axis=0, keepdims=True))
                weights = weights * (1.0 / jnp.sum(weights, axis=0, keepdims=True))
                dkv_acc[texts_here, cols:] += dot_nn(weights.astype(jnp.bfloat16), g_head)
                weight_grad = dot_nt(values, g_head)
                inner = jnp.sum(weights * weight_grad, axis=0, keepdims=True)
                score_grad = (weights * (weight_grad - inner)).astype(jnp.bfloat16)
                dkv_acc[texts_here, :cols] += dot_nn(score_grad, q_head)
                total += dot_tn(score_grad, pick_head(keys, head))
            q_grad.append((total * HEAD_DIM**-0.5).astype(jnp.bfloat16))
        q_grad = jnp.concatenate(q_grad, axis=0)
        five.put(part5, step, dot_nt(q_grad, cq_w[...]).astype(jnp.bfloat16))
        five.send_core(step)
        bias_g[0:1, :] += column_sum(q_grad.astype(jnp.float32))
        cq_acc[...] += dot_tn(five.take(h2, step), q_grad)

    def norm_two(step):
        rows = five.own_rows(step)
        grad_in = five.result(step)
        _, normed, inv_std = norm_forward(x1[rows, :], gains[1:2, :], gains[1:2, :])
        stats[4:5, :] += column_sum(grad_in * normed)
        stats[5:6, :] += column_sum(grad_in)
        total = dx1[rows, :] + norm_backward(grad_in, normed, inv_std, gains[1:2, :])
        stats[6:7, :] += column_sum(total)
        dx1[rows, :] = total
        five.send_gather(step, total.astype(jnp.bfloat16))

    def last(step):
        five.gathered(step)
        grads = five.take(full5, step)
        dc1_rows = dot_nt(grads, so_w[...]).astype(jnp.bfloat16)
        five.put(dc1, step, dc1_rows)
        so_acc[...] += dot_tn(five.take(c1, step), grads)

    def output(step):
        rows = four.own_rows(step)
        total = x2[rows, :] + four.result(step) + biases[2:3, :]
        y[rows, :] = jnp.where(row_of(step, chunk, width) < valid_rows, total, 0.0).astype(jnp.bfloat16)

    half = steps // 2
    late = steps + 2

    def side(half_tick):
        tick = half_tick // 2
        for begin, first in ((0, 0), (late, half)):
            for ahead, work in ((1, output), (0, four.send_cross)):
                step = tick - begin - ahead

                @pl.when((step >= 0) & (step < half) & (half_tick % 2 == 1))
                def _():
                    work(first + step)

    stages(
        steps,
        list(
            enumerate(
                [
                    three.send_cross, norm_three, three.forward, cross,
                    five.send_cross, norm_two, five.forward, last,
                ]
            )
        ),
        ring,
        side,
        late + half + 1,
    )
    dkv[...] = dkv_acc[...].astype(jnp.bfloat16)
    bias_g[1:2, :] = column_sum(dkv[:, cols:].astype(jnp.float32))
    mine4[:cols, :] = co_acc[...].astype(jnp.bfloat16)
    cq_g[...] = cq_acc[...].astype(jnp.bfloat16)
    mine4[cols : 2 * cols, :] = so_acc[...].astype(jnp.bfloat16)
    gives = [
        pltpu.make_async_copy(cq_g, g0.at[:, pl.ds(width - cols, cols)], give_sem.at[0]),
        pltpu.make_async_copy(mine4.at[pl.ds(0, 2 * cols), :], g1.at[pl.ds(0, 2 * cols), :], give_sem.at[1]),
    ]
    for give in gives:
        give.start()

    def finish(step, carry):
        three.finish(step)
        four.finish(step, False)
        five.finish(step)
        return carry

    lax.fori_loop(0, steps, finish, 0)
    ring.finish()
    for give in gives:
        give.wait()


def turn(
    count, third, ffn_part, in_g, out_g, out_grad, lens, text_lens,
    x1, x2, h2, q2, c2, kv2, c1, gains, biases, co_w, cq_w, so_w,
):
    rows, cols = c1.shape
    own, width = x1.shape
    chunk = own // STEPS
    bf, f32 = jnp.bfloat16, jnp.float32
    shape = jax.ShapeDtypeStruct
    vmem = pl.BlockSpec(memory_space=pltpu.VMEM)
    hbm = pl.BlockSpec(memory_space=pl.ANY)
    hop = hop_scratch(own, chunk, width)
    far = [pltpu.VMEM((own, width), bf)] * 2 + hop
    return pl.pallas_call(
        functools.partial(turn_kernel, count=count),
        in_specs=[hbm] * 5 + [pl.BlockSpec(memory_space=pltpu.SMEM)] * 2 + [hbm] * 7 + [vmem] * 2 + [hbm] * 3,
        out_specs=[hbm] * 4 + [vmem] * 6,
        out_shape=[
            pltpu.HBM(in_g.shape, bf),
            pltpu.HBM(out_g.shape, bf),
            pltpu.HBM((width, width), bf),
            pltpu.HBM((width, width), bf),
            shape((own, width), bf),
            shape((own, width), f32),
            shape((rows, cols), bf),
            shape(kv2.shape, bf),
            shape((2, cols), f32),
            shape((8, width), f32),
        ],
        scratch_shapes=[pltpu.VMEM(a.shape, a.dtype) for a in (x1, x2, h2, q2, c2, kv2, c1, co_w, cq_w, so_w)]
        + [
            pltpu.SemaphoreType.DMA((10,)),
            pltpu.VMEM((width, cols), bf),
            pltpu.SemaphoreType.DMA((2,)),
            pltpu.VMEM((own, width), bf),
            pltpu.SemaphoreType.DMA,
        ]
        + far
        + far
        + [pltpu.VMEM((rows, width), bf)]
        + hop
        + [pltpu.VMEM((rows, width), bf)] * 2
        + [
            pltpu.VMEM((cols, width), f32),
            pltpu.VMEM((width, cols), f32),
            pltpu.VMEM((cols, width), f32),
            pltpu.VMEM(kv2.shape, f32),
            pltpu.SemaphoreType.DMA((2, 2)),
        ]
        + ring_scratch(count, (width // count, width)),
        compiler_params=pltpu.CompilerParams(collective_id=1, has_side_effects=True, vmem_limit_bytes=60 * MIB),
        cost_estimate=pl.CostEstimate(flops=100 * 10**9, bytes_accessed=24 * MIB, transcendentals=4 * MIB),
        name="turn",
    )(
        third, ffn_part, in_g, out_g, out_grad, lens, text_lens,
        x1, x2, h2, q2, c2, kv2, c1, gains, biases, co_w, cq_w, so_w,
    )


SMALL = 16
NORM_ROWS = 9


class Small:
    def __init__(self, count, block, near, far, sems):
        self.count, self.mine, self.near, self.far, self.sems = count, block, near, far, sems
        self.index, self.core, self.cross, _ = place()
        self.spot, *self.peers = ring_place(count)

    def near_copy(self, kind):
        owner = self.cross if kind == 2 else self.index
        return remote(self.near.at[owner], self.near.at[owner], self.sems, 0, kind, (self.cross, self.core, self.core)[kind])

    def far_copy(self, way, step):
        block = self.far.at[(self.spot + (2 * way - 1) * step + self.count) % self.count]
        return remote(block, block, self.sems, 1 + way, step, self.peers[way], "wide")

    def begin(self):
        self.near[self.index] = self.mine[...]
        self.near_copy(0).start()
        self.near_copy(1).start()

    def forward(self):
        self.near_copy(0).wait_recv()
        self.near_copy(2).start()

    def launch(self):
        self.near_copy(1).wait_recv()
        self.near_copy(2).wait_recv()
        both = self.near[0]
        for owner in range(1, NARROW):
            both += self.near[owner]
        row = lax.broadcasted_iota(jnp.int32, both.shape, 0)
        self.far[self.spot] = jnp.where(row < SMALL - NORM_ROWS, self.mine[...], both)
        self.far_copy(0, 0).start()
        self.far_copy(1, 0).start()

    def rotate(self, step):
        for way in range(2):
            steps = self.count // 2 - way

            @pl.when(step < steps)
            def _():
                self.far_copy(way, step).wait_recv()

            @pl.when(step < steps - 1)
            def _():
                self.far_copy(way, step + 1).start()

    def finish(self, out):
        for kind in range(3):
            self.near_copy(kind).wait_send()

        for way in range(2):

            def body(step, carry):
                self.far_copy(way, step).wait_send()
                return carry

            lax.fori_loop(0, self.count // 2 - way, body, 0)
        out[...] = jnp.zeros_like(out)

        def add(spot, carry):
            out[...] += self.far[spot]
            return carry

        lax.fori_loop(0, self.count, add, 0)


def last_kernel(
    g0, g1, all_units, far_dqkv, far_dkv, far_dx1, far_qkv, far_kv, self_b, cross_b, ffn_b, stats, gains,
    sum0, sum1, units_g, text_g, small_sum,
    dqkv, dkv, dx1, qkv_w, kv_w, arrive_sem, units, own_sem, part6, core6, fromx6, sem6, part7, core7, fromx7, sem7,
    block, near, far, small_sem, *ring_refs, count,
):
    steps, chunk, width = fromx6.shape
    text_steps = fromx7.shape[0]

    def ring_view(ref, way, half, shard):
        high = width // count
        return ref.at[pl.ds(pl.multiple_of(shard * high, high), high), pl.ds(half * (width // 2), width // 2)]

    ring = Ring(count, (g0, g1), (sum0, sum1), ring_view, *ring_refs)
    small = Small(count, block, near, far, small_sem)
    fetch = own_copy(all_units, units, own_sem)
    fetch.start()
    greet(*ring.peers)
    ring.start()
    arriving = moves(
        (far_dqkv, far_dkv, far_dx1, far_qkv, far_kv), (dqkv, dkv, dx1, qkv_w, kv_w), arrive_sem
    )
    for copy in arriving:
        copy.start()
    six = Hop(part6, core6, fromx6, None, sem6, chunk)
    seven = Hop(part7, core7, fromx7, None, sem7, chunk)
    fetch.wait()
    for copy in arriving:
        copy.wait()
    block[...] = jnp.zeros_like(block)
    cols = self_b.shape[1]
    for row in range(2):
        block[0:1, row * cols : (row + 1) * cols] = self_b[row : row + 1, :]
        block[0:1, (2 + row) * cols : (3 + row) * cols] = cross_b[row : row + 1, :]
        block[1 + row : 2 + row, :] = ffn_b[:, row * width : (row + 1) * width]
    block[SMALL - NORM_ROWS : SMALL - 2, :] = stats[:7, :]
    gain = gains[0:1, :]

    def project(step):
        grads = six.take(dqkv, step)
        total = dot_nt(grads[:, :cols], qkv_w[0]) + dot_nt(grads[:, cols : 2 * cols], qkv_w[1])
        six.put(part6, step, (total + dot_nt(grads[:, 2 * cols :], qkv_w[2])).astype(jnp.bfloat16))
        six.send_core(step)

    def norm_one(step):
        rows = six.own_rows(step)
        grad_in = six.result(step)
        _, normed, inv_std = norm_forward(units[rows, :].astype(jnp.float32), gain, gain)
        block[SMALL - 2 : SMALL - 1, :] += column_sum(grad_in * normed)
        block[SMALL - 1 : SMALL, :] += column_sum(grad_in)
        units_g[rows, :] = dx1[rows, :] + norm_backward(grad_in, normed, inv_std, gain)

    def text_only(work):
        def stage(step):
            @pl.when(step < text_steps)
            def _():
                work(step)

        return stage

    def text_project(step):
        seven.put(part7, step, dot_nt(seven.take(dkv, step), kv_w[...]).astype(jnp.bfloat16))
        seven.send_core(step)

    def text_result(step):
        text_g[seven.own_rows(step), :] = seven.result(step)

    ready = 2 * (steps + 1)

    def extra(half_tick):
        for when, work in enumerate((small.begin, small.forward, small.launch)):
            pl.when(half_tick == ready + when)(work)
        step = half_tick - ready - 3

        @pl.when((step >= 0) & (step < count // 2))
        def _():
            small.rotate(step)

    stages(
        steps,
        list(
            enumerate(
                [
                    project, six.send_cross, norm_one, text_only(text_project), text_only(seven.send_cross), text_only(text_result),
                ]
            )
        ),
        ring,
        extra,
        max((ready + 4 + count // 2) // 2, 2 * (count - 1)),
    )

    def finish(step, carry):
        six.finish(step, False)
        text_only(lambda s: seven.finish(s, False))(step)
        return carry

    lax.fori_loop(0, steps, finish, 0)
    ring.finish()
    small.finish(small_sum)


def last(count, g0, g1, units, dqkv, dkv, dx1, qkv_w, kv_w, *rest):
    rows = dqkv.shape[0]
    own, width = dx1.shape
    chunk = own // STEPS
    text_own = dkv.shape[0] // NARROW
    bf, f32 = jnp.bfloat16, jnp.float32
    shape = jax.ShapeDtypeStruct
    vmem = pl.BlockSpec(memory_space=pltpu.VMEM)
    hbm = pl.BlockSpec(memory_space=pl.ANY)
    hop = hop_scratch(own, chunk, width)
    return pl.pallas_call(
        functools.partial(last_kernel, count=count),
        in_specs=[hbm] * 8 + [vmem] * len(rest),
        out_specs=[hbm] * 2 + [vmem] * 3,
        out_shape=[
            pltpu.HBM(g0.shape, bf),
            pltpu.HBM(g1.shape, bf),
            shape((own, width), f32),
            shape((text_own, width), f32),
            shape((SMALL, width), f32),
        ],
        scratch_shapes=[pltpu.VMEM(a.shape, a.dtype) for a in (dqkv, dkv, dx1, qkv_w, kv_w)]
        + [pltpu.SemaphoreType.DMA((5,)), pltpu.VMEM((own, width), bf), pltpu.SemaphoreType.DMA]
        + [pltpu.VMEM((rows, width), bf)]
        + hop
        + [pltpu.VMEM((dkv.shape[0], width), bf)]
        + hop_scratch(text_own, chunk, width)
        + [
            pltpu.VMEM((SMALL, width), f32),
            pltpu.VMEM((NARROW, SMALL, width), f32),
            pltpu.VMEM((count, SMALL, width), f32),
            pltpu.SemaphoreType.DMA((2, 3, max(count // 2, 3))),
        ]
        + ring_scratch(count, (width // count, width // 2)),
        compiler_params=pltpu.CompilerParams(collective_id=2, has_side_effects=True, vmem_limit_bytes=58 * MIB),
        cost_estimate=pl.CostEstimate(flops=30 * 10**9, bytes_accessed=16 * MIB, transcendentals=0),
        name="last",
    )(g0, g1, units, dqkv, dkv, dx1, qkv_w, kv_w, *rest)


def unpack_kernel(
    sum0, sum1, small, y_in, units_in, text_in,
    qkv_g, cq_g, co_g, so_g, kv_g, gain_g, shift_g, bias_g, self_b, cross_b, ffn_b, y, units_g, text_g,
):
    cols = cq_g.shape[1]
    step = pl.program_id(0)
    y[...] = y_in[...]
    units_g[...] = units_in[...]
    text_g[...] = text_in[...]
    for part in range(3):
        qkv_g[part] = sum0[:, part * cols : (part + 1) * cols].astype(jnp.float32)
    cq_g[...] = sum0[:, 3 * cols :].astype(jnp.float32)
    for when, ref in enumerate((co_g, so_g)):

        @pl.when(step == when)
        def _():
            ref[...] = sum1[...].astype(jnp.float32)

    half = kv_g.shape[0] // 2
    for when in range(half // cols):

        @pl.when(step == 2 + when)
        def _():
            for side in range(2):
                rows = slice(side * half + when * cols, side * half + (when + 1) * cols)
                for part in range(2):
                    first = (2 * side + part) * cols
                    kv_g[rows, part, :] = sum1[:, first : first + cols].astype(jnp.float32)

    @pl.when(step == 0)
    def _():
        norms = small[SMALL - NORM_ROWS :, :]
        for ref, order in ((gain_g, (7, 4, 0)), (shift_g, (8, 5, 1)), (bias_g, (6, 3, 2))):
            for row, source in enumerate(order):
                ref[row : row + 1, :] = norms[source : source + 1, :]
        width = small.shape[1]
        for row in range(2):
            self_b[row : row + 1, :] = small[0:1, row * cols : (row + 1) * cols]
            cross_b[row : row + 1, :] = small[0:1, (2 + row) * cols : (3 + row) * cols]
            ffn_b[:, row * width : (row + 1) * width] = small[1 + row : 2 + row, :]


def unpack(sum0, sum1, small, cols, hidden, *row_outs):
    width = sum0.shape[0]
    steps = width // cols
    f32 = jnp.float32
    block = lambda a: pl.BlockSpec((a.shape[0] // steps,) + a.shape[1:], lambda i: (i, 0))
    whole = lambda a: pl.BlockSpec(a.shape, lambda i: (0,) * len(a.shape))
    fixed = [
        jax.ShapeDtypeStruct(dims, f32)
        for dims in (
            (cols, width), (cols, width), (width, 2, cols),
            (3, width), (3, width), (3, width), (2, cols), (2, cols), (1, hidden),
        )
    ]
    moving = [jax.ShapeDtypeStruct((3, width, cols), f32), jax.ShapeDtypeStruct((width, cols), f32)]
    return pl.pallas_call(
        unpack_kernel,
        grid=(steps,),
        in_specs=[block(sum0), block(sum1), whole(small)] + [block(a) for a in row_outs],
        out_specs=[pl.BlockSpec((3, cols, cols), lambda i: (0, i, 0)), block(moving[1])]
        + [whole(a) for a in fixed]
        + [block(a) for a in row_outs],
        out_shape=moving + fixed + [jax.ShapeDtypeStruct(a.shape, a.dtype) for a in row_outs],
        compiler_params=pltpu.CompilerParams(vmem_limit_bytes=60 * MIB),
        name="unpack",
    )(sum0, sum1, small, *row_outs)


def local(
    units,
    text,
    out_grad,
    unit_lengths,
    text_lengths,
    bucket_counts,
    norm_gain,
    norm_shift,
    self_qkv,
    self_bias,
    self_out,
    cross_q,
    cross_kv,
    cross_bias,
    cross_out,
    ffn_in,
    ffn_in_bias,
    ffn_out,
    out_bias,
):
    slot_live = jnp.arange(unit_lengths.shape[0], dtype=jnp.int32) < bucket_counts[0]
    lengths = jnp.where(slot_live, unit_lengths, 0)
    qkv_weights = jnp.transpose(self_qkv, (1, 0, 2))
    kv_weights = cross_kv.reshape(cross_kv.shape[0], -1)
    count = lax.axis_size("wide")
    first_in, queries, key_rows, value_rows, text_kv, self_context, self_logs = front(
        lengths, units, text, norm_gain, norm_shift, qkv_weights, self_bias, kv_weights, cross_bias
    )
    (
        ffn_part,
        third_part,
        ffn_in_grad,
        ffn_out_grad,
        second_all,
        cross_queries,
        cross_context,
        resid_one,
        resid_two,
        ffn_bias_sum,
    ) = middle(
        units,
        out_grad,
        ffn_in,
        ffn_out,
        self_out,
        cross_q,
        cross_out,
        lengths,
        text_lengths,
        self_context,
        text_kv,
        norm_gain,
        norm_shift,
        out_bias,
        cross_bias,
        ffn_in_bias,
    )
    in_sum, out_sum, grads_one, grads_two, output, resid_one_grad, context_grad, text_kv_grad, cross_bias_sum, stats = turn(
        count,
        third_part,
        ffn_part,
        ffn_in_grad,
        ffn_out_grad,
        out_grad,
        lengths,
        text_lengths,
        resid_one,
        resid_two,
        second_all,
        cross_queries,
        cross_context,
        text_kv,
        self_context,
        norm_gain,
        out_bias,
        cross_out,
        cross_q,
        self_out,
    )
    qkv_grad, grads_one, grads_two, self_bias_sum, ffn_in_grad, ffn_out_grad = back(
        lengths,
        queries,
        key_rows,
        value_rows,
        context_grad,
        self_context,
        self_logs,
        first_in,
        text,
        text_kv_grad,
        in_sum,
        out_sum,
        grads_one,
        grads_two,
    )
    summed_one, summed_two, units_grad, text_grad, small = last(
        count,
        grads_one,
        grads_two,
        units,
        qkv_grad,
        text_kv_grad,
        resid_one_grad,
        qkv_weights,
        kv_weights,
        self_bias_sum,
        cross_bias_sum,
        ffn_bias_sum,
        stats,
        norm_gain,
    )
    (
        self_qkv_grad,
        cross_q_grad,
        cross_out_grad,
        self_out_grad,
        cross_kv_grad,
        gain_grad,
        shift_grad,
        bias_grad,
        self_bias_grad,
        cross_bias_grad,
        ffn_in_bias_grad,
        output,
        units_grad,
        text_grad,
    ) = unpack(
        summed_one, summed_two, small, queries.shape[1], ffn_in_bias.shape[0], output, units_grad, text_grad
    )
    self_qkv_grad = jnp.transpose(self_qkv_grad, (1, 0, 2))
    ffn_in_bias_grad = ffn_in_bias_grad.reshape(-1)
    return (
        output,
        units_grad,
        text_grad,
        gain_grad,
        shift_grad,
        self_qkv_grad,
        self_bias_grad,
        self_out_grad,
        cross_q_grad,
        cross_kv_grad,
        cross_bias_grad,
        cross_out_grad,
        ffn_in_grad,
        ffn_in_bias_grad,
        ffn_out_grad,
        bias_grad,
    )


def solution(mesh):
    placed = (
        P("wide", None),
        P("wide", None),
        P("wide", None),
        P("wide"),
        P("wide"),
        P("wide"),
        P(),
        P(),
        P(None, None, "narrow"),
        P(None, "narrow"),
        P("narrow", None),
        P(None, "narrow"),
        P(None, None, "narrow"),
        P(None, "narrow"),
        P("narrow", None),
        P(None, "narrow"),
        P("narrow"),
        P("narrow", None),
        P(),
    )
    return jax.shard_map(
        local,
        mesh=mesh,
        in_specs=placed,
        out_specs=(
            P(("wide", "narrow"), None),
            P(("wide", "narrow"), None),
            P(("wide", "narrow"), None),
            P(),
            P(),
            P(None, None, "narrow"),
            P(None, "narrow"),
            P("narrow", None),
            P(None, "narrow"),
            P(None, None, "narrow"),
            P(None, "narrow"),
            P("narrow", None),
            P(None, "narrow"),
            P("narrow"),
            P("narrow", None),
            P(),
        ),
        check_vma=False,
    )
```

```python
import functools

import jax
import jax.numpy as jnp
from jax import lax
from jax.experimental import pallas as pl
from jax.experimental.pallas import tpu as pltpu
from jax.sharding import PartitionSpec as P

HEAD_DIM = 64


NORM_EPSILON = 1e-05
MASKED_SCORE = -1000000000.0
EXACT = lax.Precision.HIGHEST


def norm_forward(values, gain_vec, shift_vec):
    row_mean = jnp.mean(values, axis=-1, keepdims=True)
    centered = values - row_mean
    inv_std = lax.rsqrt(jnp.mean(centered * centered, axis=-1, keepdims=True) + NORM_EPSILON)
    normed = centered * inv_std
    return (normed * gain_vec + shift_vec, normed, inv_std)


def norm_backward(grad_in, normed, inv_std, gain_vec):
    scaled = grad_in * gain_vec
    inner_term = scaled - jnp.mean(scaled, axis=-1, keepdims=True)
    inner_term = inner_term - normed * jnp.mean(scaled * normed, axis=-1, keepdims=True)
    return inner_term * inv_std


BLOCK = 256
LANES = 128
MIB = 1 << 20
NARROW = 4
STEPS = 8
HIDDEN = 512
MESH = pl.DeviceIdType.MESH


def head_mask(shape, head):
    lane = lax.broadcasted_iota(jnp.int32, shape, len(shape) - 1)
    return (lane >= head * HEAD_DIM) & (lane < (head + 1) * HEAD_DIM)


def pick_head(values, head):
    return jnp.where(head_mask(values.shape, head), values, jnp.zeros_like(values))


def dot_nt(a, b):
    return lax.dot_general(a, b, (((1,), (1,)), ((), ())), preferred_element_type=jnp.float32)


def dot_nn(a, b):
    return jnp.dot(a, b, preferred_element_type=jnp.float32)


def dot_tn(a, b):
    return lax.dot_general(a, b, (((0,), (0,)), ((), ())), preferred_element_type=jnp.float32)


def column_sum(values):
    return jnp.sum(values, axis=0, keepdims=True)


def mask_diagonal(scores, axis):
    count = scores.shape[axis]
    parts = [scores] if count == BLOCK else jnp.split(scores, [count - BLOCK], axis=axis)
    keys = lax.broadcasted_iota(jnp.int32, parts[-1].shape, axis)
    queries = lax.broadcasted_iota(jnp.int32, keys.shape, 1 - axis) & (BLOCK - 1)
    parts[-1] = jnp.where(keys <= queries, parts[-1], MASKED_SCORE)
    return jnp.concatenate(parts, axis=axis)


def front_kernel(
    lens, x_ref, t_ref, g_ref, s_ref, w_ref, b_ref, kvw_ref, vb_ref, h_ref, q_ref, k_ref, v_ref, kv_ref, c_ref, log_ref
):
    length = lens[pl.program_id(0)]
    width = q_ref.shape[1]
    both = dot_nn(t_ref[...], kvw_ref[...])
    kv_ref[:, :width] = both[:, :width].astype(jnp.bfloat16)
    kv_ref[:, width:] = (both[:, width:] + vb_ref[1:2, :]).astype(jnp.bfloat16)
    for i in range(x_ref.shape[0] // BLOCK):
        rows = pl.ds(i * BLOCK, BLOCK)

        @pl.when(i * BLOCK < length)
        def _():
            normed, _, _ = norm_forward(x_ref[rows, :].astype(jnp.float32), g_ref[0:1, :], s_ref[0:1, :])
            h1 = normed.astype(jnp.bfloat16)
            h_ref[rows, :] = h1
            queries = (dot_nn(h1, w_ref[0]) + b_ref[0:1, :]).astype(jnp.bfloat16)
            q_ref[rows, :] = queries
            k_ref[rows, :] = dot_nn(h1, w_ref[1]).astype(jnp.bfloat16)
            v_ref[rows, :] = (dot_nn(h1, w_ref[2]) + b_ref[1:2, :]).astype(jnp.bfloat16)
            count = (i + 1) * BLOCK
            keys, values = k_ref[:count, :], v_ref[:count, :]
            scaled = queries * jnp.bfloat16(HEAD_DIM**-0.5)
            total = jnp.zeros((BLOCK, width), jnp.float32)
            logs = jnp.zeros((BLOCK, LANES), jnp.float32)
            lane = lax.broadcasted_iota(jnp.int32, logs.shape, 1)
            for head in range(width // HEAD_DIM):
                scores = mask_diagonal(dot_nt(pick_head(scaled, head), keys), 1)
                top = jnp.max(scores, axis=1, keepdims=True)
                weights = jnp.exp(scores - top)
                norm = jnp.sum(weights, axis=1, keepdims=True)
                total += dot_nn(weights.astype(jnp.bfloat16), pick_head(values, head)) * (1.0 / norm)
                logs = jnp.where(lane == head, top + jnp.log(norm), logs)
            log_ref[:, rows] = logs.T[: log_ref.shape[0], :]
            c_ref[rows, :] = total.astype(jnp.bfloat16)

        @pl.when(i * BLOCK >= length)
        def _():
            for ref in (h_ref, q_ref, k_ref, v_ref, c_ref):
                ref[rows, :] = jnp.zeros((BLOCK, ref.shape[1]), ref.dtype)
            log_ref[:, rows] = jnp.zeros((log_ref.shape[0], BLOCK), jnp.float32)


def front(lengths, units, text, gains, shifts, weights, bias, kv_w, cross_bias):
    rows, width = units.shape
    slots = lengths.shape[0]
    slot_rows = rows // slots
    cols = weights.shape[2]
    whole = lambda a: pl.BlockSpec(a.shape, lambda s, *_: (0,) * a.ndim)
    slot = lambda w: pl.BlockSpec((slot_rows, w), lambda s, *_: (s, 0))
    texts = lambda w: pl.BlockSpec((text.shape[0] // slots, w), lambda s, *_: (s, 0))
    logs = pl.BlockSpec((8, slot_rows), lambda s, *_: (0, s))
    shape = lambda w: jax.ShapeDtypeStruct((rows, w), jnp.bfloat16)
    far = lambda w: pltpu.HBM((rows, w), jnp.bfloat16)
    return pl.pallas_call(
        front_kernel,
        grid_spec=pltpu.PrefetchScalarGridSpec(
            num_scalar_prefetch=1,
            grid=(slots,),
            in_specs=[slot(width), texts(width)]
            + [whole(a) for a in (gains, shifts, weights, bias, kv_w, cross_bias)],
            out_specs=[slot(width), slot(cols), slot(cols), slot(cols), texts(2 * cols), slot(cols), logs],
        ),
        out_shape=[
            far(width),
            far(cols),
            far(cols),
            far(cols),
            jax.ShapeDtypeStruct((text.shape[0], 2 * cols), jnp.bfloat16),
            shape(cols),
            pltpu.HBM((8, rows), jnp.float32),
        ],
        compiler_params=pltpu.CompilerParams(vmem_limit_bytes=60 * MIB),
        cost_estimate=pl.CostEstimate(flops=20 * 10**9, bytes_accessed=16 * MIB, transcendentals=8 * MIB),
        name="front",
    )(lengths, units, text, gains, shifts, weights, bias, kv_w, cross_bias)


def back_kernel(
    lens, q_ref, k_ref, v_ref, dc_ref, c_ref, log_ref, h_ref, text_ref, dkv_ref, in_ref, out_ref, _g0, _g1,
    o_ref, g0_ref, g1_ref, b_ref, in_f32, out_f32, dk_acc, dv_acc, w_acc,
):
    in_f32[...] = in_ref[...].astype(jnp.float32)
    out_f32[...] = out_ref[...].astype(jnp.float32)
    slot, turn_now = pl.program_id(0), pl.program_id(1)
    slot_rows, width = q_ref.shape
    heads = range(width // HEAD_DIM)

    @pl.when((slot == 0) & (turn_now == 0))
    def _():
        w_acc[...] = jnp.zeros_like(w_acc)
        b_ref[...] = jnp.zeros_like(b_ref)
        kv_grad = dot_tn(text_ref[...], dkv_ref[...]).astype(jnp.bfloat16)
        half, both = g1_ref.shape[0], dkv_ref.shape[1]
        g1_ref[:, :both] = kv_grad[:half]
        g1_ref[:, both:] = kv_grad[half:]

    @pl.when(turn_now == 0)
    def _():
        dk_acc[...] = jnp.zeros_like(dk_acc)
        dv_acc[...] = jnp.zeros_like(dv_acc)
        o_ref[:, :width] = jnp.zeros((slot_rows, width), jnp.bfloat16)

    def stack(values):
        return jnp.concatenate([pick_head(values, head) for head in heads], axis=0)

    def side_by_side(values):
        return jnp.concatenate([values[head : head + 1, :] for head in heads], axis=1)

    for i in range(slot_rows // BLOCK):
        rows = pl.ds(i * BLOCK, BLOCK)

        @pl.when((turn_now == i) & (i * BLOCK < lens[slot]))
        def _():
            count = (i + 1) * BLOCK
            keys, values = k_ref[:count, :], v_ref[:count, :]
            grads = dc_ref[rows, :]
            q_heads, g_heads = stack(q_ref[rows, :] * jnp.bfloat16(HEAD_DIM**-0.5)), stack(grads)
            owners = lax.broadcasted_iota(jnp.int32, (8, width), 0)
            lanes = lax.broadcasted_iota(jnp.int32, (8, width), 1)
            inner = lax.dot_general(
                jnp.where((lanes >= owners * HEAD_DIM) & (lanes < (owners + 1) * HEAD_DIM), 1.0, 0.0),
                grads.astype(jnp.float32) * c_ref[rows, :].astype(jnp.float32),
                (((1,), (1,)), ((), ())),
                precision=EXACT,
                preferred_element_type=jnp.float32,
            )
            weights = jnp.exp(mask_diagonal(dot_nt(keys, q_heads), 0) - side_by_side(log_ref[:, rows]))
            dv_acc[:count, :] += dot_nn(weights.astype(jnp.bfloat16), g_heads)
            score_grad = (weights * (dot_nt(values, g_heads) - side_by_side(inner))).astype(jnp.bfloat16)
            dk_acc[:count, :] += dot_nn(score_grad, q_heads)
            total = jnp.zeros((BLOCK, width), jnp.float32)
            for head in heads:
                total += dot_tn(score_grad[:, head * BLOCK : (head + 1) * BLOCK], pick_head(keys, head))
            q_grad = (total * HEAD_DIM**-0.5).astype(jnp.bfloat16)
            o_ref[rows, :width] = q_grad
            b_ref[0:1, :] += column_sum(q_grad.astype(jnp.float32))

    @pl.when(turn_now == pl.num_programs(1) - 1)
    def _():
        v_grad = dv_acc[...].astype(jnp.bfloat16)
        o_ref[:, width : 2 * width] = dk_acc[...].astype(jnp.bfloat16)
        o_ref[:, 2 * width :] = v_grad
        b_ref[1:2, :] += column_sum(v_grad.astype(jnp.float32))
        for first in range(0, h_ref.shape[1], BLOCK):
            w_acc[first : first + BLOCK, :] += dot_tn(h_ref[:, first : first + BLOCK], o_ref[...])

        @pl.when(slot == pl.num_programs(0) - 1)
        def _():
            g0_ref[...] = w_acc[...].astype(jnp.bfloat16)


def back(lengths, queries, keys, values, grads, context, logs, rows_in, text, dkv, in_sum, out_sum, g0, g1):
    rows, cols = queries.shape
    width = rows_in.shape[1]
    slots = lengths.shape[0]
    bf, f32 = jnp.bfloat16, jnp.float32
    shape = jax.ShapeDtypeStruct
    slot = lambda a: pl.BlockSpec((a.shape[0] // slots, a.shape[1]), lambda s, i, *_: (s, 0))
    blocks = rows // slots // BLOCK
    piece = lambda a: pl.BlockSpec((a.shape[0] // (slots * blocks), a.shape[1]), lambda s, i, *_: (s * blocks + i, 0))
    whole = lambda a: pl.BlockSpec(a.shape, lambda s, i, *_: (0, 0))
    hbm = pl.BlockSpec(memory_space=pl.ANY)
    half = text.shape[1] // 2
    return pl.pallas_call(
        back_kernel,
        grid_spec=pltpu.PrefetchScalarGridSpec(
            num_scalar_prefetch=1,
            grid=(slots, blocks),
            in_specs=[slot(queries)] * 5
            + [pl.BlockSpec((8, rows // slots), lambda s, i, *_: (0, s))]
            + [slot(rows_in), whole(text), whole(dkv), piece(in_sum), piece(out_sum), hbm, hbm],
            out_specs=[
                pl.BlockSpec((rows // slots, 3 * cols), lambda s, i, *_: (s, 0)),
                pl.BlockSpec((width, 3 * cols), lambda s, i, *_: (0, 0)),
                pl.BlockSpec((half, width), lambda s, i, *_: (1, 0)),
                pl.BlockSpec((2, cols), lambda s, i, *_: (0, 0)),
                piece(in_sum),
                piece(out_sum),
            ],
            scratch_shapes=[pltpu.VMEM((rows // slots, cols), f32)] * 2 + [pltpu.VMEM((width, 3 * cols), f32)],
        ),
        out_shape=[
            shape((rows, 3 * cols), bf),
            pltpu.HBM(g0.shape, bf),
            pltpu.HBM(g1.shape, bf),
            shape((2, cols), f32),
            shape(in_sum.shape, f32),
            shape(out_sum.shape, f32),
        ],
        input_output_aliases={12: 1, 13: 2},
        compiler_params=pltpu.CompilerParams(vmem_limit_bytes=60 * MIB),
        cost_estimate=pl.CostEstimate(flops=30 * 10**9, bytes_accessed=40 * MIB, transcendentals=8 * MIB),
        name="back",
    )(lengths, queries, keys, values, grads, context, logs, rows_in, text, dkv, in_sum, out_sum, g0, g1)


def place():
    index = lax.axis_index("narrow")
    core = index + 1 - 2 * (index % 2)
    return index, core, (index + 2) % NARROW, (core + 2) % NARROW


def greet(*wide_peers):
    _, core, cross, _ = place()
    barrier = pltpu.get_barrier_semaphore()
    for peer in (core, cross):
        pl.semaphore_signal(barrier, inc=1, device_id={"narrow": peer}, device_id_type=MESH)
    for peer in wide_peers:
        pl.semaphore_signal(barrier, inc=1, device_id={"wide": peer}, device_id_type=MESH)
    pl.semaphore_wait(barrier, 2 + len(wide_peers))


def remote(source, target, sems, kind, step, peer, axis="narrow"):
    return pltpu.make_async_remote_copy(
        src_ref=source,
        dst_ref=target,
        send_sem=sems.at[0, kind, step],
        recv_sem=sems.at[1, kind, step],
        device_id={axis: peer},
        device_id_type=MESH,
    )


def ring_place(count):
    wide = lax.axis_index("wide")
    odd, half = wide % 2, wide // 2
    spot = odd * (half + 1) + (1 - odd) * ((count - half) % count)

    def at(where):
        high = ((where + count - 1) % count) // (count // 2)
        return (1 - high) * (2 * where - 1) + high * ((2 * (count - where)) % (2 * count))

    return spot, at((spot + 1) % count), at((spot + count - 1) % count)


class Ring:
    UNITS = 4

    def __init__(self, count, sources, outs, view, arrived, held, sems, fetch_sems, keep_sems):
        self.count, self.sources, self.outs, self.view = count, sources, outs, view
        self.arrived, self.held, self.sems = arrived, held, sems
        self.fetch_sems, self.keep_sems = fetch_sems, keep_sems
        spot, following, previous = ring_place(count)
        self.spots = (spot, (count - spot) % count)
        self.peers = (following, previous)

    def block(self, refs, unit, back_by):
        shard = (self.spots[unit // 2] + 2 * self.count - back_by) % self.count
        return self.view(refs[unit // 2], unit // 2, unit % 2, shard)

    def send(self, source, target, kind, unit, step):
        return remote(source, target, self.sems, kind * self.UNITS + unit, step, self.peers[unit // 2], "wide")

    def sum_copy(self, unit, step, first=False):
        source = self.block(self.sources, unit, 0) if first else self.arrived.at[unit, jnp.maximum(step - 1, 0)]
        return self.send(source, self.arrived.at[unit, step], 0, unit, step)

    def fetch(self, unit, step):
        slot = step % 2
        return pltpu.make_async_copy(
            self.block(self.sources, unit, step + 1), self.held.at[unit, slot], self.fetch_sems.at[unit, slot]
        )

    def keep(self, unit):
        return pltpu.make_async_copy(
            self.arrived.at[unit, self.count - 2], self.block(self.outs, unit, self.count - 1), self.keep_sems.at[unit]
        )

    def spread_copy(self, unit, step, first=False):
        target = self.block(self.outs, unit, self.count - 1 + step)
        source = self.arrived.at[unit, self.count - 2] if first else target
        return self.send(source, target, 1, unit, step)

    def start(self):
        for unit in range(self.UNITS):
            self.sum_copy(unit, 0, True).start()
            self.fetch(unit, 0).start()
            self.fetch(unit, 1).start()

    def serve(self, turn, unit):
        last = self.count - 2

        @pl.when(turn <= last)
        def _():
            self.sum_copy(unit, turn).wait_recv()
            self.fetch(unit, turn).wait()
            total = self.held[unit, turn % 2].astype(jnp.float32) + self.arrived[unit, turn].astype(jnp.float32)
            self.arrived[unit, turn] = total.astype(jnp.bfloat16)

            @pl.when(turn < last)
            def _():
                self.sum_copy(unit, turn + 1).start()

            @pl.when(turn < last - 1)
            def _():
                self.fetch(unit, turn + 2).start()

            @pl.when(turn == last)
            def _():
                self.spread_copy(unit, 0, True).start()
                self.keep(unit).start()

        @pl.when((turn > last) & (turn <= 2 * last + 1))
        def _():
            step = turn - last - 1
            self.spread_copy(unit, step).wait_recv()

            @pl.when(step < last)
            def _():
                self.spread_copy(unit, step + 1).start()

    def finish(self):
        for unit in range(self.UNITS):
            self.keep(unit).wait()

        def body(step, carry):
            for unit in range(self.UNITS):
                self.sum_copy(unit, step).wait_send()
                self.spread_copy(unit, step).wait_send()
            return carry

        lax.fori_loop(0, self.count - 1, body, 0)


def ring_scratch(count, block):
    return [
        pltpu.VMEM((Ring.UNITS, count - 1) + block, jnp.bfloat16),
        pltpu.VMEM((Ring.UNITS, 2) + block, jnp.bfloat16),
        pltpu.SemaphoreType.DMA((2, 2 * Ring.UNITS, count - 1)),
        pltpu.SemaphoreType.DMA((Ring.UNITS, 2)),
        pltpu.SemaphoreType.DMA((Ring.UNITS,)),
    ]


def own_copy(whole, own, sem):
    size = own.shape[0]
    first = pl.multiple_of(lax.axis_index("narrow") * size, size)
    return pltpu.make_async_copy(whole.at[pl.ds(first, size), :], own, sem)


def moves(sources, targets, sems):
    pairs = list(zip(sources, targets, strict=True))
    return [pltpu.make_async_copy(a, b, sems.at[slot]) for slot, (a, b) in enumerate(pairs)]


class Hop:
    KINDS = 6

    def __init__(self, part, from_core, from_cross, full, sems, chunk):
        self.part, self.from_core, self.from_cross = part, from_core, from_cross
        self.full, self.sems, self.chunk = full, sems, chunk
        self.own = part.shape[0] // NARROW
        self.index, self.core, self.cross, self.diagonal = place()

    def rows(self, owner, step):
        return pl.ds(pl.multiple_of(owner * self.own + step * self.chunk, self.chunk), self.chunk)

    def own_rows(self, step):
        return pl.ds(pl.multiple_of(step * self.chunk, self.chunk), self.chunk)

    def core_copies(self, step):
        return [
            remote(self.part.at[self.rows(owner, step)], self.from_core.at[step, slot], self.sems, slot, step, self.core)
            for slot, owner in enumerate((self.core, self.diagonal))
        ]

    def cross_copy(self, step):
        return remote(
            self.part.at[self.rows(self.cross, step)], self.from_cross.at[step], self.sems, 2, step, self.cross
        )

    def gather_copy(self, step, kind):
        owner = self.cross if kind == 5 else self.index
        rows = self.full.at[self.rows(owner, step)]
        return remote(rows, rows, self.sems, kind, step, self.cross if kind == 3 else self.core)

    def send_core(self, step):
        for copy in self.core_copies(step):
            copy.start()

    def send_cross(self, step):
        for copy in self.core_copies(step):
            copy.wait_recv()
        total = self.part[self.rows(self.cross, step), :].astype(jnp.float32)
        total += self.from_core[step, 1].astype(jnp.float32)
        self.part[self.rows(self.cross, step), :] = total.astype(jnp.bfloat16)
        self.cross_copy(step).start()

    def result(self, step):
        total = self.part[self.rows(self.index, step), :].astype(jnp.float32)
        total += self.from_core[step, 0].astype(jnp.float32)
        self.cross_copy(step).wait_recv()
        return total + self.from_cross[step].astype(jnp.float32)

    def send_gather(self, step, values):
        self.full[self.rows(self.index, step), :] = values
        self.gather_copy(step, 3).start()
        self.gather_copy(step, 4).start()

    def forward(self, step):
        self.gather_copy(step, 3).wait_recv()
        self.gather_copy(step, 5).start()

    def gathered(self, step):
        self.gather_copy(step, 4).wait_recv()
        self.gather_copy(step, 5).wait_recv()

    def sent(self, step):
        for copy in self.core_copies(step):
            copy.wait_send()
        self.cross_copy(step).wait_send()

    def finish(self, step, gather=True, parts=True):
        if parts:
            self.sent(step)
        if gather:
            for kind in (3, 4, 5):
                self.gather_copy(step, kind).wait_send()

    def take(self, ref, step):
        return jnp.concatenate([ref[self.rows(owner, step), :] for owner in range(NARROW)], axis=0)

    def put(self, ref, step, values):
        for owner in range(NARROW):
            ref[self.rows(owner, step), :] = values[owner * self.chunk : (owner + 1) * self.chunk]


def hop_scratch(own, chunk, width):
    steps = own // chunk
    return [
        pltpu.VMEM((steps, 2, chunk, width), jnp.bfloat16),
        pltpu.VMEM((steps, chunk, width), jnp.bfloat16),
        pltpu.SemaphoreType.DMA((2, Hop.KINDS, steps)),
    ]


def stages(steps, work, ring=None, extra=None, ticks=0):
    ticks = max(ticks, steps + max(delay for delay, _ in work))
    per_tick = 0 if ring is None else -(-2 * (ring.count - 1) // ticks)

    def body(tick, carry):
        for number, (delay, stage) in enumerate(work):
            step = tick - delay

            @pl.when((step >= 0) & (step < steps))
            def _():
                stage(step)

            unit = (number + 1) * Ring.UNITS // len(work) - 1
            if per_tick and unit != number * Ring.UNITS // len(work) - 1:
                if per_tick == 1:
                    ring.serve(tick, unit)
                else:
                    lax.fori_loop(0, per_tick, lambda i, c: (ring.serve(tick * per_tick + i, unit), c)[1], 0)
            if extra is not None and number in (len(work) // 2, len(work) - 1):
                extra(2 * tick + (number == len(work) - 1))
        return carry

    lax.fori_loop(0, ticks, body, 0)


def middle_kernel(
    all_units, out_grad, far_in, far_out, far_so, far_cq, far_co, lens, text_lens,
    c1, kv2, gains, shifts, biases, bias, b_in,
    ffn_part, third, in_g, out_g, far_h2, far_q2, far_c2, far_x1, far_x2, in_bias_g,
    h2, q2, c2, x1, x2, leave_sem, units, own_sem, so_w, cq_w, co_w, small_sem, w_in, w_out, weight_sem, grads_in, grads_sem, give, give_sem, in_acc, out_acc,
    part, h3, core1, fromx1, sem1, core2, fromx2, sem2,
):
    steps, chunk, width = fromx1.shape
    cols = q2.shape[1]
    slots = text_lens.shape[0]
    texts = kv2.shape[0] // slots
    slot_rows = h2.shape[0] // slots
    hidden_count = w_out.shape[0]
    near = [
        pltpu.make_async_copy(source, target, small_sem.at[slot])
        for slot, (source, target) in enumerate(((far_so, so_w), (far_cq, cq_w), (far_co, co_w)))
    ]
    for fetch in near:
        fetch.start()
    fetches = [
        own_copy(all_units, units, own_sem),
        pltpu.make_async_copy(far_in, w_in, weight_sem.at[0]),
        pltpu.make_async_copy(far_out, w_out, weight_sem.at[1]),
    ]
    fetches[0].start()
    greet()
    one = Hop(part, core1, fromx1, h2, sem1, chunk)
    two = Hop(part, core2, fromx2, h3, sem2, chunk)
    scale = jnp.bfloat16(HEAD_DIM**-0.5)
    in_bias_g[...] = jnp.zeros_like(in_bias_g)
    for fetch in near:
        fetch.wait()

    leaving = moves((h2, q2, c2, x1, x2), (far_h2, far_q2, far_c2, far_x1, far_x2), leave_sem)

    def grad_copies(step):
        slot = step % 2
        return [
            pltpu.make_async_copy(
                out_grad.at[one.rows(owner, step), :],
                grads_in.at[slot, pl.ds(owner * chunk, chunk), :],
                grads_sem.at[slot, owner],
            )
            for owner in range(NARROW)
        ]

    def give_copies(step, kind):
        slot = step % 2
        return [
            pltpu.make_async_copy(
                give.at[kind, slot, pl.ds(owner * chunk, chunk), :],
                (ffn_part, third)[kind].at[one.rows(owner, step), :],
                give_sem.at[kind, slot, owner],
            )
            for owner in range(NARROW)
        ]

    def project(step):
        one.put(part, step, dot_nn(one.take(c1, step), so_w[...]).astype(jnp.bfloat16))
        one.send_core(step)
        for when, ref in ((1, in_acc), (2, out_acc)):

            @pl.when(step == when)
            def _():
                fetches[when].start()
                ref[...] = jnp.zeros_like(ref)

    def norm_one(step):
        @pl.when(step == 0)
        def _():
            fetches[0].wait()

        rows = one.own_rows(step)
        resid = units[rows, :].astype(jnp.float32) + one.result(step) + biases[0:1, :]
        x1[rows, :] = resid
        one.send_gather(step, norm_forward(resid, gains[1:2, :], shifts[1:2, :])[0].astype(jnp.bfloat16))

    def cross(step):
        one.gathered(step)
        queries = (dot_nn(one.take(h2, step), cq_w[...]) + bias[0:1, :]).astype(jnp.bfloat16)
        one.put(q2, step, queries)
        scaled = queries * scale
        count = queries.shape[0] // slots
        place_of = lax.broadcasted_iota(jnp.int32, (count * (cols // HEAD_DIM), texts), 1)
        context = []
        for slot in range(slots):
            mine = scaled[slot * count : (slot + 1) * count]
            keys = kv2[slot * texts : (slot + 1) * texts, :cols]
            values = kv2[slot * texts : (slot + 1) * texts, cols:]
            heads = range(cols // HEAD_DIM)
            scores = dot_nt(jnp.concatenate([pick_head(mine, head) for head in heads], axis=0), keys)
            scores = jnp.where(place_of < text_lens[slot], scores, MASKED_SCORE)
            weights = jnp.exp(scores - jnp.max(scores, axis=1, keepdims=True))
            norm = jnp.sum(weights, axis=1, keepdims=True)
            mixed = dot_nn(weights.astype(jnp.bfloat16), values) * (1.0 / norm)
            total = jnp.zeros((count, cols), jnp.float32)
            for head in heads:
                total += pick_head(mixed[head * count : (head + 1) * count], head)
            context.append(total.astype(jnp.bfloat16))
        context = jnp.concatenate(context, axis=0)
        one.put(c2, step, context)
        one.sent(step)
        two.put(part, step, dot_nn(context, co_w[...]).astype(jnp.bfloat16))
        two.send_core(step)

    def norm_two(step):
        rows = one.own_rows(step)
        resid = x1[rows, :] + two.result(step) + biases[1:2, :]
        x2[rows, :] = resid
        two.send_gather(step, norm_forward(resid, gains[2:3, :], shifts[2:3, :])[0].astype(jnp.bfloat16))

    def forward_two(step):
        two.forward(step)
        for copy in grad_copies(step):
            copy.start()

    def ffn(step):
        @pl.when(step == 0)
        def _():
            fetches[1].wait()
            fetches[2].wait()

        @pl.when(step == steps - 3)
        def _():
            for copy in leaving:
                copy.start()

        two.gathered(step)
        for copy in grad_copies(step):
            copy.wait()
        rows = two.take(h3, step)
        place_in = lax.broadcasted_iota(jnp.int32, (chunk, width), 0) + step * chunk
        grads = []
        for owner in range(NARROW):
            first = owner * two.own
            valid = place_in < lens[first // slot_rows] - first % slot_rows
            values = grads_in[step % 2, owner * chunk : (owner + 1) * chunk, :]
            grads.append(jnp.where(valid, values.astype(jnp.float32), 0.0).astype(jnp.bfloat16))
        grads = jnp.concatenate(grads, axis=0)
        out = jnp.zeros(rows.shape, jnp.float32)
        back_out = jnp.zeros(rows.shape, jnp.float32)
        for begin in range(0, hidden_count, HIDDEN):
            some = slice(begin, begin + HIDDEN)
            pre = dot_nn(rows, w_in[:, some]) + b_in[:, some]
            cdf = 0.5 + 0.5 * lax.erf(pre * (0.5**0.5))
            pdf = jnp.exp(-0.5 * pre * pre) * 0.3989422804014327
            hidden = (pre * cdf).astype(jnp.bfloat16)
            pre_low = ((cdf + pre * pdf) * dot_nt(grads, w_out[some, :])).astype(jnp.bfloat16)
            in_bias_g[:, some] += column_sum(pre_low.astype(jnp.float32))
            out += dot_nn(hidden, w_out[some, :])
            back_out += dot_nt(pre_low, w_in[:, some])
            out_acc[some, :] += dot_tn(hidden, grads)
            side, place_at = divmod(begin, width)
            in_acc[side * width : (side + 1) * width, place_at : place_at + HIDDEN] += dot_tn(rows, pre_low)

        @pl.when(step >= 2)
        def _():
            for kind in range(2):
                for copy in give_copies(step - 2, kind):
                    copy.wait()

        give[0, step % 2] = out.astype(jnp.bfloat16)
        give[1, step % 2] = back_out.astype(jnp.bfloat16)
        for kind in range(2):
            for copy in give_copies(step, kind):
                copy.start()

    stages(
        steps,
        [
            (0, project), (1, one.send_cross), (2, norm_one), (3, one.forward), (4, cross),
            (5, two.send_cross), (6, norm_two), (7, forward_two), (8, ffn),
        ],
    )

    def finish(step, carry):
        one.finish(step, True, False)
        two.finish(step)
        return carry

    lax.fori_loop(0, steps, finish, 0)
    part[...] = out_acc[...].astype(jnp.bfloat16)
    results = [pltpu.make_async_copy(part, out_g, weight_sem.at[0])]
    results[0].start()
    for side in range(hidden_count // width):
        here = pl.ds(side * width, width)
        h3[here, :] = in_acc[here, :].astype(jnp.bfloat16)
        results.append(pltpu.make_async_copy(h3.at[here, :], in_g.at[:, here], weight_sem.at[1 + side]))
        results[-1].start()
    for step in (steps - 2, steps - 1):
        for kind in range(2):
            for copy in give_copies(step, kind):
                copy.wait()
    for copy in results + leaving:
        copy.wait()


def middle(units, out_grad, w_in, w_out, so_w, cq_w, co_w, lens, text_lens, c1, kv2, gains, shifts, biases, bias, b_in):
    rows, cols = c1.shape
    own, width = rows // NARROW, units.shape[1]
    hidden_count = w_out.shape[0]
    chunk = own // STEPS
    bf, f32 = jnp.bfloat16, jnp.float32
    shape = jax.ShapeDtypeStruct
    vmem = pl.BlockSpec(memory_space=pltpu.VMEM)
    hbm = pl.BlockSpec(memory_space=pl.ANY)
    hop = hop_scratch(own, chunk, width)
    dma = pltpu.SemaphoreType.DMA
    return pl.pallas_call(
        middle_kernel,
        in_specs=[hbm] * 7 + [pl.BlockSpec(memory_space=pltpu.SMEM)] * 2 + [vmem] * 7,
        out_specs=[hbm] * 9 + [vmem],
        out_shape=[
            pltpu.HBM((rows, width), bf),
            pltpu.HBM((rows, width), bf),
            pltpu.HBM((width, hidden_count), bf),
            pltpu.HBM((hidden_count, width), bf),
            pltpu.HBM((rows, width), bf),
            pltpu.HBM((rows, cols), bf),
            pltpu.HBM((rows, cols), bf),
            pltpu.HBM((own, width), f32),
            pltpu.HBM((own, width), f32),
            shape((1, hidden_count), f32),
        ],
        scratch_shapes=[
            pltpu.VMEM((rows, width), bf),
            pltpu.VMEM((rows, cols), bf),
            pltpu.VMEM((rows, cols), bf),
            pltpu.VMEM((own, width), f32),
            pltpu.VMEM((own, width), f32),
            dma((5,)),
            pltpu.VMEM((own, width), bf),
            dma,
            pltpu.VMEM(so_w.shape, bf),
            pltpu.VMEM(cq_w.shape, bf),
            pltpu.VMEM(co_w.shape, bf),
            dma((3,)),
            pltpu.VMEM((width, hidden_count), bf),
            pltpu.VMEM((hidden_count, width), bf),
            dma((1 + hidden_count // width,)),
            pltpu.VMEM((2, NARROW * chunk, width), bf),
            dma((2, NARROW)),
            pltpu.VMEM((2, 2, NARROW * chunk, width), bf),
            dma((2, 2, NARROW)),
            pltpu.VMEM((hidden_count, width), f32),
            pltpu.VMEM((hidden_count, width), f32),
            pltpu.VMEM((rows, width), bf),
            pltpu.VMEM((rows, width), bf),
        ]
        + hop
        + hop,
        compiler_params=pltpu.CompilerParams(collective_id=0, has_side_effects=True, vmem_limit_bytes=60 * MIB),
        cost_estimate=pl.CostEstimate(flops=100 * 10**9, bytes_accessed=48 * MIB, transcendentals=8 * MIB),
        name="middle",
    )(
        units, out_grad, w_in, w_out, so_w, cq_w, co_w, lens, text_lens, c1, kv2, gains, shifts, biases, bias,
        b_in.reshape(1, -1),
    )


class FarHop(Hop):
    def fetch(self, mine, theirs, sems):
        self.mine, self.theirs = mine, theirs
        rows = lambda owner: pl.ds(pl.multiple_of(owner * self.own, self.own), self.own)
        self.fetches = [
            pltpu.make_async_copy(self.part.at[rows(owner)], ref, sems.at[slot])
            for slot, (owner, ref) in enumerate(((self.index, mine), (self.cross, theirs)))
        ]
        for copy in self.fetches:
            copy.start()

    def fetched(self):
        for copy in self.fetches:
            copy.wait()

    def cross_copy(self, step):
        return remote(
            self.theirs.at[self.own_rows(step)], self.from_cross.at[step], self.sems, 2, step, self.cross
        )

    def send_cross(self, step):
        for copy in self.core_copies(step):
            copy.wait_recv()
        total = self.theirs[self.own_rows(step), :].astype(jnp.float32)
        total += self.from_core[step, 1].astype(jnp.float32)
        self.theirs[self.own_rows(step), :] = total.astype(jnp.bfloat16)
        self.cross_copy(step).start()

    def result(self, step):
        total = self.mine[self.own_rows(step), :].astype(jnp.float32)
        total += self.from_core[step, 0].astype(jnp.float32)
        self.cross_copy(step).wait_recv()
        return total + self.from_cross[step].astype(jnp.float32)


def left_here(lens, own, rows):
    first = lax.axis_index("narrow") * own
    slot_rows = rows // lens.shape[0]
    return lens[first // slot_rows] - first % slot_rows


def row_of(step, chunk, width):
    return lax.broadcasted_iota(jnp.int32, (chunk, width), 0) + step * chunk


def turn_kernel(
    third, ffn_part, in_g, out_g, out_grad, lens, text_lens,
    far_x1, far_x2, far_h2, far_q2, far_c2, far_kv2, far_c1, gains, biases, far_co, far_cq, far_so,
    in_sum, out_sum, g0, g1, y, dx1, dc1, dkv, bias_g, stats,
    x1, x2, h2, q2, c2, kv2, c1, co_w, cq_w, so_w, arrive_sem, cq_g, give_sem, e_own, own_sem, mine3, theirs3, core3, fromx3, sem3, mine4, theirs4, core4, fromx4, sem4,
    part5, core5, fromx5, sem5, full3, full5, co_acc, cq_acc, so_acc, dkv_acc, fetch_sem,
    *ring_refs, count,
):
    steps, chunk, width = fromx5.shape
    cols = q2.shape[1]
    slots = bias_g.shape[0]
    texts = kv2.shape[0] // slots

    def ring_view(ref, way, half, shard):
        high = width // count
        if way == 0:
            return ref.at[pl.ds(pl.multiple_of(shard * high, high), high), pl.ds(half * width, width)]
        return ref.at[pl.ds(pl.multiple_of(shard * 2 * high + half * high, high), high), :]

    ring = Ring(count, (in_g, out_g), (in_sum, out_sum), ring_view, *ring_refs)
    fetch = own_copy(out_grad, e_own, own_sem)
    fetch.start()
    greet(*ring.peers)
    ring.start()
    three = FarHop(third, core3, fromx3, full3, sem3, chunk)
    four = FarHop(ffn_part, core4, fromx4, None, sem4, chunk)
    five = Hop(part5, core5, fromx5, full5, sem5, chunk)
    arriving = moves(
        (far_x2, far_x1, far_h2, far_q2, far_c2, far_kv2, far_c1, far_co, far_cq, far_so),
        (x2, x1, h2, q2, c2, kv2, c1, co_w, cq_w, so_w),
        arrive_sem,
    )
    three.fetch(mine3, theirs3, fetch_sem.at[0])
    for copy in arriving:
        copy.start()
    four.fetch(mine4, theirs4, fetch_sem.at[1])

    def start(step, carry):
        three.send_core(step)
        four.send_core(step)
        return carry

    lax.fori_loop(0, steps, start, 0)
    for ref in (co_acc, cq_acc, so_acc, dkv_acc, bias_g, stats):
        ref[...] = jnp.zeros_like(ref)
    three.fetched()
    four.fetched()
    fetch.wait()
    for copy in arriving:
        copy.wait()
    valid_rows = left_here(lens, x1.shape[0], h2.shape[0])
    scale = jnp.bfloat16(HEAD_DIM**-0.5)

    def norm_three(step):
        rows = three.own_rows(step)
        grad_in = three.result(step)
        _, normed, inv_std = norm_forward(x2[rows, :], gains[2:3, :], gains[2:3, :])
        stats[0:1, :] += column_sum(grad_in * normed)
        stats[1:2, :] += column_sum(grad_in)
        above = jnp.where(row_of(step, chunk, width) < valid_rows, e_own[rows, :].astype(jnp.float32), 0.0)
        total = above + norm_backward(grad_in, normed, inv_std, gains[2:3, :])
        stats[2:3, :] += column_sum(above)
        stats[3:4, :] += column_sum(total)
        dx1[rows, :] = total
        three.send_gather(step, total.astype(jnp.bfloat16))

    def cross(step):
        three.gathered(step)
        grads = three.take(full3, step)
        co_acc[...] += dot_tn(three.take(c2, step), grads)
        context = dot_nt(grads, co_w[...]).astype(jnp.bfloat16)
        queries = three.take(q2, step) * scale
        count = queries.shape[0] // slots
        place_of = lax.broadcasted_iota(jnp.int32, (texts, count), 0)
        q_grad = []
        for slot in range(slots):
            rows = slice(slot * count, (slot + 1) * count)
            texts_here = slice(slot * texts, (slot + 1) * texts)
            keys, values = kv2[texts_here, :cols], kv2[texts_here, cols:]
            total = jnp.zeros((count, cols), jnp.float32)
            for head in range(cols // HEAD_DIM):
                q_head, g_head = pick_head(queries[rows], head), pick_head(context[rows], head)
                scores = jnp.where(place_of < text_lens[slot], dot_nt(keys, q_head), MASKED_SCORE)
                weights = jnp.exp(scores - jnp.max(scores, axis=0, keepdims=True))
                weights = weights * (1.0 / jnp.sum(weights, axis=0, keepdims=True))
                dkv_acc[texts_here, cols:] += dot_nn(weights.astype(jnp.bfloat16), g_head)
                weight_grad = dot_nt(values, g_head)
                inner = jnp.sum(weights * weight_grad, axis=0, keepdims=True)
                score_grad = (weights * (weight_grad - inner)).astype(jnp.bfloat16)
                dkv_acc[texts_here, :cols] += dot_nn(score_grad, q_head)
                total += dot_tn(score_grad, pick_head(keys, head))
            q_grad.append((total * HEAD_DIM**-0.5).astype(jnp.bfloat16))
        q_grad = jnp.concatenate(q_grad, axis=0)
        five.put(part5, step, dot_nt(q_grad, cq_w[...]).astype(jnp.bfloat16))
        five.send_core(step)
        bias_g[0:1, :] += column_sum(q_grad.astype(jnp.float32))
        cq_acc[...] += dot_tn(five.take(h2, step), q_grad)

    def norm_two(step):
        rows = five.own_rows(step)
        grad_in = five.result(step)
        _, normed, inv_std = norm_forward(x1[rows, :], gains[1:2, :], gains[1:2, :])
        stats[4:5, :] += column_sum(grad_in * normed)
        stats[5:6, :] += column_sum(grad_in)
        total = dx1[rows, :] + norm_backward(grad_in, normed, inv_std, gains[1:2, :])
        stats[6:7, :] += column_sum(total)
        dx1[rows, :] = total
        five.send_gather(step, total.astype(jnp.bfloat16))

    def last(step):
        five.gathered(step)
        grads = five.take(full5, step)
        dc1_rows = dot_nt(grads, so_w[...]).astype(jnp.bfloat16)
        five.put(dc1, step, dc1_rows)
        so_acc[...] += dot_tn(five.take(c1, step), grads)

    def output(step):
        rows = four.own_rows(step)
        total = x2[rows, :] + four.result(step) + biases[2:3, :]
        y[rows, :] = jnp.where(row_of(step, chunk, width) < valid_rows, total, 0.0).astype(jnp.bfloat16)

    half = steps // 2
    late = steps + 2

    def side(half_tick):
        tick = half_tick // 2
        for begin, first in ((0, 0), (late, half)):
            for ahead, work in ((1, output), (0, four.send_cross)):
                step = tick - begin - ahead

                @pl.when((step >= 0) & (step < half) & (half_tick % 2 == 1))
                def _():
                    work(first + step)

    stages(
        steps,
        list(
            enumerate(
                [
                    three.send_cross, norm_three, three.forward, cross,
                    five.send_cross, norm_two, five.forward, last,
                ]
            )
        ),
        ring,
        side,
        late + half + 1,
    )
    dkv[...] = dkv_acc[...].astype(jnp.bfloat16)
    bias_g[1:2, :] = column_sum(dkv[:, cols:].astype(jnp.float32))
    mine4[:cols, :] = co_acc[...].astype(jnp.bfloat16)
    cq_g[...] = cq_acc[...].astype(jnp.bfloat16)
    mine4[cols : 2 * cols, :] = so_acc[...].astype(jnp.bfloat16)
    gives = [
        pltpu.make_async_copy(cq_g, g0.at[:, pl.ds(width - cols, cols)], give_sem.at[0]),
        pltpu.make_async_copy(mine4.at[pl.ds(0, 2 * cols), :], g1.at[pl.ds(0, 2 * cols), :], give_sem.at[1]),
    ]
    for give in gives:
        give.start()

    def finish(step, carry):
        three.finish(step)
        four.finish(step, False)
        five.finish(step)
        return carry

    lax.fori_loop(0, steps, finish, 0)
    ring.finish()
    for give in gives:
        give.wait()


def turn(
    count, third, ffn_part, in_g, out_g, out_grad, lens, text_lens,
    x1, x2, h2, q2, c2, kv2, c1, gains, biases, co_w, cq_w, so_w,
):
    rows, cols = c1.shape
    own, width = x1.shape
    chunk = own // STEPS
    bf, f32 = jnp.bfloat16, jnp.float32
    shape = jax.ShapeDtypeStruct
    vmem = pl.BlockSpec(memory_space=pltpu.VMEM)
    hbm = pl.BlockSpec(memory_space=pl.ANY)
    hop = hop_scratch(own, chunk, width)
    far = [pltpu.VMEM((own, width), bf)] * 2 + hop
    return pl.pallas_call(
        functools.partial(turn_kernel, count=count),
        in_specs=[hbm] * 5 + [pl.BlockSpec(memory_space=pltpu.SMEM)] * 2 + [hbm] * 7 + [vmem] * 2 + [hbm] * 3,
        out_specs=[hbm] * 4 + [vmem] * 6,
        out_shape=[
            pltpu.HBM(in_g.shape, bf),
            pltpu.HBM(out_g.shape, bf),
            pltpu.HBM((width, width), bf),
            pltpu.HBM((width, width), bf),
            shape((own, width), bf),
            shape((own, width), f32),
            shape((rows, cols), bf),
            shape(kv2.shape, bf),
            shape((2, cols), f32),
            shape((8, width), f32),
        ],
        scratch_shapes=[pltpu.VMEM(a.shape, a.dtype) for a in (x1, x2, h2, q2, c2, kv2, c1, co_w, cq_w, so_w)]
        + [
            pltpu.SemaphoreType.DMA((10,)),
            pltpu.VMEM((width, cols), bf),
            pltpu.SemaphoreType.DMA((2,)),
            pltpu.VMEM((own, width), bf),
            pltpu.SemaphoreType.DMA,
        ]
        + far
        + far
        + [pltpu.VMEM((rows, width), bf)]
        + hop
        + [pltpu.VMEM((rows, width), bf)] * 2
        + [
            pltpu.VMEM((cols, width), f32),
            pltpu.VMEM((width, cols), f32),
            pltpu.VMEM((cols, width), f32),
            pltpu.VMEM(kv2.shape, f32),
            pltpu.SemaphoreType.DMA((2, 2)),
        ]
        + ring_scratch(count, (width // count, width)),
        compiler_params=pltpu.CompilerParams(collective_id=1, has_side_effects=True, vmem_limit_bytes=60 * MIB),
        cost_estimate=pl.CostEstimate(flops=100 * 10**9, bytes_accessed=24 * MIB, transcendentals=4 * MIB),
        name="turn",
    )(
        third, ffn_part, in_g, out_g, out_grad, lens, text_lens,
        x1, x2, h2, q2, c2, kv2, c1, gains, biases, co_w, cq_w, so_w,
    )


SMALL = 16
NORM_ROWS = 9


class Small:
    def __init__(self, count, block, near, far, sems):
        self.count, self.mine, self.near, self.far, self.sems = count, block, near, far, sems
        self.index, self.core, self.cross, _ = place()
        self.spot, *self.peers = ring_place(count)

    def near_copy(self, kind):
        owner = self.cross if kind == 2 else self.index
        return remote(self.near.at[owner], self.near.at[owner], self.sems, 0, kind, (self.cross, self.core, self.core)[kind])

    def far_copy(self, way, step):
        block = self.far.at[(self.spot + (2 * way - 1) * step + self.count) % self.count]
        return remote(block, block, self.sems, 1 + way, step, self.peers[way], "wide")

    def begin(self):
        self.near[self.index] = self.mine[...]
        self.near_copy(0).start()
        self.near_copy(1).start()

    def forward(self):
        self.near_copy(0).wait_recv()
        self.near_copy(2).start()

    def launch(self):
        self.near_copy(1).wait_recv()
        self.near_copy(2).wait_recv()
        both = self.near[0]
        for owner in range(1, NARROW):
            both += self.near[owner]
        row = lax.broadcasted_iota(jnp.int32, both.shape, 0)
        self.far[self.spot] = jnp.where(row < SMALL - NORM_ROWS, self.mine[...], both)
        self.far_copy(0, 0).start()
        self.far_copy(1, 0).start()

    def rotate(self, step):
        for way in range(2):
            steps = self.count // 2 - way

            @pl.when(step < steps)
            def _():
                self.far_copy(way, step).wait_recv()

            @pl.when(step < steps - 1)
            def _():
                self.far_copy(way, step + 1).start()

    def finish(self, out):
        for kind in range(3):
            self.near_copy(kind).wait_send()

        for way in range(2):

            def body(step, carry):
                self.far_copy(way, step).wait_send()
                return carry

            lax.fori_loop(0, self.count // 2 - way, body, 0)
        out[...] = jnp.zeros_like(out)

        def add(spot, carry):
            out[...] += self.far[spot]
            return carry

        lax.fori_loop(0, self.count, add, 0)


def last_kernel(
    g0, g1, all_units, far_dqkv, far_dkv, far_dx1, far_qkv, far_kv, self_b, cross_b, ffn_b, stats, gains,
    sum0, sum1, units_g, text_g, small_sum,
    dqkv, dkv, dx1, qkv_w, kv_w, arrive_sem, units, own_sem, part6, core6, fromx6, sem6, part7, core7, fromx7, sem7,
    block, near, far, small_sem, *ring_refs, count,
):
    steps, chunk, width = fromx6.shape
    text_steps = fromx7.shape[0]

    def ring_view(ref, way, half, shard):
        high = width // count
        return ref.at[pl.ds(pl.multiple_of(shard * high, high), high), pl.ds(half * (width // 2), width // 2)]

    ring = Ring(count, (g0, g1), (sum0, sum1), ring_view, *ring_refs)
    small = Small(count, block, near, far, small_sem)
    fetch = own_copy(all_units, units, own_sem)
    fetch.start()
    greet(*ring.peers)
    ring.start()
    arriving = moves(
        (far_dqkv, far_dkv, far_dx1, far_qkv, far_kv), (dqkv, dkv, dx1, qkv_w, kv_w), arrive_sem
    )
    for copy in arriving:
        copy.start()
    six = Hop(part6, core6, fromx6, None, sem6, chunk)
    seven = Hop(part7, core7, fromx7, None, sem7, chunk)
    fetch.wait()
    for copy in arriving:
        copy.wait()
    block[...] = jnp.zeros_like(block)
    cols = self_b.shape[1]
    for row in range(2):
        block[0:1, row * cols : (row + 1) * cols] = self_b[row : row + 1, :]
        block[0:1, (2 + row) * cols : (3 + row) * cols] = cross_b[row : row + 1, :]
        block[1 + row : 2 + row, :] = ffn_b[:, row * width : (row + 1) * width]
    block[SMALL - NORM_ROWS : SMALL - 2, :] = stats[:7, :]
    gain = gains[0:1, :]

    def project(step):
        grads = six.take(dqkv, step)
        total = dot_nt(grads[:, :cols], qkv_w[0]) + dot_nt(grads[:, cols : 2 * cols], qkv_w[1])
        six.put(part6, step, (total + dot_nt(grads[:, 2 * cols :], qkv_w[2])).astype(jnp.bfloat16))
        six.send_core(step)

    def norm_one(step):
        rows = six.own_rows(step)
        grad_in = six.result(step)
        _, normed, inv_std = norm_forward(units[rows, :].astype(jnp.float32), gain, gain)
        block[SMALL - 2 : SMALL - 1, :] += column_sum(grad_in * normed)
        block[SMALL - 1 : SMALL, :] += column_sum(grad_in)
        units_g[rows, :] = dx1[rows, :] + norm_backward(grad_in, normed, inv_std, gain)

    def text_only(work):
        def stage(step):
            @pl.when(step < text_steps)
            def _():
                work(step)

        return stage

    def text_project(step):
        seven.put(part7, step, dot_nt(seven.take(dkv, step), kv_w[...]).astype(jnp.bfloat16))
        seven.send_core(step)

    def text_result(step):
        text_g[seven.own_rows(step), :] = seven.result(step)

    ready = 2 * (steps + 1)

    def extra(half_tick):
        for when, work in enumerate((small.begin, small.forward, small.launch)):
            pl.when(half_tick == ready + when)(work)
        step = half_tick - ready - 3

        @pl.when((step >= 0) & (step < count // 2))
        def _():
            small.rotate(step)

    stages(
        steps,
        list(
            enumerate(
                [
                    project, six.send_cross, norm_one, text_only(text_project), text_only(seven.send_cross), text_only(text_result),
                ]
            )
        ),
        ring,
        extra,
        max((ready + 4 + count // 2) // 2, 2 * (count - 1)),
    )

    def finish(step, carry):
        six.finish(step, False)
        text_only(lambda s: seven.finish(s, False))(step)
        return carry

    lax.fori_loop(0, steps, finish, 0)
    ring.finish()
    small.finish(small_sum)


def last(count, g0, g1, units, dqkv, dkv, dx1, qkv_w, kv_w, *rest):
    rows = dqkv.shape[0]
    own, width = dx1.shape
    chunk = own // STEPS
    text_own = dkv.shape[0] // NARROW
    bf, f32 = jnp.bfloat16, jnp.float32
    shape = jax.ShapeDtypeStruct
    vmem = pl.BlockSpec(memory_space=pltpu.VMEM)
    hbm = pl.BlockSpec(memory_space=pl.ANY)
    hop = hop_scratch(own, chunk, width)
    return pl.pallas_call(
        functools.partial(last_kernel, count=count),
        in_specs=[hbm] * 8 + [vmem] * len(rest),
        out_specs=[hbm] * 2 + [vmem] * 3,
        out_shape=[
            pltpu.HBM(g0.shape, bf),
            pltpu.HBM(g1.shape, bf),
            shape((own, width), f32),
            shape((text_own, width), f32),
            shape((SMALL, width), f32),
        ],
        scratch_shapes=[pltpu.VMEM(a.shape, a.dtype) for a in (dqkv, dkv, dx1, qkv_w, kv_w)]
        + [pltpu.SemaphoreType.DMA((5,)), pltpu.VMEM((own, width), bf), pltpu.SemaphoreType.DMA]
        + [pltpu.VMEM((rows, width), bf)]
        + hop
        + [pltpu.VMEM((dkv.shape[0], width), bf)]
        + hop_scratch(text_own, chunk, width)
        + [
            pltpu.VMEM((SMALL, width), f32),
            pltpu.VMEM((NARROW, SMALL, width), f32),
            pltpu.VMEM((count, SMALL, width), f32),
            pltpu.SemaphoreType.DMA((2, 3, max(count // 2, 3))),
        ]
        + ring_scratch(count, (width // count, width // 2)),
        compiler_params=pltpu.CompilerParams(collective_id=2, has_side_effects=True, vmem_limit_bytes=58 * MIB),
        cost_estimate=pl.CostEstimate(flops=30 * 10**9, bytes_accessed=16 * MIB, transcendentals=0),
        name="last",
    )(g0, g1, units, dqkv, dkv, dx1, qkv_w, kv_w, *rest)


def unpack_kernel(
    sum0, sum1, small, y_in, units_in, text_in,
    qkv_g, cq_g, co_g, so_g, kv_g, gain_g, shift_g, bias_g, self_b, cross_b, ffn_b, y, units_g, text_g,
):
    cols = cq_g.shape[1]
    step = pl.program_id(0)
    y[...] = y_in[...]
    units_g[...] = units_in[...]
    text_g[...] = text_in[...]
    for part in range(3):
        qkv_g[part] = sum0[:, part * cols : (part + 1) * cols].astype(jnp.float32)
    cq_g[...] = sum0[:, 3 * cols :].astype(jnp.float32)
    for when, ref in enumerate((co_g, so_g)):

        @pl.when(step == when)
        def _():
            ref[...] = sum1[...].astype(jnp.float32)

    half = kv_g.shape[0] // 2
    for when in range(half // cols):

        @pl.when(step == 2 + when)
        def _():
            for side in range(2):
                rows = slice(side * half + when * cols, side * half + (when + 1) * cols)
                for part in range(2):
                    first = (2 * side + part) * cols
                    kv_g[rows, part, :] = sum1[:, first : first + cols].astype(jnp.float32)

    @pl.when(step == 0)
    def _():
        norms = small[SMALL - NORM_ROWS :, :]
        for ref, order in ((gain_g, (7, 4, 0)), (shift_g, (8, 5, 1)), (bias_g, (6, 3, 2))):
            for row, source in enumerate(order):
                ref[row : row + 1, :] = norms[source : source + 1, :]
        width = small.shape[1]
        for row in range(2):
            self_b[row : row + 1, :] = small[0:1, row * cols : (row + 1) * cols]
            cross_b[row : row + 1, :] = small[0:1, (2 + row) * cols : (3 + row) * cols]
            ffn_b[:, row * width : (row + 1) * width] = small[1 + row : 2 + row, :]


def unpack(sum0, sum1, small, cols, hidden, *row_outs):
    width = sum0.shape[0]
    steps = width // cols
    f32 = jnp.float32
    block = lambda a: pl.BlockSpec((a.shape[0] // steps,) + a.shape[1:], lambda i: (i, 0))
    whole = lambda a: pl.BlockSpec(a.shape, lambda i: (0,) * len(a.shape))
    fixed = [
        jax.ShapeDtypeStruct(dims, f32)
        for dims in (
            (cols, width), (cols, width), (width, 2, cols),
            (3, width), (3, width), (3, width), (2, cols), (2, cols), (1, hidden),
        )
    ]
    moving = [jax.ShapeDtypeStruct((3, width, cols), f32), jax.ShapeDtypeStruct((width, cols), f32)]
    return pl.pallas_call(
        unpack_kernel,
        grid=(steps,),
        in_specs=[block(sum0), block(sum1), whole(small)] + [block(a) for a in row_outs],
        out_specs=[pl.BlockSpec((3, cols, cols), lambda i: (0, i, 0)), block(moving[1])]
        + [whole(a) for a in fixed]
        + [block(a) for a in row_outs],
        out_shape=moving + fixed + [jax.ShapeDtypeStruct(a.shape, a.dtype) for a in row_outs],
        compiler_params=pltpu.CompilerParams(vmem_limit_bytes=60 * MIB),
        name="unpack",
    )(sum0, sum1, small, *row_outs)


def local(
    units,
    text,
    out_grad,
    unit_lengths,
    text_lengths,
    bucket_counts,
    norm_gain,
    norm_shift,
    self_qkv,
    self_bias,
    self_out,
    cross_q,
    cross_kv,
    cross_bias,
    cross_out,
    ffn_in,
    ffn_in_bias,
    ffn_out,
    out_bias,
):
    slot_live = jnp.arange(unit_lengths.shape[0], dtype=jnp.int32) < bucket_counts[0]
    lengths = jnp.where(slot_live, unit_lengths, 0)
    qkv_weights = jnp.transpose(self_qkv, (1, 0, 2))
    kv_weights = cross_kv.reshape(cross_kv.shape[0], -1)
    count = lax.axis_size("wide")
    first_in, queries, key_rows, value_rows, text_kv, self_context, self_logs = front(
        lengths, units, text, norm_gain, norm_shift, qkv_weights, self_bias, kv_weights, cross_bias
    )
    (
        ffn_part,
        third_part,
        ffn_in_grad,
        ffn_out_grad,
        second_all,
        cross_queries,
        cross_context,
        resid_one,
        resid_two,
        ffn_bias_sum,
    ) = middle(
        units,
        out_grad,
        ffn_in,
        ffn_out,
        self_out,
        cross_q,
        cross_out,
        lengths,
        text_lengths,
        self_context,
        text_kv,
        norm_gain,
        norm_shift,
        out_bias,
        cross_bias,
        ffn_in_bias,
    )
    in_sum, out_sum, grads_one, grads_two, output, resid_one_grad, context_grad, text_kv_grad, cross_bias_sum, stats = turn(
        count,
        third_part,
        ffn_part,
        ffn_in_grad,
        ffn_out_grad,
        out_grad,
        lengths,
        text_lengths,
        resid_one,
        resid_two,
        second_all,
        cross_queries,
        cross_context,
        text_kv,
        self_context,
        norm_gain,
        out_bias,
        cross_out,
        cross_q,
        self_out,
    )
    qkv_grad, grads_one, grads_two, self_bias_sum, ffn_in_grad, ffn_out_grad = back(
        lengths,
        queries,
        key_rows,
        value_rows,
        context_grad,
        self_context,
        self_logs,
        first_in,
        text,
        text_kv_grad,
        in_sum,
        out_sum,
        grads_one,
        grads_two,
    )
    summed_one, summed_two, units_grad, text_grad, small = last(
        count,
        grads_one,
        grads_two,
        units,
        qkv_grad,
        text_kv_grad,
        resid_one_grad,
        qkv_weights,
        kv_weights,
        self_bias_sum,
        cross_bias_sum,
        ffn_bias_sum,
        stats,
        norm_gain,
    )
    (
        self_qkv_grad,
        cross_q_grad,
        cross_out_grad,
        self_out_grad,
        cross_kv_grad,
        gain_grad,
        shift_grad,
        bias_grad,
        self_bias_grad,
        cross_bias_grad,
        ffn_in_bias_grad,
        output,
        units_grad,
        text_grad,
    ) = unpack(
        summed_one, summed_two, small, queries.shape[1], ffn_in_bias.shape[0], output, units_grad, text_grad
    )
    self_qkv_grad = jnp.transpose(self_qkv_grad, (1, 0, 2))
    ffn_in_bias_grad = ffn_in_bias_grad.reshape(-1)
    return (
        output,
        units_grad,
        text_grad,
        gain_grad,
        shift_grad,
        self_qkv_grad,
        self_bias_grad,
        self_out_grad,
        cross_q_grad,
        cross_kv_grad,
        cross_bias_grad,
        cross_out_grad,
        ffn_in_grad,
        ffn_in_bias_grad,
        ffn_out_grad,
        bias_grad,
    )


def solution(mesh):
    placed = (
        P("wide", None),
        P("wide", None),
        P("wide", None),
        P("wide"),
        P("wide"),
        P("wide"),
        P(),
        P(),
        P(None, None, "narrow"),
        P(None, "narrow"),
        P("narrow", None),
        P(None, "narrow"),
        P(None, None, "narrow"),
        P(None, "narrow"),
        P("narrow", None),
        P(None, "narrow"),
        P("narrow"),
        P("narrow", None),
        P(),
    )
    return jax.shard_map(
        local,
        mesh=mesh,
        in_specs=placed,
        out_specs=(
            P(("wide", "narrow"), None),
            P(("wide", "narrow"), None),
            P(("wide", "narrow"), None),
            P(),
            P(),
            P(None, None, "narrow"),
            P(None, "narrow"),
            P("narrow", None),
            P(None, "narrow"),
            P(None, None, "narrow"),
            P(None, "narrow"),
            P("narrow", None),
            P(None, "narrow"),
            P("narrow"),
            P("narrow", None),
            P(),
        ),
        check_vma=False,
    )
```
